32 devices in a mesh: lat: 4 (over z), lon: 8 (over y, x, core).
Axes of the slice: x: 2, y: 2, z: 4, core: 2. Of those that a mesh axis runs over, the one named last changes fastest.
Arguments:
- atm_flux: bfloat16 [8, 256, 1024], P(None, 'lat', 'lon'), may hold values from -6 to 6
- sea_mask: int32 [256, 1024], P('lat', 'lon'), may hold values 0 or 1
- src_block: int32 [8192], P(('lat', 'lon')), may hold values from 0 to 63
- dest_dev: int32 [8192, 1], P(('lat', 'lon')), may hold values from 0 to 31; in each aligned block of 256 rows (0 to 255, 256 to 511, ...) at most 16 rows name the same one
- dest_block: int32 [8192], P(('lat', 'lon')), may hold values from 0 to 31
- intersection_weights: bfloat16 [8192, 128, 128], P(('lat', 'lon')), may hold values from -0.5 to 0.5
- coupling: float32 [4, 8], replicated, may hold values from -2 to 2
- inverses: float32 [4, 128, 8, 80, 80], P(None, 'lat', 'lon'), may hold values from -2 to 2
- ocean_state: float32 [4, 80, 128, 1024], P(None, None, 'lat', 'lon'), may hold values from -6 to 6
- depth_levels: int32 [128, 1024], P('lat', 'lon'), may hold values from 0 to 80
Outputs:
- ocean_out: float32 [4, 80, 128, 1024], P(None, None, 'lat', 'lon')
The draws below stay inside these ranges and needn't reach their ends.
Inputs may be any that keep to these rules, and one draw needn't show every extreme that they name: `dest_dev`: among the 256 pairs of one device no destination device is named more than 16 times, and in every draw some device names one destination exactly 16 times.
All inputs are finite; a program needn't handle non-finite values. No bound on the sum of `sea_mask` on one device may be relied on, other than what follows from the above.
Results may differ from the reference program's by a relative error of at most 0.0003.
Values sent between devices are 32-bit elements; how exact they have to be, the bound alone decides.
No kernel may reach another device: no remote copies, remote signals or barrier semaphores. Data moves between devices by JAX's collectives and lax.ppermute only.
A program may use at most 128 MiB of HBM per device.

```python
import math
import jax
import jax.numpy as jnp
import numpy as np
from jax import lax

F = 8
Q = 4
LEV = 80
OX = 128
AX = 128
AY = 64
OY = 32
K = 256
CAP = 16
PAIRS = 8192
ALAT = 256
ALON = 1024
OLAT = 128
OLON = 1024
N_LAT = 4
N_LON = 8


def draw_inverses(key, part):
    first_key, second_key = jax.random.split(jax.random.fold_in(key, 17))
    shape = (Q, OLAT, N_LON, LEV, LEV)
    noise = jnp.clip(jax.random.normal(first_key, shape, jnp.float32), -4.0, 4.0) * (0.3 / math.sqrt(LEV))
    diagonal = jax.random.uniform(second_key, (Q, OLAT, N_LON, 1, LEV), jnp.float32, 0.6, 1.2)
    levels = jnp.arange(LEV, dtype=jnp.int32)
    unit = (levels[:, None] == levels[None, :]).astype(jnp.float32)
    return noise + unit * diagonal


def place_ends(result, rng, low, top_value):
    longest = result.shape.index(max(result.shape))
    spots = []
    for shift in (0, 1):
        where = [jax.random.randint(jax.random.fold_in(rng, axis), (), 0, length) for axis, length in enumerate(result.shape)]
        where[longest] = (where[longest] + shift) % result.shape[longest]
        spots.append(tuple(where))
    return result.at[spots[0]].set(low).at[spots[1]].set(top_value)


def block_scale(rng, shape, cuts, least, largest):
    loudness = 1.0
    for dim, parts in cuts:
        heights = jax.random.uniform(jax.random.fold_in(jax.random.fold_in(rng, 6), dim), (parts,), jnp.float32, least / len(cuts), largest / len(cuts))
        loudness = loudness * jnp.repeat(jnp.exp(heights), shape[dim] // parts).reshape((-1,) + (1,) * (len(shape) - 1 - dim))
    return loudness


def deal_out(rng, own, number, rows, amount, top, bound, skew):
    order = jax.random.permutation(rng, amount)
    heavy_load, ordinary = load_shares(amount, rows * top, bound, skew, True), load_shares(amount, rows * top, bound, skew, False)
    places = jnp.arange(amount)

    def named(lengths, turn):
        used = int((lengths > 0).sum())
        fixed = max(1, used // 4)
        shifted = fixed + (places - fixed + turn * (used - fixed)) % max(1, amount - fixed)
        return jnp.zeros((amount,), jnp.int32).at[order[jnp.where(places < fixed, places, shifted)]].set(jnp.asarray(lengths, jnp.int32))

    lengths = jnp.where(number % 4 == 0, named(heavy_load, number // 4), named(ordinary, number - number // 4 - 1))
    mixed = jax.random.permutation(jax.random.fold_in(own, 3), amount)
    giver, taker = mixed[0:amount // 2 * 2:2], mixed[1:amount // 2 * 2:2]
    slack = jnp.minimum(lengths[giver] - 1, bound - lengths[taker]) // 2
    slack = jnp.where((giver == order[0]) | (taker == order[0]) | (lengths[taker] == 0), 0, jnp.maximum(slack, 0))
    shifted = jax.random.randint(jax.random.fold_in(own, 4), (amount // 2,), 0, 1 << 20) % (slack + 1)
    lengths = lengths.at[giver].add(-shifted).at[taker].add(shifted)
    items = jnp.searchsorted(jnp.cumsum(lengths), jnp.arange(rows * top), side="right").astype(jnp.int32)
    grid = items.reshape(top, rows).T
    grid = grid[jax.random.permutation(jax.random.fold_in(own, 1), rows)]
    turn = jax.random.randint(jax.random.fold_in(own, 2), (rows, 1), 0, top)
    return jnp.take_along_axis(grid, (jnp.arange(top)[None, :] + turn) % top, axis=1)


def load_shares(number_of, total, reach, slope, full):
    weights = [(1 << 20) // math.isqrt(standing ** slope) + 1 for standing in range(1, number_of + 1)]
    largest = reach if full else min(reach, max(-(-total // number_of), total * weights[0] // sum(weights)))
    least = 1 if total - largest >= number_of - 1 else 0
    given, surplus = [largest] + [least] * (number_of - 1), total - largest - least * (number_of - 1)
    while surplus > 0:
        movable = [i for i in range(1, number_of) if given[i] < largest] or [i for i in range(1, number_of) if given[i] < reach]
        mass, budget = sum([weights[i] for i in movable]), surplus
        for i in movable:
            more = min(reach - given[i], max(1, budget * weights[i] // mass), surplus)
            given[i] = given[i] + more
            surplus = surplus - more
    return np.array(given)


def bell_draw(key, shape, deviation, reach, cuts=(), kind=jnp.bfloat16):
    entries = deviation * jax.random.normal(key, shape, jnp.float32)
    if cuts:
        entries = entries * block_scale(key, shape, cuts, -0.22, 0.18)
    return jnp.clip(entries, -reach, reach).astype(kind)


def setup_inputs(seed: int = 0) -> dict:
    splits = jax.random.split(jax.random.key(seed), 11)
    atm_flux = bell_draw(splits[0], (F, ALAT, ALON), 1.0, 6.0, ((1, 4), (2, 8)))
    sea_mask = place_ends((jax.random.randint(splits[1], (ALAT, ALON), 0, 10) < 7).astype(jnp.int32), jax.random.fold_in(splits[1], 1), 0, 1)
    src_block = place_ends(jax.random.randint(splits[2], (PAIRS,), 0, AY), jax.random.fold_in(splits[2], 1), 0, AY - 1).astype(jnp.int32)
    dest_dev_keys = jax.random.split(jax.random.fold_in(splits[3], 1), PAIRS // K)
    dest_dev_turns = jax.random.permutation(jax.random.fold_in(splits[3], 3), PAIRS // K)
    dest_dev = jax.vmap(lambda own, number: deal_out(jax.random.fold_in(splits[3], 2), own, number, K, N_LAT * N_LON, 1, CAP, 1))(dest_dev_keys, dest_dev_turns).reshape((PAIRS, 1))
    dest_block = place_ends(jax.random.randint(splits[4], (PAIRS,), 0, OY), jax.random.fold_in(splits[4], 1), 0, OY - 1).astype(jnp.int32)
    intersection_weights = bell_draw(splits[5], (PAIRS, AX, OX), AX ** -0.5, 0.5, ((0, 32),))
    coupling = bell_draw(splits[6], (Q, F), F ** -0.5, 2.0, (), jnp.float32)
    inverses = draw_inverses(jax.random.fold_in(splits[10], 71), 0)
    ocean_state = bell_draw(splits[8], (Q, LEV, OLAT, OLON), 1.0, 6.0, ((2, 4), (3, 8)), jnp.float32)
    depth_levels = place_ends(jax.random.randint(splits[9], (OLAT, OLON), 0, LEV + 1), jax.random.fold_in(splits[9], 1), 0, LEV).astype(jnp.int32)
    return dict(atm_flux=atm_flux, sea_mask=sea_mask, src_block=src_block, dest_dev=dest_dev, dest_block=dest_block, intersection_weights=intersection_weights, coupling=coupling, inverses=inverses, ocean_state=ocean_state, depth_levels=depth_levels)


diffusion_rate = 0.2


def reference(atm_flux, sea_mask, src_block, dest_dev, dest_block, intersection_weights, coupling, inverses, ocean_state, depth_levels):
    dev_total = N_LAT * N_LON
    masked = atm_flux * sea_mask.astype(jnp.bfloat16)
    pair_dev = jnp.arange(dev_total * K, dtype=jnp.int32) // K
    row_index = (pair_dev // N_LON) * AY + src_block
    col_index = (pair_dev % N_LON)[:, None] * AX + jnp.arange(AX, dtype=jnp.int32)[None, :]
    taken = masked[:, row_index[:, None], col_index]
    taken = jnp.transpose(taken, (1, 0, 2)).reshape(dev_total, K, F, AX)
    weights_dev = intersection_weights.reshape(dev_total, K, AX, OX)

    def regrid(pieces):
        rows_part, weights_part = pieces
        return jnp.einsum("kfa,kao->kfo", rows_part.astype(jnp.float32), weights_part.astype(jnp.float32), precision=lax.Precision.HIGHEST)

    contrib = lax.map(regrid, (taken, weights_dev)).reshape(dev_total * K, F, OX)
    target = dest_dev[:, 0] * OY + dest_block
    summed = jax.ops.segment_sum(contrib, target, num_segments=dev_total * OY)
    flux = summed.reshape(N_LAT, N_LON, OY, F, OX).transpose(3, 0, 2, 1, 4).reshape(F, N_LAT * OY, N_LON * OX)
    forcing = jnp.einsum("qf,fij->qij", coupling, flux, precision=lax.Precision.HIGHEST)
    levels = jnp.arange(LEV, dtype=jnp.int32)[:, None, None]
    active = levels < depth_levels[None]
    surface = ocean_state[:, 0] + forcing
    rhs = jnp.concatenate([surface[:, None], ocean_state[:, 1:]], axis=1)
    rhs = jnp.where(active[None], rhs, jnp.float32(0.0))
    rhs_blocks = rhs.reshape(Q, LEV, N_LAT * OY, N_LON, OX)
    solved = jnp.einsum("qinlm,qminx->qlinx", inverses, rhs_blocks, precision=lax.Precision.HIGHEST)
    solved = solved.reshape(Q, LEV, N_LAT * OY, N_LON * OX)
    mixed = jnp.where(active[None], solved, ocean_state)
    mixed_pad = jnp.pad(mixed, ((0, 0), (0, 0), (1, 1), (0, 0)))
    active_pad = jnp.pad(active, ((0, 0), (1, 1), (0, 0)))
    neighbours = [
        (jnp.roll(mixed, -1, axis=3), jnp.roll(active, -1, axis=2)),
        (jnp.roll(mixed, 1, axis=3), jnp.roll(active, 1, axis=2)),
        (mixed_pad[:, :, 2:], active_pad[:, 2:]),
        (mixed_pad[:, :, :-2], active_pad[:, :-2]),
    ]
    total = jnp.zeros_like(mixed)
    for values, flags in neighbours:
        total = total + jnp.where(flags[None], values - mixed, jnp.float32(0.0))
    return mixed + diffusion_rate * jnp.where(active[None], total, jnp.float32(0.0))
```

```python
import functools

import jax
import jax.numpy as jnp
from jax import lax
from jax.experimental import pallas as pl
from jax.experimental.pallas import tpu as pltpu
from jax.sharding import PartitionSpec as P

diffusion_rate = 0.2
LANES = 128
SUB = 8
f32 = jnp.float32
bf16 = jnp.bfloat16


def split(x):
    high = x.astype(bf16)
    return high, (x - high.astype(f32)).astype(bf16)


def iota(shape, dim):
    return lax.broadcasted_iota(jnp.int32, shape, dim)


def regrid_kernel(cap, batch, unroll, src, dev, blk, coupling, atm, mask, weights, out, rows, count):
    step = pl.program_id(0)
    fluxes, atm_rows, _ = atm.shape
    fields = coupling.shape[0]
    devices = out.shape[0]

    @pl.when(step == 0)
    def _():
        def clear(d, carry):
            count[d] = 0
            out[d, 0 : fields * cap] = jnp.zeros((fields * cap, LANES), f32)
            out[d, fields * cap :] = jnp.full((SUB, LANES), -1.0, f32)
            return carry

        lax.fori_loop(0, devices, clear, 0)
        for tile in range(atm_rows // 16):
            here = slice(tile * 16, tile * 16 + 16)
            sea = mask[here, :].astype(f32)
            flux = [atm[f, here, :].astype(f32) * sea for f in range(fluxes)]
            for q in range(fields):
                total = coupling[q, 0] * flux[0]
                for f in range(1, fluxes):
                    total = total + coupling[q, f] * flux[f]
                high = total.astype(bf16).astype(f32)
                rows[pl.ds(tile * 16 * SUB + q, 16, stride=SUB), :] = high
                rows[pl.ds(tile * 16 * SUB + fields + q, 16, stride=SUB), :] = total - high

    lane = iota((1, LANES), 1) % cap

    def some(k, carry):
        for u in range(unroll):
            n = k * unroll + u
            p = step * batch + n
            d = dev[p]
            slot = jnp.minimum(count[d], cap - 1)
            count[d] = slot + 1
            x = rows[pl.ds(pl.multiple_of(src[p] * SUB, SUB), SUB), :].astype(bf16)
            both = jnp.dot(x, weights[n], preferred_element_type=f32)
            total = both[0:fields] + both[fields : 2 * fields]
            for q in range(fields):
                out[d, pl.ds(q * cap + slot, 1), :] = total[q : q + 1]
            ids = out[d, pl.ds(fields * cap, 1), :]
            out[d, pl.ds(fields * cap, 1), :] = jnp.where(lane == slot, blk[p].astype(f32), ids)
        return carry

    lax.fori_loop(0, batch // unroll, some, 0)


def regrid(cap, devices, src, dev, blk, coupling, atm, mask, weights):
    pairs, depth, width = weights.shape
    fields = coupling.shape[0]
    batch = 32
    whole = pl.BlockSpec(memory_space=pltpu.VMEM)
    smem = pl.BlockSpec(memory_space=pltpu.SMEM)
    tall = fields * cap + SUB
    return pl.pallas_call(
        functools.partial(regrid_kernel, cap, batch, 8),
        grid=(pairs // batch,),
        in_specs=[smem, smem, smem, smem, whole, whole, pl.BlockSpec((batch, depth, width), lambda s: (s, 0, 0))],
        out_specs=pl.BlockSpec((devices, tall, LANES), lambda s: (0, 0, 0)),
        out_shape=jax.ShapeDtypeStruct((devices, tall, LANES), f32),
        scratch_shapes=[
            pltpu.VMEM((atm.shape[1] * SUB, LANES), f32),
            pltpu.SMEM((devices,), jnp.int32),
        ],
        compiler_params=pltpu.CompilerParams(vmem_limit_bytes=24 << 20),
        cost_estimate=pl.CostEstimate(flops=2 * 8 * pairs * depth * width, bytes_accessed=10 << 20, transcendentals=0),
        name="regrid",
    )(src, dev, blk, coupling, atm, mask, weights)


def mix_kernel(depth_ref, state, inv, mixed, north, south, side):
    chunk = pl.program_id(1)
    chunks = pl.num_programs(1)
    levels = state.shape[1]
    oy = depth_ref.shape[0]
    flat = state.reshape(levels * SUB, LANES)
    level = iota((levels, LANES), 0)
    lane = iota((levels, LANES), 1)

    def message(ref, value, depth_row, matrix):
        ref[0, 0:levels] = value
        square = jnp.concatenate([matrix, jnp.zeros((levels, LANES - levels), f32)], axis=1)
        square = jnp.concatenate([square, jnp.zeros((LANES - levels, LANES), f32)], axis=0)
        first = square.T[0:1]
        ref[0, levels : levels + SUB] = jnp.concatenate(
            [depth_row.astype(f32), first, jnp.zeros((SUB - 2, LANES), f32)], axis=0
        )

    @pl.when(chunk == 0)
    def _():
        side[0, 0:levels] = jnp.zeros((levels, LANES), f32)
        turned = jnp.concatenate([depth_ref[...].astype(f32), jnp.zeros((LANES - oy, LANES), f32)], axis=0).T
        edge = turned[0:1] + pltpu.roll(turned[LANES - SUB :], oy, 1)[SUB - 1 : SUB]
        side[0, levels : levels + SUB] = jnp.broadcast_to(edge, (SUB, LANES))

    depth = depth_ref[pl.ds(pl.multiple_of(chunk * SUB, SUB), SUB), :]
    edges = side[0, 0:levels]
    for i in range(SUB):
        active = level < depth[i : i + 1]
        x = flat[pl.ds(i, levels, stride=SUB), :]
        a = inv[0, i, 0]
        a_high, a_low = split(a)
        r_high, r_low = split(jnp.where(active, x, 0.0))
        product = jnp.dot(
            jnp.concatenate([a_high, a_low], axis=0),
            jnp.concatenate([r_high, r_low], axis=1),
            preferred_element_type=f32,
        )
        solved = product[:levels, :LANES] + (product[levels:, :LANES] + product[:levels, LANES:])
        m = jnp.where(active, solved, x)
        mixed[0, i] = m
        row = chunk * SUB + i
        edges = jnp.where(lane == row, m[:, 0:1], edges)
        edges = jnp.where(lane == oy + row, m[:, LANES - 1 : LANES], edges)
        edges = jnp.where(lane == 2 * oy + row, a[:, 0:1], edges)
        if i == 0:

            @pl.when(chunk == 0)
            def _():
                message(north, m, depth[0:1], a)

        if i == SUB - 1:

            @pl.when(chunk == chunks - 1)
            def _():
                message(south, m, depth[SUB - 1 : SUB], a)

    side[0, 0:levels] = edges


def mix(depth, state, inverses):
    fields, levels, oy, ox = state.shape
    edge = pl.BlockSpec((1, levels + SUB, ox), lambda q, c: (q, 0, 0))
    edge_shape = jax.ShapeDtypeStruct((fields, levels + SUB, ox), f32)
    return pl.pallas_call(
        mix_kernel,
        grid=(fields, oy // SUB),
        in_specs=[
            pl.BlockSpec(memory_space=pltpu.VMEM),
            pl.BlockSpec((1, levels, SUB, ox), lambda q, c: (q, 0, c, 0)),
            pl.BlockSpec((1, SUB, 1, levels, levels), lambda q, c: (q, c, 0, 0, 0)),
        ],
        out_specs=[pl.BlockSpec((1, SUB, levels, ox), lambda q, c: (q, c, 0, 0)), edge, edge, edge],
        out_shape=[jax.ShapeDtypeStruct((fields, oy, levels, ox), f32), edge_shape, edge_shape, edge_shape],
        compiler_params=pltpu.CompilerParams(vmem_limit_bytes=24 << 20),
        cost_estimate=pl.CostEstimate(flops=2 * 4 * fields * oy * levels * levels * ox, bytes_accessed=16 << 20, transcendentals=0),
        name="mix",
    )(depth, state, inverses)


def gather_kernel(cap, fields, oy, recv, forcing, edges):
    devices = recv.shape[0]
    group = LANES // cap
    lane = iota((1, LANES), 1) // cap
    row = iota((oy, LANES), 0).astype(f32)
    totals = [jnp.zeros((oy, LANES), f32) for _ in range(fields)]
    for tile in range(devices // group):
        ids = jnp.full((1, LANES), -1.0, f32)
        for s in range(group):
            ids = jnp.where(lane == s, recv[tile * group + s, fields * cap : fields * cap + 1, :], ids)
        hot = (row == ids).astype(f32).astype(bf16)
        for q in range(fields):
            x = jnp.concatenate(
                [recv[tile * group + s, q * cap : (q + 1) * cap, :] for s in range(group)], axis=0
            )
            high, low = split(x)
            totals[q] = totals[q] + (
                jnp.dot(hot, high, preferred_element_type=f32) + jnp.dot(hot, low, preferred_element_type=f32)
            )
    everything = jnp.concatenate(totals, axis=0)
    forcing[...] = everything
    turned = everything.T
    edges[...] = jnp.concatenate(
        [t[0:1] for t in totals]
        + [t[oy - 1 : oy] for t in totals]
        + [turned[0:1], turned[LANES - 1 : LANES], jnp.zeros((2 * SUB - 2 * fields - 2, LANES), f32)],
        axis=0,
    )


def gather(cap, fields, oy, recv):
    whole = pl.BlockSpec(memory_space=pltpu.VMEM)
    return pl.pallas_call(
        functools.partial(gather_kernel, cap, fields, oy),
        in_specs=[whole],
        out_specs=[whole, whole],
        out_shape=[jax.ShapeDtypeStruct((fields * oy, LANES), f32), jax.ShapeDtypeStruct((2 * SUB, LANES), f32)],
        compiler_params=pltpu.CompilerParams(vmem_limit_bytes=24 << 20),
        name="gather",
    )(recv)


def finish_kernel(
    depth_ref, forcing, own, mixed, above, below, north, south, east, west, g_north, g_south, g_east, g_west,
    out, z_above, z_below, z_east, z_west, column, bounds,
):
    chunk = pl.program_id(0)
    chunks = pl.num_programs(0)
    fields, _, levels, _ = mixed.shape
    oy = depth_ref.shape[0]
    level = iota((levels, LANES), 0)
    lanes = iota((SUB, LANES), 1)
    start = chunk * SUB
    flat = out.reshape(fields * levels * SUB, LANES)

    def outer_row(ref, g_ref, first):
        return ref[0, levels : levels + 1, :].astype(jnp.int32)

    def from_neighbour(target, ref, g_ref, first):
        names = jnp.concatenate(
            [ref[q, levels + 1 : levels + 2, :] for q in range(fields)]
            + [jnp.zeros((LANES - fields, LANES), f32)],
            axis=0,
        ).T
        active = level < outer_row(ref, g_ref, first)
        for q in range(fields):
            value = ref[q, 0:levels] + names[0:levels, q : q + 1] * g_ref[first + q : first + q + 1, :]
            target[q] = jnp.where(active, value, 0.0)

    def from_here(target, ref, row):
        active = level < depth_ref[pl.ds(row, 1), :]
        for q in range(fields):
            a = pltpu.roll(own[q, 0:levels], 2 * LANES - (2 * oy + row), 1)
            value = ref[q, 0] + a[:, 0:1] * forcing[pl.ds(q * oy + row, 1), :]
            target[q] = jnp.where(active, value, 0.0)

    @pl.when(chunk == 0)
    def _():
        from_neighbour(z_above, north, g_north, fields)
        for target, ref, g_ref, line, place in (
            (z_east, east, g_east, 2 * fields, 0),
            (z_west, west, g_west, 2 * fields + 1, oy),
        ):
            shift = (LANES - place) % LANES
            depth = ref[0, levels : levels + SUB, :]
            depth = pltpu.roll(depth, shift, 1) if shift else depth
            active = level < depth[0:1].astype(jnp.int32)
            line_all = jnp.broadcast_to(g_ref[line : line + 1, :], (SUB, LANES))
            for q in range(fields):
                value = ref[q, 0:levels]
                value = pltpu.roll(value, shift, 1) if shift else value
                a = pltpu.roll(ref[q, 0:levels], LANES - 2 * oy, 1)
                g = pltpu.roll(line_all, (LANES - q * oy) % LANES, 1) if q else line_all
                target[q] = jnp.where(active, value + a * g[0:1], 0.0)

    @pl.when(chunk > 0)
    def _():
        from_here(z_above, above, start - 1)
        for q in range(fields):
            z_east[q] = pltpu.roll(z_east[q], LANES - SUB, 1)
            z_west[q] = pltpu.roll(z_west[q], LANES - SUB, 1)

    @pl.when(chunk == chunks - 1)
    def _():
        from_neighbour(z_below, south, g_south, 0)

    @pl.when(chunk < chunks - 1)
    def _():
        from_here(z_below, below, start + SUB)

    for q in range(fields):
        column[q] = pltpu.roll(own[q, 0:levels], 2 * LANES - (2 * oy + start), 1)

    depth = depth_ref[pl.ds(pl.multiple_of(start, SUB), SUB), :]
    up = jnp.where(chunk == 0, outer_row(north, g_north, fields), depth_ref[pl.ds(jnp.maximum(start - 1, 0), 1), :])
    down = jnp.where(
        chunk == chunks - 1,
        outer_row(south, g_south, 0),
        depth_ref[pl.ds(jnp.minimum(start + SUB, oy - 1), 1), :],
    )
    def upright(ref, place):
        line = jnp.broadcast_to(ref[0, levels : levels + 1, :], (SUB, LANES))
        here = jnp.where(lanes == iota((SUB, LANES), 0) + place + start, line, 0.0)
        return jnp.sum(here, axis=1, keepdims=True).astype(jnp.int32)

    bounds[0] = jnp.where(lanes == LANES - 1, upright(east, 0), pltpu.roll(depth, LANES - 1, 1))
    bounds[1] = jnp.where(lanes == 0, upright(west, oy), pltpu.roll(depth, 1, 1))

    tile_level = iota((SUB, LANES), 0)

    def tile(t, carry):
        first = pl.multiple_of(t * SUB, SUB)
        here = pl.ds(first, SUB)
        lev = tile_level + first
        row_depth = [up] + [depth[i : i + 1] for i in range(SUB)] + [down]
        act = [lev < d for d in row_depth]
        one = [jnp.where(a, 1.0, 0.0) for a in act]
        scale, keep = [], []
        for i in range(SUB):
            sides = jnp.where(lev < bounds[0, i : i + 1], 1.0, 0.0) + jnp.where(lev < bounds[1, i : i + 1], 1.0, 0.0)
            scale.append(diffusion_rate * one[i + 1])
            keep.append(1.0 - scale[i] * ((one[i] + one[i + 2]) + sides))
        for q in range(fields):
            a = column[q, here, :]
            ze, zw = z_east[q, here, :], z_west[q, here, :]
            z, m = [z_above[q, here, :]], []
            for i in range(SUB):
                m0 = mixed[q, i, here, :]
                forced = m0 + a[:, i : i + 1] * forcing[pl.ds(q * oy + start + i, 1), :]
                z.append(jnp.where(act[i + 1], forced, 0.0))
                m.append(jnp.where(act[i + 1], forced, m0))
            z.append(z_below[q, here, :])
            for i in range(SUB):
                to_east = pltpu.roll(jnp.where(lanes == 0, ze[:, i : i + 1], z[i + 1]), LANES - 1, 1)
                to_west = pltpu.roll(jnp.where(lanes == LANES - 1, zw[:, i : i + 1], z[i + 1]), 1, 1)
                result = m[i] * keep[i] + scale[i] * ((z[i] + z[i + 2]) + (to_east + to_west))
                flat[pl.ds(q * levels * SUB + first * SUB + i, SUB, stride=SUB), :] = result
        return carry

    lax.fori_loop(0, levels // SUB, tile, 0)


def finish(depth, forcing, own, mixed, halos, g_halos):
    fields, oy, levels, ox = mixed.shape
    whole = pl.BlockSpec(memory_space=pltpu.VMEM)
    edge = pltpu.VMEM((fields, levels, ox), f32)
    return pl.pallas_call(
        finish_kernel,
        grid=(oy // SUB,),
        in_specs=[
            whole,
            whole,
            whole,
            pl.BlockSpec((fields, SUB, levels, ox), lambda c: (0, c, 0, 0)),
            pl.BlockSpec((fields, 1, levels, ox), lambda c: (0, jnp.maximum(c * SUB - 1, 0), 0, 0)),
            pl.BlockSpec((fields, 1, levels, ox), lambda c: (0, jnp.minimum(c * SUB + SUB, oy - 1), 0, 0)),
        ]
        + [whole] * 8,
        out_specs=pl.BlockSpec((fields, levels, SUB, ox), lambda c: (0, 0, c, 0)),
        out_shape=jax.ShapeDtypeStruct((fields, levels, oy, ox), f32),
        scratch_shapes=[edge, edge, edge, edge, edge, pltpu.VMEM((2, SUB, ox), jnp.int32)],
        compiler_params=pltpu.CompilerParams(vmem_limit_bytes=32 << 20),
        cost_estimate=pl.CostEstimate(flops=20 * fields * oy * levels * ox, bytes_accessed=12 << 20, transcendentals=0),
        name="finish",
    )(depth, forcing, own, mixed, mixed, mixed, *halos, *g_halos)


def shift(x, axis, step, wrap):
    count = lax.axis_size(axis)
    pairs = [(i, (i + step) % count) for i in range(count) if wrap or 0 <= i + step < count]
    return lax.ppermute(x, axis, pairs)


def on_device(
    atm_flux, sea_mask, src_block, dest_dev, dest_block, intersection_weights, coupling, inverses, ocean_state,
    depth_levels,
):
    devices = lax.axis_size("lat") * lax.axis_size("lon")
    fields, levels, oy, ox = ocean_state.shape
    cap = max(SUB, 2 * src_block.shape[0] // devices)
    slots = regrid(
        cap, devices, src_block, dest_dev[:, 0], dest_block, coupling, atm_flux, sea_mask, intersection_weights
    )
    received = lax.all_to_all(slots, ("lat", "lon"), 0, 0, tiled=True)
    mixed, north, south, side = mix(depth_levels, ocean_state, inverses)
    halos = (
        shift(south, "lat", 1, False),
        shift(north, "lat", -1, False),
        shift(side, "lon", -1, True),
        shift(side, "lon", 1, True),
    )
    forcing, edges = gather(cap, fields, oy, received)
    g_halos = (
        shift(edges, "lat", 1, False),
        shift(edges, "lat", -1, False),
        shift(edges, "lon", -1, True),
        shift(edges, "lon", 1, True),
    )
    return finish(depth_levels, forcing, side, mixed, halos, g_halos)


def solution(mesh):
    placed = (
        P(None, "lat", "lon"),
        P("lat", "lon"),
        P(("lat", "lon")),
        P(("lat", "lon"), None),
        P(("lat", "lon")),
        P(("lat", "lon"), None, None),
        P(),
        P(None, "lat", "lon", None, None),
        P(None, None, "lat", "lon"),
        P("lat", "lon"),
    )
    return jax.shard_map(
        on_device,
        mesh=mesh,
        in_specs=placed,
        out_specs=P(None, None, "lat", "lon"),
        check_vma=False,
    )
```

```python
import functools

import jax
import jax.numpy as jnp
from jax import lax
from jax.experimental import pallas as pl
from jax.experimental.pallas import tpu as pltpu
from jax.sharding import PartitionSpec as P

diffusion_rate = 0.2
LANES = 128
HALF = 64
SUB = 8
f32 = jnp.float32
bf16 = jnp.bfloat16
HBM = pl.BlockSpec(memory_space=pltpu.HBM)
VMEM = pl.BlockSpec(memory_space=pltpu.VMEM)


def split(x):
    high = x.astype(bf16)
    return high, (x - high.astype(f32)).astype(bf16)


def in_hbm(*arrays):
    return [pltpu.with_memory_space_constraint(x, pltpu.HBM) for x in arrays]


def iota(shape, dim):
    return lax.broadcasted_iota(jnp.int32, shape, dim)


def matmul(a, b):
    return jnp.dot(a, b, preferred_element_type=f32)


def padded_rows(x, rows):
    return x if x.shape[0] == rows else jnp.concatenate([x, jnp.zeros((rows - x.shape[0], LANES), x.dtype)], axis=0)


def regrid_kernel(
    cap, lon, oy, batch, src_h, dev_h, blk_h, coupling_h, atm_h, mask_h, weights_h,
    out, rows, ids, count, src, dev, blk, coupling, atm, mask, weights, small_sem, big_sem,
):
    fluxes, atm_rows, _ = atm.shape
    fields = coupling.shape[0]
    devices = out.shape[0]
    per = fields * cap
    parts = weights.shape[0] // batch

    def big(k):
        here = pl.ds(pl.multiple_of(k * batch, batch), batch)
        return pltpu.make_async_copy(weights_h.at[here], weights.at[here], big_sem.at[k])

    small = [
        pltpu.make_async_copy(a, b, small_sem.at[k])
        for k, (a, b) in enumerate(
            (
                (coupling_h, coupling), (atm_h, atm), (mask_h, mask),
                (src_h, src), (dev_h, dev), (blk_h, blk),
            )
        )
    ]
    for copy in small:
        copy.start()
    for k in range(parts):
        big(k).start()

    def clear(d, carry):
        count[d] = 0
        out[d] = jnp.zeros(out.shape[1:], f32)
        return carry

    lax.fori_loop(0, devices, clear, 0)
    ids[...] = jnp.full(ids.shape, -1, jnp.int32)
    for copy in small:
        copy.wait()
    for tile in range(atm_rows // 16):
        here = slice(tile * 16, tile * 16 + 16)
        sea = mask[here, :].astype(f32)
        flux = [atm[f, here, :].astype(f32) * sea for f in range(fluxes)]
        for q in range(fields):
            total = coupling[q, 0] * flux[0]
            for f in range(1, fluxes):
                total = total + coupling[q, f] * flux[f]
            high = total.astype(bf16).astype(f32)
            rows[pl.ds(tile * 16 * SUB + q, 16, stride=SUB), :] = high
            rows[pl.ds(tile * 16 * SUB + fields + q, 16, stride=SUB), :] = total - high

    lane = iota((1, LANES), 1)
    lane_slot = (lane % per) // fields
    lane_row = (lane % fields) * oy

    def part(k, carry):
        big(k).wait()
        for u in range(batch):
            p = k * batch + u
            d = dev[p]
            slot = jnp.minimum(count[d], cap - 1)
            count[d] = slot + 1
            x = rows[pl.ds(pl.multiple_of(src[p] * SUB, SUB), SUB), :].astype(bf16)
            both = matmul(x, weights[p])
            out[d, pl.ds(slot * fields, fields), :] = both[0:fields] + both[fields : 2 * fields]
            line = ids[pl.ds(d, 1), :]
            ids[pl.ds(d, 1), :] = jnp.where(lane_slot == slot, lane_row + blk[p], line)
        return carry

    lax.fori_loop(0, parts, part, 0)

    wide = iota((SUB, LANES), 1)
    tall = iota((SUB, LANES), 0)
    first_half = wide < HALF
    wanted = jnp.where(
        (tall < fields) & first_half,
        tall * oy + oy - 1,
        jnp.where((tall >= fields) & ~first_half, (tall - fields) * oy, -5),
    )

    def halo(d):
        east = jnp.where(d % lon == lon - 1, d - (lon - 1), d + 1)
        west = jnp.where(d % lon == 0, d + (lon - 1), d - 1)
        own = ids[pl.ds(d, 1), :].astype(f32)
        sides = jnp.where(lane < HALF, ids[pl.ds(east, 1), :], ids[pl.ds(west, 1), :]).astype(f32)
        turned = jnp.concatenate(
            [padded_rows(out[east, 0:per], HALF), padded_rows(out[west, 0:per], HALF)], axis=0
        ).T
        columns = jnp.where(lane < HALF, turned[0:1], turned[LANES - 1 : LANES])
        out[d, per : per + SUB] = jnp.concatenate([own, sides, columns, jnp.zeros((SUB - 3, LANES), f32)], axis=0)
        north = jnp.maximum(d - lon, 0)
        south = jnp.minimum(d + lon, devices - 1)
        named = jnp.where(
            first_half,
            jnp.where(d >= lon, ids[pl.ds(north, 1), :], -9),
            jnp.where(d < devices - lon, ids[pl.ds(south, 1), :], -9),
        )
        chosen = jnp.where(named == wanted, 1.0, 0.0).astype(bf16)
        high, low = split(
            jnp.concatenate([padded_rows(out[north, 0:per], HALF), padded_rows(out[south, 0:per], HALF)], axis=0)
        )
        both = matmul(chosen, jnp.concatenate([high, low], axis=1))
        out[d, per + SUB : per + 2 * SUB] = both[:, :LANES] + both[:, LANES:]

    def halos(k, carry):
        for u in range(4):
            halo(k * 4 + u)
        return carry

    lax.fori_loop(0, devices // 4, halos, 0)


def regrid(cap, devices, lon, oy, src, dev, blk, coupling, atm, mask, weights):
    pairs, depth, width = weights.shape
    fields = coupling.shape[0]
    batch = 32
    tall = fields * cap + 2 * SUB
    return pl.pallas_call(
        functools.partial(regrid_kernel, cap, lon, oy, batch),
        in_specs=[HBM] * 7,
        out_specs=VMEM,
        out_shape=jax.ShapeDtypeStruct((devices, tall, LANES), f32),
        scratch_shapes=[
            pltpu.VMEM((atm.shape[1] * SUB, LANES), f32),
            pltpu.VMEM((devices, LANES), jnp.int32),
            pltpu.SMEM((devices,), jnp.int32),
            pltpu.SMEM(src.shape, jnp.int32),
            pltpu.SMEM(dev.shape, jnp.int32),
            pltpu.SMEM(blk.shape, jnp.int32),
            pltpu.SMEM(coupling.shape, f32),
            pltpu.VMEM(atm.shape, bf16),
            pltpu.VMEM(mask.shape, jnp.int32),
            pltpu.VMEM(weights.shape, bf16),
            pltpu.SemaphoreType.DMA((6,)),
            pltpu.SemaphoreType.DMA((pairs // batch,)),
        ],
        compiler_params=pltpu.CompilerParams(vmem_limit_bytes=20 << 20),
        cost_estimate=pl.CostEstimate(flops=2 * 8 * pairs * depth * width, bytes_accessed=10 << 20, transcendentals=0),
        name="regrid",
    )(*in_hbm(src, dev, blk, coupling, atm, mask, weights))


def mix_kernel(depth_h, state_h, inv_h, mixed, north, south, side, depth_ref, state, inv, sems):
    fields, levels, oy, _ = state.shape
    copies = [pltpu.make_async_copy(depth_h, depth_ref, sems.at[2 * fields])]
    copies[0].start()
    for q in range(fields):
        for k, (a, b) in enumerate(((state_h, state), (inv_h, inv))):
            pltpu.make_async_copy(a.at[q], b.at[q], sems.at[2 * q + k]).start()
    copies[0].wait()
    level = iota((levels, LANES), 0)
    lane = iota((levels, LANES), 1)
    pick_row = iota((LANES, LANES), 0)
    pick_lane = iota((LANES, LANES), 1)
    turned = padded_rows(depth_ref[...].astype(f32), LANES).T
    edge_depth = turned[0:1] + pltpu.roll(turned[LANES - SUB :], oy, 1)[SUB - 1 : SUB]

    def message(ref, q, row):
        ref[q, 0:levels] = mixed[q, row]
        square = jnp.concatenate([inv[q, row, 0], jnp.zeros((levels, LANES - levels), f32)], axis=1)
        first = padded_rows(square, LANES).T[0:1]
        ref[q, levels : levels + SUB] = jnp.concatenate(
            [depth_ref[row : row + 1, :].astype(f32), first, jnp.zeros((SUB - 2, LANES), f32)], axis=0
        )

    def field(q, carry):
        for k, (a, b) in enumerate(((state_h, state), (inv_h, inv))):
            pltpu.make_async_copy(a.at[q], b.at[q], sems.at[2 * q + k]).wait()
        flat = state.at[q].reshape(levels * oy, LANES)

        def chunk(c, edges):
            for i in range(SUB):
                row = c * SUB + i
                active = level < depth_ref[pl.ds(row, 1), :]
                x = flat[pl.ds(row, levels, stride=oy), :]
                a = inv[q, row, 0]
                a_high, a_low = split(a)
                r_high, r_low = split(jnp.where(active, x, 0.0))
                product = matmul(
                    jnp.concatenate([a_high, a_low], axis=0), jnp.concatenate([r_high, r_low], axis=1)
                )
                solved = product[:levels, :LANES] + (product[levels:, :LANES] + product[:levels, LANES:])
                m = jnp.where(active, solved, x)
                mixed[q, row] = m
                m_high, m_low = split(m)
                pick = (
                    ((pick_row == 0) & (pick_lane == row)) | ((pick_row == LANES - 1) & (pick_lane == oy + row))
                ).astype(f32).astype(bf16)
                edges = edges + matmul(
                    jnp.concatenate([m_high, m_low], axis=1), jnp.concatenate([pick, pick], axis=0)
                )
                edges = jnp.where(lane == 2 * oy + row, a[:, 0:1], edges)
            return edges

        side[q, 0:levels] = lax.fori_loop(0, oy // SUB, chunk, jnp.zeros((levels, LANES), f32))
        side[q, levels : levels + SUB] = jnp.broadcast_to(edge_depth, (SUB, LANES))
        message(north, q, 0)
        message(south, q, oy - 1)
        return carry

    lax.fori_loop(0, fields, field, 0)


def mix(depth, state, inverses):
    fields, levels, oy, ox = state.shape
    edge_shape = jax.ShapeDtypeStruct((fields, levels + SUB, ox), f32)
    return pl.pallas_call(
        mix_kernel,
        in_specs=[HBM] * 3,
        out_specs=[VMEM] * 4,
        out_shape=[jax.ShapeDtypeStruct((fields, oy, levels, ox), f32), edge_shape, edge_shape, edge_shape],
        scratch_shapes=[
            pltpu.VMEM(depth.shape, jnp.int32),
            pltpu.VMEM(state.shape, f32),
            pltpu.VMEM(inverses.shape, f32),
            pltpu.SemaphoreType.DMA((2 * fields + 1,)),
        ],
        compiler_params=pltpu.CompilerParams(vmem_limit_bytes=28 << 20),
        cost_estimate=pl.CostEstimate(flops=2 * 4 * fields * oy * levels * levels * ox, bytes_accessed=16 << 20, transcendentals=0),
        name="mix",
    )(*in_hbm(depth, state, inverses))


def finish_kernel(
    cap, recv, depth_ref, own, mixed, north, south, east, west,
    out_h, forcing, z, m, keep, column, halo, z_north, z_south, stage, sems,
):
    fields, oy, levels, _ = mixed.shape
    devices = recv.shape[0]
    per = fields * cap
    group = LANES // per
    level = iota((levels, LANES), 0)
    lanes = iota((levels, LANES), 1)
    square_row = iota((LANES, LANES), 0)
    square_lane = iota((LANES, LANES), 1)
    line = iota((1, LANES), 1)

    total = jnp.zeros((LANES, 2 * LANES), f32)
    for tile in range(devices // group):
        ids = recv[tile * group, per : per + 1, :]
        for s in range(1, group):
            ids = jnp.where(line // per == s, recv[tile * group + s, per : per + 1, :], ids)
        hot = jnp.where(square_row.astype(f32) == ids, 1.0, 0.0).astype(bf16)
        high, low = split(jnp.concatenate([recv[tile * group + s, 0:per, :] for s in range(group)], axis=0))
        total = total + matmul(hot, jnp.concatenate([high, low], axis=1))
    forcing[...] = total[:, :LANES] + total[:, LANES:]
    rows = recv[0, per + SUB : per + 2 * SUB, :]
    for d in range(1, devices):
        rows = rows + recv[d, per + SUB : per + 2 * SUB, :]
    spread = jnp.zeros((oy, LANES), f32)
    row = iota((oy, LANES), 0).astype(f32)
    lane_base = ((line % fields) * oy).astype(f32)
    for d in range(devices):
        spread = spread + jnp.where(
            recv[d, per + 1 : per + 2, :] - lane_base == row, recv[d, per + 2 : per + 3, :], 0.0
        )
    high, low = split(padded_rows(spread, LANES).T)
    small_row, small_lane = iota((SUB, LANES), 0), iota((SUB, LANES), 1)
    pick = jnp.where(
        (small_lane % fields == small_row % fields)
        & (small_lane % HALF < per)
        & ((small_lane < HALF) == (small_row < fields)),
        1.0,
        0.0,
    ).astype(bf16)
    columns = matmul(pick, high) + matmul(pick, low)

    depth = depth_ref[...]
    wide = iota((oy, LANES), 1)

    def upright(ref, place):
        value = jnp.where(wide == iota((oy, LANES), 0) + place, ref[0, levels : levels + 1, :], 0.0)
        return jnp.sum(value, axis=1, keepdims=True).astype(jnp.int32)

    to_east = jnp.where(wide == LANES - 1, upright(east, 0), pltpu.roll(depth, LANES - 1, 1))
    to_west = jnp.where(wide == 0, upright(west, oy), pltpu.roll(depth, 1, 1))
    to_north = jnp.concatenate([north[0, levels : levels + 1, :].astype(jnp.int32), depth[: oy - 1]], axis=0)
    to_south = jnp.concatenate([depth[1:], south[0, levels : levels + 1, :].astype(jnp.int32)], axis=0)
    for i in range(oy):
        sides = jnp.where(level < to_east[i : i + 1], diffusion_rate, 0.0)
        for other in (to_west, to_north, to_south):
            sides = sides + jnp.where(level < other[i : i + 1], diffusion_rate, 0.0)
        keep[i] = jnp.where(level < depth[i : i + 1], 1.0 - sides, 1.0)

    def outer(target, ref, first):
        names = padded_rows(
            jnp.concatenate([ref[q, levels + 1 : levels + 2, :] for q in range(fields)], axis=0), LANES
        ).T
        active = level < ref[0, levels : levels + 1, :].astype(jnp.int32)
        for q in range(fields):
            value = ref[q, 0:levels] + names[0:levels, q : q + 1] * rows[first + q : first + q + 1]
            target[q] = jnp.where(active, value, 0.0)

    outer(z_north, north, 0)
    outer(z_south, south, fields)
    east_depth = east[0, levels : levels + 1, :].astype(jnp.int32)
    west_depth = west[0, levels : levels + 1, :].astype(jnp.int32)
    west_columns = pltpu.roll(columns, oy, 1)
    for q in range(fields):
        z_east = east[q, 0:levels] + pltpu.roll(east[q, 0:levels], LANES - 2 * oy, 1) * columns[q : q + 1]
        z_east = jnp.where(level < east_depth, z_east, 0.0)
        z_west = west[q, 0:levels] + pltpu.roll(west[q, 0:levels], LANES - oy, 1) * west_columns[fields + q : fields + q + 1]
        z_west = jnp.where(level < west_depth, z_west, 0.0)
        both = jnp.where(lanes < oy, z_east, z_west)
        high = both.astype(bf16).astype(f32)
        halo[q] = jnp.where(lanes < HALF, high, pltpu.roll(both - high, HALF, 1)).astype(bf16)
        a = own[q, 0:levels]
        first = pltpu.roll(a, LANES - 2 * oy, 1)
        low = pltpu.roll(a, LANES - oy, 1)
        low = low - low.astype(bf16).astype(f32)
        column[q] = jnp.where(
            lanes < oy, first, jnp.where(lanes < 2 * oy, low, jnp.where(lanes < 3 * oy, a, 0.0))
        ).astype(bf16)

    to_both = jnp.where(
        (square_row == square_lane + 1) | (square_row == square_lane - 1), 1.0, 0.0
    ).astype(bf16)
    own_row = iota((oy, LANES), 0)

    def field(q, carry):
        z[0] = z_north[q]
        z[oy + 1] = z_south[q]
        g_high, g_low = split(forcing[pl.ds(pl.multiple_of(q * oy, oy), oy), :])
        g_high, g_low = g_high.astype(f32), g_low.astype(f32)

        def solve(c, carry):
            for i in range(SUB):
                r = c * SUB + i
                here = own_row == r
                high = jnp.where(here, g_high, 0.0)
                low = jnp.where(here, g_low, 0.0)
                spread = padded_rows(jnp.concatenate([high, high, low], axis=0), LANES).astype(bf16)
                m0 = mixed[q, r]
                forced = m0 + matmul(column[q], spread)
                active = level < depth_ref[pl.ds(r, 1), :]
                z[r + 1] = jnp.where(active, forced, 0.0)
                m[r] = jnp.where(active, forced, m0)
            return carry

        lax.fori_loop(0, oy // SUB, solve, 0)
        flat = stage.at[q].reshape(levels * oy, LANES)

        def diffuse(c, carry):
            for i in range(SUB):
                r = c * SUB + i
                high, low = split(z[r + 1])
                edge = jnp.where(
                    ((square_row % HALF == r) & (square_lane == LANES - 1))
                    | ((square_row % HALF == oy + r) & (square_lane == 0)),
                    1.0,
                    0.0,
                ).astype(bf16)
                sides = matmul(
                    jnp.concatenate([high, low, halo[q]], axis=1),
                    jnp.concatenate([to_both, to_both, edge], axis=0),
                )
                scale = jnp.where(level < depth_ref[pl.ds(r, 1), :], diffusion_rate, 0.0)
                flat[pl.ds(r, levels, stride=oy), :] = m[r] * keep[r] + scale * ((z[r] + z[r + 2]) + sides)
            return carry

        lax.fori_loop(0, oy // SUB, diffuse, 0)
        pltpu.make_async_copy(stage.at[q], out_h.at[q], sems.at[q]).start()
        return carry

    lax.fori_loop(0, fields, field, 0)
    for q in range(fields):
        pltpu.make_async_copy(stage.at[q], out_h.at[q], sems.at[q]).wait()


def finish(cap, received, depth, own, mixed, halos):
    fields, oy, levels, ox = mixed.shape
    edge = pltpu.VMEM((fields, levels, ox), f32)
    return pl.pallas_call(
        functools.partial(finish_kernel, cap),
        in_specs=[VMEM] * 8,
        out_specs=HBM,
        out_shape=jax.ShapeDtypeStruct((fields, levels, oy, ox), f32),
        scratch_shapes=[
            pltpu.VMEM((fields * oy, ox), f32),
            pltpu.VMEM((oy + 2, levels, ox), f32),
            pltpu.VMEM((oy, levels, ox), f32),
            pltpu.VMEM((oy, levels, ox), f32),
            pltpu.VMEM((fields, levels, ox), bf16),
            pltpu.VMEM((fields, levels, ox), bf16),
            edge,
            edge,
            pltpu.VMEM((fields, levels, oy, ox), f32),
            pltpu.SemaphoreType.DMA((fields,)),
        ],
        compiler_params=pltpu.CompilerParams(vmem_limit_bytes=24 << 20),
        cost_estimate=pl.CostEstimate(flops=20 * fields * oy * levels * ox, bytes_accessed=12 << 20, transcendentals=0),
        name="finish",
    )(received, depth, own, mixed, *halos)


def shift(x, axis, step, wrap):
    count = lax.axis_size(axis)
    pairs = [(i, (i + step) % count) for i in range(count) if wrap or 0 <= i + step < count]
    return lax.ppermute(x, axis, pairs)


def on_device(
    atm_flux, sea_mask, src_block, dest_dev, dest_block, intersection_weights, coupling, inverses, ocean_state,
    depth_levels,
):
    lon = lax.axis_size("lon")
    devices = lax.axis_size("lat") * lon
    oy = ocean_state.shape[2]
    cap = max(SUB, 2 * src_block.shape[0] // devices)
    slots = regrid(
        cap, devices, lon, oy, src_block, dest_dev[:, 0], dest_block, coupling, atm_flux, sea_mask,
        intersection_weights,
    )
    received = lax.all_to_all(slots, ("lat", "lon"), 0, 0, tiled=True)
    mixed, north, south, side = mix(depth_levels, ocean_state, inverses)
    halos = (
        shift(south, "lat", 1, False),
        shift(north, "lat", -1, False),
        shift(side, "lon", -1, True),
        shift(side, "lon", 1, True),
    )
    return finish(cap, received, depth_levels, side, mixed, halos)


def solution(mesh):
    placed = (
        P(None, "lat", "lon"),
        P("lat", "lon"),
        P(("lat", "lon")),
        P(("lat", "lon"), None),
        P(("lat", "lon")),
        P(("lat", "lon"), None, None),
        P(),
        P(None, "lat", "lon", None, None),
        P(None, None, "lat", "lon"),
        P("lat", "lon"),
    )
    return jax.shard_map(
        on_device,
        mesh=mesh,
        in_specs=placed,
        out_specs=P(None, None, "lat", "lon"),
        check_vma=False,
    )
```

```python
import functools

import jax
import jax.numpy as jnp
from jax import lax
from jax.experimental import pallas as pl
from jax.experimental.pallas import tpu as pltpu
from jax.sharding import PartitionSpec as P

diffusion_rate = 0.2
LANES = 128
HALF = 64
SUB = 8
f32 = jnp.float32
bf16 = jnp.bfloat16
HBM = pl.BlockSpec(memory_space=pltpu.HBM)
VMEM = pl.BlockSpec(memory_space=pltpu.VMEM)


def split(x):
    high = x.astype(bf16)
    return high, (x - high.astype(f32)).astype(bf16)


def in_hbm(*arrays):
    return [pltpu.with_memory_space_constraint(x, pltpu.HBM) for x in arrays]


def iota(shape, dim):
    return lax.broadcasted_iota(jnp.int32, shape, dim)


def matmul(a, b):
    return jnp.dot(a, b, preferred_element_type=f32)


def padded_rows(x, rows):
    return x if x.shape[0] == rows else jnp.concatenate([x, jnp.zeros((rows - x.shape[0], LANES), x.dtype)], axis=0)


def regrid_kernel(
    cap, lon, oy, batch, src_h, dev_h, blk_h, coupling_h, atm_h, mask_h, weights_h,
    out, rows, ids, count, src, dev, blk, coupling, atm, mask, weights, small_sem, big_sem,
):
    fluxes, atm_rows, _ = atm.shape
    fields = coupling.shape[0]
    devices = out.shape[0]
    per = fields * cap
    parts = weights.shape[0] // batch

    def big(k):
        here = pl.ds(pl.multiple_of(k * batch, batch), batch)
        return pltpu.make_async_copy(weights_h.at[here], weights.at[here], big_sem.at[k])

    small = [
        pltpu.make_async_copy(a, b, small_sem.at[k])
        for k, (a, b) in enumerate(
            (
                (coupling_h, coupling), (atm_h, atm), (mask_h, mask),
                (src_h, src), (dev_h, dev), (blk_h, blk),
            )
        )
    ]
    for copy in small:
        copy.start()
    for k in range(parts):
        big(k).start()

    def clear(d, carry):
        count[d] = 0
        out[d] = jnp.zeros(out.shape[1:], f32)
        return carry

    lax.fori_loop(0, devices, clear, 0)
    ids[...] = jnp.full(ids.shape, -1, jnp.int32)
    for copy in small:
        copy.wait()
    for tile in range(atm_rows // 16):
        here = slice(tile * 16, tile * 16 + 16)
        sea = mask[here, :].astype(f32)
        flux = [atm[f, here, :].astype(f32) * sea for f in range(fluxes)]
        for q in range(fields):
            total = coupling[q, 0] * flux[0]
            for f in range(1, fluxes):
                total = total + coupling[q, f] * flux[f]
            high = total.astype(bf16).astype(f32)
            rows[pl.ds(tile * 16 * SUB + q, 16, stride=SUB), :] = high
            rows[pl.ds(tile * 16 * SUB + fields + q, 16, stride=SUB), :] = total - high

    lane = iota((1, LANES), 1)
    lane_slot = (lane % per) // fields
    lane_row = (lane % fields) * oy

    def part(k, carry):
        big(k).wait()
        for u in range(batch):
            p = k * batch + u
            d = dev[p]
            slot = jnp.minimum(count[d], cap - 1)
            count[d] = slot + 1
            x = rows[pl.ds(pl.multiple_of(src[p] * SUB, SUB), SUB), :].astype(bf16)
            both = matmul(x, weights[p])
            out[d, pl.ds(slot * fields, fields), :] = both[0:fields] + both[fields : 2 * fields]
            line = ids[pl.ds(d, 1), :]
            ids[pl.ds(d, 1), :] = jnp.where(lane_slot == slot, lane_row + blk[p], line)
        return carry

    lax.fori_loop(0, parts, part, 0)

    tall = iota((SUB, LANES), 0)
    wide = iota((SUB, LANES), 1)
    wanted = jnp.where(tall < fields, tall * oy + oy - 1, (tall - fields) * oy)
    wanted = jnp.where(wide % HALF < per, wanted, -5)

    def neighbours(d):
        east = jnp.where(d % lon == lon - 1, d - (lon - 1), d + 1)
        west = jnp.where(d % lon == 0, d + (lon - 1), d - 1)
        return east, west

    def halo(k):
        d = 2 * k
        stack = jnp.concatenate([padded_rows(out[d + u, 0:per], HALF) for u in range(2)], axis=0)
        turned = stack.T
        first, last = turned[0:1], turned[LANES - 1 : LANES]
        first_swapped = pltpu.roll(turned[0:SUB], HALF, 1)[0:1]
        last_swapped = pltpu.roll(turned[LANES - SUB : LANES], HALF, 1)[SUB - 1 : SUB]
        high, low = split(stack)
        for u in range(2):
            east, west = neighbours(d + u)
            out[d + u, per : per + 1] = ids[pl.ds(d + u, 1), :].astype(f32)
            sides = jnp.where(lane < HALF, ids[pl.ds(east, 1), :], ids[pl.ds(west, 1), :])
            out[d + u, per + 1 : per + 2] = sides.astype(f32)
            column = first if u == 0 else first_swapped
            out[west, per + 2 : per + 3] = jnp.where(lane < HALF, column, out[west, per + 2 : per + 3])
            column = last_swapped if u == 0 else last
            out[east, per + 2 : per + 3] = jnp.where(lane < HALF, out[east, per + 2 : per + 3], column)
            chosen = jnp.where(ids[pl.ds(d + u, 1), :] == wanted, 1.0, 0.0).astype(bf16)
            here = slice(u * HALF, u * HALF + HALF)
            sums = matmul(chosen, jnp.concatenate([high[here], low[here]], axis=0))

            @pl.when(d + u < devices - lon)
            def _():
                out[d + u + lon, per + SUB : per + SUB + fields] = sums[0:fields]

            @pl.when(d + u >= lon)
            def _():
                out[d + u - lon, per + SUB + fields : per + SUB + 2 * fields] = sums[fields : 2 * fields]

    def halos(k, carry):
        for u in range(2):
            halo(k * 2 + u)
        return carry

    lax.fori_loop(0, devices // 4, halos, 0)


def regrid(cap, devices, lon, oy, src, dev, blk, coupling, atm, mask, weights):
    pairs, depth, width = weights.shape
    fields = coupling.shape[0]
    batch = 32
    tall = fields * cap + 2 * SUB
    return pl.pallas_call(
        functools.partial(regrid_kernel, cap, lon, oy, batch),
        in_specs=[HBM] * 7,
        out_specs=VMEM,
        out_shape=jax.ShapeDtypeStruct((devices, tall, LANES), f32),
        scratch_shapes=[
            pltpu.VMEM((atm.shape[1] * SUB, LANES), f32),
            pltpu.VMEM((devices, LANES), jnp.int32),
            pltpu.SMEM((devices,), jnp.int32),
            pltpu.SMEM(src.shape, jnp.int32),
            pltpu.SMEM(dev.shape, jnp.int32),
            pltpu.SMEM(blk.shape, jnp.int32),
            pltpu.SMEM(coupling.shape, f32),
            pltpu.VMEM(atm.shape, bf16),
            pltpu.VMEM(mask.shape, jnp.int32),
            pltpu.VMEM(weights.shape, bf16),
            pltpu.SemaphoreType.DMA((6,)),
            pltpu.SemaphoreType.DMA((pairs // batch,)),
        ],
        compiler_params=pltpu.CompilerParams(vmem_limit_bytes=20 << 20),
        cost_estimate=pl.CostEstimate(flops=2 * 8 * pairs * depth * width, bytes_accessed=10 << 20, transcendentals=0),
        name="regrid",
    )(*in_hbm(src, dev, blk, coupling, atm, mask, weights))


def mix_kernel(
    depth_h, state_h, inv_h, mixed_h, first_h, north, south, side, depth_ref, mixed, inv, first, in_sems, out_sems
):
    fields, oy, levels, _ = mixed.shape
    depth_copy = pltpu.make_async_copy(depth_h, depth_ref, in_sems.at[2 * fields])
    depth_copy.start()
    for q in range(fields):
        for i in range(oy):
            pltpu.make_async_copy(state_h.at[q, :, i, :], mixed.at[q, i], in_sems.at[2 * q]).start()
        pltpu.make_async_copy(inv_h.at[q], inv.at[q], in_sems.at[2 * q + 1]).start()
    depth_copy.wait()
    level = iota((levels, LANES), 0)
    lane = iota((levels, LANES), 1)
    line = iota((1, LANES), 1)
    edge_depth = jnp.zeros((SUB, LANES), f32)
    for i in range(oy):
        turned = pltpu.roll(jnp.broadcast_to(depth_ref[i : i + 1, :].astype(f32), (SUB, LANES)), 2 * i + 1, 1)
        edge_depth = jnp.where(line // 2 == i, turned, edge_depth)

    def message(ref, q, row):
        ref[q, 0:levels] = mixed[q, row]
        names = padded_rows(first[q, row], LANES).T[0:1]
        ref[q, levels : levels + SUB] = jnp.concatenate(
            [depth_ref[row : row + 1, :].astype(f32), names, jnp.zeros((SUB - 2, LANES), f32)], axis=0
        )

    def field(q, carry):
        pltpu.make_async_copy(mixed_h.at[q], mixed.at[q], in_sems.at[2 * q]).wait()
        pltpu.make_async_copy(inv_h.at[q], inv.at[q], in_sems.at[2 * q + 1]).wait()

        def chunk(c, edges):
            here = jnp.zeros((levels, LANES), f32)
            for i in range(SUB):
                row = c * SUB + i
                active = level < depth_ref[pl.ds(row, 1), :]
                x = mixed[q, row]
                a = inv[q, row, 0]
                a_high, a_low = split(a)
                r_high, r_low = split(jnp.where(active, x, 0.0))
                product = matmul(
                    jnp.concatenate([a_high, a_low], axis=0), jnp.concatenate([r_high, r_low], axis=1)
                )
                solved = product[:levels, :LANES] + (product[levels:, :LANES] + product[:levels, LANES:])
                m = jnp.where(active, solved, x)
                mixed[q, row] = m
                column = jnp.broadcast_to(a[:, 0:1], (levels, LANES))
                first[q, row] = column
                here = jnp.where(lane // 2 == i, pltpu.roll(m, 2 * i + 1, 1), here)
                here = jnp.where(lane // 2 == HALF // 2 + i, column, here)
            return edges + pltpu.roll(here, 2 * SUB * c, 1)

        side[q, 0:levels] = lax.fori_loop(0, oy // SUB, chunk, jnp.zeros((levels, LANES), f32))
        side[q, levels : levels + SUB] = edge_depth
        message(north, q, 0)
        message(south, q, oy - 1)
        pltpu.make_async_copy(mixed.at[q], mixed_h.at[q], out_sems.at[2 * q]).start()
        pltpu.make_async_copy(first.at[q], first_h.at[q], out_sems.at[2 * q + 1]).start()
        return carry

    lax.fori_loop(0, fields, field, 0)
    for q in range(fields):
        pltpu.make_async_copy(mixed.at[q], mixed_h.at[q], out_sems.at[2 * q]).wait()
        pltpu.make_async_copy(first.at[q], first_h.at[q], out_sems.at[2 * q + 1]).wait()


def mix(depth, state, inverses):
    fields, levels, oy, ox = state.shape
    edge_shape = jax.ShapeDtypeStruct((fields, levels + SUB, ox), f32)
    full = (fields, oy, levels, ox)
    return pl.pallas_call(
        mix_kernel,
        in_specs=[HBM] * 3,
        out_specs=[HBM] * 2 + [VMEM] * 3,
        out_shape=[pltpu.HBM(full, f32), pltpu.HBM(full, f32), edge_shape, edge_shape, edge_shape],
        scratch_shapes=[
            pltpu.VMEM(depth.shape, jnp.int32),
            pltpu.VMEM(full, f32),
            pltpu.VMEM(inverses.shape, f32),
            pltpu.VMEM(full, f32),
            pltpu.SemaphoreType.DMA((2 * fields + 1,)),
            pltpu.SemaphoreType.DMA((2 * fields,)),
        ],
        compiler_params=pltpu.CompilerParams(vmem_limit_bytes=32 << 20),
        cost_estimate=pl.CostEstimate(flops=2 * 4 * fields * oy * levels * levels * ox, bytes_accessed=16 << 20, transcendentals=0),
        name="mix",
    )(*in_hbm(depth, state, inverses))


def finish_kernel(
    cap, recv, depth_ref, mixed_h, first_h, north, south, east, west,
    out_h, forcing, z, keep, halo, z_north, z_south, mixed, first, stage, in_sems, out_sems,
):
    fields, oy, levels, _ = mixed.shape
    devices = recv.shape[0]
    per = fields * cap
    group = LANES // per
    level = iota((levels, LANES), 0)
    lanes = iota((levels, LANES), 1)
    square_row = iota((LANES, LANES), 0)
    square_lane = iota((LANES, LANES), 1)
    line = iota((1, LANES), 1)
    even = line % 2 == 0
    for q in range(fields):
        pltpu.make_async_copy(mixed_h.at[q], mixed.at[q], in_sems.at[2 * q]).start()
        pltpu.make_async_copy(first_h.at[q], first.at[q], in_sems.at[2 * q + 1]).start()

    total = jnp.zeros((LANES, 2 * LANES), f32)
    for tile in range(devices // group):
        ids = recv[tile * group, per : per + 1, :]
        for s in range(1, group):
            ids = jnp.where(line // per == s, recv[tile * group + s, per : per + 1, :], ids)
        hot = jnp.where(square_row.astype(f32) == ids, 1.0, 0.0).astype(bf16)
        high, low = split(jnp.concatenate([recv[tile * group + s, 0:per, :] for s in range(group)], axis=0))
        total = total + matmul(hot, jnp.concatenate([high, low], axis=1))
    forcing[...] = total[:, :LANES] + total[:, LANES:]
    rows = recv[0, per + SUB : per + 2 * SUB, :]
    for d in range(1, devices):
        rows = rows + recv[d, per + SUB : per + 2 * SUB, :]
    spread = jnp.zeros((2 * oy, LANES), f32)
    row = iota((2 * oy, LANES), 0).astype(f32)
    lane_base = ((line % fields) * oy).astype(f32)
    lane_side = (line // HALF).astype(f32)
    for d in range(devices):
        place = 2.0 * (recv[d, per + 1 : per + 2, :] - lane_base) + lane_side
        spread = spread + jnp.where(place == row, recv[d, per + 2 : per + 3, :], 0.0)
    high, low = split(padded_rows(spread, LANES).T)
    small_row, small_lane = iota((SUB, LANES), 0), iota((SUB, LANES), 1)
    pick = jnp.where((small_lane % fields == small_row) & (small_lane % HALF < per), 1.0, 0.0).astype(bf16)
    columns = matmul(pick, high) + matmul(pick, low)

    depth = depth_ref[...]
    wide = iota((oy, LANES), 1)

    def upright(ref, place):
        value = jnp.where(wide == 2 * iota((oy, LANES), 0) + place, ref[0, levels : levels + 1, :], 0.0)
        return jnp.sum(value, axis=1, keepdims=True).astype(jnp.int32)

    to_east = jnp.where(wide == LANES - 1, upright(east, 1), pltpu.roll(depth, LANES - 1, 1))
    to_west = jnp.where(wide == 0, upright(west, 0), pltpu.roll(depth, 1, 1))
    to_north = jnp.concatenate([north[0, levels : levels + 1, :].astype(jnp.int32), depth[: oy - 1]], axis=0)
    to_south = jnp.concatenate([depth[1:], south[0, levels : levels + 1, :].astype(jnp.int32)], axis=0)
    for i in range(oy):
        sides = jnp.where(level < to_east[i : i + 1], diffusion_rate, 0.0)
        for other in (to_west, to_north, to_south):
            sides = sides + jnp.where(level < other[i : i + 1], diffusion_rate, 0.0)
        keep[i] = jnp.where(level < depth[i : i + 1], 1.0 - sides, 1.0)

    def outer(target, ref, start):
        names = padded_rows(
            jnp.concatenate([ref[q, levels + 1 : levels + 2, :] for q in range(fields)], axis=0), LANES
        ).T
        active = level < ref[0, levels : levels + 1, :].astype(jnp.int32)
        for q in range(fields):
            value = ref[q, 0:levels] + names[0:levels, q : q + 1] * rows[start + q : start + q + 1]
            target[q] = jnp.where(active, value, 0.0)

    outer(z_north, north, 0)
    outer(z_south, south, fields)
    for q in range(fields):
        cells = jnp.where(even, pltpu.roll(east[q], LANES - 1, 1), pltpu.roll(west[q], 1, 1))
        names = pltpu.roll(jnp.where(even, east[q], west[q]), HALF, 1)
        active = level < cells[levels : levels + 1].astype(jnp.int32)
        value = cells[0:levels] + names[0:levels] * columns[q : q + 1]
        halo[q] = jnp.where(active & (line < 2 * oy), value, 0.0)

    both = jnp.where((square_row == square_lane + 1) | (square_row == square_lane - 1), 1.0, 0.0).astype(bf16)
    both = jnp.concatenate([both, both], axis=0)
    ends = (lanes == 0) | (lanes == LANES - 1)

    def field(q, carry):
        pltpu.make_async_copy(mixed_h.at[q], mixed.at[q], in_sems.at[2 * q]).wait()
        pltpu.make_async_copy(first_h.at[q], first.at[q], in_sems.at[2 * q + 1]).wait()
        z[0] = z_north[q]
        z[oy + 1] = z_south[q]

        def solve(c, carry):
            for i in range(SUB):
                r = c * SUB + i
                m0 = mixed[q, r]
                forced = m0 + first[q, r] * forcing[pl.ds(q * oy + r, 1), :]
                active = level < depth_ref[pl.ds(r, 1), :]
                z[r + 1] = jnp.where(active, forced, 0.0)
                mixed[q, r] = jnp.where(active, forced, m0)
            return carry

        lax.fori_loop(0, oy // SUB, solve, 0)

        def diffuse(c, carry):
            start = c * SUB
            high, low = split(z[pl.ds(start + 1, SUB)].reshape(SUB * levels, LANES))
            sides = matmul(jnp.concatenate([high, low], axis=1), both)
            edge = pltpu.roll(halo[q], (LANES - 2 * SUB * c) % LANES, 1)
            for i in range(SUB):
                r = start + i
                outside = jnp.where(ends, pltpu.roll(edge, LANES - 1 - 2 * i, 1), 0.0)
                around = (z[r] + z[r + 2]) + (sides[i * levels : (i + 1) * levels] + outside)
                scale = jnp.where(level < depth_ref[pl.ds(r, 1), :], diffusion_rate, 0.0)
                stage[q, r] = mixed[q, r] * keep[r] + scale * around
                pltpu.make_async_copy(stage.at[q, r], out_h.at[q, :, r, :], out_sems.at[q]).start()
            return carry

        lax.fori_loop(0, oy // SUB, diffuse, 0)
        return carry

    lax.fori_loop(0, fields, field, 0)
    for q in range(fields):
        pltpu.make_async_copy(stage.at[q], mixed_h.at[q], out_sems.at[q]).wait()


def finish(cap, received, depth, mixed, first, halos):
    fields, oy, levels, ox = mixed.shape
    edge = pltpu.VMEM((fields, levels, ox), f32)
    full = pltpu.VMEM((fields, oy, levels, ox), f32)
    return pl.pallas_call(
        functools.partial(finish_kernel, cap),
        in_specs=[VMEM] * 2 + [HBM] * 2 + [VMEM] * 4,
        out_specs=HBM,
        out_shape=pltpu.HBM((fields, levels, oy, ox), f32),
        scratch_shapes=[
            pltpu.VMEM((fields * oy, ox), f32),
            pltpu.VMEM((oy + 2, levels, ox), f32),
            pltpu.VMEM((oy, levels, ox), f32),
            edge,
            edge,
            edge,
            full,
            full,
            full,
            pltpu.SemaphoreType.DMA((2 * fields,)),
            pltpu.SemaphoreType.DMA((fields,)),
        ],
        compiler_params=pltpu.CompilerParams(vmem_limit_bytes=32 << 20),
        cost_estimate=pl.CostEstimate(flops=20 * fields * oy * levels * ox, bytes_accessed=12 << 20, transcendentals=0),
        name="finish",
    )(received, depth, *in_hbm(mixed, first), *halos)


def shift(x, axis, step, wrap):
    count = lax.axis_size(axis)
    pairs = [(i, (i + step) % count) for i in range(count) if wrap or 0 <= i + step < count]
    return lax.ppermute(x, axis, pairs)


def on_device(
    atm_flux, sea_mask, src_block, dest_dev, dest_block, intersection_weights, coupling, inverses, ocean_state,
    depth_levels,
):
    lon = lax.axis_size("lon")
    devices = lax.axis_size("lat") * lon
    oy = ocean_state.shape[2]
    cap = max(SUB, 2 * src_block.shape[0] // devices)
    slots = regrid(
        cap, devices, lon, oy, src_block, dest_dev[:, 0], dest_block, coupling, atm_flux, sea_mask,
        intersection_weights,
    )
    received = lax.all_to_all(slots, ("lat", "lon"), 0, 0, tiled=True)
    mixed, first, north, south, side = mix(depth_levels, ocean_state, inverses)
    halos = (
        shift(south, "lat", 1, False),
        shift(north, "lat", -1, False),
        shift(side, "lon", -1, True),
        shift(side, "lon", 1, True),
    )
    return finish(cap, received, depth_levels, mixed, first, halos)


def solution(mesh):
    placed = (
        P(None, "lat", "lon"),
        P("lat", "lon"),
        P(("lat", "lon")),
        P(("lat", "lon"), None),
        P(("lat", "lon")),
        P(("lat", "lon"), None, None),
        P(),
        P(None, "lat", "lon", None, None),
        P(None, None, "lat", "lon"),
        P("lat", "lon"),
    )
    return jax.shard_map(
        on_device,
        mesh=mesh,
        in_specs=placed,
        out_specs=P(None, None, "lat", "lon"),
        check_vma=False,
    )
```

```python
import functools

import jax
import jax.numpy as jnp
from jax import lax
from jax.experimental import pallas as pl
from jax.experimental.pallas import tpu as pltpu
from jax.sharding import PartitionSpec as P

diffusion_rate = 0.2
LANES = 128
HALF = 64
SUB = 8
f32 = jnp.float32
bf16 = jnp.bfloat16
HBM = pl.BlockSpec(memory_space=pltpu.HBM)
VMEM = pl.BlockSpec(memory_space=pltpu.VMEM)


def split(x):
    high = x.astype(bf16)
    return high, (x - high.astype(f32)).astype(bf16)


def in_hbm(*arrays):
    return [pltpu.with_memory_space_constraint(x, pltpu.HBM) for x in arrays]


def iota(shape, dim):
    return lax.broadcasted_iota(jnp.int32, shape, dim)


def matmul(a, b):
    return jnp.dot(a, b, preferred_element_type=f32)


def padded_rows(x, rows):
    return x if x.shape[0] == rows else jnp.concatenate([x, jnp.zeros((rows - x.shape[0], LANES), x.dtype)], axis=0)


def regrid_kernel(
    cap, lat, lon, oy, batch, src_h, dev_h, blk_h, coupling_h, atm_h, mask_h, weights_h,
    out, rows, ids, count, src, dev, blk, coupling, atm, mask, weights, small_sem, big_sem,
):
    fluxes, atm_rows, _ = atm.shape
    fields = coupling.shape[0]
    devices = out.shape[0]
    per = fields * cap
    parts = weights.shape[0] // batch

    def big(k):
        here = pl.ds(pl.multiple_of(k * batch, batch), batch)
        return pltpu.make_async_copy(weights_h.at[here], weights.at[here], big_sem.at[k])

    small = [
        pltpu.make_async_copy(a, b, small_sem.at[k])
        for k, (a, b) in enumerate(
            (
                (coupling_h, coupling), (atm_h, atm), (mask_h, mask),
                (src_h, src), (dev_h, dev), (blk_h, blk),
            )
        )
    ]
    for copy in small:
        copy.start()
    for k in range(parts):
        big(k).start()

    def clear(d, carry):
        count[d] = 0
        out[d] = jnp.zeros(out.shape[1:], f32)
        return carry

    lax.fori_loop(0, devices, clear, 0)
    ids[...] = jnp.full(ids.shape, -1, jnp.int32)
    for copy in small:
        copy.wait()
    for tile in range(atm_rows // 16):
        here = slice(tile * 16, tile * 16 + 16)
        sea = mask[here, :].astype(f32)
        flux = [atm[f, here, :].astype(f32) * sea for f in range(fluxes)]
        for q in range(fields):
            total = coupling[q, 0] * flux[0]
            for f in range(1, fluxes):
                total = total + coupling[q, f] * flux[f]
            high = total.astype(bf16).astype(f32)
            rows[pl.ds(tile * 16 * SUB + q, 16, stride=SUB), :] = high
            rows[pl.ds(tile * 16 * SUB + fields + q, 16, stride=SUB), :] = total - high

    lane = iota((1, LANES), 1)
    lane_slot = (lane % per) // fields
    lane_row = (lane % fields) * oy

    def place(d):
        return lax.rem(d, lon) * lat + lax.div(d, lon)

    def part(k, carry):
        big(k).wait()
        for u in range(0, batch, 2):
            p = k * batch + u
            x = jnp.concatenate(
                [rows[pl.ds(pl.multiple_of(src[p + v] * SUB, SUB), SUB), :] for v in range(2)], axis=0
            ).astype(bf16)
            both = matmul(x, jnp.concatenate([weights[p], weights[p + 1]], axis=1))
            for v in range(2):
                d = dev[p + v]
                slot = jnp.minimum(count[d], cap - 1)
                count[d] = slot + 1
                half = both[v * SUB : v * SUB + SUB, v * LANES : (v + 1) * LANES]
                out[place(d), pl.ds(slot * fields, fields), :] = half[0:fields] + half[fields : 2 * fields]
                line = ids[pl.ds(d, 1), :]
                ids[pl.ds(d, 1), :] = jnp.where(lane_slot == slot, lane_row + blk[p + v], line)
        return carry

    lax.fori_loop(0, parts, part, 0)

    def halo(k):
        d = 2 * k
        turned = jnp.concatenate(
            [padded_rows(out[place(d + u), 0:per], HALF) for u in range(2)], axis=0
        ).T
        first, last = turned[0:1], turned[LANES - 1 : LANES]
        first_swapped = pltpu.roll(turned[0:SUB], HALF, 1)[0:1]
        last_swapped = pltpu.roll(turned[LANES - SUB : LANES], HALF, 1)[SUB - 1 : SUB]
        for u in range(2):
            b = lax.rem(d + u, lon)
            east = jnp.where(b == lon - 1, d + u - (lon - 1), d + u + 1)
            west = jnp.where(b == 0, d + u + (lon - 1), d + u - 1)
            here, to_east, to_west = place(d + u), place(east), place(west)
            out[here, per : per + 1] = ids[pl.ds(d + u, 1), :].astype(f32)
            sides = jnp.where(lane < HALF, ids[pl.ds(east, 1), :], ids[pl.ds(west, 1), :])
            out[here, per + 1 : per + 2] = sides.astype(f32)
            column = first if u == 0 else first_swapped
            out[to_west, per + 2 : per + 3] = jnp.where(lane < HALF, column, out[to_west, per + 2 : per + 3])
            column = last_swapped if u == 0 else last
            out[to_east, per + 2 : per + 3] = jnp.where(lane < HALF, out[to_east, per + 2 : per + 3], column)

    def halos(k, carry):
        for u in range(4):
            halo(k * 4 + u)
        return carry

    lax.fori_loop(0, devices // 8, halos, 0)


def regrid(cap, lat, lon, oy, src, dev, blk, coupling, atm, mask, weights):
    pairs, depth, width = weights.shape
    fields = coupling.shape[0]
    batch = 32
    devices = lat * lon
    tall = fields * cap + SUB
    return pl.pallas_call(
        functools.partial(regrid_kernel, cap, lat, lon, oy, batch),
        in_specs=[HBM] * 7,
        out_specs=VMEM,
        out_shape=jax.ShapeDtypeStruct((devices, tall, LANES), f32),
        scratch_shapes=[
            pltpu.VMEM((atm.shape[1] * SUB, LANES), f32),
            pltpu.VMEM((devices, LANES), jnp.int32),
            pltpu.SMEM((devices,), jnp.int32),
            pltpu.SMEM(src.shape, jnp.int32),
            pltpu.SMEM(dev.shape, jnp.int32),
            pltpu.SMEM(blk.shape, jnp.int32),
            pltpu.SMEM(coupling.shape, f32),
            pltpu.VMEM(atm.shape, bf16),
            pltpu.VMEM(mask.shape, jnp.int32),
            pltpu.VMEM(weights.shape, bf16),
            pltpu.SemaphoreType.DMA((6,)),
            pltpu.SemaphoreType.DMA((pairs // batch,)),
        ],
        compiler_params=pltpu.CompilerParams(vmem_limit_bytes=20 << 20),
        cost_estimate=pl.CostEstimate(flops=2 * 8 * pairs * depth * width, bytes_accessed=10 << 20, transcendentals=0),
        name="regrid",
    )(*in_hbm(src, dev, blk, coupling, atm, mask, weights))


def mix_kernel(
    depth_h, state_h, inv_h, mixed_h, first_h, north, south, side, depth_ref, mixed, inv, first, in_sems, out_sems
):
    fields, oy, levels, _ = mixed.shape
    depth_copy = pltpu.make_async_copy(depth_h, depth_ref, in_sems.at[2 * fields])
    depth_copy.start()
    for q in range(fields):
        for i in range(oy):
            pltpu.make_async_copy(state_h.at[q, :, i, :], mixed.at[q, i], in_sems.at[2 * q]).start()
        pltpu.make_async_copy(inv_h.at[q], inv.at[q], in_sems.at[2 * q + 1]).start()
    depth_copy.wait()
    level = iota((levels, LANES), 0)
    lane = iota((levels, LANES), 1)
    line = iota((1, LANES), 1)
    edge_depth = jnp.zeros((SUB, LANES), f32)
    for i in range(oy):
        turned = pltpu.roll(jnp.broadcast_to(depth_ref[i : i + 1, :].astype(f32), (SUB, LANES)), 2 * i + 1, 1)
        edge_depth = jnp.where(line // 2 == i, turned, edge_depth)

    def message(ref, q, row):
        ref[q, 0:levels] = mixed[q, row]
        names = padded_rows(first[q, row], LANES).T[0:1]
        ref[q, levels : levels + SUB] = jnp.concatenate(
            [depth_ref[row : row + 1, :].astype(f32), names, jnp.zeros((SUB - 2, LANES), f32)], axis=0
        )

    def field(q, carry):
        pltpu.make_async_copy(mixed_h.at[q], mixed.at[q], in_sems.at[2 * q]).wait()
        pltpu.make_async_copy(inv_h.at[q], inv.at[q], in_sems.at[2 * q + 1]).wait()

        def chunk(c, edges):
            here = jnp.zeros((levels, LANES), f32)
            for i in range(SUB):
                row = c * SUB + i
                active = level < depth_ref[pl.ds(row, 1), :]
                x = mixed[q, row]
                a = inv[q, row, 0]
                a_high, a_low = split(a)
                r_high, r_low = split(jnp.where(active, x, 0.0))
                product = matmul(
                    jnp.concatenate([a_high, a_low], axis=0), jnp.concatenate([r_high, r_low], axis=1)
                )
                solved = product[:levels, :LANES] + (product[levels:, :LANES] + product[:levels, LANES:])
                m = jnp.where(active, solved, x)
                mixed[q, row] = m
                column = jnp.broadcast_to(a[:, 0:1], (levels, LANES))
                first[q, row] = column
                here = jnp.where(lane // 2 == i, pltpu.roll(m, 2 * i + 1, 1), here)
                here = jnp.where(lane // 2 == HALF // 2 + i, column, here)
            return edges + pltpu.roll(here, 2 * SUB * c, 1)

        side[q, 0:levels] = lax.fori_loop(0, oy // SUB, chunk, jnp.zeros((levels, LANES), f32))
        side[q, levels : levels + SUB] = edge_depth
        message(north, q, 0)
        message(south, q, oy - 1)
        pltpu.make_async_copy(mixed.at[q], mixed_h.at[q], out_sems.at[2 * q]).start()
        pltpu.make_async_copy(first.at[q], first_h.at[q], out_sems.at[2 * q + 1]).start()
        return carry

    lax.fori_loop(0, fields, field, 0)
    for q in range(fields):
        pltpu.make_async_copy(mixed.at[q], mixed_h.at[q], out_sems.at[2 * q]).wait()
        pltpu.make_async_copy(first.at[q], first_h.at[q], out_sems.at[2 * q + 1]).wait()


def mix(depth, state, inverses):
    fields, levels, oy, ox = state.shape
    edge_shape = jax.ShapeDtypeStruct((fields, levels + SUB, ox), f32)
    full = (fields, oy, levels, ox)
    return pl.pallas_call(
        mix_kernel,
        in_specs=[HBM] * 3,
        out_specs=[HBM] * 2 + [VMEM] * 3,
        out_shape=[pltpu.HBM(full, f32), pltpu.HBM(full, f32), edge_shape, edge_shape, edge_shape],
        scratch_shapes=[
            pltpu.VMEM(depth.shape, jnp.int32),
            pltpu.VMEM(full, f32),
            pltpu.VMEM(inverses.shape, f32),
            pltpu.VMEM(full, f32),
            pltpu.SemaphoreType.DMA((2 * fields + 1,)),
            pltpu.SemaphoreType.DMA((2 * fields,)),
        ],
        compiler_params=pltpu.CompilerParams(vmem_limit_bytes=32 << 20),
        cost_estimate=pl.CostEstimate(flops=2 * 4 * fields * oy * levels * levels * ox, bytes_accessed=16 << 20, transcendentals=0),
        name="mix",
    )(*in_hbm(depth, state, inverses))


def collect_kernel(cap, fields, oy, recv, out):
    lat = out.shape[0]
    lon = recv.shape[0] // lat
    per = fields * cap
    group = LANES // per
    forced = fields * oy
    square_row = iota((LANES, LANES), 0).astype(f32)
    line = iota((1, LANES), 1)
    row = iota((2 * oy, LANES), 0).astype(f32)
    lane_base = ((line % fields) * oy).astype(f32)
    lane_side = (line // HALF).astype(f32)
    small_row, small_lane = iota((SUB, LANES), 0), iota((SUB, LANES), 1)
    pick = jnp.where((small_lane % fields == small_row) & (small_lane % HALF < per), 1.0, 0.0).astype(bf16)
    nothing = jnp.zeros((fields, LANES), f32)
    for a in range(lat):
        total = jnp.zeros((LANES, 2 * LANES), f32)
        for tile in range(lon // group):
            places = [(tile * group + s) * lat + a for s in range(group)]
            ids = recv[places[0], per : per + 1, :]
            for s in range(1, group):
                ids = jnp.where(line // per == s, recv[places[s], per : per + 1, :], ids)
            hot = jnp.where(square_row == ids, 1.0, 0.0).astype(bf16)
            high, low = split(jnp.concatenate([recv[p, 0:per, :] for p in places], axis=0))
            total = total + matmul(hot, jnp.concatenate([high, low], axis=1))
        total = total[:, :LANES] + total[:, LANES:]
        out[a, 0:forced] = total
        if a == 0:
            out[a, forced : forced + fields] = nothing
        if a == lat - 1:
            out[a, forced + fields : forced + 2 * fields] = nothing
        for q in range(fields):
            if a + 1 < lat:
                out[a + 1, forced + q : forced + q + 1] = total[q * oy + oy - 1 : q * oy + oy]
            if a > 0:
                out[a - 1, forced + fields + q : forced + fields + q + 1] = total[q * oy : q * oy + 1]
        spread = jnp.zeros((2 * oy, LANES), f32)
        for b in range(lon):
            place = 2.0 * (recv[b * lat + a, per + 1 : per + 2, :] - lane_base) + lane_side
            spread = spread + jnp.where(place == row, recv[b * lat + a, per + 2 : per + 3, :], 0.0)
        high, low = split(padded_rows(spread, LANES).T)
        out[a, forced + SUB : forced + 2 * SUB] = matmul(pick, high) + matmul(pick, low)


def collect(cap, fields, oy, lat, received):
    return pl.pallas_call(
        functools.partial(collect_kernel, cap, fields, oy),
        in_specs=[VMEM],
        out_specs=VMEM,
        out_shape=jax.ShapeDtypeStruct((lat, fields * oy + 2 * SUB, LANES), f32),
        compiler_params=pltpu.CompilerParams(vmem_limit_bytes=16 << 20),
        name="collect",
    )(received)


def finish_kernel(
    recv, depth_ref, mixed_h, first_h, north, south, east, west,
    out_h, forcing, z, keep, halo, z_north, z_south, mixed, first, stage, in_sems, out_sems,
):
    fields, oy, levels, _ = mixed.shape
    level = iota((levels, LANES), 0)
    lanes = iota((levels, LANES), 1)
    square_row = iota((LANES, LANES), 0)
    square_lane = iota((LANES, LANES), 1)
    line = iota((1, LANES), 1)
    even = line % 2 == 0
    for q in range(fields):
        pltpu.make_async_copy(mixed_h.at[q], mixed.at[q], in_sems.at[2 * q]).start()
        pltpu.make_async_copy(first_h.at[q], first.at[q], in_sems.at[2 * q + 1]).start()

    total = recv[0]
    for a in range(1, recv.shape[0]):
        total = total + recv[a]
    forced_rows = fields * oy
    forcing[...] = total[0:forced_rows]
    rows = total[forced_rows : forced_rows + SUB]
    columns = total[forced_rows + SUB :]

    depth = depth_ref[...]
    wide = iota((oy, LANES), 1)

    def upright(ref, place):
        value = jnp.where(wide == 2 * iota((oy, LANES), 0) + place, ref[0, levels : levels + 1, :], 0.0)
        return jnp.sum(value, axis=1, keepdims=True).astype(jnp.int32)

    to_east = jnp.where(wide == LANES - 1, upright(east, 1), pltpu.roll(depth, LANES - 1, 1))
    to_west = jnp.where(wide == 0, upright(west, 0), pltpu.roll(depth, 1, 1))
    to_north = jnp.concatenate([north[0, levels : levels + 1, :].astype(jnp.int32), depth[: oy - 1]], axis=0)
    to_south = jnp.concatenate([depth[1:], south[0, levels : levels + 1, :].astype(jnp.int32)], axis=0)
    for i in range(oy):
        sides = jnp.where(level < to_east[i : i + 1], diffusion_rate, 0.0)
        for other in (to_west, to_north, to_south):
            sides = sides + jnp.where(level < other[i : i + 1], diffusion_rate, 0.0)
        keep[i] = jnp.where(level < depth[i : i + 1], 1.0 - sides, 1.0)

    def outer(target, ref, start):
        names = padded_rows(
            jnp.concatenate([ref[q, levels + 1 : levels + 2, :] for q in range(fields)], axis=0), LANES
        ).T
        active = level < ref[0, levels : levels + 1, :].astype(jnp.int32)
        for q in range(fields):
            value = ref[q, 0:levels] + names[0:levels, q : q + 1] * rows[start + q : start + q + 1]
            target[q] = jnp.where(active, value, 0.0)

    outer(z_north, north, 0)
    outer(z_south, south, fields)
    for q in range(fields):
        cells = jnp.where(even, pltpu.roll(east[q], LANES - 1, 1), pltpu.roll(west[q], 1, 1))
        names = pltpu.roll(jnp.where(even, east[q], west[q]), HALF, 1)
        active = level < cells[levels : levels + 1].astype(jnp.int32)
        value = cells[0:levels] + names[0:levels] * columns[q : q + 1]
        halo[q] = jnp.where(active & (line < 2 * oy), value, 0.0)

    both = jnp.where((square_row == square_lane + 1) | (square_row == square_lane - 1), 1.0, 0.0).astype(bf16)
    both = jnp.concatenate([both, both], axis=0)
    ends = (lanes == 0) | (lanes == LANES - 1)

    def field(q, carry):
        pltpu.make_async_copy(mixed_h.at[q], mixed.at[q], in_sems.at[2 * q]).wait()
        pltpu.make_async_copy(first_h.at[q], first.at[q], in_sems.at[2 * q + 1]).wait()
        z[0] = z_north[q]
        z[oy + 1] = z_south[q]

        def solve(c, carry):
            for i in range(SUB):
                r = c * SUB + i
                m0 = mixed[q, r]
                forced = m0 + first[q, r] * forcing[pl.ds(q * oy + r, 1), :]
                active = level < depth_ref[pl.ds(r, 1), :]
                z[r + 1] = jnp.where(active, forced, 0.0)
                mixed[q, r] = jnp.where(active, forced, m0)
            return carry

        lax.fori_loop(0, oy // SUB, solve, 0)

        def diffuse(c, carry):
            start = c * SUB
            high, low = split(z[pl.ds(start + 1, SUB)].reshape(SUB * levels, LANES))
            sides = matmul(jnp.concatenate([high, low], axis=1), both)
            edge = pltpu.roll(halo[q], (LANES - 2 * SUB * c) % LANES, 1)
            for i in range(SUB):
                r = start + i
                outside = jnp.where(ends, pltpu.roll(edge, LANES - 1 - 2 * i, 1), 0.0)
                around = (z[r] + z[r + 2]) + (sides[i * levels : (i + 1) * levels] + outside)
                scale = jnp.where(level < depth_ref[pl.ds(r, 1), :], diffusion_rate, 0.0)
                stage[q, r] = mixed[q, r] * keep[r] + scale * around
                pltpu.make_async_copy(stage.at[q, r], out_h.at[q, :, r, :], out_sems.at[q]).start()
            return carry

        lax.fori_loop(0, oy // SUB, diffuse, 0)
        return carry

    lax.fori_loop(0, fields, field, 0)
    for q in range(fields):
        pltpu.make_async_copy(stage.at[q], mixed_h.at[q], out_sems.at[q]).wait()


def finish(received, depth, mixed, first, halos):
    fields, oy, levels, ox = mixed.shape
    edge = pltpu.VMEM((fields, levels, ox), f32)
    full = pltpu.VMEM((fields, oy, levels, ox), f32)
    return pl.pallas_call(
        finish_kernel,
        in_specs=[VMEM] * 2 + [HBM] * 2 + [VMEM] * 4,
        out_specs=HBM,
        out_shape=pltpu.HBM((fields, levels, oy, ox), f32),
        scratch_shapes=[
            pltpu.VMEM((fields * oy, ox), f32),
            pltpu.VMEM((oy + 2, levels, ox), f32),
            pltpu.VMEM((oy, levels, ox), f32),
            edge,
            edge,
            edge,
            full,
            full,
            full,
            pltpu.SemaphoreType.DMA((2 * fields,)),
            pltpu.SemaphoreType.DMA((fields,)),
        ],
        compiler_params=pltpu.CompilerParams(vmem_limit_bytes=32 << 20),
        cost_estimate=pl.CostEstimate(flops=20 * fields * oy * levels * ox, bytes_accessed=12 << 20, transcendentals=0),
        name="finish",
    )(received, depth, *in_hbm(mixed, first), *halos)


def shift(x, axis, step, wrap):
    count = lax.axis_size(axis)
    pairs = [(i, (i + step) % count) for i in range(count) if wrap or 0 <= i + step < count]
    return lax.ppermute(x, axis, pairs)


def on_device(
    atm_flux, sea_mask, src_block, dest_dev, dest_block, intersection_weights, coupling, inverses, ocean_state,
    depth_levels,
):
    lat, lon = lax.axis_size("lat"), lax.axis_size("lon")
    fields, _, oy, _ = ocean_state.shape
    cap = max(SUB, 2 * src_block.shape[0] // (lat * lon))
    slots = regrid(
        cap, lat, lon, oy, src_block, dest_dev[:, 0], dest_block, coupling, atm_flux, sea_mask,
        intersection_weights,
    )
    in_plane = lax.all_to_all(slots, "lon", 0, 0, tiled=True)
    mixed, first, north, south, side = mix(depth_levels, ocean_state, inverses)
    halos = (
        shift(south, "lat", 1, False),
        shift(north, "lat", -1, False),
        shift(side, "lon", -1, True),
        shift(side, "lon", 1, True),
    )
    received = lax.all_to_all(collect(cap, fields, oy, lat, in_plane), "lat", 0, 0, tiled=True)
    return finish(received, depth_levels, mixed, first, halos)


def solution(mesh):
    placed = (
        P(None, "lat", "lon"),
        P("lat", "lon"),
        P(("lat", "lon")),
        P(("lat", "lon"), None),
        P(("lat", "lon")),
        P(("lat", "lon"), None, None),
        P(),
        P(None, "lat", "lon", None, None),
        P(None, None, "lat", "lon"),
        P("lat", "lon"),
    )
    return jax.shard_map(
        on_device,
        mesh=mesh,
        in_specs=placed,
        out_specs=P(None, None, "lat", "lon"),
        check_vma=False,
    )
```

```python
import functools

import jax
import jax.numpy as jnp
from jax import lax
from jax.experimental import pallas as pl
from jax.experimental.pallas import tpu as pltpu
from jax.sharding import PartitionSpec as P

diffusion_rate = 0.2
LANES = 128
HALF = 64
SUB = 8
f32 = jnp.float32
bf16 = jnp.bfloat16
HBM = pl.BlockSpec(memory_space=pltpu.HBM)
VMEM = pl.BlockSpec(memory_space=pltpu.VMEM)


def split(x):
    high = x.astype(bf16)
    return high, (x - high.astype(f32)).astype(bf16)


def in_hbm(*arrays):
    return [pltpu.with_memory_space_constraint(x, pltpu.HBM) for x in arrays]


def iota(shape, dim):
    return lax.broadcasted_iota(jnp.int32, shape, dim)


def matmul(a, b):
    return jnp.dot(a, b, preferred_element_type=f32)


def padded_rows(x, rows):
    return x if x.shape[0] == rows else jnp.concatenate([x, jnp.zeros((rows - x.shape[0], LANES), x.dtype)], axis=0)


def regrid_kernel(
    cap, lat, lon, oy, batch, src_h, dev_h, blk_h, coupling_h, atm_h, mask_h, weights_h,
    out, rows, ids, count, src, dev, blk, coupling, atm, mask, weights, small_sem, big_sem,
):
    fluxes, atm_rows, _ = atm.shape
    fields = coupling.shape[0]
    devices = out.shape[0]
    per = fields * cap
    parts = weights.shape[0] // batch

    def big(k):
        here = pl.ds(pl.multiple_of(k * batch, batch), batch)
        return pltpu.make_async_copy(weights_h.at[here], weights.at[here], big_sem.at[k])

    small = [
        pltpu.make_async_copy(a, b, small_sem.at[k])
        for k, (a, b) in enumerate(
            (
                (coupling_h, coupling), (atm_h, atm), (mask_h, mask),
                (src_h, src), (dev_h, dev), (blk_h, blk),
            )
        )
    ]
    for copy in small:
        copy.start()
    for k in range(parts):
        big(k).start()

    def clear(d, carry):
        count[d] = 0
        out[d] = jnp.zeros(out.shape[1:], f32)
        return carry

    lax.fori_loop(0, devices, clear, 0)
    ids[...] = jnp.full(ids.shape, -1, jnp.int32)
    for copy in small:
        copy.wait()
    for tile in range(atm_rows // 16):
        here = slice(tile * 16, tile * 16 + 16)
        sea = mask[here, :].astype(f32)
        flux = [atm[f, here, :].astype(f32) * sea for f in range(fluxes)]
        for q in range(fields):
            total = coupling[q, 0] * flux[0]
            for f in range(1, fluxes):
                total = total + coupling[q, f] * flux[f]
            high = total.astype(bf16).astype(f32)
            rows[pl.ds(tile * 16 * SUB + q, 16, stride=SUB), :] = high
            rows[pl.ds(tile * 16 * SUB + fields + q, 16, stride=SUB), :] = total - high

    lane = iota((1, LANES), 1)
    lane_slot = (lane % per) // fields
    lane_row = (lane % fields) * oy

    def place(d):
        return lax.rem(d, lon) * lat + lax.div(d, lon)

    def part(k, carry):
        big(k).wait()
        for u in range(0, batch, 2):
            p = k * batch + u
            x = jnp.concatenate(
                [rows[pl.ds(pl.multiple_of(src[p + v] * SUB, SUB), SUB), :] for v in range(2)], axis=0
            ).astype(bf16)
            both = matmul(x, jnp.concatenate([weights[p], weights[p + 1]], axis=1))
            for v in range(2):
                d = dev[p + v]
                slot = jnp.minimum(count[d], cap - 1)
                count[d] = slot + 1
                half = both[v * SUB : v * SUB + SUB, v * LANES : (v + 1) * LANES]
                out[place(d), pl.ds(slot * fields, fields), :] = half[0:fields] + half[fields : 2 * fields]
                line = ids[pl.ds(d, 1), :]
                ids[pl.ds(d, 1), :] = jnp.where(lane_slot == slot, lane_row + blk[p + v], line)
        return carry

    lax.fori_loop(0, parts, part, 0)

    def halo(k):
        d = 2 * k
        turned = jnp.concatenate(
            [padded_rows(out[place(d + u), 0:per], HALF) for u in range(2)], axis=0
        ).T
        first, last = turned[0:1], turned[LANES - 1 : LANES]
        first_swapped = pltpu.roll(turned[0:SUB], HALF, 1)[0:1]
        last_swapped = pltpu.roll(turned[LANES - SUB : LANES], HALF, 1)[SUB - 1 : SUB]
        for u in range(2):
            b = lax.rem(d + u, lon)
            east = jnp.where(b == lon - 1, d + u - (lon - 1), d + u + 1)
            west = jnp.where(b == 0, d + u + (lon - 1), d + u - 1)
            here, to_east, to_west = place(d + u), place(east), place(west)
            out[here, per : per + 1] = ids[pl.ds(d + u, 1), :].astype(f32)
            sides = jnp.where(lane < HALF, ids[pl.ds(east, 1), :], ids[pl.ds(west, 1), :])
            out[here, per + 1 : per + 2] = sides.astype(f32)
            column = first if u == 0 else first_swapped
            out[to_west, per + 2 : per + 3] = jnp.where(lane < HALF, column, out[to_west, per + 2 : per + 3])
            column = last_swapped if u == 0 else last
            out[to_east, per + 2 : per + 3] = jnp.where(lane < HALF, out[to_east, per + 2 : per + 3], column)

    def halos(k, carry):
        for u in range(4):
            halo(k * 4 + u)
        return carry

    lax.fori_loop(0, devices // 8, halos, 0)


def regrid(cap, lat, lon, oy, src, dev, blk, coupling, atm, mask, weights):
    pairs, depth, width = weights.shape
    fields = coupling.shape[0]
    batch = 32
    devices = lat * lon
    tall = fields * cap + SUB
    return pl.pallas_call(
        functools.partial(regrid_kernel, cap, lat, lon, oy, batch),
        in_specs=[HBM] * 7,
        out_specs=VMEM,
        out_shape=jax.ShapeDtypeStruct((devices, tall, LANES), f32),
        scratch_shapes=[
            pltpu.VMEM((atm.shape[1] * SUB, LANES), f32),
            pltpu.VMEM((devices, LANES), jnp.int32),
            pltpu.SMEM((devices,), jnp.int32),
            pltpu.SMEM(src.shape, jnp.int32),
            pltpu.SMEM(dev.shape, jnp.int32),
            pltpu.SMEM(blk.shape, jnp.int32),
            pltpu.SMEM(coupling.shape, f32),
            pltpu.VMEM(atm.shape, bf16),
            pltpu.VMEM(mask.shape, jnp.int32),
            pltpu.VMEM(weights.shape, bf16),
            pltpu.SemaphoreType.DMA((6,)),
            pltpu.SemaphoreType.DMA((pairs // batch,)),
        ],
        compiler_params=pltpu.CompilerParams(vmem_limit_bytes=20 << 20),
        cost_estimate=pl.CostEstimate(flops=2 * 8 * pairs * depth * width, bytes_accessed=10 << 20, transcendentals=0),
        name="regrid",
    )(*in_hbm(src, dev, blk, coupling, atm, mask, weights))


def mix_kernel(
    depth_h, state_h, inv_h, mixed_h, first_h, north, south, side,
    depth_ref, state, mixed, inv, first, in_sems, out_sems,
):
    fields, oy, levels, _ = mixed.shape
    depth_copy = pltpu.make_async_copy(depth_h, depth_ref, in_sems.at[2 * fields])
    depth_copy.start()
    for q in range(fields):
        for i in range(oy):
            pltpu.make_async_copy(state_h.at[q, :, i, :], state.at[q, i], in_sems.at[2 * q]).start()
        pltpu.make_async_copy(inv_h.at[q], inv.at[q], in_sems.at[2 * q + 1]).start()
    depth_copy.wait()
    level = iota((levels, LANES), 0)
    lane = iota((levels, LANES), 1)
    line = iota((1, LANES), 1)
    edge_depth = jnp.zeros((SUB, LANES), f32)
    for i in range(oy):
        turned = pltpu.roll(jnp.broadcast_to(depth_ref[i : i + 1, :].astype(f32), (SUB, LANES)), 2 * i + 1, 1)
        edge_depth = jnp.where(line // 2 == i, turned, edge_depth)

    def message(ref, q, row):
        ref[q, 0:levels] = mixed[q, row]
        names = padded_rows(first[q, row], LANES).T[0:1]
        ref[q, levels : levels + SUB] = jnp.concatenate(
            [depth_ref[row : row + 1, :].astype(f32), names, jnp.zeros((SUB - 2, LANES), f32)], axis=0
        )

    def field(q, carry):
        pltpu.make_async_copy(mixed_h.at[q], state.at[q], in_sems.at[2 * q]).wait()
        pltpu.make_async_copy(inv_h.at[q], inv.at[q], in_sems.at[2 * q + 1]).wait()

        def chunk(c, edges):
            here = jnp.zeros((levels, LANES), f32)
            for i in range(SUB):
                row = c * SUB + i
                active = level < depth_ref[pl.ds(row, 1), :]
                x = state[q, row]
                a = inv[q, row, 0]
                a_high, a_low = split(a)
                r_high, r_low = split(jnp.where(active, x, 0.0))
                product = matmul(
                    jnp.concatenate([a_high, a_low], axis=0), jnp.concatenate([r_high, r_low], axis=1)
                )
                solved = product[:levels, :LANES] + (product[levels:, :LANES] + product[:levels, LANES:])
                m = jnp.where(active, solved, x)
                mixed[q, row] = m
                column = jnp.broadcast_to(a[:, 0:1], (levels, LANES))
                first[q, row] = column
                here = jnp.where(lane // 2 == i, pltpu.roll(m, 2 * i + 1, 1), here)
                here = jnp.where(lane // 2 == HALF // 2 + i, column, here)
            return edges + pltpu.roll(here, 2 * SUB * c, 1)

        side[q, 0:levels] = lax.fori_loop(0, oy // SUB, chunk, jnp.zeros((levels, LANES), f32))
        side[q, levels : levels + SUB] = edge_depth
        message(north, q, 0)
        message(south, q, oy - 1)
        pltpu.make_async_copy(mixed.at[q], mixed_h.at[q], out_sems.at[2 * q]).start()
        pltpu.make_async_copy(first.at[q], first_h.at[q], out_sems.at[2 * q + 1]).start()
        return carry

    lax.fori_loop(0, fields, field, 0)
    for q in range(fields):
        pltpu.make_async_copy(mixed.at[q], mixed_h.at[q], out_sems.at[2 * q]).wait()
        pltpu.make_async_copy(first.at[q], first_h.at[q], out_sems.at[2 * q + 1]).wait()


def mix(depth, state, inverses):
    fields, levels, oy, ox = state.shape
    edge_shape = jax.ShapeDtypeStruct((fields, levels + SUB, ox), f32)
    full = (fields, oy, levels, ox)
    return pl.pallas_call(
        mix_kernel,
        in_specs=[HBM] * 3,
        out_specs=[HBM] * 2 + [VMEM] * 3,
        out_shape=[pltpu.HBM(full, f32), pltpu.HBM(full, f32), edge_shape, edge_shape, edge_shape],
        scratch_shapes=[
            pltpu.VMEM(depth.shape, jnp.int32),
            pltpu.VMEM(full, f32),
            pltpu.VMEM(full, f32),
            pltpu.VMEM(inverses.shape, f32),
            pltpu.VMEM(full, f32),
            pltpu.SemaphoreType.DMA((2 * fields + 1,)),
            pltpu.SemaphoreType.DMA((2 * fields,)),
        ],
        compiler_params=pltpu.CompilerParams(vmem_limit_bytes=32 << 20),
        cost_estimate=pl.CostEstimate(flops=2 * 4 * fields * oy * levels * levels * ox, bytes_accessed=16 << 20, transcendentals=0),
        name="mix",
    )(*in_hbm(depth, state, inverses))


def collect_kernel(cap, fields, oy, recv, after, out):
    lat = out.shape[0]
    lon = recv.shape[0] // lat
    per = fields * cap
    group = LANES // per
    forced = fields * oy
    square_row = iota((LANES, LANES), 0).astype(f32)
    line = iota((1, LANES), 1)
    row = iota((2 * oy, LANES), 0).astype(f32)
    lane_base = ((line % fields) * oy).astype(f32)
    lane_side = (line // HALF).astype(f32)
    small_row, small_lane = iota((SUB, LANES), 0), iota((SUB, LANES), 1)
    pick = jnp.where((small_lane % fields == small_row) & (small_lane % HALF < per), 1.0, 0.0).astype(bf16)
    nothing = jnp.zeros((fields, LANES), f32)
    for a in range(lat):
        total = jnp.zeros((LANES, 2 * LANES), f32)
        for tile in range(lon // group):
            places = [(tile * group + s) * lat + a for s in range(group)]
            ids = recv[places[0], per : per + 1, :]
            for s in range(1, group):
                ids = jnp.where(line // per == s, recv[places[s], per : per + 1, :], ids)
            hot = jnp.where(square_row == ids, 1.0, 0.0).astype(bf16)
            high, low = split(jnp.concatenate([recv[p, 0:per, :] for p in places], axis=0))
            total = total + matmul(hot, jnp.concatenate([high, low], axis=1))
        total = total[:, :LANES] + total[:, LANES:]
        out[a, 0:forced] = total
        if a == 0:
            out[a, forced : forced + fields] = nothing
        if a == lat - 1:
            out[a, forced + fields : forced + 2 * fields] = nothing
        for q in range(fields):
            if a + 1 < lat:
                out[a + 1, forced + q : forced + q + 1] = total[q * oy + oy - 1 : q * oy + oy]
            if a > 0:
                out[a - 1, forced + fields + q : forced + fields + q + 1] = total[q * oy : q * oy + 1]
        spread = jnp.zeros((2 * oy, LANES), f32)
        for b in range(lon):
            place = 2.0 * (recv[b * lat + a, per + 1 : per + 2, :] - lane_base) + lane_side
            spread = spread + jnp.where(place == row, recv[b * lat + a, per + 2 : per + 3, :], 0.0)
        high, low = split(padded_rows(spread, LANES).T)
        out[a, forced + SUB : forced + 2 * SUB] = matmul(pick, high) + matmul(pick, low)


def collect(cap, fields, oy, lat, received, after):
    return pl.pallas_call(
        functools.partial(collect_kernel, cap, fields, oy),
        in_specs=[VMEM, pl.BlockSpec(memory_space=pl.ANY)],
        out_specs=VMEM,
        out_shape=jax.ShapeDtypeStruct((lat, fields * oy + 2 * SUB, LANES), f32),
        compiler_params=pltpu.CompilerParams(vmem_limit_bytes=16 << 20),
        name="collect",
    )(received, after)


def finish_kernel(
    recv, depth_ref, mixed_h, first_h, north, south, east, west,
    out_h, forcing, z, keep, halo, z_north, z_south, mixed, first, stage, in_sems, out_sems,
):
    fields, oy, levels, _ = mixed.shape
    level = iota((levels, LANES), 0)
    lanes = iota((levels, LANES), 1)
    square_row = iota((LANES, LANES), 0)
    square_lane = iota((LANES, LANES), 1)
    line = iota((1, LANES), 1)
    even = line % 2 == 0
    for q in range(fields):
        pltpu.make_async_copy(mixed_h.at[q], mixed.at[q], in_sems.at[2 * q]).start()
        pltpu.make_async_copy(first_h.at[q], first.at[q], in_sems.at[2 * q + 1]).start()

    total = recv[0]
    for a in range(1, recv.shape[0]):
        total = total + recv[a]
    forced_rows = fields * oy
    forcing[...] = total[0:forced_rows]
    rows = total[forced_rows : forced_rows + SUB]
    columns = total[forced_rows + SUB :]

    depth = depth_ref[...]
    wide = iota((oy, LANES), 1)

    def upright(ref, place):
        value = jnp.where(wide == 2 * iota((oy, LANES), 0) + place, ref[0, levels : levels + 1, :], 0.0)
        return jnp.sum(value, axis=1, keepdims=True).astype(jnp.int32)

    to_east = jnp.where(wide == LANES - 1, upright(east, 1), pltpu.roll(depth, LANES - 1, 1))
    to_west = jnp.where(wide == 0, upright(west, 0), pltpu.roll(depth, 1, 1))
    to_north = jnp.concatenate([north[0, levels : levels + 1, :].astype(jnp.int32), depth[: oy - 1]], axis=0)
    to_south = jnp.concatenate([depth[1:], south[0, levels : levels + 1, :].astype(jnp.int32)], axis=0)
    for i in range(oy):
        sides = jnp.where(level < to_east[i : i + 1], diffusion_rate, 0.0)
        for other in (to_west, to_north, to_south):
            sides = sides + jnp.where(level < other[i : i + 1], diffusion_rate, 0.0)
        keep[i] = 1.0 - sides

    def outer(target, ref, start):
        names = padded_rows(
            jnp.concatenate([ref[q, levels + 1 : levels + 2, :] for q in range(fields)], axis=0), LANES
        ).T
        active = level < ref[0, levels : levels + 1, :].astype(jnp.int32)
        for q in range(fields):
            value = ref[q, 0:levels] + names[0:levels, q : q + 1] * rows[start + q : start + q + 1]
            target[q] = jnp.where(active, value, 0.0)

    outer(z_north, north, 0)
    outer(z_south, south, fields)
    for q in range(fields):
        cells = jnp.where(even, pltpu.roll(east[q], LANES - 1, 1), pltpu.roll(west[q], 1, 1))
        names = pltpu.roll(jnp.where(even, east[q], west[q]), HALF, 1)
        active = level < cells[levels : levels + 1].astype(jnp.int32)
        value = cells[0:levels] + names[0:levels] * columns[q : q + 1]
        halo[q] = jnp.where(active & (line < 2 * oy), value, 0.0)

    both = jnp.where((square_row == square_lane + 1) | (square_row == square_lane - 1), 1.0, 0.0).astype(bf16)
    both = jnp.concatenate([both, both], axis=0)
    ends = (lanes == 0) | (lanes == LANES - 1)

    def field(q, carry):
        pltpu.make_async_copy(mixed_h.at[q], mixed.at[q], in_sems.at[2 * q]).wait()
        pltpu.make_async_copy(first_h.at[q], first.at[q], in_sems.at[2 * q + 1]).wait()
        z[0] = z_north[q]
        z[oy + 1] = z_south[q]

        def solve(c, carry):
            for i in range(SUB):
                r = c * SUB + i
                forced = mixed[q, r] + first[q, r] * forcing[pl.ds(q * oy + r, 1), :]
                z[r + 1] = jnp.where(level < depth_ref[pl.ds(r, 1), :], forced, 0.0)
            return carry

        lax.fori_loop(0, oy // SUB, solve, 0)

        def diffuse(c, carry):
            start = c * SUB
            high, low = split(z[pl.ds(start + 1, SUB)].reshape(SUB * levels, LANES))
            sides = matmul(jnp.concatenate([high, low], axis=1), both)
            edge = pltpu.roll(halo[q], (LANES - 2 * SUB * c) % LANES, 1)
            for i in range(SUB):
                r = start + i
                outside = jnp.where(ends, pltpu.roll(edge, LANES - 1 - 2 * i, 1), 0.0)
                around = (z[r] + z[r + 2]) + (sides[i * levels : (i + 1) * levels] + outside)
                active = level < depth_ref[pl.ds(r, 1), :]
                stage[q, r] = jnp.where(active, z[r + 1] * keep[r] + diffusion_rate * around, mixed[q, r])
            for i in range(SUB):
                r = start + i
                pltpu.make_async_copy(stage.at[q, r], out_h.at[q, :, r, :], out_sems.at[q]).start()
            return carry

        lax.fori_loop(0, oy // SUB, diffuse, 0)
        return carry

    lax.fori_loop(0, fields, field, 0)
    for q in range(fields):
        pltpu.make_async_copy(stage.at[q], mixed_h.at[q], out_sems.at[q]).wait()


def finish(received, depth, mixed, first, halos):
    fields, oy, levels, ox = mixed.shape
    edge = pltpu.VMEM((fields, levels, ox), f32)
    full = pltpu.VMEM((fields, oy, levels, ox), f32)
    return pl.pallas_call(
        finish_kernel,
        in_specs=[VMEM] * 2 + [HBM] * 2 + [VMEM] * 4,
        out_specs=HBM,
        out_shape=pltpu.HBM((fields, levels, oy, ox), f32),
        scratch_shapes=[
            pltpu.VMEM((fields * oy, ox), f32),
            pltpu.VMEM((oy + 2, levels, ox), f32),
            pltpu.VMEM((oy, levels, ox), f32),
            edge,
            edge,
            edge,
            full,
            full,
            full,
            pltpu.SemaphoreType.DMA((2 * fields,)),
            pltpu.SemaphoreType.DMA((fields,)),
        ],
        compiler_params=pltpu.CompilerParams(vmem_limit_bytes=32 << 20),
        cost_estimate=pl.CostEstimate(flops=20 * fields * oy * levels * ox, bytes_accessed=12 << 20, transcendentals=0),
        name="finish",
    )(received, depth, *in_hbm(mixed, first), *halos)


def shift(x, axis, step, wrap):
    count = lax.axis_size(axis)
    pairs = [(i, (i + step) % count) for i in range(count) if wrap or 0 <= i + step < count]
    return lax.ppermute(x, axis, pairs)


def on_device(
    atm_flux, sea_mask, src_block, dest_dev, dest_block, intersection_weights, coupling, inverses, ocean_state,
    depth_levels,
):
    lat, lon = lax.axis_size("lat"), lax.axis_size("lon")
    fields, _, oy, _ = ocean_state.shape
    cap = max(SUB, 2 * src_block.shape[0] // (lat * lon))
    slots = regrid(
        cap, lat, lon, oy, src_block, dest_dev[:, 0], dest_block, coupling, atm_flux, sea_mask,
        intersection_weights,
    )
    in_plane = lax.all_to_all(slots, "lon", 0, 0, tiled=True)
    mixed, first, north, south, side = mix(depth_levels, ocean_state, inverses)
    halos = (
        shift(south, "lat", 1, False),
        shift(north, "lat", -1, False),
        shift(side, "lon", -1, True),
        shift(side, "lon", 1, True),
    )
    received = lax.all_to_all(collect(cap, fields, oy, lat, in_plane, side), "lat", 0, 0, tiled=True)
    return finish(received, depth_levels, mixed, first, halos)


def solution(mesh):
    placed = (
        P(None, "lat", "lon"),
        P("lat", "lon"),
        P(("lat", "lon")),
        P(("lat", "lon"), None),
        P(("lat", "lon")),
        P(("lat", "lon"), None, None),
        P(),
        P(None, "lat", "lon", None, None),
        P(None, None, "lat", "lon"),
        P("lat", "lon"),
    )
    return jax.shard_map(
        on_device,
        mesh=mesh,
        in_specs=placed,
        out_specs=P(None, None, "lat", "lon"),
        check_vma=False,
    )
```

```python
import functools

import jax
import jax.numpy as jnp
from jax import lax
from jax.experimental import pallas as pl
from jax.experimental.pallas import tpu as pltpu
from jax.sharding import PartitionSpec as P

diffusion_rate = 0.2
LANES = 128
HALF = 64
SUB = 8
f32 = jnp.float32
bf16 = jnp.bfloat16
HBM = pl.BlockSpec(memory_space=pltpu.HBM)
VMEM = pl.BlockSpec(memory_space=pltpu.VMEM)


def split(x):
    high = x.astype(bf16)
    return high, (x - high.astype(f32)).astype(bf16)


def in_hbm(*arrays):
    return [pltpu.with_memory_space_constraint(x, pltpu.HBM) for x in arrays]


def iota(shape, dim):
    return lax.broadcasted_iota(jnp.int32, shape, dim)


def matmul(a, b):
    return jnp.dot(a, b, preferred_element_type=f32)


def padded_rows(x, rows):
    return x if x.shape[0] == rows else jnp.concatenate([x, jnp.zeros((rows - x.shape[0], LANES), x.dtype)], axis=0)


def regrid_kernel(
    cap, lat, lon, oy, batch, src_h, dev_h, blk_h, coupling_h, atm_h, mask_h, weights_h,
    out_h, out, rows, ids, count, src, dev, blk, coupling, atm, mask, weights, small_sem, big_sem, out_sem,
):
    fluxes, atm_rows, _ = atm.shape
    fields = coupling.shape[0]
    devices = out.shape[0]
    per = fields * cap
    parts = weights.shape[0] // batch

    def big(k):
        here = pl.ds(pl.multiple_of(k * batch, batch), batch)
        return pltpu.make_async_copy(weights_h.at[here], weights.at[here], big_sem.at[k])

    small = [
        pltpu.make_async_copy(a, b, small_sem.at[k])
        for k, (a, b) in enumerate(
            (
                (coupling_h, coupling), (atm_h, atm), (mask_h, mask),
                (src_h, src), (dev_h, dev), (blk_h, blk),
            )
        )
    ]
    for copy in small:
        copy.start()
    for k in range(parts):
        big(k).start()

    def clear(d, carry):
        count[d] = 0
        out[d] = jnp.zeros(out.shape[1:], f32)
        return carry

    lax.fori_loop(0, devices, clear, 0)
    ids[...] = jnp.full(ids.shape, -1, jnp.int32)
    for copy in small:
        copy.wait()
    for tile in range(atm_rows // 16):
        here = slice(tile * 16, tile * 16 + 16)
        sea = mask[here, :].astype(f32)
        flux = [atm[f, here, :].astype(f32) * sea for f in range(fluxes)]
        for q in range(fields):
            total = coupling[q, 0] * flux[0]
            for f in range(1, fluxes):
                total = total + coupling[q, f] * flux[f]
            high = total.astype(bf16).astype(f32)
            rows[pl.ds(tile * 16 * SUB + q, 16, stride=SUB), :] = high
            rows[pl.ds(tile * 16 * SUB + fields + q, 16, stride=SUB), :] = total - high

    lane = iota((1, LANES), 1)
    lane_slot = (lane % per) // fields
    lane_row = (lane % fields) * oy

    def place(d):
        return lax.rem(d, lon) * lat + lax.div(d, lon)

    def part(k, carry):
        big(k).wait()
        for u in range(0, batch, 2):
            p = k * batch + u
            x = jnp.concatenate(
                [rows[pl.ds(pl.multiple_of(src[p + v] * SUB, SUB), SUB), :] for v in range(2)], axis=0
            ).astype(bf16)
            both = matmul(x, jnp.concatenate([weights[p], weights[p + 1]], axis=1))
            for v in range(2):
                d = dev[p + v]
                slot = jnp.minimum(count[d], cap - 1)
                count[d] = slot + 1
                half = both[v * SUB : v * SUB + SUB, v * LANES : (v + 1) * LANES]
                out[place(d), pl.ds(slot * fields, fields), :] = half[0:fields] + half[fields : 2 * fields]
                line = ids[pl.ds(d, 1), :]
                ids[pl.ds(d, 1), :] = jnp.where(lane_slot == slot, lane_row + blk[p + v], line)
        return carry

    lax.fori_loop(0, parts, part, 0)

    def send(k, start, stop):
        return pltpu.make_async_copy(out.at[:, start:stop, :], out_h.at[:, start:stop, :], out_sem.at[k])

    send(0, 0, per).start()

    def halo(k):
        d = 2 * k
        turned = jnp.concatenate(
            [padded_rows(out[place(d + u), 0:per], HALF) for u in range(2)], axis=0
        ).T
        first, last = turned[0:1], turned[LANES - 1 : LANES]
        first_swapped = pltpu.roll(turned[0:SUB], HALF, 1)[0:1]
        last_swapped = pltpu.roll(turned[LANES - SUB : LANES], HALF, 1)[SUB - 1 : SUB]
        for u in range(2):
            b = lax.rem(d + u, lon)
            east = jnp.where(b == lon - 1, d + u - (lon - 1), d + u + 1)
            west = jnp.where(b == 0, d + u + (lon - 1), d + u - 1)
            here, to_east, to_west = place(d + u), place(east), place(west)
            out[here, per : per + 1] = ids[pl.ds(d + u, 1), :].astype(f32)
            sides = jnp.where(lane < HALF, ids[pl.ds(east, 1), :], ids[pl.ds(west, 1), :])
            out[here, per + 1 : per + 2] = sides.astype(f32)
            column = first if u == 0 else first_swapped
            out[to_west, per + 2 : per + 3] = jnp.where(lane < HALF, column, out[to_west, per + 2 : per + 3])
            column = last_swapped if u == 0 else last
            out[to_east, per + 2 : per + 3] = jnp.where(lane < HALF, out[to_east, per + 2 : per + 3], column)

    def halos(k, carry):
        for u in range(4):
            halo(k * 4 + u)
        return carry

    lax.fori_loop(0, devices // 8, halos, 0)
    send(1, per, per + SUB).start()
    send(0, 0, per).wait()
    send(1, per, per + SUB).wait()


def regrid(cap, lat, lon, oy, src, dev, blk, coupling, atm, mask, weights):
    pairs, depth, width = weights.shape
    fields = coupling.shape[0]
    batch = 32
    devices = lat * lon
    tall = fields * cap + SUB
    return pl.pallas_call(
        functools.partial(regrid_kernel, cap, lat, lon, oy, batch),
        in_specs=[HBM] * 7,
        out_specs=HBM,
        out_shape=pltpu.HBM((devices, tall, LANES), f32),
        scratch_shapes=[
            pltpu.VMEM((devices, tall, LANES), f32),
            pltpu.VMEM((atm.shape[1] * SUB, LANES), f32),
            pltpu.VMEM((devices, LANES), jnp.int32),
            pltpu.SMEM((devices,), jnp.int32),
            pltpu.SMEM(src.shape, jnp.int32),
            pltpu.SMEM(dev.shape, jnp.int32),
            pltpu.SMEM(blk.shape, jnp.int32),
            pltpu.SMEM(coupling.shape, f32),
            pltpu.VMEM(atm.shape, bf16),
            pltpu.VMEM(mask.shape, jnp.int32),
            pltpu.VMEM(weights.shape, bf16),
            pltpu.SemaphoreType.DMA((6,)),
            pltpu.SemaphoreType.DMA((pairs // batch,)),
            pltpu.SemaphoreType.DMA((2,)),
        ],
        compiler_params=pltpu.CompilerParams(vmem_limit_bytes=20 << 20),
        cost_estimate=pl.CostEstimate(flops=2 * 8 * pairs * depth * width, bytes_accessed=10 << 20, transcendentals=0),
        name="regrid",
    )(*in_hbm(src, dev, blk, coupling, atm, mask, weights))


def mix_kernel(
    depth_h, state_h, inv_h, mixed_h, north, south, side, depth_ref, state, mixed, inv, in_sems, out_sems
):
    fields, oy, levels, _ = mixed.shape
    depth_copy = pltpu.make_async_copy(depth_h, depth_ref, in_sems.at[2 * fields])
    depth_copy.start()
    for q in range(fields):
        for i in range(oy):
            pltpu.make_async_copy(state_h.at[q, :, i, :], state.at[q, i], in_sems.at[2 * q]).start()
        pltpu.make_async_copy(inv_h.at[q], inv.at[q], in_sems.at[2 * q + 1]).start()
    depth_copy.wait()
    level = iota((levels, LANES), 0)
    lane = iota((levels, LANES), 1)
    line = iota((1, LANES), 1)
    edge_depth = jnp.zeros((SUB, LANES), f32)
    for i in range(oy):
        turned = pltpu.roll(jnp.broadcast_to(depth_ref[i : i + 1, :].astype(f32), (SUB, LANES)), 2 * i + 1, 1)
        edge_depth = jnp.where(line // 2 == i, turned, edge_depth)

    def message(ref, q, row):
        ref[q, 0:levels] = mixed[q, row]
        square = jnp.concatenate([inv[q, row, 0], jnp.zeros((levels, LANES - levels), f32)], axis=1)
        names = padded_rows(square, LANES).T[0:1]
        ref[q, levels : levels + SUB] = jnp.concatenate(
            [depth_ref[row : row + 1, :].astype(f32), names, jnp.zeros((SUB - 2, LANES), f32)], axis=0
        )

    def field(q, carry):
        pltpu.make_async_copy(mixed_h.at[q], state.at[q], in_sems.at[2 * q]).wait()
        pltpu.make_async_copy(inv_h.at[q], inv.at[q], in_sems.at[2 * q + 1]).wait()

        def chunk(c, edges):
            here = jnp.zeros((levels, LANES), f32)
            for i in range(SUB):
                row = c * SUB + i
                active = level < depth_ref[pl.ds(row, 1), :]
                x = state[q, row]
                a = inv[q, row, 0]
                a_high, a_low = split(a)
                r_high, r_low = split(jnp.where(active, x, 0.0))
                product = matmul(
                    jnp.concatenate([a_high, a_low], axis=0), jnp.concatenate([r_high, r_low], axis=1)
                )
                solved = product[:levels, :LANES] + (product[levels:, :LANES] + product[:levels, LANES:])
                m = jnp.where(active, solved, x)
                mixed[q, row] = m
                here = jnp.where(lane // 2 == i, pltpu.roll(m, 2 * i + 1, 1), here)
                here = jnp.where(lane // 2 == HALF // 2 + i, a[:, 0:1], here)
            return edges + pltpu.roll(here, 2 * SUB * c, 1)

        side[q, 0:levels] = lax.fori_loop(0, oy // SUB, chunk, jnp.zeros((levels, LANES), f32))
        side[q, levels : levels + SUB] = edge_depth
        message(north, q, 0)
        message(south, q, oy - 1)
        pltpu.make_async_copy(mixed.at[q], mixed_h.at[q], out_sems.at[q]).start()
        return carry

    lax.fori_loop(0, fields, field, 0)
    for q in range(fields):
        pltpu.make_async_copy(mixed.at[q], mixed_h.at[q], out_sems.at[q]).wait()


def mix(depth, state, inverses):
    fields, levels, oy, ox = state.shape
    edge_shape = jax.ShapeDtypeStruct((fields, levels + SUB, ox), f32)
    full = (fields, oy, levels, ox)
    return pl.pallas_call(
        mix_kernel,
        in_specs=[HBM] * 3,
        out_specs=[HBM] + [VMEM] * 3,
        out_shape=[pltpu.HBM(full, f32), edge_shape, edge_shape, edge_shape],
        scratch_shapes=[
            pltpu.VMEM(depth.shape, jnp.int32),
            pltpu.VMEM(full, f32),
            pltpu.VMEM(full, f32),
            pltpu.VMEM(inverses.shape, f32),
            pltpu.SemaphoreType.DMA((2 * fields + 1,)),
            pltpu.SemaphoreType.DMA((fields,)),
        ],
        compiler_params=pltpu.CompilerParams(vmem_limit_bytes=32 << 20),
        cost_estimate=pl.CostEstimate(flops=2 * 4 * fields * oy * levels * levels * ox, bytes_accessed=16 << 20, transcendentals=0),
        name="mix",
    )(*in_hbm(depth, state, inverses))


def collect_kernel(cap, fields, oy, recv, after_north, after_south, out):
    lat = out.shape[0]
    lon = recv.shape[0] // lat
    per = fields * cap
    group = LANES // per
    forced = fields * oy
    square_row = iota((LANES, LANES), 0).astype(f32)
    line = iota((1, LANES), 1)
    row = iota((2 * oy, LANES), 0).astype(f32)
    lane_base = ((line % fields) * oy).astype(f32)
    lane_side = (line // HALF).astype(f32)
    small_row, small_lane = iota((SUB, LANES), 0), iota((SUB, LANES), 1)
    pick = jnp.where((small_lane % fields == small_row) & (small_lane % HALF < per), 1.0, 0.0).astype(bf16)
    nothing = jnp.zeros((fields, LANES), f32)
    for a in range(lat):
        total = jnp.zeros((LANES, 2 * LANES), f32)
        for tile in range(lon // group):
            places = [(tile * group + s) * lat + a for s in range(group)]
            ids = recv[places[0], per : per + 1, :]
            for s in range(1, group):
                ids = jnp.where(line // per == s, recv[places[s], per : per + 1, :], ids)
            hot = jnp.where(square_row == ids, 1.0, 0.0).astype(bf16)
            high, low = split(jnp.concatenate([recv[p, 0:per, :] for p in places], axis=0))
            total = total + matmul(hot, jnp.concatenate([high, low], axis=1))
        total = total[:, :LANES] + total[:, LANES:]
        out[a, 0:forced] = total
        if a == 0:
            out[a, forced : forced + fields] = nothing
        if a == lat - 1:
            out[a, forced + fields : forced + 2 * fields] = nothing
        for q in range(fields):
            if a + 1 < lat:
                out[a + 1, forced + q : forced + q + 1] = total[q * oy + oy - 1 : q * oy + oy]
            if a > 0:
                out[a - 1, forced + fields + q : forced + fields + q + 1] = total[q * oy : q * oy + 1]
        spread = jnp.zeros((2 * oy, LANES), f32)
        for b in range(lon):
            place = 2.0 * (recv[b * lat + a, per + 1 : per + 2, :] - lane_base) + lane_side
            spread = spread + jnp.where(place == row, recv[b * lat + a, per + 2 : per + 3, :], 0.0)
        high, low = split(padded_rows(spread, LANES).T)
        out[a, forced + SUB : forced + 2 * SUB] = matmul(pick, high) + matmul(pick, low)


def collect(cap, fields, oy, lat, received, after):
    return pl.pallas_call(
        functools.partial(collect_kernel, cap, fields, oy),
        in_specs=[VMEM] + [pl.BlockSpec(memory_space=pl.ANY)] * 2,
        out_specs=VMEM,
        out_shape=jax.ShapeDtypeStruct((lat, fields * oy + 2 * SUB, LANES), f32),
        compiler_params=pltpu.CompilerParams(vmem_limit_bytes=16 << 20),
        name="collect",
    )(received, *after)


def finish_kernel(
    recv, depth_ref, mixed_h, own_h, north_h, south_h, east_h, west_h,
    out_h, own, north, south, east, west, forcing, z, keep, halo, z_north, z_south, mixed, stage,
    edge_sems, in_sems, out_sems,
):
    fields, oy, levels, _ = mixed.shape
    level = iota((levels, LANES), 0)
    lanes = iota((levels, LANES), 1)
    square_row = iota((LANES, LANES), 0)
    square_lane = iota((LANES, LANES), 1)
    line = iota((1, LANES), 1)
    even = line % 2 == 0
    edges = [
        pltpu.make_async_copy(a, b, edge_sems.at[k])
        for k, (a, b) in enumerate(
            ((own_h, own), (north_h, north), (south_h, south), (east_h, east), (west_h, west))
        )
    ]
    for copy in edges:
        copy.start()

    def load(q, c):
        here = (q, pl.ds(pl.multiple_of(c * SUB, SUB), SUB))
        return pltpu.make_async_copy(mixed_h.at[here], mixed.at[here], in_sems.at[q, c])

    for q in range(fields):
        for c in range(oy // SUB):
            load(q, c).start()

    total = recv[0]
    for a in range(1, recv.shape[0]):
        total = total + recv[a]
    forced_rows = fields * oy
    forcing[...] = total[0:forced_rows]
    rows = total[forced_rows : forced_rows + SUB]
    columns = total[forced_rows + SUB :]

    for copy in edges:
        copy.wait()
    depth = depth_ref[...]
    wide = iota((oy, LANES), 1)

    def upright(ref, place):
        value = jnp.where(wide == 2 * iota((oy, LANES), 0) + place, ref[0, levels : levels + 1, :], 0.0)
        return jnp.sum(value, axis=1, keepdims=True).astype(jnp.int32)

    to_east = jnp.where(wide == LANES - 1, upright(east, 1), pltpu.roll(depth, LANES - 1, 1))
    to_west = jnp.where(wide == 0, upright(west, 0), pltpu.roll(depth, 1, 1))
    to_north = jnp.concatenate([north[0, levels : levels + 1, :].astype(jnp.int32), depth[: oy - 1]], axis=0)
    to_south = jnp.concatenate([depth[1:], south[0, levels : levels + 1, :].astype(jnp.int32)], axis=0)
    for i in range(oy):
        sides = jnp.where(level < to_east[i : i + 1], diffusion_rate, 0.0)
        for other in (to_west, to_north, to_south):
            sides = sides + jnp.where(level < other[i : i + 1], diffusion_rate, 0.0)
        keep[i] = 1.0 - sides

    def outer(target, ref, start):
        names = padded_rows(
            jnp.concatenate([ref[q, levels + 1 : levels + 2, :] for q in range(fields)], axis=0), LANES
        ).T
        active = level < ref[0, levels : levels + 1, :].astype(jnp.int32)
        for q in range(fields):
            value = ref[q, 0:levels] + names[0:levels, q : q + 1] * rows[start + q : start + q + 1]
            target[q] = jnp.where(active, value, 0.0)

    outer(z_north, north, 0)
    outer(z_south, south, fields)
    for q in range(fields):
        cells = jnp.where(even, pltpu.roll(east[q], LANES - 1, 1), pltpu.roll(west[q], 1, 1))
        names = pltpu.roll(jnp.where(even, east[q], west[q]), HALF, 1)
        active = level < cells[levels : levels + 1].astype(jnp.int32)
        value = cells[0:levels] + names[0:levels] * columns[q : q + 1]
        halo[q] = jnp.where(active & (line < 2 * oy), value, 0.0)

    both = jnp.where((square_row == square_lane + 1) | (square_row == square_lane - 1), 1.0, 0.0).astype(bf16)
    both = jnp.concatenate([both, both], axis=0)
    ends = (lanes == 0) | (lanes == LANES - 1)

    def field(q, carry):
        z[0] = z_north[q]
        z[oy + 1] = z_south[q]

        def solve(c, carry):
            load(q, c).wait()
            names = pltpu.roll(own[q, 0:levels], (LANES - 2 * SUB * c) % LANES, 1)
            for i in range(SUB):
                r = c * SUB + i
                forced = mixed[q, r] + names[:, HALF + 2 * i : HALF + 2 * i + 1] * forcing[pl.ds(q * oy + r, 1), :]
                z[r + 1] = jnp.where(level < depth_ref[pl.ds(r, 1), :], forced, 0.0)
            return carry

        lax.fori_loop(0, oy // SUB, solve, 0)

        def diffuse(c, carry):
            start = c * SUB
            high, low = split(z[pl.ds(start + 1, SUB)].reshape(SUB * levels, LANES))
            sides = matmul(jnp.concatenate([high, low], axis=1), both)
            edge = pltpu.roll(halo[q], (LANES - 2 * SUB * c) % LANES, 1)
            for i in range(SUB):
                r = start + i
                outside = jnp.where(ends, pltpu.roll(edge, LANES - 1 - 2 * i, 1), 0.0)
                around = (z[r] + z[r + 2]) + (sides[i * levels : (i + 1) * levels] + outside)
                active = level < depth_ref[pl.ds(r, 1), :]
                stage[q, r] = jnp.where(active, z[r + 1] * keep[r] + diffusion_rate * around, mixed[q, r])
            for i in range(SUB):
                r = start + i
                pltpu.make_async_copy(stage.at[q, r], out_h.at[q, :, r, :], out_sems.at[q]).start()
            return carry

        lax.fori_loop(0, oy // SUB, diffuse, 0)
        return carry

    lax.fori_loop(0, fields, field, 0)
    for q in range(fields):
        pltpu.make_async_copy(stage.at[q], mixed_h.at[q], out_sems.at[q]).wait()


def finish(received, depth, own, mixed, halos):
    fields, oy, levels, ox = mixed.shape
    edge = pltpu.VMEM((fields, levels, ox), f32)
    message = pltpu.VMEM((fields, levels + SUB, ox), f32)
    full = pltpu.VMEM((fields, oy, levels, ox), f32)
    return pl.pallas_call(
        finish_kernel,
        in_specs=[VMEM] * 2 + [HBM] * 6,
        out_specs=HBM,
        out_shape=pltpu.HBM((fields, levels, oy, ox), f32),
        scratch_shapes=[message] * 5
        + [
            pltpu.VMEM((fields * oy, ox), f32),
            pltpu.VMEM((oy + 2, levels, ox), f32),
            pltpu.VMEM((oy, levels, ox), f32),
            edge,
            edge,
            edge,
            full,
            full,
            pltpu.SemaphoreType.DMA((5,)),
            pltpu.SemaphoreType.DMA((fields, oy // SUB)),
            pltpu.SemaphoreType.DMA((fields,)),
        ],
        compiler_params=pltpu.CompilerParams(vmem_limit_bytes=32 << 20),
        cost_estimate=pl.CostEstimate(flops=20 * fields * oy * levels * ox, bytes_accessed=12 << 20, transcendentals=0),
        name="finish",
    )(received, depth, *in_hbm(mixed, own, *halos))


def shift(x, axis, step, wrap):
    count = lax.axis_size(axis)
    pairs = [(i, (i + step) % count) for i in range(count) if wrap or 0 <= i + step < count]
    return lax.ppermute(x, axis, pairs)


def on_device(
    atm_flux, sea_mask, src_block, dest_dev, dest_block, intersection_weights, coupling, inverses, ocean_state,
    depth_levels,
):
    lat, lon = lax.axis_size("lat"), lax.axis_size("lon")
    fields, _, oy, _ = ocean_state.shape
    cap = max(SUB, 2 * src_block.shape[0] // (lat * lon))
    slots = regrid(
        cap, lat, lon, oy, src_block, dest_dev[:, 0], dest_block, coupling, atm_flux, sea_mask,
        intersection_weights,
    )
    in_plane = lax.all_to_all(slots, "lon", 0, 0, tiled=True)
    mixed, north, south, side = mix(depth_levels, ocean_state, inverses)
    halos = (
        shift(south, "lat", 1, False),
        shift(north, "lat", -1, False),
        shift(side, "lon", -1, True),
        shift(side, "lon", 1, True),
    )
    received = lax.all_to_all(collect(cap, fields, oy, lat, in_plane, halos[0:2]), "lat", 0, 0, tiled=True)
    return finish(received, depth_levels, side, mixed, halos)


def solution(mesh):
    placed = (
        P(None, "lat", "lon"),
        P("lat", "lon"),
        P(("lat", "lon")),
        P(("lat", "lon"), None),
        P(("lat", "lon")),
        P(("lat", "lon"), None, None),
        P(),
        P(None, "lat", "lon", None, None),
        P(None, None, "lat", "lon"),
        P("lat", "lon"),
    )
    return jax.shard_map(
        on_device,
        mesh=mesh,
        in_specs=placed,
        out_specs=P(None, None, "lat", "lon"),
        check_vma=False,
    )
```

```python
import functools

import jax
import jax.numpy as jnp
from jax import lax
from jax.experimental import pallas as pl
from jax.experimental.pallas import tpu as pltpu
from jax.sharding import PartitionSpec as P

diffusion_rate = 0.2
LANES = 128
HALF = 64
SUB = 8
f32 = jnp.float32
bf16 = jnp.bfloat16
HBM = pl.BlockSpec(memory_space=pltpu.HBM)
VMEM = pl.BlockSpec(memory_space=pltpu.VMEM)


def split(x):
    high = x.astype(bf16)
    return high, (x - high.astype(f32)).astype(bf16)


def in_hbm(*arrays):
    return [pltpu.with_memory_space_constraint(x, pltpu.HBM) for x in arrays]


def iota(shape, dim):
    return lax.broadcasted_iota(jnp.int32, shape, dim)


def matmul(a, b):
    return jnp.dot(a, b, preferred_element_type=f32)


def padded_rows(x, rows):
    return x if x.shape[0] == rows else jnp.concatenate([x, jnp.zeros((rows - x.shape[0], LANES), x.dtype)], axis=0)


def regrid_kernel(
    cap, lat, lon, oy, batch, src_h, dev_h, blk_h, coupling_h, atm_h, mask_h, weights_h,
    out_h, out, rows, ids, count, src, dev, blk, coupling, atm, mask, weights, small_sem, big_sem, out_sem,
):
    fluxes, atm_rows, _ = atm.shape
    fields = coupling.shape[0]
    devices = out.shape[0]
    per = fields * cap
    parts = weights.shape[0] // batch

    def big(k):
        here = pl.ds(pl.multiple_of(k * batch, batch), batch)
        return pltpu.make_async_copy(weights_h.at[here], weights.at[here], big_sem.at[k])

    small = [
        pltpu.make_async_copy(a, b, small_sem.at[k])
        for k, (a, b) in enumerate(
            (
                (coupling_h, coupling), (atm_h, atm), (mask_h, mask),
                (src_h, src), (dev_h, dev), (blk_h, blk),
            )
        )
    ]
    for copy in small:
        copy.start()
    for k in range(parts):
        big(k).start()

    def clear(d, carry):
        count[d] = 0
        out[d] = jnp.zeros(out.shape[1:], f32)
        return carry

    lax.fori_loop(0, devices, clear, 0)
    ids[...] = jnp.full(ids.shape, -1, jnp.int32)
    for copy in small:
        copy.wait()
    for tile in range(atm_rows // 16):
        here = slice(tile * 16, tile * 16 + 16)
        sea = mask[here, :].astype(f32)
        flux = [atm[f, here, :].astype(f32) * sea for f in range(fluxes)]
        for q in range(fields):
            total = coupling[q, 0] * flux[0]
            for f in range(1, fluxes):
                total = total + coupling[q, f] * flux[f]
            high = total.astype(bf16).astype(f32)
            rows[pl.ds(tile * 16 * SUB + q, 16, stride=SUB), :] = high
            rows[pl.ds(tile * 16 * SUB + fields + q, 16, stride=SUB), :] = total - high

    lane = iota((1, LANES), 1)
    lane_slot = (lane % per) // fields
    lane_row = (lane % fields) * oy

    def place(d):
        return lax.rem(d, lon) * lat + lax.div(d, lon)

    def part(k, carry):
        big(k).wait()
        for u in range(0, batch, 2):
            p = k * batch + u
            x = jnp.concatenate(
                [rows[pl.ds(pl.multiple_of(src[p + v] * SUB, SUB), SUB), :] for v in range(2)], axis=0
            ).astype(bf16)
            both = matmul(x, jnp.concatenate([weights[p], weights[p + 1]], axis=1))
            for v in range(2):
                d = dev[p + v]
                slot = jnp.minimum(count[d], cap - 1)
                count[d] = slot + 1
                half = both[v * SUB : v * SUB + SUB, v * LANES : (v + 1) * LANES]
                out[place(d), pl.ds(slot * fields, fields), :] = half[0:fields] + half[fields : 2 * fields]
                line = ids[pl.ds(d, 1), :]
                ids[pl.ds(d, 1), :] = jnp.where(lane_slot == slot, lane_row + blk[p + v], line)
        return carry

    lax.fori_loop(0, parts, part, 0)

    def send(k, start, stop):
        return pltpu.make_async_copy(out.at[:, start:stop, :], out_h.at[:, start:stop, :], out_sem.at[k])

    send(0, 0, per).start()

    def halo(k):
        d = 2 * k
        turned = jnp.concatenate(
            [padded_rows(out[place(d + u), 0:per], HALF) for u in range(2)], axis=0
        ).T
        first, last = turned[0:1], turned[LANES - 1 : LANES]
        first_swapped = pltpu.roll(turned[0:SUB], HALF, 1)[0:1]
        last_swapped = pltpu.roll(turned[LANES - SUB : LANES], HALF, 1)[SUB - 1 : SUB]
        for u in range(2):
            b = lax.rem(d + u, lon)
            east = jnp.where(b == lon - 1, d + u - (lon - 1), d + u + 1)
            west = jnp.where(b == 0, d + u + (lon - 1), d + u - 1)
            here, to_east, to_west = place(d + u), place(east), place(west)
            out[here, per : per + 1] = ids[pl.ds(d + u, 1), :].astype(f32)
            sides = jnp.where(lane < HALF, ids[pl.ds(east, 1), :], ids[pl.ds(west, 1), :])
            out[here, per + 1 : per + 2] = sides.astype(f32)
            column = first if u == 0 else first_swapped
            out[to_west, per + 2 : per + 3] = jnp.where(lane < HALF, column, out[to_west, per + 2 : per + 3])
            column = last_swapped if u == 0 else last
            out[to_east, per + 2 : per + 3] = jnp.where(lane < HALF, out[to_east, per + 2 : per + 3], column)

    def halos(k, carry):
        for u in range(4):
            halo(k * 4 + u)
        return carry

    lax.fori_loop(0, devices // 8, halos, 0)
    send(1, per, per + SUB).start()
    send(0, 0, per).wait()
    send(1, per, per + SUB).wait()


def regrid(cap, lat, lon, oy, src, dev, blk, coupling, atm, mask, weights):
    pairs, depth, width = weights.shape
    fields = coupling.shape[0]
    batch = 32
    devices = lat * lon
    tall = fields * cap + SUB
    return pl.pallas_call(
        functools.partial(regrid_kernel, cap, lat, lon, oy, batch),
        in_specs=[HBM] * 7,
        out_specs=HBM,
        out_shape=pltpu.HBM((devices, tall, LANES), f32),
        scratch_shapes=[
            pltpu.VMEM((devices, tall, LANES), f32),
            pltpu.VMEM((atm.shape[1] * SUB, LANES), f32),
            pltpu.VMEM((devices, LANES), jnp.int32),
            pltpu.SMEM((devices,), jnp.int32),
            pltpu.SMEM(src.shape, jnp.int32),
            pltpu.SMEM(dev.shape, jnp.int32),
            pltpu.SMEM(blk.shape, jnp.int32),
            pltpu.SMEM(coupling.shape, f32),
            pltpu.VMEM(atm.shape, bf16),
            pltpu.VMEM(mask.shape, jnp.int32),
            pltpu.VMEM(weights.shape, bf16),
            pltpu.SemaphoreType.DMA((6,)),
            pltpu.SemaphoreType.DMA((pairs // batch,)),
            pltpu.SemaphoreType.DMA((2,)),
        ],
        compiler_params=pltpu.CompilerParams(vmem_limit_bytes=20 << 20),
        cost_estimate=pl.CostEstimate(flops=2 * 8 * pairs * depth * width, bytes_accessed=10 << 20, transcendentals=0),
        name="regrid",
    )(*in_hbm(src, dev, blk, coupling, atm, mask, weights))


def solve_row(a, x, active):
    levels = x.shape[0]
    a_high, a_low = split(a)
    r_high, r_low = split(jnp.where(active, x, 0.0))
    product = matmul(jnp.concatenate([a_high, a_low], axis=0), jnp.concatenate([r_high, r_low], axis=1))
    solved = product[:levels, :LANES] + (product[levels:, :LANES] + product[:levels, LANES:])
    return jnp.where(active, solved, x)


def outer_rows_kernel(depth_h, state_h, inv_h, north, south, depth_ref, state, inv, sems):
    _, fields, levels, _ = state.shape
    oy = depth_ref.shape[0]
    ends = (0, oy - 1)
    copies = [pltpu.make_async_copy(depth_h, depth_ref, sems.at[2 * fields, 0])]
    for q in range(fields):
        for k, row in enumerate(ends):
            copies.append(pltpu.make_async_copy(state_h.at[q, :, row, :], state.at[k, q], sems.at[2 * q, k]))
            copies.append(pltpu.make_async_copy(inv_h.at[q, row, 0], inv.at[k, q], sems.at[2 * q + 1, k]))
    for copy in copies:
        copy.start()
    level = iota((levels, LANES), 0)
    for copy in copies:
        copy.wait()
    for k, (row, ref) in enumerate(zip(ends, (north, south))):
        depth = depth_ref[row : row + 1, :]
        names = jnp.zeros((levels, LANES), f32)
        for q in range(fields):
            a = inv[k, q]
            ref[q, 0:levels] = solve_row(a, state[k, q], level < depth)
            names = jnp.where(iota((levels, LANES), 1) == q, a[:, 0:1], names)
        names = padded_rows(names, LANES).T
        for q in range(fields):
            ref[q, levels : levels + SUB] = jnp.concatenate(
                [depth.astype(f32), names[q : q + 1], jnp.zeros((SUB - 2, LANES), f32)], axis=0
            )


def outer_rows(depth, state, inverses):
    fields, levels, _, ox = state.shape
    edge_shape = jax.ShapeDtypeStruct((fields, levels + SUB, ox), f32)
    return pl.pallas_call(
        outer_rows_kernel,
        in_specs=[HBM] * 3,
        out_specs=[VMEM] * 2,
        out_shape=[edge_shape, edge_shape],
        scratch_shapes=[
            pltpu.VMEM(depth.shape, jnp.int32),
            pltpu.VMEM((2, fields, levels, ox), f32),
            pltpu.VMEM((2, fields, levels, levels), f32),
            pltpu.SemaphoreType.DMA((2 * fields + 1, 2)),
        ],
        compiler_params=pltpu.CompilerParams(vmem_limit_bytes=8 << 20),
        cost_estimate=pl.CostEstimate(flops=16 * fields * levels * levels * ox, bytes_accessed=1 << 20, transcendentals=0),
        name="outer_rows",
    )(*in_hbm(depth, state, inverses))


def mix_kernel(
    depth_h, state_h, inv_h, after, mixed_h, first_h, side,
    depth_ref, state, mixed, inv, first, in_sems, out_sems,
):
    fields, oy, levels, _ = mixed.shape
    depth_copy = pltpu.make_async_copy(depth_h, depth_ref, in_sems.at[2 * fields])
    depth_copy.start()
    for q in range(fields):
        for i in range(oy):
            pltpu.make_async_copy(state_h.at[q, :, i, :], state.at[q, i], in_sems.at[2 * q]).start()
        pltpu.make_async_copy(inv_h.at[q], inv.at[q], in_sems.at[2 * q + 1]).start()
    depth_copy.wait()
    level = iota((levels, LANES), 0)
    lane = iota((levels, LANES), 1)
    line = iota((1, LANES), 1)
    edge_depth = jnp.zeros((SUB, LANES), f32)
    for i in range(oy):
        turned = pltpu.roll(jnp.broadcast_to(depth_ref[i : i + 1, :].astype(f32), (SUB, LANES)), 2 * i + 1, 1)
        edge_depth = jnp.where(line // 2 == i, turned, edge_depth)

    def field(q, carry):
        pltpu.make_async_copy(mixed_h.at[q], state.at[q], in_sems.at[2 * q]).wait()
        pltpu.make_async_copy(inv_h.at[q], inv.at[q], in_sems.at[2 * q + 1]).wait()

        def chunk(c, edges):
            cells = jnp.zeros((levels, LANES), bf16)
            names = jnp.zeros((levels, LANES), f32)
            for i in range(SUB):
                row = c * SUB + i
                a = inv[q, row, 0]
                m = solve_row(a, state[q, row], level < depth_ref[pl.ds(row, 1), :])
                mixed[q, row] = m
                column = jnp.broadcast_to(a[:, 0:1], (levels, LANES))
                first[q, row] = column
                cells = jnp.where(lane // 2 == i, pltpu.roll(m.astype(bf16), 2 * i + 1, 1), cells)
                names = jnp.where(lane // 2 == HALF // 2 + i, column, names)
            return edges + pltpu.roll(cells.astype(f32) + names, 2 * SUB * c, 1)

        side[q, 0:levels] = lax.fori_loop(0, oy // SUB, chunk, jnp.zeros((levels, LANES), f32))
        side[q, levels : levels + SUB] = edge_depth
        pltpu.make_async_copy(mixed.at[q], mixed_h.at[q], out_sems.at[2 * q]).start()
        pltpu.make_async_copy(first.at[q], first_h.at[q], out_sems.at[2 * q + 1]).start()
        return carry

    lax.fori_loop(0, fields, field, 0)
    for q in range(fields):
        pltpu.make_async_copy(mixed.at[q], mixed_h.at[q], out_sems.at[2 * q]).wait()
        pltpu.make_async_copy(first.at[q], first_h.at[q], out_sems.at[2 * q + 1]).wait()


def mix(depth, state, inverses, after):
    fields, levels, oy, ox = state.shape
    edge_shape = jax.ShapeDtypeStruct((fields, levels + SUB, ox), f32)
    full = (fields, oy, levels, ox)
    return pl.pallas_call(
        mix_kernel,
        in_specs=[HBM] * 3 + [pl.BlockSpec(memory_space=pl.ANY)],
        out_specs=[HBM] * 2 + [VMEM],
        out_shape=[pltpu.HBM(full, f32), pltpu.HBM(full, f32), edge_shape],
        scratch_shapes=[
            pltpu.VMEM(depth.shape, jnp.int32),
            pltpu.VMEM(full, f32),
            pltpu.VMEM(full, f32),
            pltpu.VMEM(inverses.shape, f32),
            pltpu.VMEM(full, f32),
            pltpu.SemaphoreType.DMA((2 * fields + 1,)),
            pltpu.SemaphoreType.DMA((2 * fields,)),
        ],
        compiler_params=pltpu.CompilerParams(vmem_limit_bytes=32 << 20),
        cost_estimate=pl.CostEstimate(flops=2 * 4 * fields * oy * levels * levels * ox, bytes_accessed=16 << 20, transcendentals=0),
        name="mix",
    )(*in_hbm(depth, state, inverses), after)


def collect_kernel(cap, fields, oy, recv, after_mix, after_north, after_south, out):
    lat = out.shape[0]
    lon = recv.shape[0] // lat
    per = fields * cap
    group = LANES // per
    forced = fields * oy
    square_row = iota((LANES, LANES), 0).astype(f32)
    line = iota((1, LANES), 1)
    row = iota((2 * oy, LANES), 0).astype(f32)
    lane_base = ((line % fields) * oy).astype(f32)
    lane_side = (line // HALF).astype(f32)
    small_row, small_lane = iota((SUB, LANES), 0), iota((SUB, LANES), 1)
    pick = jnp.where((small_lane % fields == small_row) & (small_lane % HALF < per), 1.0, 0.0).astype(bf16)
    nothing = jnp.zeros((fields, LANES), f32)
    for a in range(lat):
        total = jnp.zeros((LANES, 2 * LANES), f32)
        for tile in range(lon // group):
            places = [(tile * group + s) * lat + a for s in range(group)]
            ids = recv[places[0], per : per + 1, :]
            for s in range(1, group):
                ids = jnp.where(line // per == s, recv[places[s], per : per + 1, :], ids)
            hot = jnp.where(square_row == ids, 1.0, 0.0).astype(bf16)
            high, low = split(jnp.concatenate([recv[p, 0:per, :] for p in places], axis=0))
            total = total + matmul(hot, jnp.concatenate([high, low], axis=1))
        total = total[:, :LANES] + total[:, LANES:]
        out[a, 0:forced] = total
        if a == 0:
            out[a, forced : forced + fields] = nothing
        if a == lat - 1:
            out[a, forced + fields : forced + 2 * fields] = nothing
        for q in range(fields):
            if a + 1 < lat:
                out[a + 1, forced + q : forced + q + 1] = total[q * oy + oy - 1 : q * oy + oy]
            if a > 0:
                out[a - 1, forced + fields + q : forced + fields + q + 1] = total[q * oy : q * oy + 1]
        spread = jnp.zeros((2 * oy, LANES), f32)
        for b in range(lon):
            place = 2.0 * (recv[b * lat + a, per + 1 : per + 2, :] - lane_base) + lane_side
            spread = spread + jnp.where(place == row, recv[b * lat + a, per + 2 : per + 3, :], 0.0)
        high, low = split(padded_rows(spread, LANES).T)
        out[a, forced + SUB : forced + 2 * SUB] = matmul(pick, high) + matmul(pick, low)


def collect(cap, fields, oy, lat, received, after):
    return pl.pallas_call(
        functools.partial(collect_kernel, cap, fields, oy),
        in_specs=[VMEM] + [pl.BlockSpec(memory_space=pl.ANY)] * 3,
        out_specs=VMEM,
        out_shape=jax.ShapeDtypeStruct((lat, fields * oy + 2 * SUB, LANES), f32),
        compiler_params=pltpu.CompilerParams(vmem_limit_bytes=16 << 20),
        name="collect",
    )(received, *after)


def finish_kernel(
    recv, depth_ref, mixed_h, first_h, north_h, south_h, east, west,
    out_h, north, south, forcing, z, keep, halo, z_north, z_south, mixed, first, stage, edge_sems, in_sems, out_sems,
):
    fields, oy, levels, _ = mixed.shape
    level = iota((levels, LANES), 0)
    lanes = iota((levels, LANES), 1)
    square_row = iota((LANES, LANES), 0)
    square_lane = iota((LANES, LANES), 1)
    line = iota((1, LANES), 1)
    even = line % 2 == 0
    edges = [
        pltpu.make_async_copy(a, b, edge_sems.at[k])
        for k, (a, b) in enumerate(((north_h, north), (south_h, south)))
    ]
    for copy in edges:
        copy.start()

    def loads(q, c):
        here = (q, pl.ds(pl.multiple_of(c * SUB, SUB), SUB))
        return [
            pltpu.make_async_copy(a.at[here], b.at[here], in_sems.at[k, q, c])
            for k, (a, b) in enumerate(((mixed_h, mixed), (first_h, first)))
        ]

    for q in range(fields):
        for c in range(oy // SUB):
            for copy in loads(q, c):
                copy.start()

    total = recv[0]
    for a in range(1, recv.shape[0]):
        total = total + recv[a]
    forced_rows = fields * oy
    forcing[...] = total[0:forced_rows]
    rows = total[forced_rows : forced_rows + SUB]
    columns = total[forced_rows + SUB :]

    for copy in edges:
        copy.wait()
    depth = depth_ref[...]
    wide = iota((oy, LANES), 1)

    def upright(ref, place):
        value = jnp.where(wide == 2 * iota((oy, LANES), 0) + place, ref[0, levels : levels + 1, :], 0.0)
        return jnp.sum(value, axis=1, keepdims=True).astype(jnp.int32)

    to_east = jnp.where(wide == LANES - 1, upright(east, 1), pltpu.roll(depth, LANES - 1, 1))
    to_west = jnp.where(wide == 0, upright(west, 0), pltpu.roll(depth, 1, 1))
    to_north = jnp.concatenate([north[0, levels : levels + 1, :].astype(jnp.int32), depth[: oy - 1]], axis=0)
    to_south = jnp.concatenate([depth[1:], south[0, levels : levels + 1, :].astype(jnp.int32)], axis=0)
    for i in range(oy):
        sides = jnp.where(level < to_east[i : i + 1], diffusion_rate, 0.0)
        for other in (to_west, to_north, to_south):
            sides = sides + jnp.where(level < other[i : i + 1], diffusion_rate, 0.0)
        keep[i] = 1.0 - sides

    def outer(target, ref, start):
        names = padded_rows(
            jnp.concatenate([ref[q, levels + 1 : levels + 2, :] for q in range(fields)], axis=0), LANES
        ).T
        active = level < ref[0, levels : levels + 1, :].astype(jnp.int32)
        for q in range(fields):
            value = ref[q, 0:levels] + names[0:levels, q : q + 1] * rows[start + q : start + q + 1]
            target[q] = jnp.where(active, value, 0.0)

    outer(z_north, north, 0)
    outer(z_south, south, fields)
    for q in range(fields):
        cells = jnp.where(even, pltpu.roll(east[q], LANES - 1, 1), pltpu.roll(west[q], 1, 1))
        names = pltpu.roll(jnp.where(even, east[q], west[q]), HALF, 1)
        active = level < cells[levels : levels + 1].astype(jnp.int32)
        value = cells[0:levels] + names[0:levels] * columns[q : q + 1]
        halo[q] = jnp.where(active & (line < 2 * oy), value, 0.0).astype(bf16)

    both = jnp.where((square_row == square_lane + 1) | (square_row == square_lane - 1), 1.0, 0.0).astype(bf16)
    both = jnp.concatenate([both, both], axis=0)
    ends = (lanes == 0) | (lanes == LANES - 1)

    def field(q, carry):
        z[0] = z_north[q]
        z[oy + 1] = z_south[q]

        def solve(c, carry):
            for copy in loads(q, c):
                copy.wait()
            for i in range(SUB):
                r = c * SUB + i
                forced = mixed[q, r] + first[q, r] * forcing[pl.ds(q * oy + r, 1), :]
                z[r + 1] = jnp.where(level < depth_ref[pl.ds(r, 1), :], forced, 0.0)
            return carry

        lax.fori_loop(0, oy // SUB, solve, 0)

        def diffuse(c, carry):
            start = c * SUB
            high, low = split(z[pl.ds(start + 1, SUB)].reshape(SUB * levels, LANES))
            sides = matmul(jnp.concatenate([high, low], axis=1), both)
            edge = pltpu.roll(halo[q].astype(f32), (LANES - 2 * SUB * c) % LANES, 1).astype(bf16)
            for i in range(SUB):
                r = start + i
                outside = jnp.where(ends, pltpu.roll(edge, LANES - 1 - 2 * i, 1).astype(f32), 0.0)
                around = (z[r] + z[r + 2]) + (sides[i * levels : (i + 1) * levels] + outside)
                active = level < depth_ref[pl.ds(r, 1), :]
                stage[q, r] = jnp.where(active, z[r + 1] * keep[r] + diffusion_rate * around, mixed[q, r])
            for i in range(SUB):
                r = start + i
                pltpu.make_async_copy(stage.at[q, r], out_h.at[q, :, r, :], out_sems.at[q]).start()
            return carry

        lax.fori_loop(0, oy // SUB, diffuse, 0)
        return carry

    lax.fori_loop(0, fields, field, 0)
    for q in range(fields):
        pltpu.make_async_copy(stage.at[q], mixed_h.at[q], out_sems.at[q]).wait()


def finish(received, depth, mixed, first, halos):
    fields, oy, levels, ox = mixed.shape
    edge = pltpu.VMEM((fields, levels, ox), f32)
    message = pltpu.VMEM((fields, levels + SUB, ox), f32)
    full = pltpu.VMEM((fields, oy, levels, ox), f32)
    return pl.pallas_call(
        finish_kernel,
        in_specs=[VMEM] * 2 + [HBM] * 4 + [VMEM] * 2,
        out_specs=HBM,
        out_shape=pltpu.HBM((fields, levels, oy, ox), f32),
        scratch_shapes=[
            message,
            message,
            pltpu.VMEM((fields * oy, ox), f32),
            pltpu.VMEM((oy + 2, levels, ox), f32),
            pltpu.VMEM((oy, levels, ox), f32),
            pltpu.VMEM((fields, levels, ox), bf16),
            edge,
            edge,
            full,
            full,
            full,
            pltpu.SemaphoreType.DMA((2,)),
            pltpu.SemaphoreType.DMA((2, fields, oy // SUB)),
            pltpu.SemaphoreType.DMA((fields,)),
        ],
        compiler_params=pltpu.CompilerParams(vmem_limit_bytes=32 << 20),
        cost_estimate=pl.CostEstimate(flops=20 * fields * oy * levels * ox, bytes_accessed=12 << 20, transcendentals=0),
        name="finish",
    )(received, depth, *in_hbm(mixed, first, *halos[0:2]), *halos[2:])


def shift(x, axis, step, wrap):
    count = lax.axis_size(axis)
    pairs = [(i, (i + step) % count) for i in range(count) if wrap or 0 <= i + step < count]
    return lax.ppermute(x, axis, pairs)


def on_device(
    atm_flux, sea_mask, src_block, dest_dev, dest_block, intersection_weights, coupling, inverses, ocean_state,
    depth_levels,
):
    lat, lon = lax.axis_size("lat"), lax.axis_size("lon")
    fields, _, oy, _ = ocean_state.shape
    cap = max(SUB, 2 * src_block.shape[0] // (lat * lon))
    slots = regrid(
        cap, lat, lon, oy, src_block, dest_dev[:, 0], dest_block, coupling, atm_flux, sea_mask,
        intersection_weights,
    )
    in_plane = lax.all_to_all(slots, "lon", 0, 0, tiled=True)
    north, south = outer_rows(depth_levels, ocean_state, inverses)
    mixed, first, side = mix(depth_levels, ocean_state, inverses, north)
    halos = (
        shift(south, "lat", 1, False),
        shift(north, "lat", -1, False),
        shift(side, "lon", -1, True),
        shift(side, "lon", 1, True),
    )
    received = lax.all_to_all(collect(cap, fields, oy, lat, in_plane, (side, *halos[0:2])), "lat", 0, 0, tiled=True)
    return finish(received, depth_levels, mixed, first, halos)


def solution(mesh):
    placed = (
        P(None, "lat", "lon"),
        P("lat", "lon"),
        P(("lat", "lon")),
        P(("lat", "lon"), None),
        P(("lat", "lon")),
        P(("lat", "lon"), None, None),
        P(),
        P(None, "lat", "lon", None, None),
        P(None, None, "lat", "lon"),
        P("lat", "lon"),
    )
    return jax.shard_map(
        on_device,
        mesh=mesh,
        in_specs=placed,
        out_specs=P(None, None, "lat", "lon"),
        check_vma=False,
    )
```

```python
import functools

import jax
import jax.numpy as jnp
from jax import lax
from jax.experimental import pallas as pl
from jax.experimental.pallas import tpu as pltpu
from jax.sharding import PartitionSpec as P

diffusion_rate = 0.2
LANES = 128
HALF = 64
SUB = 8
f32 = jnp.float32
bf16 = jnp.bfloat16
HBM = pl.BlockSpec(memory_space=pltpu.HBM)
VMEM = pl.BlockSpec(memory_space=pltpu.VMEM)


def split(x):
    high = x.astype(bf16)
    return high, (x - high.astype(f32)).astype(bf16)


def in_hbm(*arrays):
    return [pltpu.with_memory_space_constraint(x, pltpu.HBM) for x in arrays]


def iota(shape, dim):
    return lax.broadcasted_iota(jnp.int32, shape, dim)


def matmul(a, b):
    return jnp.dot(a, b, preferred_element_type=f32)


def padded_rows(x, rows):
    return x if x.shape[0] == rows else jnp.concatenate([x, jnp.zeros((rows - x.shape[0], LANES), x.dtype)], axis=0)


def regrid_kernel(
    cap, lat, lon, oy, batch, src_h, dev_h, blk_h, coupling_h, atm_h, mask_h, weights_h,
    out_h, out, rows, ids, count, src, dev, blk, coupling, atm, mask, weights, small_sem, big_sem, out_sem,
):
    fluxes, atm_rows, _ = atm.shape
    fields = coupling.shape[0]
    devices = out.shape[0]
    per = fields * cap
    parts = weights.shape[0] // batch
    ahead = min(3, parts)

    def big(k):
        here = pl.ds(pl.multiple_of(k * batch, batch), batch)
        return pltpu.make_async_copy(weights_h.at[here], weights.at[here], big_sem.at[k])

    small = [
        pltpu.make_async_copy(a, b, small_sem.at[k])
        for k, (a, b) in enumerate(
            (
                (coupling_h, coupling), (atm_h, atm), (mask_h, mask),
                (src_h, src), (dev_h, dev), (blk_h, blk),
            )
        )
    ]
    for copy in small:
        copy.start()
    for k in range(ahead):
        big(k).start()

    def clear(d, carry):
        count[d] = 0
        out[d] = jnp.zeros(out.shape[1:], f32)
        return carry

    lax.fori_loop(0, devices, clear, 0)
    ids[...] = jnp.full(ids.shape, -1, jnp.int32)
    for copy in small:
        copy.wait()
    for tile in range(atm_rows // 16):
        here = slice(tile * 16, tile * 16 + 16)
        sea = mask[here, :].astype(f32)
        flux = [atm[f, here, :].astype(f32) * sea for f in range(fluxes)]
        for q in range(fields):
            total = coupling[q, 0] * flux[0]
            for f in range(1, fluxes):
                total = total + coupling[q, f] * flux[f]
            high = total.astype(bf16).astype(f32)
            rows[pl.ds(tile * 16 * SUB + q, 16, stride=SUB), :] = high
            rows[pl.ds(tile * 16 * SUB + fields + q, 16, stride=SUB), :] = total - high

    lane = iota((1, LANES), 1)
    lane_slot = (lane % per) // fields
    lane_row = (lane % fields) * oy

    def place(d):
        return lax.rem(d, lon) * lat + lax.div(d, lon)

    def part(k, carry):
        big(k).wait()

        @pl.when(k + ahead < parts)
        def _():
            big(k + ahead).start()

        for u in range(0, batch, 2):
            p = k * batch + u
            x = jnp.concatenate(
                [rows[pl.ds(pl.multiple_of(src[p + v] * SUB, SUB), SUB), :] for v in range(2)], axis=0
            ).astype(bf16)
            both = matmul(x, jnp.concatenate([weights[p], weights[p + 1]], axis=1))
            for v in range(2):
                d = dev[p + v]
                slot = jnp.minimum(count[d], cap - 1)
                count[d] = slot + 1
                half = both[v * SUB : v * SUB + SUB, v * LANES : (v + 1) * LANES]
                out[place(d), pl.ds(slot * fields, fields), :] = half[0:fields] + half[fields : 2 * fields]
                line = ids[pl.ds(d, 1), :]
                ids[pl.ds(d, 1), :] = jnp.where(lane_slot == slot, lane_row + blk[p + v], line)
        return carry

    lax.fori_loop(0, parts, part, 0)

    def send(k, start, stop):
        return pltpu.make_async_copy(out.at[:, start:stop, :], out_h.at[:, start:stop, :], out_sem.at[k])

    send(0, 0, per).start()

    def halo(k):
        d = 2 * k
        turned = jnp.concatenate(
            [padded_rows(out[place(d + u), 0:per], HALF) for u in range(2)], axis=0
        ).T
        first, last = turned[0:1], turned[LANES - 1 : LANES]
        first_swapped = pltpu.roll(turned[0:SUB], HALF, 1)[0:1]
        last_swapped = pltpu.roll(turned[LANES - SUB : LANES], HALF, 1)[SUB - 1 : SUB]
        for u in range(2):
            b = lax.rem(d + u, lon)
            east = jnp.where(b == lon - 1, d + u - (lon - 1), d + u + 1)
            west = jnp.where(b == 0, d + u + (lon - 1), d + u - 1)
            here, to_east, to_west = place(d + u), place(east), place(west)
            out[here, per : per + 1] = ids[pl.ds(d + u, 1), :].astype(f32)
            sides = jnp.where(lane < HALF, ids[pl.ds(east, 1), :], ids[pl.ds(west, 1), :])
            out[here, per + 1 : per + 2] = sides.astype(f32)
            column = first if u == 0 else first_swapped
            out[to_west, per + 2 : per + 3] = jnp.where(lane < HALF, column, out[to_west, per + 2 : per + 3])
            column = last_swapped if u == 0 else last
            out[to_east, per + 2 : per + 3] = jnp.where(lane < HALF, out[to_east, per + 2 : per + 3], column)

    def halos(k, carry):
        for u in range(4):
            halo(k * 4 + u)
        return carry

    lax.fori_loop(0, devices // 8, halos, 0)
    send(1, per, per + SUB).start()
    send(0, 0, per).wait()
    send(1, per, per + SUB).wait()


def regrid(cap, lat, lon, oy, src, dev, blk, coupling, atm, mask, weights):
    pairs, depth, width = weights.shape
    fields = coupling.shape[0]
    batch = 32
    devices = lat * lon
    tall = fields * cap + SUB
    return pl.pallas_call(
        functools.partial(regrid_kernel, cap, lat, lon, oy, batch),
        in_specs=[HBM] * 7,
        out_specs=HBM,
        out_shape=pltpu.HBM((devices, tall, LANES), f32),
        scratch_shapes=[
            pltpu.VMEM((devices, tall, LANES), f32),
            pltpu.VMEM((atm.shape[1] * SUB, LANES), f32),
            pltpu.VMEM((devices, LANES), jnp.int32),
            pltpu.SMEM((devices,), jnp.int32),
            pltpu.SMEM(src.shape, jnp.int32),
            pltpu.SMEM(dev.shape, jnp.int32),
            pltpu.SMEM(blk.shape, jnp.int32),
            pltpu.SMEM(coupling.shape, f32),
            pltpu.VMEM(atm.shape, bf16),
            pltpu.VMEM(mask.shape, jnp.int32),
            pltpu.VMEM(weights.shape, bf16),
            pltpu.SemaphoreType.DMA((6,)),
            pltpu.SemaphoreType.DMA((pairs // batch,)),
            pltpu.SemaphoreType.DMA((2,)),
        ],
        compiler_params=pltpu.CompilerParams(vmem_limit_bytes=20 << 20),
        cost_estimate=pl.CostEstimate(flops=2 * 8 * pairs * depth * width, bytes_accessed=10 << 20, transcendentals=0),
        name="regrid",
    )(*in_hbm(src, dev, blk, coupling, atm, mask, weights))


def solve_row(a, x, active):
    levels = x.shape[0]
    a_high, a_low = split(a)
    r_high, r_low = split(jnp.where(active, x, 0.0))
    product = matmul(jnp.concatenate([a_high, a_low], axis=0), jnp.concatenate([r_high, r_low], axis=1))
    solved = product[:levels, :LANES] + (product[levels:, :LANES] + product[:levels, LANES:])
    return jnp.where(active, solved, x)


def outer_rows_kernel(depth_h, state_h, inv_h, north, south, depth_ref, state, inv, sems):
    _, fields, levels, _ = state.shape
    oy = depth_ref.shape[0]
    ends = (0, oy - 1)
    copies = [pltpu.make_async_copy(depth_h, depth_ref, sems.at[2 * fields, 0])]
    for q in range(fields):
        for k, row in enumerate(ends):
            copies.append(pltpu.make_async_copy(state_h.at[q, :, row, :], state.at[k, q], sems.at[2 * q, k]))
            copies.append(pltpu.make_async_copy(inv_h.at[q, row, 0], inv.at[k, q], sems.at[2 * q + 1, k]))
    for copy in copies:
        copy.start()
    level = iota((levels, LANES), 0)
    for copy in copies:
        copy.wait()
    for k, (row, ref) in enumerate(zip(ends, (north, south))):
        depth = depth_ref[row : row + 1, :]
        names = jnp.zeros((levels, LANES), f32)
        for q in range(fields):
            a = inv[k, q]
            ref[q, 0:levels] = solve_row(a, state[k, q], level < depth)
            names = jnp.where(iota((levels, LANES), 1) == q, a[:, 0:1], names)
        names = padded_rows(names, LANES).T
        for q in range(fields):
            ref[q, levels : levels + SUB] = jnp.concatenate(
                [depth.astype(f32), names[q : q + 1], jnp.zeros((SUB - 2, LANES), f32)], axis=0
            )


def outer_rows(depth, state, inverses):
    fields, levels, _, ox = state.shape
    edge_shape = jax.ShapeDtypeStruct((fields, levels + SUB, ox), f32)
    return pl.pallas_call(
        outer_rows_kernel,
        in_specs=[HBM] * 3,
        out_specs=[VMEM] * 2,
        out_shape=[edge_shape, edge_shape],
        scratch_shapes=[
            pltpu.VMEM(depth.shape, jnp.int32),
            pltpu.VMEM((2, fields, levels, ox), f32),
            pltpu.VMEM((2, fields, levels, levels), f32),
            pltpu.SemaphoreType.DMA((2 * fields + 1, 2)),
        ],
        compiler_params=pltpu.CompilerParams(vmem_limit_bytes=8 << 20),
        cost_estimate=pl.CostEstimate(flops=16 * fields * levels * levels * ox, bytes_accessed=1 << 20, transcendentals=0),
        name="outer_rows",
    )(*in_hbm(depth, state, inverses))


def mix_kernel(
    depth_h, state_h, inv_h, after, mixed_h, first_h, side,
    depth_ref, state, mixed, inv, first, in_sems, out_sems,
):
    fields, oy, levels, _ = mixed.shape
    depth_copy = pltpu.make_async_copy(depth_h, depth_ref, in_sems.at[2 * fields, 0])
    depth_copy.start()

    def load(q, c):
        for i in range(SUB):
            row = c * SUB + i
            pltpu.make_async_copy(state_h.at[q, :, row, :], state.at[q, row], in_sems.at[2 * q, c]).start()
        here = (q, pl.ds(c * SUB, SUB))
        pltpu.make_async_copy(inv_h.at[here], inv.at[here], in_sems.at[2 * q + 1, c]).start()

    for c in range(oy // SUB):
        load(0, c)
    depth_copy.wait()
    level = iota((levels, LANES), 0)
    lane = iota((levels, LANES), 1)
    line = iota((1, LANES), 1)
    edge_depth = jnp.zeros((SUB, LANES), f32)
    for i in range(oy):
        turned = pltpu.roll(jnp.broadcast_to(depth_ref[i : i + 1, :].astype(f32), (SUB, LANES)), 2 * i + 1, 1)
        edge_depth = jnp.where(line // 2 == i, turned, edge_depth)

    def field(q, carry):
        def chunk(c, edges):
            here = (q, pl.ds(pl.multiple_of(c * SUB, SUB), SUB))
            pltpu.make_async_copy(mixed_h.at[here], state.at[here], in_sems.at[2 * q, c]).wait()
            pltpu.make_async_copy(inv_h.at[here], inv.at[here], in_sems.at[2 * q + 1, c]).wait()

            @pl.when(q + 1 < fields)
            def _():
                load(q + 1, c)

            cells = jnp.zeros((levels, LANES), f32)
            names = jnp.zeros((levels, LANES), f32)
            for i in range(SUB):
                row = c * SUB + i
                a = inv[q, row, 0]
                m = solve_row(a, state[q, row], level < depth_ref[pl.ds(row, 1), :])
                mixed[q, row] = m
                column = jnp.broadcast_to(a[:, 0:1], (levels, LANES))
                first[q, row] = column
                cells = jnp.where(lane // 2 == i, pltpu.roll(m, 2 * i + 1, 1), cells)
                names = jnp.where(lane // 2 == HALF // 2 + i, column, names)
            pltpu.make_async_copy(mixed.at[here], mixed_h.at[here], out_sems.at[2 * q]).start()
            pltpu.make_async_copy(first.at[here], first_h.at[here], out_sems.at[2 * q + 1]).start()
            return edges + pltpu.roll(cells + names, 2 * SUB * c, 1)

        side[q, 0:levels] = lax.fori_loop(0, oy // SUB, chunk, jnp.zeros((levels, LANES), f32))
        side[q, levels : levels + SUB] = edge_depth
        return carry

    lax.fori_loop(0, fields, field, 0)
    for q in range(fields):
        pltpu.make_async_copy(mixed.at[q], mixed_h.at[q], out_sems.at[2 * q]).wait()
        pltpu.make_async_copy(first.at[q], first_h.at[q], out_sems.at[2 * q + 1]).wait()


def mix(depth, state, inverses, after):
    fields, levels, oy, ox = state.shape
    edge_shape = jax.ShapeDtypeStruct((fields, levels + SUB, ox), f32)
    full = (fields, oy, levels, ox)
    return pl.pallas_call(
        mix_kernel,
        in_specs=[HBM] * 3 + [pl.BlockSpec(memory_space=pl.ANY)],
        out_specs=[HBM] * 2 + [VMEM],
        out_shape=[pltpu.HBM(full, f32), pltpu.HBM(full, f32), edge_shape],
        scratch_shapes=[
            pltpu.VMEM(depth.shape, jnp.int32),
            pltpu.VMEM(full, f32),
            pltpu.VMEM(full, f32),
            pltpu.VMEM(inverses.shape, f32),
            pltpu.VMEM(full, f32),
            pltpu.SemaphoreType.DMA((2 * fields + 1, oy // SUB)),
            pltpu.SemaphoreType.DMA((2 * fields,)),
        ],
        compiler_params=pltpu.CompilerParams(vmem_limit_bytes=32 << 20),
        cost_estimate=pl.CostEstimate(flops=2 * 4 * fields * oy * levels * levels * ox, bytes_accessed=16 << 20, transcendentals=0),
        name="mix",
    )(*in_hbm(depth, state, inverses), after)


def collect_kernel(cap, fields, oy, recv, after_mix, after_north, after_south, out):
    lat = out.shape[0]
    lon = recv.shape[0] // lat
    per = fields * cap
    group = LANES // per
    forced = fields * oy
    square_row = iota((LANES, LANES), 0).astype(f32)
    line = iota((1, LANES), 1)
    row = iota((2 * oy, LANES), 0).astype(f32)
    lane_base = ((line % fields) * oy).astype(f32)
    lane_side = (line // HALF).astype(f32)
    small_row, small_lane = iota((SUB, LANES), 0), iota((SUB, LANES), 1)
    pick = jnp.where((small_lane % fields == small_row) & (small_lane % HALF < per), 1.0, 0.0).astype(bf16)
    nothing = jnp.zeros((fields, LANES), f32)
    for a in range(lat):
        total = jnp.zeros((LANES, 2 * LANES), f32)
        for tile in range(lon // group):
            places = [(tile * group + s) * lat + a for s in range(group)]
            ids = recv[places[0], per : per + 1, :]
            for s in range(1, group):
                ids = jnp.where(line // per == s, recv[places[s], per : per + 1, :], ids)
            hot = jnp.where(square_row == ids, 1.0, 0.0).astype(bf16)
            high, low = split(jnp.concatenate([recv[p, 0:per, :] for p in places], axis=0))
            total = total + matmul(hot, jnp.concatenate([high, low], axis=1))
        total = total[:, :LANES] + total[:, LANES:]
        out[a, 0:forced] = total
        if a == 0:
            out[a, forced : forced + fields] = nothing
        if a == lat - 1:
            out[a, forced + fields : forced + 2 * fields] = nothing
        for q in range(fields):
            if a + 1 < lat:
                out[a + 1, forced + q : forced + q + 1] = total[q * oy + oy - 1 : q * oy + oy]
            if a > 0:
                out[a - 1, forced + fields + q : forced + fields + q + 1] = total[q * oy : q * oy + 1]
        spread = jnp.zeros((2 * oy, LANES), f32)
        for b in range(lon):
            place = 2.0 * (recv[b * lat + a, per + 1 : per + 2, :] - lane_base) + lane_side
            spread = spread + jnp.where(place == row, recv[b * lat + a, per + 2 : per + 3, :], 0.0)
        high, low = split(padded_rows(spread, LANES).T)
        out[a, forced + SUB : forced + 2 * SUB] = matmul(pick, high) + matmul(pick, low)


def collect(cap, fields, oy, lat, received, after):
    return pl.pallas_call(
        functools.partial(collect_kernel, cap, fields, oy),
        in_specs=[VMEM] + [pl.BlockSpec(memory_space=pl.ANY)] * 3,
        out_specs=VMEM,
        out_shape=jax.ShapeDtypeStruct((lat, fields * oy + 2 * SUB, LANES), f32),
        compiler_params=pltpu.CompilerParams(vmem_limit_bytes=16 << 20),
        name="collect",
    )(received, *after)


def finish_kernel(
    recv, depth_ref, mixed_h, first_h, north_h, south_h, east, west,
    out_h, north, south, forcing, z, keep, halo, z_north, z_south, mixed, first, stage, edge_sems, in_sems, out_sems,
):
    fields, oy, levels, _ = mixed.shape
    level = iota((levels, LANES), 0)
    lanes = iota((levels, LANES), 1)
    square_row = iota((LANES, LANES), 0)
    square_lane = iota((LANES, LANES), 1)
    line = iota((1, LANES), 1)
    even = line % 2 == 0
    edges = [
        pltpu.make_async_copy(a, b, edge_sems.at[k])
        for k, (a, b) in enumerate(((north_h, north), (south_h, south)))
    ]
    for copy in edges:
        copy.start()

    def loads(q, c):
        here = (q, pl.ds(pl.multiple_of(c * SUB, SUB), SUB))
        return [
            pltpu.make_async_copy(a.at[here], b.at[here], in_sems.at[k, q, c])
            for k, (a, b) in enumerate(((mixed_h, mixed), (first_h, first)))
        ]

    for c in range(oy // SUB):
        for copy in loads(0, c):
            copy.start()

    total = recv[0]
    for a in range(1, recv.shape[0]):
        total = total + recv[a]
    forced_rows = fields * oy
    forcing[...] = total[0:forced_rows]
    rows = total[forced_rows : forced_rows + SUB]
    columns = total[forced_rows + SUB :]

    for copy in edges:
        copy.wait()
    depth = depth_ref[...]
    wide = iota((oy, LANES), 1)

    def upright(ref, place):
        value = jnp.where(wide == 2 * iota((oy, LANES), 0) + place, ref[0, levels : levels + 1, :], 0.0)
        return jnp.sum(value, axis=1, keepdims=True).astype(jnp.int32)

    to_east = jnp.where(wide == LANES - 1, upright(east, 1), pltpu.roll(depth, LANES - 1, 1))
    to_west = jnp.where(wide == 0, upright(west, 0), pltpu.roll(depth, 1, 1))
    to_north = jnp.concatenate([north[0, levels : levels + 1, :].astype(jnp.int32), depth[: oy - 1]], axis=0)
    to_south = jnp.concatenate([depth[1:], south[0, levels : levels + 1, :].astype(jnp.int32)], axis=0)
    for i in range(oy):
        sides = jnp.where(level < to_east[i : i + 1], diffusion_rate, 0.0)
        for other in (to_west, to_north, to_south):
            sides = sides + jnp.where(level < other[i : i + 1], diffusion_rate, 0.0)
        keep[i] = 1.0 - sides

    def outer(target, ref, start):
        names = padded_rows(
            jnp.concatenate([ref[q, levels + 1 : levels + 2, :] for q in range(fields)], axis=0), LANES
        ).T
        active = level < ref[0, levels : levels + 1, :].astype(jnp.int32)
        for q in range(fields):
            value = ref[q, 0:levels] + names[0:levels, q : q + 1] * rows[start + q : start + q + 1]
            target[q] = jnp.where(active, value, 0.0)

    outer(z_north, north, 0)
    outer(z_south, south, fields)
    for q in range(fields):
        cells = jnp.where(even, pltpu.roll(east[q], LANES - 1, 1), pltpu.roll(west[q], 1, 1))
        names = pltpu.roll(jnp.where(even, east[q], west[q]), HALF, 1)
        active = level < cells[levels : levels + 1].astype(jnp.int32)
        value = cells[0:levels] + names[0:levels] * columns[q : q + 1]
        halo[q] = jnp.where(active & (line < 2 * oy), value, 0.0)

    both = jnp.where((square_row == square_lane + 1) | (square_row == square_lane - 1), 1.0, 0.0).astype(bf16)
    both = jnp.concatenate([both, both], axis=0)
    ends = (lanes == 0) | (lanes == LANES - 1)

    def field(q, carry):
        z[0] = z_north[q]
        z[oy + 1] = z_south[q]

        def solve(c, carry):
            for copy in loads(q, c):
                copy.wait()

            @pl.when(q + 1 < fields)
            def _():
                for copy in loads(q + 1, c):
                    copy.start()

            for i in range(SUB):
                r = c * SUB + i
                forced = mixed[q, r] + first[q, r] * forcing[pl.ds(q * oy + r, 1), :]
                z[r + 1] = jnp.where(level < depth_ref[pl.ds(r, 1), :], forced, 0.0)
            return carry

        lax.fori_loop(0, oy // SUB, solve, 0)

        def diffuse(c, carry):
            start = c * SUB
            high, low = split(z[pl.ds(start + 1, SUB)].reshape(SUB * levels, LANES))
            sides = matmul(jnp.concatenate([high, low], axis=1), both)
            edge = pltpu.roll(halo[q], (LANES - 2 * SUB * c) % LANES, 1)
            for i in range(SUB):
                r = start + i
                outside = jnp.where(ends, pltpu.roll(edge, LANES - 1 - 2 * i, 1), 0.0)
                around = (z[r] + z[r + 2]) + (sides[i * levels : (i + 1) * levels] + outside)
                active = level < depth_ref[pl.ds(r, 1), :]
                stage[q, r] = jnp.where(active, z[r + 1] * keep[r] + diffusion_rate * around, mixed[q, r])
            for i in range(SUB):
                r = start + i
                pltpu.make_async_copy(stage.at[q, r], out_h.at[q, :, r, :], out_sems.at[q]).start()
            return carry

        lax.fori_loop(0, oy // SUB, diffuse, 0)
        return carry

    lax.fori_loop(0, fields, field, 0)
    for q in range(fields):
        pltpu.make_async_copy(stage.at[q], mixed_h.at[q], out_sems.at[q]).wait()


def finish(received, depth, mixed, first, halos):
    fields, oy, levels, ox = mixed.shape
    edge = pltpu.VMEM((fields, levels, ox), f32)
    message = pltpu.VMEM((fields, levels + SUB, ox), f32)
    full = pltpu.VMEM((fields, oy, levels, ox), f32)
    return pl.pallas_call(
        finish_kernel,
        in_specs=[VMEM] * 2 + [HBM] * 4 + [VMEM] * 2,
        out_specs=HBM,
        out_shape=pltpu.HBM((fields, levels, oy, ox), f32),
        scratch_shapes=[
            message,
            message,
            pltpu.VMEM((fields * oy, ox), f32),
            pltpu.VMEM((oy + 2, levels, ox), f32),
            pltpu.VMEM((oy, levels, ox), f32),
            edge,
            edge,
            edge,
            full,
            full,
            full,
            pltpu.SemaphoreType.DMA((2,)),
            pltpu.SemaphoreType.DMA((2, fields, oy // SUB)),
            pltpu.SemaphoreType.DMA((fields,)),
        ],
        compiler_params=pltpu.CompilerParams(vmem_limit_bytes=32 << 20),
        cost_estimate=pl.CostEstimate(flops=20 * fields * oy * levels * ox, bytes_accessed=12 << 20, transcendentals=0),
        name="finish",
    )(received, depth, *in_hbm(mixed, first, *halos[0:2]), *halos[2:])


def shift(x, axis, step, wrap):
    count = lax.axis_size(axis)
    pairs = [(i, (i + step) % count) for i in range(count) if wrap or 0 <= i + step < count]
    return lax.ppermute(x, axis, pairs)


def on_device(
    atm_flux, sea_mask, src_block, dest_dev, dest_block, intersection_weights, coupling, inverses, ocean_state,
    depth_levels,
):
    lat, lon = lax.axis_size("lat"), lax.axis_size("lon")
    fields, _, oy, _ = ocean_state.shape
    cap = max(SUB, 2 * src_block.shape[0] // (lat * lon))
    slots = regrid(
        cap, lat, lon, oy, src_block, dest_dev[:, 0], dest_block, coupling, atm_flux, sea_mask,
        intersection_weights,
    )
    in_plane = lax.all_to_all(slots, "lon", 0, 0, tiled=True)
    north, south = outer_rows(depth_levels, ocean_state, inverses)
    mixed, first, side = mix(depth_levels, ocean_state, inverses, north)
    halos = (
        shift(south, "lat", 1, False),
        shift(north, "lat", -1, False),
        shift(side, "lon", -1, True),
        shift(side, "lon", 1, True),
    )
    received = lax.all_to_all(collect(cap, fields, oy, lat, in_plane, (side, *halos[0:2])), "lat", 0, 0, tiled=True)
    return finish(received, depth_levels, mixed, first, halos)


def solution(mesh):
    placed = (
        P(None, "lat", "lon"),
        P("lat", "lon"),
        P(("lat", "lon")),
        P(("lat", "lon"), None),
        P(("lat", "lon")),
        P(("lat", "lon"), None, None),
        P(),
        P(None, "lat", "lon", None, None),
        P(None, None, "lat", "lon"),
        P("lat", "lon"),
    )
    return jax.shard_map(
        on_device,
        mesh=mesh,
        in_specs=placed,
        out_specs=P(None, None, "lat", "lon"),
        check_vma=False,
    )
```

```python
import functools

import jax
import jax.numpy as jnp
from jax import lax
from jax.experimental import pallas as pl
from jax.experimental.pallas import tpu as pltpu
from jax.sharding import PartitionSpec as P

diffusion_rate = 0.2
LANES = 128
HALF = 64
SUB = 8
f32 = jnp.float32
bf16 = jnp.bfloat16
HBM = pl.BlockSpec(memory_space=pltpu.HBM)
VMEM = pl.BlockSpec(memory_space=pltpu.VMEM)


def split(x):
    high = x.astype(bf16)
    return high, (x - high.astype(f32)).astype(bf16)


def in_hbm(*arrays):
    return [pltpu.with_memory_space_constraint(x, pltpu.HBM) for x in arrays]


def iota(shape, dim):
    return lax.broadcasted_iota(jnp.int32, shape, dim)


def matmul(a, b):
    return jnp.dot(a, b, preferred_element_type=f32)


def padded_rows(x, rows):
    return x if x.shape[0] == rows else jnp.concatenate([x, jnp.zeros((rows - x.shape[0], LANES), x.dtype)], axis=0)


def regrid_kernel(
    cap, lat, lon, oy, batch, src_h, dev_h, blk_h, coupling_h, atm_h, mask_h, weights_h,
    out_h, out, rows, ids, count, src, dev, blk, coupling, atm, mask, weights, small_sem, big_sem, out_sem,
):
    fluxes, atm_rows, _ = atm.shape
    fields = coupling.shape[0]
    devices = out.shape[0]
    per = fields * cap
    parts = weights.shape[0] // batch
    ahead = min(3, parts)

    def big(k):
        here = pl.ds(pl.multiple_of(k * batch, batch), batch)
        return pltpu.make_async_copy(weights_h.at[here], weights.at[here], big_sem.at[k])

    small = [
        pltpu.make_async_copy(a, b, small_sem.at[k])
        for k, (a, b) in enumerate(
            (
                (coupling_h, coupling), (atm_h, atm), (mask_h, mask),
                (src_h, src), (dev_h, dev), (blk_h, blk),
            )
        )
    ]
    for copy in small:
        copy.start()
    for k in range(ahead):
        big(k).start()

    def clear(d, carry):
        count[d] = 0
        out[d] = jnp.zeros(out.shape[1:], f32)
        return carry

    lax.fori_loop(0, devices, clear, 0)
    ids[...] = jnp.full(ids.shape, -1, jnp.int32)
    for copy in small:
        copy.wait()
    for tile in range(atm_rows // 16):
        here = slice(tile * 16, tile * 16 + 16)
        sea = mask[here, :].astype(f32)
        flux = [atm[f, here, :].astype(f32) * sea for f in range(fluxes)]
        for q in range(fields):
            total = coupling[q, 0] * flux[0]
            for f in range(1, fluxes):
                total = total + coupling[q, f] * flux[f]
            high = total.astype(bf16).astype(f32)
            rows[pl.ds(tile * 16 * SUB + q, 16, stride=SUB), :] = high
            rows[pl.ds(tile * 16 * SUB + fields + q, 16, stride=SUB), :] = total - high

    lane = iota((1, LANES), 1)
    lane_slot = (lane % per) // fields
    lane_row = (lane % fields) * oy

    bits = lon.bit_length() - 1

    def place(d):
        if lon == 1 << bits:
            return (d & (lon - 1)) * lat + lax.shift_right_logical(d, bits)
        return lax.rem(d, lon) * lat + lax.div(d, lon)

    def part(k, carry):
        big(k).wait()

        @pl.when(k + ahead < parts)
        def _():
            big(k + ahead).start()

        for u in range(0, batch, 2):
            p = k * batch + u
            x = jnp.concatenate(
                [rows[pl.ds(pl.multiple_of(src[p + v] * SUB, SUB), SUB), :] for v in range(2)], axis=0
            ).astype(bf16)
            both = matmul(x, jnp.concatenate([weights[p], weights[p + 1]], axis=1))
            for v in range(2):
                d = dev[p + v]
                slot = jnp.minimum(count[d], cap - 1)
                count[d] = slot + 1
                half = both[v * SUB : v * SUB + SUB, v * LANES : (v + 1) * LANES]
                out[place(d), pl.ds(slot * fields, fields), :] = half[0:fields] + half[fields : 2 * fields]
                line = ids[pl.ds(d, 1), :]
                ids[pl.ds(d, 1), :] = jnp.where(lane_slot == slot, lane_row + blk[p + v], line)
        return carry

    lax.fori_loop(0, parts, part, 0)

    def send(k, start, stop):
        return pltpu.make_async_copy(out.at[:, start:stop, :], out_h.at[:, start:stop, :], out_sem.at[k])

    send(0, 0, per).start()

    def halo(k):
        d = 2 * k
        turned = jnp.concatenate(
            [padded_rows(out[place(d + u), 0:per], HALF) for u in range(2)], axis=0
        ).T
        first, last = turned[0:1], turned[LANES - 1 : LANES]
        first_swapped = pltpu.roll(turned[0:SUB], HALF, 1)[0:1]
        last_swapped = pltpu.roll(turned[LANES - SUB : LANES], HALF, 1)[SUB - 1 : SUB]
        for u in range(2):
            b = lax.rem(d + u, lon)
            east = jnp.where(b == lon - 1, d + u - (lon - 1), d + u + 1)
            west = jnp.where(b == 0, d + u + (lon - 1), d + u - 1)
            here, to_east, to_west = place(d + u), place(east), place(west)
            out[here, per : per + 1] = ids[pl.ds(d + u, 1), :].astype(f32)
            sides = jnp.where(lane < HALF, ids[pl.ds(east, 1), :], ids[pl.ds(west, 1), :])
            out[here, per + 1 : per + 2] = sides.astype(f32)
            column = first if u == 0 else first_swapped
            out[to_west, per + 2 : per + 3] = jnp.where(lane < HALF, column, out[to_west, per + 2 : per + 3])
            column = last_swapped if u == 0 else last
            out[to_east, per + 2 : per + 3] = jnp.where(lane < HALF, out[to_east, per + 2 : per + 3], column)

    def halos(k, carry):
        for u in range(4):
            halo(k * 4 + u)
        return carry

    lax.fori_loop(0, devices // 8, halos, 0)
    send(1, per, per + SUB).start()
    send(0, 0, per).wait()
    send(1, per, per + SUB).wait()


def regrid(cap, lat, lon, oy, src, dev, blk, coupling, atm, mask, weights):
    pairs, depth, width = weights.shape
    fields = coupling.shape[0]
    batch = 32
    devices = lat * lon
    tall = fields * cap + SUB
    return pl.pallas_call(
        functools.partial(regrid_kernel, cap, lat, lon, oy, batch),
        in_specs=[HBM] * 7,
        out_specs=HBM,
        out_shape=pltpu.HBM((devices, tall, LANES), f32),
        scratch_shapes=[
            pltpu.VMEM((devices, tall, LANES), f32),
            pltpu.VMEM((atm.shape[1] * SUB, LANES), f32),
            pltpu.VMEM((devices, LANES), jnp.int32),
            pltpu.SMEM((devices,), jnp.int32),
            pltpu.SMEM(src.shape, jnp.int32),
            pltpu.SMEM(dev.shape, jnp.int32),
            pltpu.SMEM(blk.shape, jnp.int32),
            pltpu.SMEM(coupling.shape, f32),
            pltpu.VMEM(atm.shape, bf16),
            pltpu.VMEM(mask.shape, jnp.int32),
            pltpu.VMEM(weights.shape, bf16),
            pltpu.SemaphoreType.DMA((6,)),
            pltpu.SemaphoreType.DMA((pairs // batch,)),
            pltpu.SemaphoreType.DMA((2,)),
        ],
        compiler_params=pltpu.CompilerParams(vmem_limit_bytes=20 << 20),
        cost_estimate=pl.CostEstimate(flops=2 * 8 * pairs * depth * width, bytes_accessed=10 << 20, transcendentals=0),
        name="regrid",
    )(*in_hbm(src, dev, blk, coupling, atm, mask, weights))


def solve_row(a, x, active):
    levels = x.shape[0]
    a_high, a_low = split(a)
    r_high, r_low = split(jnp.where(active, x, 0.0))
    product = matmul(jnp.concatenate([a_high, a_low], axis=0), jnp.concatenate([r_high, r_low], axis=1))
    solved = product[:levels, :LANES] + (product[levels:, :LANES] + product[:levels, LANES:])
    return jnp.where(active, solved, x)


def outer_rows_kernel(depth_h, state_h, inv_h, north, south, depth_ref, state, inv, sems):
    _, fields, levels, _ = state.shape
    oy = depth_ref.shape[0]
    ends = (0, oy - 1)
    copies = [pltpu.make_async_copy(depth_h, depth_ref, sems.at[2 * fields, 0])]
    for q in range(fields):
        for k, row in enumerate(ends):
            copies.append(pltpu.make_async_copy(state_h.at[q, :, row, :], state.at[k, q], sems.at[2 * q, k]))
            copies.append(pltpu.make_async_copy(inv_h.at[q, row, 0], inv.at[k, q], sems.at[2 * q + 1, k]))
    for copy in copies:
        copy.start()
    level = iota((levels, LANES), 0)
    for copy in copies:
        copy.wait()
    for k, (row, ref) in enumerate(zip(ends, (north, south))):
        depth = depth_ref[row : row + 1, :]
        names = jnp.zeros((levels, LANES), f32)
        for q in range(fields):
            a = inv[k, q]
            ref[q, 0:levels] = solve_row(a, state[k, q], level < depth)
            names = jnp.where(iota((levels, LANES), 1) == q, a[:, 0:1], names)
        names = padded_rows(names, LANES).T
        for q in range(fields):
            ref[q, levels : levels + SUB] = jnp.concatenate(
                [depth.astype(f32), names[q : q + 1], jnp.zeros((SUB - 2, LANES), f32)], axis=0
            )


def outer_rows(depth, state, inverses):
    fields, levels, _, ox = state.shape
    edge_shape = jax.ShapeDtypeStruct((fields, levels + SUB, ox), f32)
    return pl.pallas_call(
        outer_rows_kernel,
        in_specs=[HBM] * 3,
        out_specs=[VMEM] * 2,
        out_shape=[edge_shape, edge_shape],
        scratch_shapes=[
            pltpu.VMEM(depth.shape, jnp.int32),
            pltpu.VMEM((2, fields, levels, ox), f32),
            pltpu.VMEM((2, fields, levels, levels), f32),
            pltpu.SemaphoreType.DMA((2 * fields + 1, 2)),
        ],
        compiler_params=pltpu.CompilerParams(vmem_limit_bytes=8 << 20),
        cost_estimate=pl.CostEstimate(flops=16 * fields * levels * levels * ox, bytes_accessed=1 << 20, transcendentals=0),
        name="outer_rows",
    )(*in_hbm(depth, state, inverses))


def mix_kernel(
    depth_h, state_h, inv_h, after, mixed_h, first_h, side,
    depth_ref, state, mixed, inv, first, in_sems, out_sems,
):
    fields, oy, levels, _ = mixed.shape
    depth_copy = pltpu.make_async_copy(depth_h, depth_ref, in_sems.at[2 * fields, 0])
    depth_copy.start()

    def load(q, c):
        for i in range(SUB):
            row = c * SUB + i
            pltpu.make_async_copy(state_h.at[q, :, row, :], state.at[q, row], in_sems.at[2 * q, c]).start()
        here = (q, pl.ds(c * SUB, SUB))
        pltpu.make_async_copy(inv_h.at[here], inv.at[here], in_sems.at[2 * q + 1, c]).start()

    for c in range(oy // SUB):
        load(0, c)
    depth_copy.wait()
    level = iota((levels, LANES), 0)
    lane = iota((levels, LANES), 1)
    line = iota((1, LANES), 1)
    edge_depth = jnp.zeros((SUB, LANES), f32)
    for i in range(oy):
        turned = pltpu.roll(jnp.broadcast_to(depth_ref[i : i + 1, :].astype(f32), (SUB, LANES)), 2 * i + 1, 1)
        edge_depth = jnp.where(line // 2 == i, turned, edge_depth)

    def field(q, carry):
        def chunk(c, edges):
            here = (q, pl.ds(pl.multiple_of(c * SUB, SUB), SUB))
            pltpu.make_async_copy(mixed_h.at[here], state.at[here], in_sems.at[2 * q, c]).wait()
            pltpu.make_async_copy(inv_h.at[here], inv.at[here], in_sems.at[2 * q + 1, c]).wait()

            @pl.when(q + 1 < fields)
            def _():
                load(q + 1, c)

            cells = jnp.zeros((levels, LANES), f32)
            names = jnp.zeros((levels, LANES), f32)
            for i in range(SUB):
                row = c * SUB + i
                a = inv[q, row, 0]
                m = solve_row(a, state[q, row], level < depth_ref[pl.ds(row, 1), :])
                mixed[q, row] = m
                column = jnp.broadcast_to(a[:, 0:1], (levels, LANES))
                first[q, row] = column
                cells = jnp.where(lane // 2 == i, pltpu.roll(m, 2 * i + 1, 1), cells)
                names = jnp.where(lane // 2 == HALF // 2 + i, column, names)
            pltpu.make_async_copy(mixed.at[here], mixed_h.at[here], out_sems.at[2 * q]).start()
            pltpu.make_async_copy(first.at[here], first_h.at[here], out_sems.at[2 * q + 1]).start()
            return edges + pltpu.roll(cells + names, 2 * SUB * c, 1)

        side[q, 0:levels] = lax.fori_loop(0, oy // SUB, chunk, jnp.zeros((levels, LANES), f32))
        side[q, levels : levels + SUB] = edge_depth
        return carry

    lax.fori_loop(0, fields, field, 0)
    for q in range(fields):
        pltpu.make_async_copy(mixed.at[q], mixed_h.at[q], out_sems.at[2 * q]).wait()
        pltpu.make_async_copy(first.at[q], first_h.at[q], out_sems.at[2 * q + 1]).wait()


def mix(depth, state, inverses, after):
    fields, levels, oy, ox = state.shape
    edge_shape = jax.ShapeDtypeStruct((fields, levels + SUB, ox), f32)
    full = (fields, oy, levels, ox)
    return pl.pallas_call(
        mix_kernel,
        in_specs=[HBM] * 3 + [pl.BlockSpec(memory_space=pl.ANY)],
        out_specs=[HBM] * 2 + [VMEM],
        out_shape=[pltpu.HBM(full, f32), pltpu.HBM(full, f32), edge_shape],
        scratch_shapes=[
            pltpu.VMEM(depth.shape, jnp.int32),
            pltpu.VMEM(full, f32),
            pltpu.VMEM(full, f32),
            pltpu.VMEM(inverses.shape, f32),
            pltpu.VMEM(full, f32),
            pltpu.SemaphoreType.DMA((2 * fields + 1, oy // SUB)),
            pltpu.SemaphoreType.DMA((2 * fields,)),
        ],
        compiler_params=pltpu.CompilerParams(vmem_limit_bytes=32 << 20),
        cost_estimate=pl.CostEstimate(flops=2 * 4 * fields * oy * levels * levels * ox, bytes_accessed=16 << 20, transcendentals=0),
        name="mix",
    )(*in_hbm(depth, state, inverses), after)


def collect_kernel(cap, fields, oy, recv, after_mix, after_north, after_south, out):
    lat = out.shape[0]
    lon = recv.shape[0] // lat
    per = fields * cap
    group = LANES // per
    forced = fields * oy
    square_row = iota((LANES, LANES), 0).astype(f32)
    line = iota((1, LANES), 1)
    row = iota((2 * oy, LANES), 0).astype(f32)
    lane_base = ((line % fields) * oy).astype(f32)
    lane_side = (line // HALF).astype(f32)
    small_row, small_lane = iota((SUB, LANES), 0), iota((SUB, LANES), 1)
    pick = jnp.where((small_lane % fields == small_row) & (small_lane % HALF < per), 1.0, 0.0).astype(bf16)
    nothing = jnp.zeros((fields, LANES), f32)
    for a in range(lat):
        total = jnp.zeros((LANES, 2 * LANES), f32)
        for tile in range(lon // group):
            places = [(tile * group + s) * lat + a for s in range(group)]
            ids = recv[places[0], per : per + 1, :]
            for s in range(1, group):
                ids = jnp.where(line // per == s, recv[places[s], per : per + 1, :], ids)
            hot = jnp.where(square_row == ids, 1.0, 0.0).astype(bf16)
            high, low = split(jnp.concatenate([recv[p, 0:per, :] for p in places], axis=0))
            total = total + matmul(hot, jnp.concatenate([high, low], axis=1))
        total = total[:, :LANES] + total[:, LANES:]
        out[a, 0:forced] = total
        if a == 0:
            out[a, forced : forced + fields] = nothing
        if a == lat - 1:
            out[a, forced + fields : forced + 2 * fields] = nothing
        for q in range(fields):
            if a + 1 < lat:
                out[a + 1, forced + q : forced + q + 1] = total[q * oy + oy - 1 : q * oy + oy]
            if a > 0:
                out[a - 1, forced + fields + q : forced + fields + q + 1] = total[q * oy : q * oy + 1]
        spread = jnp.zeros((2 * oy, LANES), f32)
        for b in range(lon):
            place = 2.0 * (recv[b * lat + a, per + 1 : per + 2, :] - lane_base) + lane_side
            spread = spread + jnp.where(place == row, recv[b * lat + a, per + 2 : per + 3, :], 0.0)
        high, low = split(padded_rows(spread, LANES).T)
        out[a, forced + SUB : forced + 2 * SUB] = matmul(pick, high) + matmul(pick, low)


def collect(cap, fields, oy, lat, received, after):
    return pl.pallas_call(
        functools.partial(collect_kernel, cap, fields, oy),
        in_specs=[VMEM] + [pl.BlockSpec(memory_space=pl.ANY)] * 3,
        out_specs=VMEM,
        out_shape=jax.ShapeDtypeStruct((lat, fields * oy + 2 * SUB, LANES), f32),
        compiler_params=pltpu.CompilerParams(vmem_limit_bytes=16 << 20),
        name="collect",
    )(received, *after)


def finish_kernel(
    recv, depth_ref, mixed_h, first_h, north_h, south_h, east, west,
    out_h, north, south, forcing, z, keep, halo, z_north, z_south, mixed, first, stage, edge_sems, in_sems, out_sems,
):
    fields, oy, levels, _ = mixed.shape
    level = iota((levels, LANES), 0)
    lanes = iota((levels, LANES), 1)
    square_row = iota((LANES, LANES), 0)
    square_lane = iota((LANES, LANES), 1)
    line = iota((1, LANES), 1)
    even = line % 2 == 0
    edges = [
        pltpu.make_async_copy(a, b, edge_sems.at[k])
        for k, (a, b) in enumerate(((north_h, north), (south_h, south)))
    ]
    for copy in edges:
        copy.start()

    def loads(q, c):
        here = (q, pl.ds(c * SUB, SUB))
        return [
            pltpu.make_async_copy(a.at[here], b.at[here], in_sems.at[k, q, c])
            for k, (a, b) in enumerate(((mixed_h, mixed), (first_h, first)))
        ]

    for c in range(oy // SUB):
        for copy in loads(0, c):
            copy.start()

    total = recv[0]
    for a in range(1, recv.shape[0]):
        total = total + recv[a]
    forced_rows = fields * oy
    forcing[...] = total[0:forced_rows]
    rows = total[forced_rows : forced_rows + SUB]
    columns = total[forced_rows + SUB :]

    for copy in edges:
        copy.wait()
    depth = depth_ref[...]
    wide = iota((oy, LANES), 1)

    def upright(ref, place):
        value = jnp.where(wide == 2 * iota((oy, LANES), 0) + place, ref[0, levels : levels + 1, :], 0.0)
        return jnp.sum(value, axis=1, keepdims=True).astype(jnp.int32)

    to_east = jnp.where(wide == LANES - 1, upright(east, 1), pltpu.roll(depth, LANES - 1, 1))
    to_west = jnp.where(wide == 0, upright(west, 0), pltpu.roll(depth, 1, 1))
    to_north = jnp.concatenate([north[0, levels : levels + 1, :].astype(jnp.int32), depth[: oy - 1]], axis=0)
    to_south = jnp.concatenate([depth[1:], south[0, levels : levels + 1, :].astype(jnp.int32)], axis=0)
    for i in range(oy):
        sides = jnp.where(level < to_east[i : i + 1], diffusion_rate, 0.0)
        for other in (to_west, to_north, to_south):
            sides = sides + jnp.where(level < other[i : i + 1], diffusion_rate, 0.0)
        keep[i] = 1.0 - sides

    def outer(target, ref, start):
        names = padded_rows(
            jnp.concatenate([ref[q, levels + 1 : levels + 2, :] for q in range(fields)], axis=0), LANES
        ).T
        active = level < ref[0, levels : levels + 1, :].astype(jnp.int32)
        for q in range(fields):
            value = ref[q, 0:levels] + names[0:levels, q : q + 1] * rows[start + q : start + q + 1]
            target[q] = jnp.where(active, value, 0.0)

    outer(z_north, north, 0)
    outer(z_south, south, fields)
    for q in range(fields):
        cells = jnp.where(even, pltpu.roll(east[q], LANES - 1, 1), pltpu.roll(west[q], 1, 1))
        names = pltpu.roll(jnp.where(even, east[q], west[q]), HALF, 1)
        active = level < cells[levels : levels + 1].astype(jnp.int32)
        value = cells[0:levels] + names[0:levels] * columns[q : q + 1]
        halo[q] = jnp.where(active & (line < 2 * oy), value, 0.0)

    both = jnp.where((square_row == square_lane + 1) | (square_row == square_lane - 1), 1.0, 0.0).astype(bf16)
    both = jnp.concatenate([both, both], axis=0)
    ends = (lanes == 0) | (lanes == LANES - 1)

    def field(q, carry):
        @pl.when(q + 1 < fields)
        def _():
            for c in range(oy // SUB):
                for copy in loads(q + 1, c):
                    copy.start()

        z[0] = z_north[q]
        z[oy + 1] = z_south[q]
        edge = halo[q]

        def solve(c):
            for copy in loads(q, c):
                copy.wait()
            for r in range(c * SUB, (c + 1) * SUB):
                forced = mixed[q, r] + first[q, r] * forcing[pl.ds(q * oy + r, 1), :]
                z[r + 1] = jnp.where(level < depth_ref[r : r + 1, :], forced, 0.0)

        def diffuse(c):
            start = c * SUB
            high, low = split(z[start + 1 : start + 1 + SUB].reshape(SUB * levels, LANES))
            sides = matmul(jnp.concatenate([high, low], axis=1), both)
            for i in range(SUB):
                r = start + i
                outside = jnp.where(ends, pltpu.roll(edge, LANES - 1 - 2 * r, 1), 0.0)
                around = (z[r] + z[r + 2]) + (sides[i * levels : (i + 1) * levels] + outside)
                active = level < depth_ref[r : r + 1, :]
                stage[q, r] = jnp.where(active, z[r + 1] * keep[r] + diffusion_rate * around, mixed[q, r])
            for r in range(start, start + SUB):
                pltpu.make_async_copy(stage.at[q, r], out_h.at[q, :, r, :], out_sems.at[q]).start()

        solve(0)
        for c in range(1, oy // SUB):
            solve(c)
            diffuse(c - 1)
        diffuse(oy // SUB - 1)
        return carry

    lax.fori_loop(0, fields, field, 0)
    for q in range(fields):
        pltpu.make_async_copy(stage.at[q], mixed_h.at[q], out_sems.at[q]).wait()


def finish(received, depth, mixed, first, halos):
    fields, oy, levels, ox = mixed.shape
    edge = pltpu.VMEM((fields, levels, ox), f32)
    message = pltpu.VMEM((fields, levels + SUB, ox), f32)
    full = pltpu.VMEM((fields, oy, levels, ox), f32)
    return pl.pallas_call(
        finish_kernel,
        in_specs=[VMEM] * 2 + [HBM] * 4 + [VMEM] * 2,
        out_specs=HBM,
        out_shape=pltpu.HBM((fields, levels, oy, ox), f32),
        scratch_shapes=[
            message,
            message,
            pltpu.VMEM((fields * oy, ox), f32),
            pltpu.VMEM((oy + 2, levels, ox), f32),
            pltpu.VMEM((oy, levels, ox), f32),
            edge,
            edge,
            edge,
            full,
            full,
            full,
            pltpu.SemaphoreType.DMA((2,)),
            pltpu.SemaphoreType.DMA((2, fields, oy // SUB)),
            pltpu.SemaphoreType.DMA((fields,)),
        ],
        compiler_params=pltpu.CompilerParams(vmem_limit_bytes=32 << 20),
        cost_estimate=pl.CostEstimate(flops=20 * fields * oy * levels * ox, bytes_accessed=12 << 20, transcendentals=0),
        name="finish",
    )(received, depth, *in_hbm(mixed, first, *halos[0:2]), *halos[2:])


def shift(x, axis, step, wrap):
    count = lax.axis_size(axis)
    pairs = [(i, (i + step) % count) for i in range(count) if wrap or 0 <= i + step < count]
    return lax.ppermute(x, axis, pairs)


def on_device(
    atm_flux, sea_mask, src_block, dest_dev, dest_block, intersection_weights, coupling, inverses, ocean_state,
    depth_levels,
):
    lat, lon = lax.axis_size("lat"), lax.axis_size("lon")
    fields, _, oy, _ = ocean_state.shape
    cap = max(SUB, 2 * src_block.shape[0] // (lat * lon))
    slots = regrid(
        cap, lat, lon, oy, src_block, dest_dev[:, 0], dest_block, coupling, atm_flux, sea_mask,
        intersection_weights,
    )
    in_plane = lax.all_to_all(slots, "lon", 0, 0, tiled=True)
    north, south = outer_rows(depth_levels, ocean_state, inverses)
    mixed, first, side = mix(depth_levels, ocean_state, inverses, north)
    halos = (
        shift(south, "lat", 1, False),
        shift(north, "lat", -1, False),
        shift(side, "lon", -1, True),
        shift(side, "lon", 1, True),
    )
    received = lax.all_to_all(collect(cap, fields, oy, lat, in_plane, (side, *halos[0:2])), "lat", 0, 0, tiled=True)
    return finish(received, depth_levels, mixed, first, halos)


def solution(mesh):
    placed = (
        P(None, "lat", "lon"),
        P("lat", "lon"),
        P(("lat", "lon")),
        P(("lat", "lon"), None),
        P(("lat", "lon")),
        P(("lat", "lon"), None, None),
        P(),
        P(None, "lat", "lon", None, None),
        P(None, None, "lat", "lon"),
        P("lat", "lon"),
    )
    return jax.shard_map(
        on_device,
        mesh=mesh,
        in_specs=placed,
        out_specs=P(None, None, "lat", "lon"),
        check_vma=False,
    )
```

```python
import functools

import jax
import jax.numpy as jnp
from jax import lax
from jax.experimental import pallas as pl
from jax.experimental.pallas import tpu as pltpu
from jax.sharding import PartitionSpec as P

diffusion_rate = 0.2
LANES = 128
HALF = 64
SUB = 8
f32 = jnp.float32
bf16 = jnp.bfloat16
HBM = pl.BlockSpec(memory_space=pltpu.HBM)
VMEM = pl.BlockSpec(memory_space=pltpu.VMEM)


def split(x):
    high = x.astype(bf16)
    return high, (x - high.astype(f32)).astype(bf16)


def in_hbm(*arrays):
    return [pltpu.with_memory_space_constraint(x, pltpu.HBM) for x in arrays]


def iota(shape, dim):
    return lax.broadcasted_iota(jnp.int32, shape, dim)


def matmul(a, b):
    return jnp.dot(a, b, preferred_element_type=f32)


def padded_rows(x, rows):
    return x if x.shape[0] == rows else jnp.concatenate([x, jnp.zeros((rows - x.shape[0], LANES), x.dtype)], axis=0)


def solve_row(a, x, active):
    levels = x.shape[0]
    a_high, a_low = split(a)
    r_high, r_low = split(jnp.where(active, x, 0.0))
    product = matmul(jnp.concatenate([a_high, a_low], axis=0), jnp.concatenate([r_high, r_low], axis=1))
    solved = product[:levels, :LANES] + (product[levels:, :LANES] + product[:levels, LANES:])
    return jnp.where(active, solved, x)


def outer_messages(refs, depth_ref, state, inv):
    _, fields, levels, _ = state.shape
    oy = depth_ref.shape[0]
    level = iota((levels, LANES), 0)
    for k, (row, ref) in enumerate(zip((0, oy - 1), refs)):
        depth = depth_ref[row : row + 1, :]
        names = jnp.zeros((levels, LANES), f32)
        for q in range(fields):
            a = inv[k, q]
            ref[q, 0:levels] = solve_row(a, state[k, q], level < depth)
            names = jnp.where(iota((levels, LANES), 1) == q, a[:, 0:1], names)
        names = padded_rows(names, LANES).T
        for q in range(fields):
            ref[q, levels : levels + SUB] = jnp.concatenate(
                [depth.astype(f32), names[q : q + 1], jnp.zeros((SUB - 2, LANES), f32)], axis=0
            )


def regrid_kernel(
    cap, lat, lon, oy, batch,
    src_h, dev_h, blk_h, coupling_h, atm_h, mask_h, weights_h, depth_h, state_h, inv_h,
    out_h, north, south,
    out, rows, ids, count, src, dev, blk, coupling, atm, mask, weights, depth_ref, state, inv,
    small_sem, outer_sem, big_sem, out_sem,
):
    fluxes, atm_rows, _ = atm.shape
    fields = coupling.shape[0]
    devices = out.shape[0]
    per = fields * cap
    parts = weights.shape[0] // batch
    ahead = min(3, parts)

    def big(k):
        here = pl.ds(pl.multiple_of(k * batch, batch), batch)
        return pltpu.make_async_copy(weights_h.at[here], weights.at[here], big_sem.at[k])

    small = [
        pltpu.make_async_copy(a, b, small_sem.at[k])
        for k, (a, b) in enumerate(
            (
                (coupling_h, coupling), (atm_h, atm), (mask_h, mask),
                (src_h, src), (dev_h, dev), (blk_h, blk),
            )
        )
    ]
    outer = [pltpu.make_async_copy(depth_h, depth_ref, outer_sem.at[2 * fields, 0])]
    for q in range(fields):
        for k, row in enumerate((0, oy - 1)):
            outer.append(pltpu.make_async_copy(state_h.at[q, :, row, :], state.at[k, q], outer_sem.at[2 * q, k]))
            outer.append(pltpu.make_async_copy(inv_h.at[q, row, 0], inv.at[k, q], outer_sem.at[2 * q + 1, k]))
    for copy in small + outer:
        copy.start()
    for k in range(ahead):
        big(k).start()

    def clear(d, carry):
        count[d] = 0
        out[d] = jnp.zeros(out.shape[1:], f32)
        return carry

    lax.fori_loop(0, devices, clear, 0)
    ids[...] = jnp.full(ids.shape, -1, jnp.int32)
    for copy in small:
        copy.wait()
    for tile in range(atm_rows // 16):
        here = slice(tile * 16, tile * 16 + 16)
        sea = mask[here, :].astype(f32)
        flux = [atm[f, here, :].astype(f32) * sea for f in range(fluxes)]
        for q in range(fields):
            total = coupling[q, 0] * flux[0]
            for f in range(1, fluxes):
                total = total + coupling[q, f] * flux[f]
            high = total.astype(bf16).astype(f32)
            rows[pl.ds(tile * 16 * SUB + q, 16, stride=SUB), :] = high
            rows[pl.ds(tile * 16 * SUB + fields + q, 16, stride=SUB), :] = total - high

    for copy in outer:
        copy.wait()
    outer_messages((north, south), depth_ref, state, inv)

    lane = iota((1, LANES), 1)
    lane_slot = (lane % per) // fields
    lane_row = (lane % fields) * oy

    bits = lon.bit_length() - 1

    def place(d):
        if lon == 1 << bits:
            return (d & (lon - 1)) * lat + lax.shift_right_logical(d, bits)
        return lax.rem(d, lon) * lat + lax.div(d, lon)

    def part(k, carry):
        big(k).wait()

        @pl.when(k + ahead < parts)
        def _():
            big(k + ahead).start()

        for u in range(0, batch, 2):
            p = k * batch + u
            x = jnp.concatenate(
                [rows[pl.ds(pl.multiple_of(src[p + v] * SUB, SUB), SUB), :] for v in range(2)], axis=0
            ).astype(bf16)
            both = matmul(x, jnp.concatenate([weights[p], weights[p + 1]], axis=1))
            for v in range(2):
                d = dev[p + v]
                slot = jnp.minimum(count[d], cap - 1)
                count[d] = slot + 1
                half = both[v * SUB : v * SUB + SUB, v * LANES : (v + 1) * LANES]
                out[place(d), pl.ds(slot * fields, fields), :] = half[0:fields] + half[fields : 2 * fields]
                line = ids[pl.ds(d, 1), :]
                ids[pl.ds(d, 1), :] = jnp.where(lane_slot == slot, lane_row + blk[p + v], line)
        return carry

    lax.fori_loop(0, parts, part, 0)

    def send(k, start, stop):
        return pltpu.make_async_copy(out.at[:, start:stop, :], out_h.at[:, start:stop, :], out_sem.at[k])

    send(0, 0, per).start()

    def halo(k):
        d = 2 * k
        turned = jnp.concatenate(
            [padded_rows(out[place(d + u), 0:per], HALF) for u in range(2)], axis=0
        ).T
        first, last = turned[0:1], turned[LANES - 1 : LANES]
        first_swapped = pltpu.roll(turned[0:SUB], HALF, 1)[0:1]
        last_swapped = pltpu.roll(turned[LANES - SUB : LANES], HALF, 1)[SUB - 1 : SUB]
        for u in range(2):
            b = lax.rem(d + u, lon)
            east = jnp.where(b == lon - 1, d + u - (lon - 1), d + u + 1)
            west = jnp.where(b == 0, d + u + (lon - 1), d + u - 1)
            here, to_east, to_west = place(d + u), place(east), place(west)
            out[here, per : per + 1] = ids[pl.ds(d + u, 1), :].astype(f32)
            sides = jnp.where(lane < HALF, ids[pl.ds(east, 1), :], ids[pl.ds(west, 1), :])
            out[here, per + 1 : per + 2] = sides.astype(f32)
            column = first if u == 0 else first_swapped
            out[to_west, per + 2 : per + 3] = jnp.where(lane < HALF, column, out[to_west, per + 2 : per + 3])
            column = last_swapped if u == 0 else last
            out[to_east, per + 2 : per + 3] = jnp.where(lane < HALF, out[to_east, per + 2 : per + 3], column)

    def halos(k, carry):
        for u in range(4):
            halo(k * 4 + u)
        return carry

    lax.fori_loop(0, devices // 8, halos, 0)
    send(1, per, per + SUB).start()
    send(0, 0, per).wait()
    send(1, per, per + SUB).wait()


def regrid(cap, lat, lon, src, dev, blk, coupling, atm, mask, weights, depth, ocean, inverses):
    pairs, cells, width = weights.shape
    fields, levels, oy, ox = ocean.shape
    message = jax.ShapeDtypeStruct((fields, levels + SUB, ox), f32)
    batch = 32
    devices = lat * lon
    tall = fields * cap + SUB
    return pl.pallas_call(
        functools.partial(regrid_kernel, cap, lat, lon, oy, batch),
        in_specs=[HBM] * 10,
        out_specs=[HBM, VMEM, VMEM],
        out_shape=[pltpu.HBM((devices, tall, LANES), f32), message, message],
        scratch_shapes=[
            pltpu.VMEM((devices, tall, LANES), f32),
            pltpu.VMEM((atm.shape[1] * SUB, LANES), f32),
            pltpu.VMEM((devices, LANES), jnp.int32),
            pltpu.SMEM((devices,), jnp.int32),
            pltpu.SMEM(src.shape, jnp.int32),
            pltpu.SMEM(dev.shape, jnp.int32),
            pltpu.SMEM(blk.shape, jnp.int32),
            pltpu.SMEM(coupling.shape, f32),
            pltpu.VMEM(atm.shape, bf16),
            pltpu.VMEM(mask.shape, jnp.int32),
            pltpu.VMEM(weights.shape, bf16),
            pltpu.VMEM(depth.shape, jnp.int32),
            pltpu.VMEM((2, fields, levels, ox), f32),
            pltpu.VMEM((2, fields, levels, levels), f32),
            pltpu.SemaphoreType.DMA((6,)),
            pltpu.SemaphoreType.DMA((2 * fields + 1, 2)),
            pltpu.SemaphoreType.DMA((pairs // batch,)),
            pltpu.SemaphoreType.DMA((2,)),
        ],
        compiler_params=pltpu.CompilerParams(vmem_limit_bytes=20 << 20),
        cost_estimate=pl.CostEstimate(flops=2 * 8 * pairs * cells * width, bytes_accessed=10 << 20, transcendentals=0),
        name="regrid",
    )(*in_hbm(src, dev, blk, coupling, atm, mask, weights, depth, ocean, inverses))


def mix_kernel(
    depth_h, state_h, inv_h, mixed_h, first_h, to_east, to_west,
    depth_ref, state, mixed, inv, first, side, in_sems, out_sems,
):
    fields, oy, levels, _ = mixed.shape
    depth_copy = pltpu.make_async_copy(depth_h, depth_ref, in_sems.at[2 * fields, 0])
    depth_copy.start()

    def load(q, c):
        for i in range(SUB):
            row = c * SUB + i
            pltpu.make_async_copy(state_h.at[q, :, row, :], state.at[q, row], in_sems.at[2 * q, c]).start()
        here = (q, pl.ds(c * SUB, SUB))
        pltpu.make_async_copy(inv_h.at[here], inv.at[here], in_sems.at[2 * q + 1, c]).start()

    for c in range(oy // SUB):
        load(0, c)
    depth_copy.wait()
    level = iota((levels, LANES), 0)
    lane = iota((levels, LANES), 1)
    line = iota((1, LANES), 1)
    edge_depth = jnp.zeros((SUB, LANES), f32)
    for i in range(oy):
        turned = pltpu.roll(jnp.broadcast_to(depth_ref[i : i + 1, :].astype(f32), (SUB, LANES)), 2 * i + 1, 1)
        edge_depth = jnp.where(line // 2 == i, turned, edge_depth)

    def field(q, carry):
        @pl.when(q + 1 < fields)
        def _():
            for c in range(oy // SUB):
                load(q + 1, c)

        cells = jnp.zeros((levels, LANES), f32)
        for c in range(oy // SUB):
            here = (q, pl.ds(c * SUB, SUB))
            pltpu.make_async_copy(mixed_h.at[here], state.at[here], in_sems.at[2 * q, c]).wait()
            pltpu.make_async_copy(inv_h.at[here], inv.at[here], in_sems.at[2 * q + 1, c]).wait()
            for row in range(c * SUB, (c + 1) * SUB):
                a = inv[q, row, 0]
                m = solve_row(a, state[q, row], level < depth_ref[row : row + 1, :])
                mixed[q, row] = m
                column = jnp.broadcast_to(a[:, 0:1], (levels, LANES))
                first[q, row] = column
                cells = jnp.where(lane // 2 == row, pltpu.roll(m, 2 * row + 1, 1), cells)
                cells = jnp.where(lane // 2 == HALF // 2 + row, column, cells)
            pltpu.make_async_copy(mixed.at[here], mixed_h.at[here], out_sems.at[2 * q]).start()
            pltpu.make_async_copy(first.at[here], first_h.at[here], out_sems.at[2 * q + 1]).start()
        side[q, 0:levels] = cells
        side[q, levels : levels + SUB] = edge_depth
        return carry

    lax.fori_loop(0, fields, field, 0)
    even = line % 2 == 0
    for k in range(fields // 2):
        to_east[k] = jnp.where(even, side[2 * k], pltpu.roll(side[2 * k + 1], 1, 1))
        to_west[k] = jnp.where(even, pltpu.roll(side[2 * k], LANES - 1, 1), side[2 * k + 1])
    for q in range(fields):
        pltpu.make_async_copy(mixed.at[q], mixed_h.at[q], out_sems.at[2 * q]).wait()
        pltpu.make_async_copy(first.at[q], first_h.at[q], out_sems.at[2 * q + 1]).wait()


def mix(depth, state, inverses):
    fields, levels, oy, ox = state.shape
    edge_shape = jax.ShapeDtypeStruct((fields // 2, levels + SUB, ox), f32)
    full = (fields, oy, levels, ox)
    return pl.pallas_call(
        mix_kernel,
        in_specs=[HBM] * 3,
        out_specs=[HBM] * 2 + [VMEM] * 2,
        out_shape=[pltpu.HBM(full, f32), pltpu.HBM(full, f32), edge_shape, edge_shape],
        scratch_shapes=[
            pltpu.VMEM(depth.shape, jnp.int32),
            pltpu.VMEM(full, f32),
            pltpu.VMEM(full, f32),
            pltpu.VMEM(inverses.shape, f32),
            pltpu.VMEM(full, f32),
            pltpu.VMEM((fields, levels + SUB, ox), f32),
            pltpu.SemaphoreType.DMA((2 * fields + 1, oy // SUB)),
            pltpu.SemaphoreType.DMA((2 * fields,)),
        ],
        compiler_params=pltpu.CompilerParams(vmem_limit_bytes=32 << 20),
        cost_estimate=pl.CostEstimate(flops=2 * 4 * fields * oy * levels * levels * ox, bytes_accessed=16 << 20, transcendentals=0),
        name="mix",
    )(*in_hbm(depth, state, inverses))


def collect_kernel(cap, fields, oy, recv, after_mix, after_north, after_south, out):
    lat = out.shape[0]
    lon = recv.shape[0] // lat
    per = fields * cap
    group = LANES // per
    forced = fields * oy
    square_row = iota((LANES, LANES), 0).astype(f32)
    line = iota((1, LANES), 1)
    row = iota((2 * oy, LANES), 0).astype(f32)
    lane_base = ((line % fields) * oy).astype(f32)
    lane_side = (line // HALF).astype(f32)
    small_row, small_lane = iota((SUB, LANES), 0), iota((SUB, LANES), 1)
    pick = jnp.where((small_lane % fields == small_row) & (small_lane % HALF < per), 1.0, 0.0).astype(bf16)
    nothing = jnp.zeros((fields, LANES), f32)
    for a in range(lat):
        total = jnp.zeros((LANES, 2 * LANES), f32)
        for tile in range(lon // group):
            places = [(tile * group + s) * lat + a for s in range(group)]
            ids = recv[places[0], per : per + 1, :]
            for s in range(1, group):
                ids = jnp.where(line // per == s, recv[places[s], per : per + 1, :], ids)
            hot = jnp.where(square_row == ids, 1.0, 0.0).astype(bf16)
            high, low = split(jnp.concatenate([recv[p, 0:per, :] for p in places], axis=0))
            total = total + matmul(hot, jnp.concatenate([high, low], axis=1))
        total = total[:, :LANES] + total[:, LANES:]
        out[a, 0:forced] = total
        if a == 0:
            out[a, forced : forced + fields] = nothing
        if a == lat - 1:
            out[a, forced + fields : forced + 2 * fields] = nothing
        for q in range(fields):
            if a + 1 < lat:
                out[a + 1, forced + q : forced + q + 1] = total[q * oy + oy - 1 : q * oy + oy]
            if a > 0:
                out[a - 1, forced + fields + q : forced + fields + q + 1] = total[q * oy : q * oy + 1]
        spread = jnp.zeros((2 * oy, LANES), f32)
        for b in range(lon):
            place = 2.0 * (recv[b * lat + a, per + 1 : per + 2, :] - lane_base) + lane_side
            spread = spread + jnp.where(place == row, recv[b * lat + a, per + 2 : per + 3, :], 0.0)
        high, low = split(padded_rows(spread, LANES).T)
        out[a, forced + SUB : forced + 2 * SUB] = matmul(pick, high) + matmul(pick, low)


def collect(cap, fields, oy, lat, received, after):
    return pl.pallas_call(
        functools.partial(collect_kernel, cap, fields, oy),
        in_specs=[VMEM] + [pl.BlockSpec(memory_space=pl.ANY)] * 3,
        out_specs=VMEM,
        out_shape=jax.ShapeDtypeStruct((lat, fields * oy + 2 * SUB, LANES), f32),
        compiler_params=pltpu.CompilerParams(vmem_limit_bytes=16 << 20),
        name="collect",
    )(received, *after)


def finish_kernel(
    recv, depth_ref, mixed_h, first_h, north_h, south_h, east, west,
    out_h, north, south, forcing, z, keep, halo, z_north, z_south, mixed, first, stage, edge_sems, in_sems, out_sems,
):
    fields, oy, levels, _ = mixed.shape
    level = iota((levels, LANES), 0)
    lanes = iota((levels, LANES), 1)
    square_row = iota((LANES, LANES), 0)
    square_lane = iota((LANES, LANES), 1)
    line = iota((1, LANES), 1)
    even = line % 2 == 0
    edges = [
        pltpu.make_async_copy(a, b, edge_sems.at[k])
        for k, (a, b) in enumerate(((north_h, north), (south_h, south)))
    ]
    for copy in edges:
        copy.start()

    def loads(q, c):
        here = (q, pl.ds(c * SUB, SUB))
        return [
            pltpu.make_async_copy(a.at[here], b.at[here], in_sems.at[k, q, c])
            for k, (a, b) in enumerate(((mixed_h, mixed), (first_h, first)))
        ]

    for c in range(oy // SUB):
        for copy in loads(0, c):
            copy.start()

    total = recv[0]
    for a in range(1, recv.shape[0]):
        total = total + recv[a]
    forced_rows = fields * oy
    forcing[...] = total[0:forced_rows]
    rows = total[forced_rows : forced_rows + SUB]
    columns = total[forced_rows + SUB :]

    for copy in edges:
        copy.wait()
    depth = depth_ref[...]
    wide = iota((oy, LANES), 1)

    def upright(ref):
        value = jnp.where(wide == 2 * iota((oy, LANES), 0), ref[0, levels : levels + 1, :], 0.0)
        return jnp.sum(value, axis=1, keepdims=True).astype(jnp.int32)

    to_east = jnp.where(wide == LANES - 1, upright(east), pltpu.roll(depth, LANES - 1, 1))
    to_west = jnp.where(wide == 0, upright(west), pltpu.roll(depth, 1, 1))
    to_north = jnp.concatenate([north[0, levels : levels + 1, :].astype(jnp.int32), depth[: oy - 1]], axis=0)
    to_south = jnp.concatenate([depth[1:], south[0, levels : levels + 1, :].astype(jnp.int32)], axis=0)
    for i in range(oy):
        sides = jnp.where(level < to_east[i : i + 1], diffusion_rate, 0.0)
        for other in (to_west, to_north, to_south):
            sides = sides + jnp.where(level < other[i : i + 1], diffusion_rate, 0.0)
        keep[i] = 1.0 - sides

    def outer(target, ref, start):
        names = padded_rows(
            jnp.concatenate([ref[q, levels + 1 : levels + 2, :] for q in range(fields)], axis=0), LANES
        ).T
        active = level < ref[0, levels : levels + 1, :].astype(jnp.int32)
        for q in range(fields):
            value = ref[q, 0:levels] + names[0:levels, q : q + 1] * rows[start + q : start + q + 1]
            target[q] = jnp.where(active, value, 0.0)

    outer(z_north, north, 0)
    outer(z_south, south, fields)
    for q in range(fields):
        if q % 2:
            cells = jnp.where(even, pltpu.roll(east[q // 2], LANES - 1, 1), west[q // 2])
        else:
            cells = jnp.where(even, east[q // 2], pltpu.roll(west[q // 2], 1, 1))
        names = pltpu.roll(cells, HALF, 1)
        active = level < cells[levels : levels + 1].astype(jnp.int32)
        value = cells[0:levels] + names[0:levels] * columns[q : q + 1]
        halo[q] = jnp.where(active & (line < 2 * oy), value, 0.0)

    both = jnp.where((square_row == square_lane + 1) | (square_row == square_lane - 1), 1.0, 0.0).astype(bf16)
    both = jnp.concatenate([both, both], axis=0)
    ends = (lanes == 0) | (lanes == LANES - 1)

    def field(q, carry):
        @pl.when(q + 1 < fields)
        def _():
            for c in range(oy // SUB):
                for copy in loads(q + 1, c):
                    copy.start()

        z[0] = z_north[q]
        z[oy + 1] = z_south[q]
        edge = halo[q]

        def solve(c):
            for copy in loads(q, c):
                copy.wait()
            for r in range(c * SUB, (c + 1) * SUB):
                forced = mixed[q, r] + first[q, r] * forcing[pl.ds(q * oy + r, 1), :]
                z[r + 1] = jnp.where(level < depth_ref[r : r + 1, :], forced, 0.0)

        def diffuse(c):
            start = c * SUB
            high, low = split(z[start + 1 : start + 1 + SUB].reshape(SUB * levels, LANES))
            sides = matmul(jnp.concatenate([high, low], axis=1), both)
            for i in range(SUB):
                r = start + i
                outside = jnp.where(ends, pltpu.roll(edge, LANES - 1 - 2 * r, 1), 0.0)
                around = (z[r] + z[r + 2]) + (sides[i * levels : (i + 1) * levels] + outside)
                active = level < depth_ref[r : r + 1, :]
                stage[q, r] = jnp.where(active, z[r + 1] * keep[r] + diffusion_rate * around, mixed[q, r])
            for r in range(start, start + SUB):
                pltpu.make_async_copy(stage.at[q, r], out_h.at[q, :, r, :], out_sems.at[q]).start()

        solve(0)
        for c in range(1, oy // SUB):
            solve(c)
            diffuse(c - 1)
        diffuse(oy // SUB - 1)
        return carry

    lax.fori_loop(0, fields, field, 0)
    for q in range(fields):
        pltpu.make_async_copy(stage.at[q], mixed_h.at[q], out_sems.at[q]).wait()


def finish(received, depth, mixed, first, halos):
    fields, oy, levels, ox = mixed.shape
    edge = pltpu.VMEM((fields, levels, ox), f32)
    message = pltpu.VMEM((fields, levels + SUB, ox), f32)
    full = pltpu.VMEM((fields, oy, levels, ox), f32)
    return pl.pallas_call(
        finish_kernel,
        in_specs=[VMEM] * 2 + [HBM] * 4 + [VMEM] * 2,
        out_specs=HBM,
        out_shape=pltpu.HBM((fields, levels, oy, ox), f32),
        scratch_shapes=[
            message,
            message,
            pltpu.VMEM((fields * oy, ox), f32),
            pltpu.VMEM((oy + 2, levels, ox), f32),
            pltpu.VMEM((oy, levels, ox), f32),
            edge,
            edge,
            edge,
            full,
            full,
            full,
            pltpu.SemaphoreType.DMA((2,)),
            pltpu.SemaphoreType.DMA((2, fields, oy // SUB)),
            pltpu.SemaphoreType.DMA((fields,)),
        ],
        compiler_params=pltpu.CompilerParams(vmem_limit_bytes=32 << 20),
        cost_estimate=pl.CostEstimate(flops=20 * fields * oy * levels * ox, bytes_accessed=12 << 20, transcendentals=0),
        name="finish",
    )(received, depth, *in_hbm(mixed, first, *halos[0:2]), *halos[2:])


def shift(x, axis, step, wrap):
    count = lax.axis_size(axis)
    pairs = [(i, (i + step) % count) for i in range(count) if wrap or 0 <= i + step < count]
    return lax.ppermute(x, axis, pairs)


def on_device(
    atm_flux, sea_mask, src_block, dest_dev, dest_block, intersection_weights, coupling, inverses, ocean_state,
    depth_levels,
):
    lat, lon = lax.axis_size("lat"), lax.axis_size("lon")
    fields, _, oy, _ = ocean_state.shape
    cap = max(SUB, 2 * src_block.shape[0] // (lat * lon))
    slots, north, south = regrid(
        cap, lat, lon, src_block, dest_dev[:, 0], dest_block, coupling, atm_flux, sea_mask,
        intersection_weights, depth_levels, ocean_state, inverses,
    )
    in_plane = lax.all_to_all(slots, "lon", 0, 0, tiled=True)
    mixed, first, to_east, to_west = mix(depth_levels, ocean_state, inverses)
    halos = (
        shift(south, "lat", 1, False),
        shift(north, "lat", -1, False),
        shift(to_west, "lon", -1, True),
        shift(to_east, "lon", 1, True),
    )
    received = lax.all_to_all(collect(cap, fields, oy, lat, in_plane, (to_east, *halos[0:2])), "lat", 0, 0, tiled=True)
    return finish(received, depth_levels, mixed, first, halos)


def solution(mesh):
    placed = (
        P(None, "lat", "lon"),
        P("lat", "lon"),
        P(("lat", "lon")),
        P(("lat", "lon"), None),
        P(("lat", "lon")),
        P(("lat", "lon"), None, None),
        P(),
        P(None, "lat", "lon", None, None),
        P(None, None, "lat", "lon"),
        P("lat", "lon"),
    )
    return jax.shard_map(
        on_device,
        mesh=mesh,
        in_specs=placed,
        out_specs=P(None, None, "lat", "lon"),
        check_vma=False,
    )
```

```python
import functools

import jax
import jax.numpy as jnp
from jax import lax
from jax.experimental import pallas as pl
from jax.experimental.pallas import tpu as pltpu
from jax.sharding import PartitionSpec as P

diffusion_rate = 0.2
LANES = 128
HALF = 64
SUB = 8
f32 = jnp.float32
bf16 = jnp.bfloat16
HBM = pl.BlockSpec(memory_space=pltpu.HBM)
VMEM = pl.BlockSpec(memory_space=pltpu.VMEM)


def split(x):
    high = x.astype(bf16)
    return high, (x - high.astype(f32)).astype(bf16)


def in_hbm(*arrays):
    return [pltpu.with_memory_space_constraint(x, pltpu.HBM) for x in arrays]


def iota(shape, dim):
    return lax.broadcasted_iota(jnp.int32, shape, dim)


def matmul(a, b):
    return jnp.dot(a, b, preferred_element_type=f32)


def padded_rows(x, rows):
    return x if x.shape[0] == rows else jnp.concatenate([x, jnp.zeros((rows - x.shape[0], LANES), x.dtype)], axis=0)


def solve_row(a, x, active):
    levels = x.shape[0]
    a_high, a_low = split(a)
    r_high, r_low = split(jnp.where(active, x, 0.0))
    product = matmul(jnp.concatenate([a_high, a_low], axis=0), jnp.concatenate([r_high, r_low], axis=1))
    solved = product[:levels, :LANES] + (product[levels:, :LANES] + product[:levels, LANES:])
    return jnp.where(active, solved, x)


def outer_messages(refs, depth_ref, state, inv):
    _, fields, levels, _ = state.shape
    oy = depth_ref.shape[0]
    level = iota((levels, LANES), 0)
    for k, (row, ref) in enumerate(zip((0, oy - 1), refs)):
        depth = depth_ref[row : row + 1, :]
        names = jnp.zeros((levels, LANES), f32)
        for q in range(fields):
            a = inv[k, q]
            ref[q, 0:levels] = solve_row(a, state[k, q], level < depth)
            names = jnp.where(iota((levels, LANES), 1) == q, a[:, 0:1], names)
        names = padded_rows(names, LANES).T
        for q in range(fields):
            ref[q, levels : levels + SUB] = jnp.concatenate(
                [depth.astype(f32), names[q : q + 1], jnp.zeros((SUB - 2, LANES), f32)], axis=0
            )


def regrid_kernel(
    cap, lat, lon, oy, batch,
    src_h, dev_h, blk_h, coupling_h, atm_h, mask_h, weights_h, depth_h, state_h, inv_h,
    out_h, north, south,
    out, rows, ids, count, src, dev, blk, coupling, atm, mask, weights, depth_ref, state, inv,
    small_sem, outer_sem, big_sem, out_sem,
):
    fluxes, atm_rows, _ = atm.shape
    fields = coupling.shape[0]
    devices = out.shape[0]
    per = fields * cap
    parts = weights.shape[0] // batch
    ahead = min(3, parts)

    def big(k):
        here = pl.ds(pl.multiple_of(k * batch, batch), batch)
        return pltpu.make_async_copy(weights_h.at[here], weights.at[here], big_sem.at[k])

    small = [
        pltpu.make_async_copy(a, b, small_sem.at[k])
        for k, (a, b) in enumerate(
            (
                (coupling_h, coupling), (atm_h, atm), (mask_h, mask),
                (src_h, src), (dev_h, dev), (blk_h, blk),
            )
        )
    ]
    outer = [pltpu.make_async_copy(depth_h, depth_ref, outer_sem.at[2 * fields, 0])]
    for q in range(fields):
        for k, row in enumerate((0, oy - 1)):
            outer.append(pltpu.make_async_copy(state_h.at[q, :, row, :], state.at[k, q], outer_sem.at[2 * q, k]))
            outer.append(pltpu.make_async_copy(inv_h.at[q, row, 0], inv.at[k, q], outer_sem.at[2 * q + 1, k]))
    for copy in small + outer:
        copy.start()
    for k in range(ahead):
        big(k).start()

    def clear(d, carry):
        count[d] = 0
        out[d] = jnp.zeros(out.shape[1:], f32)
        return carry

    lax.fori_loop(0, devices, clear, 0)
    ids[...] = jnp.full(ids.shape, -1, jnp.int32)
    for copy in small:
        copy.wait()
    for tile in range(atm_rows // 16):
        here = slice(tile * 16, tile * 16 + 16)
        sea = mask[here, :].astype(f32)
        flux = [atm[f, here, :].astype(f32) * sea for f in range(fluxes)]
        for q in range(fields):
            total = coupling[q, 0] * flux[0]
            for f in range(1, fluxes):
                total = total + coupling[q, f] * flux[f]
            high = total.astype(bf16).astype(f32)
            rows[pl.ds(tile * 16 * SUB + q, 16, stride=SUB), :] = high
            rows[pl.ds(tile * 16 * SUB + fields + q, 16, stride=SUB), :] = total - high

    for copy in outer:
        copy.wait()
    outer_messages((north, south), depth_ref, state, inv)

    lane = iota((1, LANES), 1)
    lane_slot = (lane % per) // fields
    lane_row = (lane % fields) * oy

    bits = lon.bit_length() - 1

    def place(d):
        if lon == 1 << bits:
            return (d & (lon - 1)) * lat + lax.shift_right_logical(d, bits)
        return lax.rem(d, lon) * lat + lax.div(d, lon)

    def part(k, carry):
        big(k).wait()

        @pl.when(k + ahead < parts)
        def _():
            big(k + ahead).start()

        for u in range(0, batch, 2):
            p = k * batch + u
            x = jnp.concatenate(
                [rows[pl.ds(pl.multiple_of(src[p + v] * SUB, SUB), SUB), :] for v in range(2)], axis=0
            ).astype(bf16)
            both = matmul(x, jnp.concatenate([weights[p], weights[p + 1]], axis=1))
            for v in range(2):
                d = dev[p + v]
                slot = jnp.minimum(count[d], cap - 1)
                count[d] = slot + 1
                half = both[v * SUB : v * SUB + SUB, v * LANES : (v + 1) * LANES]
                out[place(d), pl.ds(slot * fields, fields), :] = half[0:fields] + half[fields : 2 * fields]
                line = ids[pl.ds(d, 1), :]
                ids[pl.ds(d, 1), :] = jnp.where(lane_slot == slot, lane_row + blk[p + v], line)
        return carry

    lax.fori_loop(0, parts, part, 0)

    def send(k, start, stop):
        return pltpu.make_async_copy(out.at[:, start:stop, :], out_h.at[:, start:stop, :], out_sem.at[k])

    send(0, 0, per).start()

    def halo(k):
        d = 2 * k
        turned = jnp.concatenate(
            [padded_rows(out[place(d + u), 0:per], HALF) for u in range(2)], axis=0
        ).T
        first, last = turned[0:1], turned[LANES - 1 : LANES]
        first_swapped = pltpu.roll(turned[0:SUB], HALF, 1)[0:1]
        last_swapped = pltpu.roll(turned[LANES - SUB : LANES], HALF, 1)[SUB - 1 : SUB]
        for u in range(2):
            b = lax.rem(d + u, lon)
            east = jnp.where(b == lon - 1, d + u - (lon - 1), d + u + 1)
            west = jnp.where(b == 0, d + u + (lon - 1), d + u - 1)
            here, to_east, to_west = place(d + u), place(east), place(west)
            out[here, per : per + 1] = ids[pl.ds(d + u, 1), :].astype(f32)
            sides = jnp.where(lane < HALF, ids[pl.ds(east, 1), :], ids[pl.ds(west, 1), :])
            out[here, per + 1 : per + 2] = sides.astype(f32)
            column = first if u == 0 else first_swapped
            out[to_west, per + 2 : per + 3] = jnp.where(lane < HALF, column, out[to_west, per + 2 : per + 3])
            column = last_swapped if u == 0 else last
            out[to_east, per + 2 : per + 3] = jnp.where(lane < HALF, out[to_east, per + 2 : per + 3], column)

    def halos(k, carry):
        for u in range(4):
            halo(k * 4 + u)
        return carry

    lax.fori_loop(0, devices // 8, halos, 0)
    send(1, per, per + SUB).start()
    send(0, 0, per).wait()
    send(1, per, per + SUB).wait()


def regrid(cap, lat, lon, src, dev, blk, coupling, atm, mask, weights, depth, ocean, inverses):
    pairs, cells, width = weights.shape
    fields, levels, oy, ox = ocean.shape
    message = jax.ShapeDtypeStruct((fields, levels + SUB, ox), f32)
    batch = 32
    devices = lat * lon
    tall = fields * cap + SUB
    return pl.pallas_call(
        functools.partial(regrid_kernel, cap, lat, lon, oy, batch),
        in_specs=[HBM] * 10,
        out_specs=[HBM, VMEM, VMEM],
        out_shape=[pltpu.HBM((devices, tall, LANES), f32), message, message],
        scratch_shapes=[
            pltpu.VMEM((devices, tall, LANES), f32),
            pltpu.VMEM((atm.shape[1] * SUB, LANES), f32),
            pltpu.VMEM((devices, LANES), jnp.int32),
            pltpu.SMEM((devices,), jnp.int32),
            pltpu.SMEM(src.shape, jnp.int32),
            pltpu.SMEM(dev.shape, jnp.int32),
            pltpu.SMEM(blk.shape, jnp.int32),
            pltpu.SMEM(coupling.shape, f32),
            pltpu.VMEM(atm.shape, bf16),
            pltpu.VMEM(mask.shape, jnp.int32),
            pltpu.VMEM(weights.shape, bf16),
            pltpu.VMEM(depth.shape, jnp.int32),
            pltpu.VMEM((2, fields, levels, ox), f32),
            pltpu.VMEM((2, fields, levels, levels), f32),
            pltpu.SemaphoreType.DMA((6,)),
            pltpu.SemaphoreType.DMA((2 * fields + 1, 2)),
            pltpu.SemaphoreType.DMA((pairs // batch,)),
            pltpu.SemaphoreType.DMA((2,)),
        ],
        compiler_params=pltpu.CompilerParams(vmem_limit_bytes=20 << 20),
        cost_estimate=pl.CostEstimate(flops=2 * 8 * pairs * cells * width, bytes_accessed=10 << 20, transcendentals=0),
        name="regrid",
    )(*in_hbm(src, dev, blk, coupling, atm, mask, weights, depth, ocean, inverses))


def mix_kernel(
    depth_h, state_h, inv_h, mixed_h, side_h, to_east, to_west, depth_ref, state, mixed, inv, side, in_sems, out_sems
):
    fields, oy, levels, _ = mixed.shape
    depth_copy = pltpu.make_async_copy(depth_h, depth_ref, in_sems.at[2 * fields, 0])
    depth_copy.start()

    def load(q, c):
        for i in range(SUB):
            row = c * SUB + i
            pltpu.make_async_copy(state_h.at[q, :, row, :], state.at[q, row], in_sems.at[2 * q, c]).start()
        here = (q, pl.ds(c * SUB, SUB))
        pltpu.make_async_copy(inv_h.at[here], inv.at[here], in_sems.at[2 * q + 1, c]).start()

    for c in range(oy // SUB):
        load(0, c)
    depth_copy.wait()
    level = iota((levels, LANES), 0)
    lane = iota((levels, LANES), 1)
    line = iota((1, LANES), 1)
    edge_depth = jnp.zeros((SUB, LANES), f32)
    for i in range(oy):
        turned = pltpu.roll(jnp.broadcast_to(depth_ref[i : i + 1, :].astype(f32), (SUB, LANES)), 2 * i + 1, 1)
        edge_depth = jnp.where(line // 2 == i, turned, edge_depth)

    def field(q, carry):
        @pl.when(q + 1 < fields)
        def _():
            for c in range(oy // SUB):
                load(q + 1, c)

        cells = jnp.zeros((levels, LANES), f32)
        for c in range(oy // SUB):
            here = (q, pl.ds(c * SUB, SUB))
            pltpu.make_async_copy(mixed_h.at[here], state.at[here], in_sems.at[2 * q, c]).wait()
            pltpu.make_async_copy(inv_h.at[here], inv.at[here], in_sems.at[2 * q + 1, c]).wait()
            for row in range(c * SUB, (c + 1) * SUB):
                a = inv[q, row, 0]
                m = solve_row(a, state[q, row], level < depth_ref[row : row + 1, :])
                mixed[q, row] = m
                cells = jnp.where(lane // 2 == row, pltpu.roll(m, 2 * row + 1, 1), cells)
                cells = jnp.where(lane // 2 == HALF // 2 + row, a[:, 0:1], cells)
            pltpu.make_async_copy(mixed.at[here], mixed_h.at[here], out_sems.at[q]).start()
        side[q, 0:levels] = cells
        side[q, levels : levels + SUB] = edge_depth
        return carry

    lax.fori_loop(0, fields, field, 0)
    side_copy = pltpu.make_async_copy(side, side_h, out_sems.at[fields])
    side_copy.start()
    even = line % 2 == 0
    for k in range(fields // 2):
        to_east[k] = jnp.where(even, side[2 * k], pltpu.roll(side[2 * k + 1], 1, 1))
        to_west[k] = jnp.where(even, pltpu.roll(side[2 * k], LANES - 1, 1), side[2 * k + 1])
    for q in range(fields):
        pltpu.make_async_copy(mixed.at[q], mixed_h.at[q], out_sems.at[q]).wait()
    side_copy.wait()


def mix(depth, state, inverses):
    fields, levels, oy, ox = state.shape
    edge_shape = jax.ShapeDtypeStruct((fields // 2, levels + SUB, ox), f32)
    full = (fields, oy, levels, ox)
    return pl.pallas_call(
        mix_kernel,
        in_specs=[HBM] * 3,
        out_specs=[HBM] * 2 + [VMEM] * 2,
        out_shape=[pltpu.HBM(full, f32), pltpu.HBM((fields, levels + SUB, ox), f32), edge_shape, edge_shape],
        scratch_shapes=[
            pltpu.VMEM(depth.shape, jnp.int32),
            pltpu.VMEM(full, f32),
            pltpu.VMEM(full, f32),
            pltpu.VMEM(inverses.shape, f32),
            pltpu.VMEM((fields, levels + SUB, ox), f32),
            pltpu.SemaphoreType.DMA((2 * fields + 1, oy // SUB)),
            pltpu.SemaphoreType.DMA((fields + 1,)),
        ],
        compiler_params=pltpu.CompilerParams(vmem_limit_bytes=32 << 20),
        cost_estimate=pl.CostEstimate(flops=2 * 4 * fields * oy * levels * levels * ox, bytes_accessed=16 << 20, transcendentals=0),
        name="mix",
    )(*in_hbm(depth, state, inverses))


def collect_kernel(cap, fields, oy, recv, after_mix, after_north, after_south, out):
    lat = out.shape[0]
    lon = recv.shape[0] // lat
    per = fields * cap
    group = LANES // per
    forced = fields * oy
    square_row = iota((LANES, LANES), 0).astype(f32)
    line = iota((1, LANES), 1)
    row = iota((2 * oy, LANES), 0).astype(f32)
    lane_base = ((line % fields) * oy).astype(f32)
    lane_side = (line // HALF).astype(f32)
    small_row, small_lane = iota((SUB, LANES), 0), iota((SUB, LANES), 1)
    pick = jnp.where((small_lane % fields == small_row) & (small_lane % HALF < per), 1.0, 0.0).astype(bf16)
    nothing = jnp.zeros((fields, LANES), f32)
    for a in range(lat):
        total = jnp.zeros((LANES, 2 * LANES), f32)
        for tile in range(lon // group):
            places = [(tile * group + s) * lat + a for s in range(group)]
            ids = recv[places[0], per : per + 1, :]
            for s in range(1, group):
                ids = jnp.where(line // per == s, recv[places[s], per : per + 1, :], ids)
            hot = jnp.where(square_row == ids, 1.0, 0.0).astype(bf16)
            high, low = split(jnp.concatenate([recv[p, 0:per, :] for p in places], axis=0))
            total = total + matmul(hot, jnp.concatenate([high, low], axis=1))
        total = total[:, :LANES] + total[:, LANES:]
        out[a, 0:forced] = total
        if a == 0:
            out[a, forced : forced + fields] = nothing
        if a == lat - 1:
            out[a, forced + fields : forced + 2 * fields] = nothing
        for q in range(fields):
            if a + 1 < lat:
                out[a + 1, forced + q : forced + q + 1] = total[q * oy + oy - 1 : q * oy + oy]
            if a > 0:
                out[a - 1, forced + fields + q : forced + fields + q + 1] = total[q * oy : q * oy + 1]
        spread = jnp.zeros((2 * oy, LANES), f32)
        for b in range(lon):
            place = 2.0 * (recv[b * lat + a, per + 1 : per + 2, :] - lane_base) + lane_side
            spread = spread + jnp.where(place == row, recv[b * lat + a, per + 2 : per + 3, :], 0.0)
        high, low = split(padded_rows(spread, LANES).T)
        out[a, forced + SUB : forced + 2 * SUB] = matmul(pick, high) + matmul(pick, low)


def collect(cap, fields, oy, lat, received, after):
    return pl.pallas_call(
        functools.partial(collect_kernel, cap, fields, oy),
        in_specs=[VMEM] + [pl.BlockSpec(memory_space=pl.ANY)] * 3,
        out_specs=VMEM,
        out_shape=jax.ShapeDtypeStruct((lat, fields * oy + 2 * SUB, LANES), f32),
        compiler_params=pltpu.CompilerParams(vmem_limit_bytes=16 << 20),
        name="collect",
    )(received, *after)


def finish_kernel(
    recv, depth_ref, mixed_h, own_h, north_h, south_h, east, west,
    out_h, own, north, south, forcing, z, keep, halo, z_north, z_south, mixed, stage, edge_sems, in_sems, out_sems,
):
    fields, oy, levels, _ = mixed.shape
    level = iota((levels, LANES), 0)
    lanes = iota((levels, LANES), 1)
    square_row = iota((LANES, LANES), 0)
    square_lane = iota((LANES, LANES), 1)
    line = iota((1, LANES), 1)
    even = line % 2 == 0
    edges = [
        pltpu.make_async_copy(a, b, edge_sems.at[k])
        for k, (a, b) in enumerate(((own_h, own), (north_h, north), (south_h, south)))
    ]
    for copy in edges:
        copy.start()

    def load(q, c):
        here = (q, pl.ds(c * SUB, SUB))
        return pltpu.make_async_copy(mixed_h.at[here], mixed.at[here], in_sems.at[q, c])

    for c in range(oy // SUB):
        load(0, c).start()

    total = recv[0]
    for a in range(1, recv.shape[0]):
        total = total + recv[a]
    forced_rows = fields * oy
    forcing[...] = total[0:forced_rows]
    rows = total[forced_rows : forced_rows + SUB]
    columns = total[forced_rows + SUB :]

    for copy in edges:
        copy.wait()
    depth = depth_ref[...]
    wide = iota((oy, LANES), 1)

    def upright(ref):
        value = jnp.where(wide == 2 * iota((oy, LANES), 0), ref[0, levels : levels + 1, :], 0.0)
        return jnp.sum(value, axis=1, keepdims=True).astype(jnp.int32)

    to_east = jnp.where(wide == LANES - 1, upright(east), pltpu.roll(depth, LANES - 1, 1))
    to_west = jnp.where(wide == 0, upright(west), pltpu.roll(depth, 1, 1))
    to_north = jnp.concatenate([north[0, levels : levels + 1, :].astype(jnp.int32), depth[: oy - 1]], axis=0)
    to_south = jnp.concatenate([depth[1:], south[0, levels : levels + 1, :].astype(jnp.int32)], axis=0)
    for i in range(oy):
        sides = jnp.where(level < to_east[i : i + 1], diffusion_rate, 0.0)
        for other in (to_west, to_north, to_south):
            sides = sides + jnp.where(level < other[i : i + 1], diffusion_rate, 0.0)
        keep[i] = 1.0 - sides

    def outer(target, ref, start):
        names = padded_rows(
            jnp.concatenate([ref[q, levels + 1 : levels + 2, :] for q in range(fields)], axis=0), LANES
        ).T
        active = level < ref[0, levels : levels + 1, :].astype(jnp.int32)
        for q in range(fields):
            value = ref[q, 0:levels] + names[0:levels, q : q + 1] * rows[start + q : start + q + 1]
            target[q] = jnp.where(active, value, 0.0)

    outer(z_north, north, 0)
    outer(z_south, south, fields)
    for q in range(fields):
        if q % 2:
            cells = jnp.where(even, pltpu.roll(east[q // 2], LANES - 1, 1), west[q // 2])
        else:
            cells = jnp.where(even, east[q // 2], pltpu.roll(west[q // 2], 1, 1))
        names = pltpu.roll(cells, HALF, 1)
        active = level < cells[levels : levels + 1].astype(jnp.int32)
        value = cells[0:levels] + names[0:levels] * columns[q : q + 1]
        halo[q] = jnp.where(active & (line < 2 * oy), value, 0.0)

    both = jnp.where((square_row == square_lane + 1) | (square_row == square_lane - 1), 1.0, 0.0).astype(bf16)
    both = jnp.concatenate([both, both], axis=0)
    ones = jnp.ones((LANES, LANES), bf16)
    ends = (lanes == 0) | (lanes == LANES - 1)

    def field(q, carry):
        @pl.when(q + 1 < fields)
        def _():
            for c in range(oy // SUB):
                load(q + 1, c).start()

        z[0] = z_north[q]
        z[oy + 1] = z_south[q]
        edge = halo[q]
        names = own[q, 0:levels]
        high = names.astype(bf16).astype(f32)
        names = jnp.where(even, high, names - high)

        def solve(c):
            load(q, c).wait()
            rows_here = range(c * SUB, (c + 1) * SUB)
            first = matmul(
                jnp.concatenate(
                    [jnp.where(lanes // 2 == HALF // 2 + r, names, 0.0).astype(bf16) for r in rows_here], axis=0
                ),
                ones,
            )
            for i, r in enumerate(rows_here):
                first_here = first[i * levels : (i + 1) * levels]
                forced = mixed[q, r] + first_here * forcing[pl.ds(q * oy + r, 1), :]
                z[r + 1] = jnp.where(level < depth_ref[r : r + 1, :], forced, 0.0)

        def diffuse(c):
            start = c * SUB
            high, low = split(z[start + 1 : start + 1 + SUB].reshape(SUB * levels, LANES))
            sides = matmul(jnp.concatenate([high, low], axis=1), both)
            for i in range(SUB):
                r = start + i
                outside = jnp.where(ends, pltpu.roll(edge, LANES - 1 - 2 * r, 1), 0.0)
                around = (z[r] + z[r + 2]) + (sides[i * levels : (i + 1) * levels] + outside)
                active = level < depth_ref[r : r + 1, :]
                stage[q, r] = jnp.where(active, z[r + 1] * keep[r] + diffusion_rate * around, mixed[q, r])
            for r in range(start, start + SUB):
                pltpu.make_async_copy(stage.at[q, r], out_h.at[q, :, r, :], out_sems.at[q]).start()

        solve(0)
        for c in range(1, oy // SUB):
            solve(c)
            diffuse(c - 1)
        diffuse(oy // SUB - 1)
        return carry

    lax.fori_loop(0, fields, field, 0)
    for q in range(fields):
        pltpu.make_async_copy(stage.at[q], mixed_h.at[q], out_sems.at[q]).wait()


def finish(received, depth, mixed, own, halos):
    fields, oy, levels, ox = mixed.shape
    edge = pltpu.VMEM((fields, levels, ox), f32)
    message = pltpu.VMEM((fields, levels + SUB, ox), f32)
    full = pltpu.VMEM((fields, oy, levels, ox), f32)
    return pl.pallas_call(
        finish_kernel,
        in_specs=[VMEM] * 2 + [HBM] * 4 + [VMEM] * 2,
        out_specs=HBM,
        out_shape=pltpu.HBM((fields, levels, oy, ox), f32),
        scratch_shapes=[
            message,
            message,
            message,
            pltpu.VMEM((fields * oy, ox), f32),
            pltpu.VMEM((oy + 2, levels, ox), f32),
            pltpu.VMEM((oy, levels, ox), f32),
            edge,
            edge,
            edge,
            full,
            full,
            pltpu.SemaphoreType.DMA((3,)),
            pltpu.SemaphoreType.DMA((fields, oy // SUB)),
            pltpu.SemaphoreType.DMA((fields,)),
        ],
        compiler_params=pltpu.CompilerParams(vmem_limit_bytes=32 << 20),
        cost_estimate=pl.CostEstimate(flops=20 * fields * oy * levels * ox, bytes_accessed=12 << 20, transcendentals=0),
        name="finish",
    )(received, depth, *in_hbm(mixed, own, *halos[0:2]), *halos[2:])


def shift(x, axis, step, wrap):
    count = lax.axis_size(axis)
    pairs = [(i, (i + step) % count) for i in range(count) if wrap or 0 <= i + step < count]
    return lax.ppermute(x, axis, pairs)


def on_device(
    atm_flux, sea_mask, src_block, dest_dev, dest_block, intersection_weights, coupling, inverses, ocean_state,
    depth_levels,
):
    lat, lon = lax.axis_size("lat"), lax.axis_size("lon")
    fields, _, oy, _ = ocean_state.shape
    cap = max(SUB, 2 * src_block.shape[0] // (lat * lon))
    slots, north, south = regrid(
        cap, lat, lon, src_block, dest_dev[:, 0], dest_block, coupling, atm_flux, sea_mask,
        intersection_weights, depth_levels, ocean_state, inverses,
    )
    in_plane = lax.all_to_all(slots, "lon", 0, 0, tiled=True)
    mixed, side, to_east, to_west = mix(depth_levels, ocean_state, inverses)
    halos = (
        shift(south, "lat", 1, False),
        shift(north, "lat", -1, False),
        shift(to_west, "lon", -1, True),
        shift(to_east, "lon", 1, True),
    )
    received = lax.all_to_all(collect(cap, fields, oy, lat, in_plane, (to_east, *halos[0:2])), "lat", 0, 0, tiled=True)
    return finish(received, depth_levels, mixed, side, halos)


def solution(mesh):
    placed = (
        P(None, "lat", "lon"),
        P("lat", "lon"),
        P(("lat", "lon")),
        P(("lat", "lon"), None),
        P(("lat", "lon")),
        P(("lat", "lon"), None, None),
        P(),
        P(None, "lat", "lon", None, None),
        P(None, None, "lat", "lon"),
        P("lat", "lon"),
    )
    return jax.shard_map(
        on_device,
        mesh=mesh,
        in_specs=placed,
        out_specs=P(None, None, "lat", "lon"),
        check_vma=False,
    )
```

```python
import functools

import jax
import jax.numpy as jnp
from jax import lax
from jax.experimental import pallas as pl
from jax.experimental.pallas import tpu as pltpu
from jax.sharding import PartitionSpec as P

diffusion_rate = 0.2
LANES = 128
HALF = 64
SUB = 8
f32 = jnp.float32
bf16 = jnp.bfloat16
HBM = pl.BlockSpec(memory_space=pltpu.HBM)
VMEM = pl.BlockSpec(memory_space=pltpu.VMEM)


def split(x):
    high = x.astype(bf16)
    return high, (x - high.astype(f32)).astype(bf16)


def in_hbm(*arrays):
    return [pltpu.with_memory_space_constraint(x, pltpu.HBM) for x in arrays]


def iota(shape, dim):
    return lax.broadcasted_iota(jnp.int32, shape, dim)


def matmul(a, b):
    return jnp.dot(a, b, preferred_element_type=f32)


def padded_rows(x, rows):
    return x if x.shape[0] == rows else jnp.concatenate([x, jnp.zeros((rows - x.shape[0], LANES), x.dtype)], axis=0)


def solve_row(a, x, active):
    levels = x.shape[0]
    a_high, a_low = split(a)
    r_high, r_low = split(jnp.where(active, x, 0.0))
    product = matmul(jnp.concatenate([a_high, a_low], axis=0), jnp.concatenate([r_high, r_low], axis=1))
    solved = product[:levels, :LANES] + (product[levels:, :LANES] + product[:levels, LANES:])
    return jnp.where(active, solved, x)


def outer_messages(refs, depth_ref, state, inv):
    _, fields, levels, _ = state.shape
    oy = depth_ref.shape[0]
    level = iota((levels, LANES), 0)
    for k, (row, ref) in enumerate(zip((0, oy - 1), refs)):
        depth = depth_ref[row : row + 1, :]
        names = jnp.zeros((levels, LANES), f32)
        for q in range(fields):
            a = inv[k, q]
            ref[q, 0:levels] = solve_row(a, state[k, q], level < depth)
            names = jnp.where(iota((levels, LANES), 1) == q, a[:, 0:1], names)
        names = padded_rows(names, LANES).T
        for q in range(fields):
            ref[q, levels : levels + SUB] = jnp.concatenate(
                [depth.astype(f32), names[q : q + 1], jnp.zeros((SUB - 2, LANES), f32)], axis=0
            )


def extra_rows(lat):
    return -(-3 * lat // SUB) * SUB


def regrid_kernel(
    cap, lat, lon, oy, batch,
    src_h, dev_h, blk_h, coupling_h, atm_h, mask_h, weights_h, depth_h, state_h, inv_h,
    out_h, north, south,
    out, rows, ids, count, src, dev, blk, coupling, atm, mask, weights, depth_ref, state, inv,
    small_sem, outer_sem, big_sem, out_sem,
):
    fluxes, atm_rows, _ = atm.shape
    fields = coupling.shape[0]
    devices = lat * lon
    per = fields * cap
    slot_rows = lat * per
    parts = weights.shape[0] // batch
    ahead = min(2, parts)

    def big(k):
        here = pl.ds(pl.multiple_of(k * batch, batch), batch)
        return pltpu.make_async_copy(weights_h.at[here], weights.at[here], big_sem.at[k])

    small = [
        pltpu.make_async_copy(a, b, small_sem.at[k])
        for k, (a, b) in enumerate(
            (
                (coupling_h, coupling), (atm_h, atm), (mask_h, mask),
                (src_h, src), (dev_h, dev), (blk_h, blk),
            )
        )
    ]
    outer = [pltpu.make_async_copy(depth_h, depth_ref, outer_sem.at[2 * fields, 0])]
    for q in range(fields):
        for k, row in enumerate((0, oy - 1)):
            outer.append(pltpu.make_async_copy(state_h.at[q, :, row, :], state.at[k, q], outer_sem.at[2 * q, k]))
            outer.append(pltpu.make_async_copy(inv_h.at[q, row, 0], inv.at[k, q], outer_sem.at[2 * q + 1, k]))
    for copy in small + outer:
        copy.start()
    for k in range(ahead):
        big(k).start()

    def clear_count(d, carry):
        count[d] = 0
        return carry

    def clear(b, carry):
        out[b] = jnp.zeros(out.shape[1:], f32)
        return carry

    lax.fori_loop(0, devices, clear_count, 0)
    lax.fori_loop(0, lon, clear, 0)
    ids[...] = jnp.full(ids.shape, -1, jnp.int32)
    for copy in small:
        copy.wait()
    for tile in range(atm_rows // 16):
        here = slice(tile * 16, tile * 16 + 16)
        sea = mask[here, :].astype(f32)
        flux = [atm[f, here, :].astype(f32) * sea for f in range(fluxes)]
        for q in range(fields):
            total = coupling[q, 0] * flux[0]
            for f in range(1, fluxes):
                total = total + coupling[q, f] * flux[f]
            high = total.astype(bf16).astype(f32)
            rows[pl.ds(tile * 16 * SUB + q, 16, stride=SUB), :] = high
            rows[pl.ds(tile * 16 * SUB + fields + q, 16, stride=SUB), :] = total - high

    for copy in outer:
        copy.wait()
    outer_messages((north, south), depth_ref, state, inv)

    lane = iota((1, LANES), 1)
    lane_slot = (lane % per) // fields
    lane_row = (lane % fields) * oy

    bits = lon.bit_length() - 1

    def place(d):
        if lon == 1 << bits:
            return lax.shift_right_logical(d, bits), d & (lon - 1)
        return lax.div(d, lon), lax.rem(d, lon)

    def extra(d, k):
        a, b = place(d)
        return b, pl.ds(slot_rows + 3 * a + k, 1)

    def slots(d):
        a, b = place(d)
        return padded_rows(out[b, pl.ds(pl.multiple_of(a * per, per), per), :], HALF)

    def part(k, carry):
        big(k).wait()

        @pl.when(k + ahead < parts)
        def _():
            big(k + ahead).start()

        for u in range(0, batch, 2):
            p = k * batch + u
            x = jnp.concatenate(
                [rows[pl.ds(pl.multiple_of(src[p + v] * SUB, SUB), SUB), :] for v in range(2)], axis=0
            ).astype(bf16)
            both = matmul(x, jnp.concatenate([weights[p], weights[p + 1]], axis=1))
            for v in range(2):
                d = dev[p + v]
                slot = jnp.minimum(count[d], cap - 1)
                count[d] = slot + 1
                half = both[v * SUB : v * SUB + SUB, v * LANES : (v + 1) * LANES]
                a, b = place(d)
                out[b, pl.ds(a * per + slot * fields, fields), :] = half[0:fields] + half[fields : 2 * fields]
                line = ids[pl.ds(d, 1), :]
                ids[pl.ds(d, 1), :] = jnp.where(lane_slot == slot, lane_row + blk[p + v], line)
        return carry

    lax.fori_loop(0, parts, part, 0)

    def send(k, start, stop):
        return pltpu.make_async_copy(out.at[:, start:stop, :], out_h.at[:, start:stop, :], out_sem.at[k])

    send(0, 0, slot_rows).start()

    def halo(k):
        d = 2 * k
        turned = jnp.concatenate([slots(d + u) for u in range(2)], axis=0).T
        first, last = turned[0:1], turned[LANES - 1 : LANES]
        first_swapped = pltpu.roll(turned[0:SUB], HALF, 1)[0:1]
        last_swapped = pltpu.roll(turned[LANES - SUB : LANES], HALF, 1)[SUB - 1 : SUB]
        for u in range(2):
            _, b = place(d + u)
            east = jnp.where(b == lon - 1, d + u - (lon - 1), d + u + 1)
            west = jnp.where(b == 0, d + u + (lon - 1), d + u - 1)
            out[extra(d + u, 0)] = ids[pl.ds(d + u, 1), :].astype(f32)
            sides = jnp.where(lane < HALF, ids[pl.ds(east, 1), :], ids[pl.ds(west, 1), :])
            out[extra(d + u, 1)] = sides.astype(f32)
            column = first if u == 0 else first_swapped
            out[extra(west, 2)] = jnp.where(lane < HALF, column, out[extra(west, 2)])
            column = last_swapped if u == 0 else last
            out[extra(east, 2)] = jnp.where(lane < HALF, out[extra(east, 2)], column)

    def halos(k, carry):
        for u in range(4):
            halo(k * 4 + u)
        return carry

    lax.fori_loop(0, devices // 8, halos, 0)
    send(1, slot_rows, out.shape[1]).start()
    send(0, 0, slot_rows).wait()
    send(1, slot_rows, out.shape[1]).wait()


def regrid(cap, lat, lon, src, dev, blk, coupling, atm, mask, weights, depth, ocean, inverses):
    pairs, cells, width = weights.shape
    fields, levels, oy, ox = ocean.shape
    message = jax.ShapeDtypeStruct((fields, levels + SUB, ox), f32)
    batch = 64
    devices = lat * lon
    tall = lat * fields * cap + extra_rows(lat)
    return pl.pallas_call(
        functools.partial(regrid_kernel, cap, lat, lon, oy, batch),
        in_specs=[HBM] * 10,
        out_specs=[HBM, VMEM, VMEM],
        out_shape=[pltpu.HBM((lon, tall, LANES), f32), message, message],
        scratch_shapes=[
            pltpu.VMEM((lon, tall, LANES), f32),
            pltpu.VMEM((atm.shape[1] * SUB, LANES), f32),
            pltpu.VMEM((devices, LANES), jnp.int32),
            pltpu.SMEM((devices,), jnp.int32),
            pltpu.SMEM(src.shape, jnp.int32),
            pltpu.SMEM(dev.shape, jnp.int32),
            pltpu.SMEM(blk.shape, jnp.int32),
            pltpu.SMEM(coupling.shape, f32),
            pltpu.VMEM(atm.shape, bf16),
            pltpu.VMEM(mask.shape, jnp.int32),
            pltpu.VMEM(weights.shape, bf16),
            pltpu.VMEM(depth.shape, jnp.int32),
            pltpu.VMEM((2, fields, levels, ox), f32),
            pltpu.VMEM((2, fields, levels, levels), f32),
            pltpu.SemaphoreType.DMA((6,)),
            pltpu.SemaphoreType.DMA((2 * fields + 1, 2)),
            pltpu.SemaphoreType.DMA((pairs // batch,)),
            pltpu.SemaphoreType.DMA((2,)),
        ],
        compiler_params=pltpu.CompilerParams(vmem_limit_bytes=20 << 20),
        cost_estimate=pl.CostEstimate(flops=2 * 8 * pairs * cells * width, bytes_accessed=10 << 20, transcendentals=0),
        name="regrid",
    )(*in_hbm(src, dev, blk, coupling, atm, mask, weights, depth, ocean, inverses))


def mix_kernel(
    depth_h, state_h, inv_h, mixed_h, side_h, to_east, to_west, depth_ref, state, mixed, inv, side, in_sems, out_sems
):
    fields, oy, levels, _ = mixed.shape
    depth_copy = pltpu.make_async_copy(depth_h, depth_ref, in_sems.at[2 * fields, 0])
    depth_copy.start()

    def load(q, c):
        for i in range(SUB):
            row = c * SUB + i
            pltpu.make_async_copy(state_h.at[q, :, row, :], state.at[q, row], in_sems.at[2 * q, c]).start()
        here = (q, pl.ds(c * SUB, SUB))
        pltpu.make_async_copy(inv_h.at[here], inv.at[here], in_sems.at[2 * q + 1, c]).start()

    for c in range(oy // SUB):
        load(0, c)
    depth_copy.wait()
    level = iota((levels, LANES), 0)
    lane = iota((levels, LANES), 1)
    line = iota((1, LANES), 1)
    edge_depth = jnp.zeros((SUB, LANES), f32)
    for i in range(oy):
        turned = pltpu.roll(jnp.broadcast_to(depth_ref[i : i + 1, :].astype(f32), (SUB, LANES)), 2 * i + 1, 1)
        edge_depth = jnp.where(line // 2 == i, turned, edge_depth)

    def field(q, carry):
        @pl.when(q + 1 < fields)
        def _():
            for c in range(oy // SUB):
                load(q + 1, c)

        cells = jnp.zeros((levels, LANES), f32)
        for c in range(oy // SUB):
            here = (q, pl.ds(c * SUB, SUB))
            pltpu.make_async_copy(mixed_h.at[here], state.at[here], in_sems.at[2 * q, c]).wait()
            pltpu.make_async_copy(inv_h.at[here], inv.at[here], in_sems.at[2 * q + 1, c]).wait()
            for row in range(c * SUB, (c + 1) * SUB):
                a = inv[q, row, 0]
                m = solve_row(a, state[q, row], level < depth_ref[row : row + 1, :])
                mixed[q, row] = m
                cells = jnp.where(lane // 2 == row, pltpu.roll(m, 2 * row + 1, 1), cells)
                cells = jnp.where(lane // 2 == HALF // 2 + row, a[:, 0:1], cells)
            pltpu.make_async_copy(mixed.at[here], mixed_h.at[here], out_sems.at[q]).start()
        side[q, 0:levels] = cells
        side[q, levels : levels + SUB] = edge_depth
        return carry

    lax.fori_loop(0, fields, field, 0)
    side_copy = pltpu.make_async_copy(side, side_h, out_sems.at[fields])
    side_copy.start()
    even = line % 2 == 0
    for k in range(fields // 2):
        to_east[k] = jnp.where(even, side[2 * k], pltpu.roll(side[2 * k + 1], 1, 1))
        to_west[k] = jnp.where(even, pltpu.roll(side[2 * k], LANES - 1, 1), side[2 * k + 1])
    for q in range(fields):
        pltpu.make_async_copy(mixed.at[q], mixed_h.at[q], out_sems.at[q]).wait()
    side_copy.wait()


def mix(depth, state, inverses):
    fields, levels, oy, ox = state.shape
    edge_shape = jax.ShapeDtypeStruct((fields // 2, levels + SUB, ox), f32)
    full = (fields, oy, levels, ox)
    return pl.pallas_call(
        mix_kernel,
        in_specs=[HBM] * 3,
        out_specs=[HBM] * 2 + [VMEM] * 2,
        out_shape=[pltpu.HBM(full, f32), pltpu.HBM((fields, levels + SUB, ox), f32), edge_shape, edge_shape],
        scratch_shapes=[
            pltpu.VMEM(depth.shape, jnp.int32),
            pltpu.VMEM(full, f32),
            pltpu.VMEM(full, f32),
            pltpu.VMEM(inverses.shape, f32),
            pltpu.VMEM((fields, levels + SUB, ox), f32),
            pltpu.SemaphoreType.DMA((2 * fields + 1, oy // SUB)),
            pltpu.SemaphoreType.DMA((fields + 1,)),
        ],
        compiler_params=pltpu.CompilerParams(vmem_limit_bytes=32 << 20),
        cost_estimate=pl.CostEstimate(flops=2 * 4 * fields * oy * levels * levels * ox, bytes_accessed=16 << 20, transcendentals=0),
        name="mix",
    )(*in_hbm(depth, state, inverses))


def collect_kernel(cap, fields, oy, recv, after_mix, after_north, after_south, out):
    lat = out.shape[0]
    lon = recv.shape[0]
    per = fields * cap
    slot_rows = lat * per
    group = LANES // per
    forced = fields * oy
    square_row = iota((LANES, LANES), 0).astype(f32)
    line = iota((1, LANES), 1)
    row = iota((2 * oy, LANES), 0).astype(f32)
    lane_base = ((line % fields) * oy).astype(f32)
    lane_side = (line // HALF).astype(f32)
    small_row, small_lane = iota((SUB, LANES), 0), iota((SUB, LANES), 1)
    pick = jnp.where((small_lane % fields == small_row) & (small_lane % HALF < per), 1.0, 0.0).astype(bf16)
    nothing = jnp.zeros((fields, LANES), f32)
    for a in range(lat):
        total = jnp.zeros((LANES, 2 * LANES), f32)
        for tile in range(lon // group):
            places = [tile * group + s for s in range(group)]
            named = slice(slot_rows + 3 * a, slot_rows + 3 * a + 1)
            ids = recv[places[0], named, :]
            for s in range(1, group):
                ids = jnp.where(line // per == s, recv[places[s], named, :], ids)
            hot = jnp.where(square_row == ids, 1.0, 0.0).astype(bf16)
            high, low = split(jnp.concatenate([recv[p, a * per : (a + 1) * per, :] for p in places], axis=0))
            total = total + matmul(hot, jnp.concatenate([high, low], axis=1))
        total = total[:, :LANES] + total[:, LANES:]
        out[a, 0:forced] = total
        if a == 0:
            out[a, forced : forced + fields] = nothing
        if a == lat - 1:
            out[a, forced + fields : forced + 2 * fields] = nothing
        for q in range(fields):
            if a + 1 < lat:
                out[a + 1, forced + q : forced + q + 1] = total[q * oy + oy - 1 : q * oy + oy]
            if a > 0:
                out[a - 1, forced + fields + q : forced + fields + q + 1] = total[q * oy : q * oy + 1]
        spread = jnp.zeros((2 * oy, LANES), f32)
        for b in range(lon):
            extra = recv[b, slot_rows + 3 * a + 1 : slot_rows + 3 * a + 3, :]
            place = 2.0 * (extra[0:1] - lane_base) + lane_side
            spread = spread + jnp.where(place == row, extra[1:2], 0.0)
        high, low = split(padded_rows(spread, LANES).T)
        out[a, forced + SUB : forced + 2 * SUB] = matmul(pick, high) + matmul(pick, low)


def collect(cap, fields, oy, lat, received, after):
    return pl.pallas_call(
        functools.partial(collect_kernel, cap, fields, oy),
        in_specs=[VMEM] + [pl.BlockSpec(memory_space=pl.ANY)] * 3,
        out_specs=VMEM,
        out_shape=jax.ShapeDtypeStruct((lat, fields * oy + 2 * SUB, LANES), f32),
        compiler_params=pltpu.CompilerParams(vmem_limit_bytes=16 << 20),
        name="collect",
    )(received, *after)


def finish_kernel(
    recv, depth_ref, mixed_h, own_h, north_h, south_h, east, west,
    out_h, own, north, south, forcing, z, keep, halo, z_north, z_south, mixed, stage, edge_sems, in_sems, out_sems,
):
    fields, oy, levels, _ = mixed.shape
    level = iota((levels, LANES), 0)
    lanes = iota((levels, LANES), 1)
    square_row = iota((LANES, LANES), 0)
    square_lane = iota((LANES, LANES), 1)
    line = iota((1, LANES), 1)
    even = line % 2 == 0
    edges = [
        pltpu.make_async_copy(a, b, edge_sems.at[k])
        for k, (a, b) in enumerate(((own_h, own), (north_h, north), (south_h, south)))
    ]
    for copy in edges:
        copy.start()

    def load(q, c):
        here = (q, pl.ds(c * SUB, SUB))
        return pltpu.make_async_copy(mixed_h.at[here], mixed.at[here], in_sems.at[q, c])

    for c in range(oy // SUB):
        load(0, c).start()

    total = recv[0]
    for a in range(1, recv.shape[0]):
        total = total + recv[a]
    forced_rows = fields * oy
    forcing[...] = total[0:forced_rows]
    rows = total[forced_rows : forced_rows + SUB]
    columns = total[forced_rows + SUB :]

    for copy in edges:
        copy.wait()
    depth = depth_ref[...]
    wide = iota((oy, LANES), 1)

    def upright(ref):
        value = jnp.where(wide == 2 * iota((oy, LANES), 0), ref[0, levels : levels + 1, :], 0.0)
        return jnp.sum(value, axis=1, keepdims=True).astype(jnp.int32)

    to_east = jnp.where(wide == LANES - 1, upright(east), pltpu.roll(depth, LANES - 1, 1))
    to_west = jnp.where(wide == 0, upright(west), pltpu.roll(depth, 1, 1))
    to_north = jnp.concatenate([north[0, levels : levels + 1, :].astype(jnp.int32), depth[: oy - 1]], axis=0)
    to_south = jnp.concatenate([depth[1:], south[0, levels : levels + 1, :].astype(jnp.int32)], axis=0)
    for i in range(oy):
        sides = jnp.where(level < to_east[i : i + 1], diffusion_rate, 0.0)
        for other in (to_west, to_north, to_south):
            sides = sides + jnp.where(level < other[i : i + 1], diffusion_rate, 0.0)
        keep[i] = 1.0 - sides

    def outer(target, ref, start):
        names = padded_rows(
            jnp.concatenate([ref[q, levels + 1 : levels + 2, :] for q in range(fields)], axis=0), LANES
        ).T
        active = level < ref[0, levels : levels + 1, :].astype(jnp.int32)
        for q in range(fields):
            value = ref[q, 0:levels] + names[0:levels, q : q + 1] * rows[start + q : start + q + 1]
            target[q] = jnp.where(active, value, 0.0)

    outer(z_north, north, 0)
    outer(z_south, south, fields)
    for q in range(fields):
        if q % 2:
            cells = jnp.where(even, pltpu.roll(east[q // 2], LANES - 1, 1), west[q // 2])
        else:
            cells = jnp.where(even, east[q // 2], pltpu.roll(west[q // 2], 1, 1))
        names = pltpu.roll(cells, HALF, 1)
        active = level < cells[levels : levels + 1].astype(jnp.int32)
        value = cells[0:levels] + names[0:levels] * columns[q : q + 1]
        halo[q] = jnp.where(active & (line < 2 * oy), value, 0.0)

    both = jnp.where((square_row == square_lane + 1) | (square_row == square_lane - 1), 1.0, 0.0).astype(bf16)
    both = jnp.concatenate([both, both], axis=0)
    nothing = jnp.zeros((LANES, LANES), f32)
    ends = (square_lane == jnp.where(square_row % 2 == 0, LANES - 1, 0)).astype(f32)
    spread = jnp.concatenate(
        [jnp.concatenate([nothing + 1.0, nothing], axis=1), jnp.concatenate([nothing, ends], axis=1)], axis=0
    ).astype(bf16)

    def field(q, carry):
        @pl.when(q + 1 < fields)
        def _():
            for c in range(oy // SUB):
                load(q + 1, c).start()

        z[0] = z_north[q]
        z[oy + 1] = z_south[q]
        edge = halo[q]
        high = edge.astype(bf16).astype(f32)
        edge = jnp.where(lanes < HALF, high, pltpu.roll(edge - high, HALF, 1))
        names = own[q, 0:levels]
        high = names.astype(bf16).astype(f32)
        names = jnp.where(even, high, names - high)

        def solve(c):
            load(q, c).wait()
            rows_here = range(c * SUB, (c + 1) * SUB)
            places = jnp.concatenate(
                [
                    jnp.concatenate(
                        [
                            jnp.where(lanes // 2 == HALF // 2 + r, names, 0.0).astype(bf16),
                            jnp.where((lanes % HALF) // 2 == r, edge, 0.0).astype(bf16),
                        ],
                        axis=1,
                    )
                    for r in rows_here
                ],
                axis=0,
            )
            placed = matmul(places, spread)
            first = placed[:, :LANES]
            for i, r in enumerate(rows_here):
                first_here = first[i * levels : (i + 1) * levels]
                forced = mixed[q, r] + first_here * forcing[pl.ds(q * oy + r, 1), :]
                z[r + 1] = jnp.where(level < depth_ref[r : r + 1, :], forced, 0.0)
            return placed[:, LANES:]

        def diffuse(c, outside):
            start = c * SUB
            high, low = split(z[start + 1 : start + 1 + SUB].reshape(SUB * levels, LANES))
            sides = matmul(jnp.concatenate([high, low], axis=1), both)
            for i in range(SUB):
                r = start + i
                here = slice(i * levels, (i + 1) * levels)
                around = (z[r] + z[r + 2]) + (sides[here] + outside[here])
                active = level < depth_ref[r : r + 1, :]
                stage[q, r] = jnp.where(active, z[r + 1] * keep[r] + diffusion_rate * around, mixed[q, r])
            for r in range(start, start + SUB):
                pltpu.make_async_copy(stage.at[q, r], out_h.at[q, :, r, :], out_sems.at[q]).start()

        outside = solve(0)
        for c in range(1, oy // SUB):
            following = solve(c)
            diffuse(c - 1, outside)
            outside = following
        diffuse(oy // SUB - 1, outside)
        return carry

    lax.fori_loop(0, fields, field, 0)
    for q in range(fields):
        pltpu.make_async_copy(stage.at[q], mixed_h.at[q], out_sems.at[q]).wait()


def finish(received, depth, mixed, own, halos):
    fields, oy, levels, ox = mixed.shape
    edge = pltpu.VMEM((fields, levels, ox), f32)
    message = pltpu.VMEM((fields, levels + SUB, ox), f32)
    full = pltpu.VMEM((fields, oy, levels, ox), f32)
    return pl.pallas_call(
        finish_kernel,
        in_specs=[VMEM] * 2 + [HBM] * 4 + [VMEM] * 2,
        out_specs=HBM,
        out_shape=pltpu.HBM((fields, levels, oy, ox), f32),
        scratch_shapes=[
            message,
            message,
            message,
            pltpu.VMEM((fields * oy, ox), f32),
            pltpu.VMEM((oy + 2, levels, ox), f32),
            pltpu.VMEM((oy, levels, ox), f32),
            edge,
            edge,
            edge,
            full,
            full,
            pltpu.SemaphoreType.DMA((3,)),
            pltpu.SemaphoreType.DMA((fields, oy // SUB)),
            pltpu.SemaphoreType.DMA((fields,)),
        ],
        compiler_params=pltpu.CompilerParams(vmem_limit_bytes=32 << 20),
        cost_estimate=pl.CostEstimate(flops=20 * fields * oy * levels * ox, bytes_accessed=12 << 20, transcendentals=0),
        name="finish",
    )(received, depth, *in_hbm(mixed, own, *halos[0:2]), *halos[2:])


def shift(x, axis, step, wrap):
    count = lax.axis_size(axis)
    pairs = [(i, (i + step) % count) for i in range(count) if wrap or 0 <= i + step < count]
    return lax.ppermute(x, axis, pairs)


def on_device(
    atm_flux, sea_mask, src_block, dest_dev, dest_block, intersection_weights, coupling, inverses, ocean_state,
    depth_levels,
):
    lat, lon = lax.axis_size("lat"), lax.axis_size("lon")
    fields, _, oy, _ = ocean_state.shape
    cap = max(SUB, 2 * src_block.shape[0] // (lat * lon))
    slots, north, south = regrid(
        cap, lat, lon, src_block, dest_dev[:, 0], dest_block, coupling, atm_flux, sea_mask,
        intersection_weights, depth_levels, ocean_state, inverses,
    )
    in_plane = lax.all_to_all(slots, "lon", 0, 0, tiled=True)
    mixed, side, to_east, to_west = mix(depth_levels, ocean_state, inverses)
    halos = (
        shift(south, "lat", 1, False),
        shift(north, "lat", -1, False),
        shift(to_west, "lon", -1, True),
        shift(to_east, "lon", 1, True),
    )
    received = lax.all_to_all(collect(cap, fields, oy, lat, in_plane, (to_east, *halos[0:2])), "lat", 0, 0, tiled=True)
    return finish(received, depth_levels, mixed, side, halos)


def solution(mesh):
    placed = (
        P(None, "lat", "lon"),
        P("lat", "lon"),
        P(("lat", "lon")),
        P(("lat", "lon"), None),
        P(("lat", "lon")),
        P(("lat", "lon"), None, None),
        P(),
        P(None, "lat", "lon", None, None),
        P(None, None, "lat", "lon"),
        P("lat", "lon"),
    )
    return jax.shard_map(
        on_device,
        mesh=mesh,
        in_specs=placed,
        out_specs=P(None, None, "lat", "lon"),
        check_vma=False,
    )
```

```python
import functools

import jax
import jax.numpy as jnp
from jax import lax
from jax.experimental import pallas as pl
from jax.experimental.pallas import tpu as pltpu
from jax.sharding import PartitionSpec as P

diffusion_rate = 0.2
LANES = 128
HALF = 64
SUB = 8
f32 = jnp.float32
bf16 = jnp.bfloat16
HBM = pl.BlockSpec(memory_space=pltpu.HBM)
VMEM = pl.BlockSpec(memory_space=pltpu.VMEM)


def split(x):
    high = x.astype(bf16)
    return high, (x - high.astype(f32)).astype(bf16)


def in_hbm(*arrays):
    return [pltpu.with_memory_space_constraint(x, pltpu.HBM) for x in arrays]


def iota(shape, dim):
    return lax.broadcasted_iota(jnp.int32, shape, dim)


def matmul(a, b):
    return jnp.dot(a, b, preferred_element_type=f32)


def padded_rows(x, rows):
    return x if x.shape[0] == rows else jnp.concatenate([x, jnp.zeros((rows - x.shape[0], LANES), x.dtype)], axis=0)


def solve_row(a, x, active):
    levels = x.shape[0]
    a_high, a_low = split(a)
    r_high, r_low = split(jnp.where(active, x, 0.0))
    product = matmul(jnp.concatenate([a_high, a_low], axis=0), jnp.concatenate([r_high, r_low], axis=1))
    solved = product[:levels, :LANES] + (product[levels:, :LANES] + product[:levels, LANES:])
    return jnp.where(active, solved, x)


def outer_messages(refs, depth_ref, state, inv):
    _, fields, levels, _ = state.shape
    oy = depth_ref.shape[0]
    level = iota((levels, LANES), 0)
    for k, (row, ref) in enumerate(zip((0, oy - 1), refs)):
        depth = depth_ref[row : row + 1, :]
        names = jnp.zeros((levels, LANES), f32)
        for q in range(fields):
            a = inv[k, q]
            ref[q, 0:levels] = solve_row(a, state[k, q], level < depth)
            names = jnp.where(iota((levels, LANES), 1) == q, a[:, 0:1], names)
        names = padded_rows(names, LANES).T
        for q in range(fields):
            ref[q, levels : levels + SUB] = jnp.concatenate(
                [depth.astype(f32), names[q : q + 1], jnp.zeros((SUB - 2, LANES), f32)], axis=0
            )


def extra_rows(lat):
    return -(-3 * lat // SUB) * SUB


def regrid_kernel(
    cap, lat, lon, oy, batch,
    src_h, dev_h, blk_h, coupling_h, atm_h, mask_h, weights_h, depth_h, state_h, inv_h,
    out_h, north, south,
    out, rows, ids, count, src, dev, blk, coupling, atm, mask, weights, depth_ref, state, inv,
    small_sem, outer_sem, big_sem, out_sem,
):
    fluxes, atm_rows, _ = atm.shape
    fields = coupling.shape[0]
    devices = lat * lon
    per = fields * cap
    slot_rows = lat * per
    parts = weights.shape[0] // batch
    ahead = min(2, parts)

    def big(k):
        here = pl.ds(pl.multiple_of(k * batch, batch), batch)
        return pltpu.make_async_copy(weights_h.at[here], weights.at[here], big_sem.at[k])

    small = [
        pltpu.make_async_copy(a, b, small_sem.at[k])
        for k, (a, b) in enumerate(
            (
                (coupling_h, coupling), (atm_h, atm), (mask_h, mask),
                (src_h, src), (dev_h, dev), (blk_h, blk),
            )
        )
    ]
    outer = [pltpu.make_async_copy(depth_h, depth_ref, outer_sem.at[2 * fields, 0])]
    for q in range(fields):
        for k, row in enumerate((0, oy - 1)):
            outer.append(pltpu.make_async_copy(state_h.at[q, :, row, :], state.at[k, q], outer_sem.at[2 * q, k]))
            outer.append(pltpu.make_async_copy(inv_h.at[q, row, 0], inv.at[k, q], outer_sem.at[2 * q + 1, k]))
    for copy in small + outer:
        copy.start()
    for k in range(ahead):
        big(k).start()

    def clear_count(d, carry):
        count[d] = 0
        return carry

    def clear(b, carry):
        out[b] = jnp.zeros(out.shape[1:], f32)
        return carry

    lax.fori_loop(0, devices, clear_count, 0)
    lax.fori_loop(0, lon, clear, 0)
    ids[...] = jnp.full(ids.shape, -1, jnp.int32)
    for copy in small:
        copy.wait()
    for tile in range(atm_rows // 16):
        here = slice(tile * 16, tile * 16 + 16)
        sea = mask[here, :].astype(f32)
        flux = [atm[f, here, :].astype(f32) * sea for f in range(fluxes)]
        for q in range(fields):
            total = coupling[q, 0] * flux[0]
            for f in range(1, fluxes):
                total = total + coupling[q, f] * flux[f]
            high = total.astype(bf16).astype(f32)
            rows[pl.ds(tile * 16 * SUB + q, 16, stride=SUB), :] = high
            rows[pl.ds(tile * 16 * SUB + fields + q, 16, stride=SUB), :] = total - high

    for copy in outer:
        copy.wait()
    outer_messages((north, south), depth_ref, state, inv)

    lane = iota((1, LANES), 1)
    lane_slot = (lane % per) // fields
    lane_row = (lane % fields) * oy

    bits = lon.bit_length() - 1

    def place(d):
        if lon == 1 << bits:
            return lax.shift_right_logical(d, bits), d & (lon - 1)
        return lax.div(d, lon), lax.rem(d, lon)

    def extra(d, k):
        a, b = place(d)
        return b, pl.ds(slot_rows + 3 * a + k, 1)

    def slots(d):
        a, b = place(d)
        return padded_rows(out[b, pl.ds(pl.multiple_of(a * per, per), per), :], HALF)

    def part(k, carry):
        big(k).wait()

        @pl.when(k + ahead < parts)
        def _():
            big(k + ahead).start()

        for u in range(0, batch, 2):
            p = k * batch + u
            x = jnp.concatenate(
                [rows[pl.ds(pl.multiple_of(src[p + v] * SUB, SUB), SUB), :] for v in range(2)], axis=0
            ).astype(bf16)
            both = matmul(x, jnp.concatenate([weights[p], weights[p + 1]], axis=1))
            for v in range(2):
                d = dev[p + v]
                slot = jnp.minimum(count[d], cap - 1)
                count[d] = slot + 1
                half = both[v * SUB : v * SUB + SUB, v * LANES : (v + 1) * LANES]
                a, b = place(d)
                out[b, pl.ds(a * per + slot * fields, fields), :] = half[0:fields] + half[fields : 2 * fields]
                line = ids[pl.ds(d, 1), :]
                ids[pl.ds(d, 1), :] = jnp.where(lane_slot == slot, lane_row + blk[p + v], line)
        return carry

    lax.fori_loop(0, parts, part, 0)

    def send(k, start, stop):
        return pltpu.make_async_copy(out.at[:, start:stop, :], out_h.at[:, start:stop, :], out_sem.at[k])

    send(0, 0, slot_rows).start()

    def halo(k):
        d = 2 * k
        turned = jnp.concatenate([slots(d + u) for u in range(2)], axis=0).T
        first, last = turned[0:1], turned[LANES - 1 : LANES]
        first_swapped = pltpu.roll(turned[0:SUB], HALF, 1)[0:1]
        last_swapped = pltpu.roll(turned[LANES - SUB : LANES], HALF, 1)[SUB - 1 : SUB]
        for u in range(2):
            _, b = place(d + u)
            east = jnp.where(b == lon - 1, d + u - (lon - 1), d + u + 1)
            west = jnp.where(b == 0, d + u + (lon - 1), d + u - 1)
            out[extra(d + u, 0)] = ids[pl.ds(d + u, 1), :].astype(f32)
            sides = jnp.where(lane < HALF, ids[pl.ds(east, 1), :], ids[pl.ds(west, 1), :])
            out[extra(d + u, 1)] = sides.astype(f32)
            column = first if u == 0 else first_swapped
            out[extra(west, 2)] = jnp.where(lane < HALF, column, out[extra(west, 2)])
            column = last_swapped if u == 0 else last
            out[extra(east, 2)] = jnp.where(lane < HALF, out[extra(east, 2)], column)

    def halos(k, carry):
        for u in range(4):
            halo(k * 4 + u)
        return carry

    lax.fori_loop(0, devices // 8, halos, 0)
    send(1, slot_rows, out.shape[1]).start()
    send(0, 0, slot_rows).wait()
    send(1, slot_rows, out.shape[1]).wait()


def regrid(cap, lat, lon, src, dev, blk, coupling, atm, mask, weights, depth, ocean, inverses):
    pairs, cells, width = weights.shape
    fields, levels, oy, ox = ocean.shape
    message = jax.ShapeDtypeStruct((fields, levels + SUB, ox), f32)
    batch = 64
    devices = lat * lon
    tall = lat * fields * cap + extra_rows(lat)
    return pl.pallas_call(
        functools.partial(regrid_kernel, cap, lat, lon, oy, batch),
        in_specs=[HBM] * 10,
        out_specs=[HBM, VMEM, VMEM],
        out_shape=[pltpu.HBM((lon, tall, LANES), f32), message, message],
        scratch_shapes=[
            pltpu.VMEM((lon, tall, LANES), f32),
            pltpu.VMEM((atm.shape[1] * SUB, LANES), f32),
            pltpu.VMEM((devices, LANES), jnp.int32),
            pltpu.SMEM((devices,), jnp.int32),
            pltpu.SMEM(src.shape, jnp.int32),
            pltpu.SMEM(dev.shape, jnp.int32),
            pltpu.SMEM(blk.shape, jnp.int32),
            pltpu.SMEM(coupling.shape, f32),
            pltpu.VMEM(atm.shape, bf16),
            pltpu.VMEM(mask.shape, jnp.int32),
            pltpu.VMEM(weights.shape, bf16),
            pltpu.VMEM(depth.shape, jnp.int32),
            pltpu.VMEM((2, fields, levels, ox), f32),
            pltpu.VMEM((2, fields, levels, levels), f32),
            pltpu.SemaphoreType.DMA((6,)),
            pltpu.SemaphoreType.DMA((2 * fields + 1, 2)),
            pltpu.SemaphoreType.DMA((pairs // batch,)),
            pltpu.SemaphoreType.DMA((2,)),
        ],
        compiler_params=pltpu.CompilerParams(vmem_limit_bytes=20 << 20),
        cost_estimate=pl.CostEstimate(flops=2 * 8 * pairs * cells * width, bytes_accessed=10 << 20, transcendentals=0),
        name="regrid",
    )(*in_hbm(src, dev, blk, coupling, atm, mask, weights, depth, ocean, inverses))


def mix_kernel(
    depth_h, state_h, inv_h, mixed_h, side_h, to_east, to_west, depth_ref, state, mixed, inv, side, in_sems, out_sems
):
    fields, oy, levels, _ = mixed.shape
    depth_copy = pltpu.make_async_copy(depth_h, depth_ref, in_sems.at[2 * fields, 0])
    depth_copy.start()

    def load(q, c):
        for i in range(SUB):
            row = c * SUB + i
            pltpu.make_async_copy(state_h.at[q, :, row, :], state.at[q, row], in_sems.at[2 * q, c]).start()
        here = (q, pl.ds(c * SUB, SUB))
        pltpu.make_async_copy(inv_h.at[here], inv.at[here], in_sems.at[2 * q + 1, c]).start()

    for c in range(oy // SUB):
        load(0, c)
    depth_copy.wait()
    level = iota((levels, LANES), 0)
    lane = iota((levels, LANES), 1)
    line = iota((1, LANES), 1)
    edge_depth = jnp.zeros((SUB, LANES), f32)
    for i in range(oy):
        turned = pltpu.roll(jnp.broadcast_to(depth_ref[i : i + 1, :].astype(f32), (SUB, LANES)), 2 * i + 1, 1)
        edge_depth = jnp.where(line // 2 == i, turned, edge_depth)

    def field(q, carry):
        @pl.when(q + 1 < fields)
        def _():
            for c in range(oy // SUB):
                load(q + 1, c)

        cells = jnp.zeros((levels, LANES), f32)
        for c in range(oy // SUB):
            here = (q, pl.ds(c * SUB, SUB))
            pltpu.make_async_copy(mixed_h.at[here], state.at[here], in_sems.at[2 * q, c]).wait()
            pltpu.make_async_copy(inv_h.at[here], inv.at[here], in_sems.at[2 * q + 1, c]).wait()
            for row in range(c * SUB, (c + 1) * SUB):
                a = inv[q, row, 0]
                m = solve_row(a, state[q, row], level < depth_ref[row : row + 1, :])
                mixed[q, row] = m
                cells = jnp.where(lane // 2 == row, pltpu.roll(m, 2 * row + 1, 1), cells)
                cells = jnp.where(lane // 2 == HALF // 2 + row, a[:, 0:1], cells)
            pltpu.make_async_copy(mixed.at[here], mixed_h.at[here], out_sems.at[q]).start()
        side[q, 0:levels] = cells
        side[q, levels : levels + SUB] = edge_depth
        return carry

    lax.fori_loop(0, fields, field, 0)
    side_copy = pltpu.make_async_copy(side, side_h, out_sems.at[fields])
    side_copy.start()
    even = line % 2 == 0
    for k in range(fields // 2):
        to_east[k] = jnp.where(even, side[2 * k], pltpu.roll(side[2 * k + 1], 1, 1))
        to_west[k] = jnp.where(even, pltpu.roll(side[2 * k], LANES - 1, 1), side[2 * k + 1])
    for q in range(fields):
        pltpu.make_async_copy(mixed.at[q], mixed_h.at[q], out_sems.at[q]).wait()
    side_copy.wait()


def mix(depth, state, inverses):
    fields, levels, oy, ox = state.shape
    edge_shape = jax.ShapeDtypeStruct((fields // 2, levels + SUB, ox), f32)
    full = (fields, oy, levels, ox)
    return pl.pallas_call(
        mix_kernel,
        in_specs=[HBM] * 3,
        out_specs=[HBM] * 2 + [VMEM] * 2,
        out_shape=[pltpu.HBM(full, f32), pltpu.HBM((fields, levels + SUB, ox), f32), edge_shape, edge_shape],
        scratch_shapes=[
            pltpu.VMEM(depth.shape, jnp.int32),
            pltpu.VMEM(full, f32),
            pltpu.VMEM(full, f32),
            pltpu.VMEM(inverses.shape, f32),
            pltpu.VMEM((fields, levels + SUB, ox), f32),
            pltpu.SemaphoreType.DMA((2 * fields + 1, oy // SUB)),
            pltpu.SemaphoreType.DMA((fields + 1,)),
        ],
        compiler_params=pltpu.CompilerParams(vmem_limit_bytes=32 << 20),
        cost_estimate=pl.CostEstimate(flops=2 * 4 * fields * oy * levels * levels * ox, bytes_accessed=16 << 20, transcendentals=0),
        name="mix",
    )(*in_hbm(depth, state, inverses))


def collect_kernel(cap, fields, oy, recv, after_mix, after_north, after_south, out):
    lat = out.shape[0]
    lon = recv.shape[0]
    per = fields * cap
    slot_rows = lat * per
    group = LANES // per
    forced = fields * oy
    square_row = iota((LANES, LANES), 0).astype(f32)
    line = iota((1, LANES), 1)
    row = iota((2 * oy, LANES), 0).astype(f32)
    lane_base = ((line % fields) * oy).astype(f32)
    lane_side = (line // HALF).astype(f32)
    small_row, small_lane = iota((SUB, LANES), 0), iota((SUB, LANES), 1)
    pick = jnp.where((small_lane % fields == small_row) & (small_lane % HALF < per), 1.0, 0.0).astype(bf16)
    nothing = jnp.zeros((fields, LANES), f32)
    for a in range(lat):
        total = jnp.zeros((LANES, 2 * LANES), f32)
        for tile in range(lon // group):
            places = [tile * group + s for s in range(group)]
            named = slice(slot_rows + 3 * a, slot_rows + 3 * a + 1)
            ids = recv[places[0], named, :]
            for s in range(1, group):
                ids = jnp.where(line // per == s, recv[places[s], named, :], ids)
            hot = jnp.where(square_row == ids, 1.0, 0.0).astype(bf16)
            high, low = split(jnp.concatenate([recv[p, a * per : (a + 1) * per, :] for p in places], axis=0))
            total = total + matmul(hot, jnp.concatenate([high, low], axis=1))
        total = total[:, :LANES] + total[:, LANES:]
        out[a, 0:forced] = total
        if a == 0:
            out[a, forced : forced + fields] = nothing
        if a == lat - 1:
            out[a, forced + fields : forced + 2 * fields] = nothing
        for q in range(fields):
            if a + 1 < lat:
                out[a + 1, forced + q : forced + q + 1] = total[q * oy + oy - 1 : q * oy + oy]
            if a > 0:
                out[a - 1, forced + fields + q : forced + fields + q + 1] = total[q * oy : q * oy + 1]
        spread = jnp.zeros((2 * oy, LANES), f32)
        for b in range(lon):
            extra = recv[b, slot_rows + 3 * a + 1 : slot_rows + 3 * a + 3, :]
            place = 2.0 * (extra[0:1] - lane_base) + lane_side
            spread = spread + jnp.where(place == row, extra[1:2], 0.0)
        high, low = split(padded_rows(spread, LANES).T)
        out[a, forced + SUB : forced + 2 * SUB] = matmul(pick, high) + matmul(pick, low)


def collect(cap, fields, oy, lat, received, after):
    return pl.pallas_call(
        functools.partial(collect_kernel, cap, fields, oy),
        in_specs=[VMEM] + [pl.BlockSpec(memory_space=pl.ANY)] * 3,
        out_specs=VMEM,
        out_shape=jax.ShapeDtypeStruct((lat, fields * oy + 2 * SUB, LANES), f32),
        compiler_params=pltpu.CompilerParams(vmem_limit_bytes=16 << 20),
        name="collect",
    )(received, *after)


def finish_kernel(
    recv, depth_ref, mixed_h, own_h, north_h, south_h, east, west,
    out_h, own, north, south, forcing, z, keep, halo, z_north, z_south, mixed, stage, edge_sems, in_sems, out_sems,
):
    fields, oy, levels, _ = mixed.shape
    level = iota((levels, LANES), 0)
    lanes = iota((levels, LANES), 1)
    square_row = iota((LANES, LANES), 0)
    square_lane = iota((LANES, LANES), 1)
    line = iota((1, LANES), 1)
    even = line % 2 == 0
    edges = [
        pltpu.make_async_copy(a, b, edge_sems.at[k])
        for k, (a, b) in enumerate(((own_h, own), (north_h, north), (south_h, south)))
    ]
    for copy in edges:
        copy.start()

    def load(q, c):
        here = (q, pl.ds(c * SUB, SUB))
        return pltpu.make_async_copy(mixed_h.at[here], mixed.at[here], in_sems.at[q, c])

    for c in range(oy // SUB):
        load(0, c).start()

    total = recv[0]
    for a in range(1, recv.shape[0]):
        total = total + recv[a]
    forced_rows = fields * oy
    forcing[...] = total[0:forced_rows]
    rows = total[forced_rows : forced_rows + SUB]
    columns = total[forced_rows + SUB :]

    for copy in edges:
        copy.wait()
    depth = depth_ref[...]
    wide = iota((oy, LANES), 1)

    def upright(ref):
        value = jnp.where(wide == 2 * iota((oy, LANES), 0), ref[0, levels : levels + 1, :], 0.0)
        return jnp.sum(value, axis=1, keepdims=True).astype(jnp.int32)

    to_east = jnp.where(wide == LANES - 1, upright(east), pltpu.roll(depth, LANES - 1, 1))
    to_west = jnp.where(wide == 0, upright(west), pltpu.roll(depth, 1, 1))
    to_north = jnp.concatenate([north[0, levels : levels + 1, :].astype(jnp.int32), depth[: oy - 1]], axis=0)
    to_south = jnp.concatenate([depth[1:], south[0, levels : levels + 1, :].astype(jnp.int32)], axis=0)
    for i in range(oy):
        sides = jnp.where(level < to_east[i : i + 1], diffusion_rate, 0.0)
        for other in (to_west, to_north, to_south):
            sides = sides + jnp.where(level < other[i : i + 1], diffusion_rate, 0.0)
        keep[i] = 1.0 - sides

    def outer(target, ref, start):
        names = padded_rows(
            jnp.concatenate([ref[q, levels + 1 : levels + 2, :] for q in range(fields)], axis=0), LANES
        ).T
        active = level < ref[0, levels : levels + 1, :].astype(jnp.int32)
        for q in range(fields):
            value = ref[q, 0:levels] + names[0:levels, q : q + 1] * rows[start + q : start + q + 1]
            target[q] = jnp.where(active, value, 0.0)

    outer(z_north, north, 0)
    outer(z_south, south, fields)
    for q in range(fields):
        if q % 2:
            cells = jnp.where(even, pltpu.roll(east[q // 2], LANES - 1, 1), west[q // 2])
        else:
            cells = jnp.where(even, east[q // 2], pltpu.roll(west[q // 2], 1, 1))
        names = pltpu.roll(cells, HALF, 1)
        active = level < cells[levels : levels + 1].astype(jnp.int32)
        value = cells[0:levels] + names[0:levels] * columns[q : q + 1]
        halo[q] = jnp.where(active & (line < 2 * oy), value, 0.0)

    both = jnp.where((square_row == square_lane + 1) | (square_row == square_lane - 1), 1.0, 0.0).astype(bf16)
    both = jnp.concatenate([both, both], axis=0)
    spread = jnp.where(
        iota((2 * SUB, SUB * LANES), 0) // 2 == iota((2 * SUB, SUB * LANES), 1) // LANES, 1.0, 0.0
    ).astype(bf16)
    ends = (lanes == 0) | (lanes == LANES - 1)

    def field(q, carry):
        @pl.when(q + 1 < fields)
        def _():
            for c in range(oy // SUB):
                load(q + 1, c).start()

        z[0] = z_north[q]
        z[oy + 1] = z_south[q]
        edge = halo[q]
        names = own[q, 0:levels]
        high = names.astype(bf16).astype(f32)
        names = jnp.where(even, high, names - high)

        def solve(c):
            load(q, c).wait()
            rows_here = range(c * SUB, (c + 1) * SUB)
            here = pltpu.roll(names, (HALF - 2 * SUB * c) % LANES, 1)[:, 0 : 2 * SUB].astype(bf16)
            first = matmul(here, spread)
            for i, r in enumerate(rows_here):
                first_here = first[:, i * LANES : (i + 1) * LANES]
                forced = mixed[q, r] + first_here * forcing[pl.ds(q * oy + r, 1), :]
                z[r + 1] = jnp.where(level < depth_ref[r : r + 1, :], forced, 0.0)

        def diffuse(c):
            start = c * SUB
            high, low = split(z[start + 1 : start + 1 + SUB].reshape(SUB * levels, LANES))
            sides = matmul(jnp.concatenate([high, low], axis=1), both)
            for i in range(SUB):
                r = start + i
                outside = jnp.where(ends, pltpu.roll(edge, LANES - 1 - 2 * r, 1), 0.0)
                around = (z[r] + z[r + 2]) + (sides[i * levels : (i + 1) * levels] + outside)
                active = level < depth_ref[r : r + 1, :]
                stage[q, r] = jnp.where(active, z[r + 1] * keep[r] + diffusion_rate * around, mixed[q, r])
            for r in range(start, start + SUB):
                pltpu.make_async_copy(stage.at[q, r], out_h.at[q, :, r, :], out_sems.at[q]).start()

        solve(0)
        for c in range(1, oy // SUB):
            solve(c)
            diffuse(c - 1)
        diffuse(oy // SUB - 1)
        return carry

    lax.fori_loop(0, fields, field, 0)
    for q in range(fields):
        pltpu.make_async_copy(stage.at[q], mixed_h.at[q], out_sems.at[q]).wait()


def finish(received, depth, mixed, own, halos):
    fields, oy, levels, ox = mixed.shape
    edge = pltpu.VMEM((fields, levels, ox), f32)
    message = pltpu.VMEM((fields, levels + SUB, ox), f32)
    full = pltpu.VMEM((fields, oy, levels, ox), f32)
    return pl.pallas_call(
        finish_kernel,
        in_specs=[VMEM] * 2 + [HBM] * 4 + [VMEM] * 2,
        out_specs=HBM,
        out_shape=pltpu.HBM((fields, levels, oy, ox), f32),
        scratch_shapes=[
            message,
            message,
            message,
            pltpu.VMEM((fields * oy, ox), f32),
            pltpu.VMEM((oy + 2, levels, ox), f32),
            pltpu.VMEM((oy, levels, ox), f32),
            edge,
            edge,
            edge,
            full,
            full,
            pltpu.SemaphoreType.DMA((3,)),
            pltpu.SemaphoreType.DMA((fields, oy // SUB)),
            pltpu.SemaphoreType.DMA((fields,)),
        ],
        compiler_params=pltpu.CompilerParams(vmem_limit_bytes=32 << 20),
        cost_estimate=pl.CostEstimate(flops=20 * fields * oy * levels * ox, bytes_accessed=12 << 20, transcendentals=0),
        name="finish",
    )(received, depth, *in_hbm(mixed, own, *halos[0:2]), *halos[2:])


def shift(x, axis, step, wrap):
    count = lax.axis_size(axis)
    pairs = [(i, (i + step) % count) for i in range(count) if wrap or 0 <= i + step < count]
    return lax.ppermute(x, axis, pairs)


def on_device(
    atm_flux, sea_mask, src_block, dest_dev, dest_block, intersection_weights, coupling, inverses, ocean_state,
    depth_levels,
):
    lat, lon = lax.axis_size("lat"), lax.axis_size("lon")
    fields, _, oy, _ = ocean_state.shape
    cap = max(SUB, 2 * src_block.shape[0] // (lat * lon))
    slots, north, south = regrid(
        cap, lat, lon, src_block, dest_dev[:, 0], dest_block, coupling, atm_flux, sea_mask,
        intersection_weights, depth_levels, ocean_state, inverses,
    )
    in_plane = lax.all_to_all(slots, "lon", 0, 0, tiled=True)
    mixed, side, to_east, to_west = mix(depth_levels, ocean_state, inverses)
    halos = (
        shift(south, "lat", 1, False),
        shift(north, "lat", -1, False),
        shift(to_west, "lon", -1, True),
        shift(to_east, "lon", 1, True),
    )
    received = lax.all_to_all(collect(cap, fields, oy, lat, in_plane, (to_east, *halos[0:2])), "lat", 0, 0, tiled=True)
    return finish(received, depth_levels, mixed, side, halos)


def solution(mesh):
    placed = (
        P(None, "lat", "lon"),
        P("lat", "lon"),
        P(("lat", "lon")),
        P(("lat", "lon"), None),
        P(("lat", "lon")),
        P(("lat", "lon"), None, None),
        P(),
        P(None, "lat", "lon", None, None),
        P(None, None, "lat", "lon"),
        P("lat", "lon"),
    )
    return jax.shard_map(
        on_device,
        mesh=mesh,
        in_specs=placed,
        out_specs=P(None, None, "lat", "lon"),
        check_vma=False,
    )
```

```python
import functools

import jax
import jax.numpy as jnp
from jax import lax
from jax.experimental import pallas as pl
from jax.experimental.pallas import tpu as pltpu
from jax.sharding import PartitionSpec as P

diffusion_rate = 0.2
LANES = 128
HALF = 64
SUB = 8
f32 = jnp.float32
bf16 = jnp.bfloat16
HBM = pl.BlockSpec(memory_space=pltpu.HBM)
VMEM = pl.BlockSpec(memory_space=pltpu.VMEM)


def split(x):
    high = x.astype(bf16)
    return high, (x - high.astype(f32)).astype(bf16)


def in_hbm(*arrays):
    return [pltpu.with_memory_space_constraint(x, pltpu.HBM) for x in arrays]


def iota(shape, dim):
    return lax.broadcasted_iota(jnp.int32, shape, dim)


def matmul(a, b):
    return jnp.dot(a, b, preferred_element_type=f32)


def padded_rows(x, rows):
    return x if x.shape[0] == rows else jnp.concatenate([x, jnp.zeros((rows - x.shape[0], LANES), x.dtype)], axis=0)


def solve_row(a, x, active):
    levels = x.shape[0]
    a_high, a_low = split(a)
    r_high, r_low = split(jnp.where(active, x, 0.0))
    product = matmul(jnp.concatenate([a_high, a_low], axis=0), jnp.concatenate([r_high, r_low], axis=1))
    solved = product[:levels, :LANES] + (product[levels:, :LANES] + product[:levels, LANES:])
    return jnp.where(active, solved, x)


def outer_messages(refs, depth_ref, state, inv):
    _, fields, levels, _ = state.shape
    oy = depth_ref.shape[0]
    level = iota((levels, LANES), 0)
    for k, (row, ref) in enumerate(zip((0, oy - 1), refs)):
        depth = depth_ref[row : row + 1, :]
        names = jnp.zeros((levels, LANES), f32)
        for q in range(fields):
            a = inv[k, q]
            ref[q, 0:levels] = solve_row(a, state[k, q], level < depth)
            names = jnp.where(iota((levels, LANES), 1) == q, a[:, 0:1], names)
        names = padded_rows(names, LANES).T
        for q in range(fields):
            ref[q, levels : levels + SUB] = jnp.concatenate(
                [depth.astype(f32), names[q : q + 1], jnp.zeros((SUB - 2, LANES), f32)], axis=0
            )


def extra_rows(lat):
    return -(-3 * lat // SUB) * SUB


def regrid_kernel(
    cap, lat, lon, oy, batch,
    src_h, dev_h, blk_h, coupling_h, atm_h, mask_h, weights_h, depth_h, state_h, inv_h,
    out_h, north, south,
    out, rows, ids, count, src, dev, blk, coupling, atm, mask, weights, depth_ref, state, inv,
    small_sem, outer_sem, big_sem, out_sem,
):
    fluxes, atm_rows, _ = atm.shape
    fields = coupling.shape[0]
    devices = lat * lon
    per = fields * cap
    slot_rows = lat * per
    parts = weights.shape[0] // batch
    ahead = min(2, parts)

    def big(k):
        here = pl.ds(pl.multiple_of(k * batch, batch), batch)
        return pltpu.make_async_copy(weights_h.at[here], weights.at[here], big_sem.at[k])

    small = [
        pltpu.make_async_copy(a, b, small_sem.at[k])
        for k, (a, b) in enumerate(
            (
                (coupling_h, coupling), (atm_h, atm), (mask_h, mask),
                (src_h, src), (dev_h, dev), (blk_h, blk),
            )
        )
    ]
    outer = [pltpu.make_async_copy(depth_h, depth_ref, outer_sem.at[2 * fields, 0])]
    for q in range(fields):
        for k, row in enumerate((0, oy - 1)):
            outer.append(pltpu.make_async_copy(state_h.at[q, :, row, :], state.at[k, q], outer_sem.at[2 * q, k]))
            outer.append(pltpu.make_async_copy(inv_h.at[q, row, 0], inv.at[k, q], outer_sem.at[2 * q + 1, k]))
    for copy in small + outer:
        copy.start()
    for k in range(ahead):
        big(k).start()

    def clear_count(d, carry):
        count[d] = 0
        return carry

    def clear(b, carry):
        out[b] = jnp.zeros(out.shape[1:], f32)
        return carry

    lax.fori_loop(0, devices, clear_count, 0)
    lax.fori_loop(0, lon, clear, 0)
    ids[...] = jnp.full(ids.shape, -1, jnp.int32)
    for copy in small:
        copy.wait()
    for tile in range(atm_rows // 16):
        here = slice(tile * 16, tile * 16 + 16)
        sea = mask[here, :].astype(f32)
        flux = [atm[f, here, :].astype(f32) * sea for f in range(fluxes)]
        for q in range(fields):
            total = coupling[q, 0] * flux[0]
            for f in range(1, fluxes):
                total = total + coupling[q, f] * flux[f]
            high = total.astype(bf16).astype(f32)
            rows[pl.ds(tile * 16 * SUB + q, 16, stride=SUB), :] = high
            rows[pl.ds(tile * 16 * SUB + fields + q, 16, stride=SUB), :] = total - high

    for copy in outer:
        copy.wait()
    outer_messages((north, south), depth_ref, state, inv)

    lane = iota((1, LANES), 1)
    lane_slot = (lane % per) // fields
    lane_row = (lane % fields) * oy

    bits = lon.bit_length() - 1

    def place(d):
        if lon == 1 << bits:
            return lax.shift_right_logical(d, bits), d & (lon - 1)
        return lax.div(d, lon), lax.rem(d, lon)

    def extra(d, k):
        a, b = place(d)
        return b, pl.ds(slot_rows + 3 * a + k, 1)

    def slots(d):
        a, b = place(d)
        return padded_rows(out[b, pl.ds(pl.multiple_of(a * per, per), per), :], HALF)

    def part(k, carry):
        big(k).wait()

        @pl.when(k + ahead < parts)
        def _():
            big(k + ahead).start()

        for u in range(0, batch, 2):
            p = k * batch + u
            x = jnp.concatenate(
                [rows[pl.ds(pl.multiple_of(src[p + v] * SUB, SUB), SUB), :] for v in range(2)], axis=0
            ).astype(bf16)
            both = matmul(x, jnp.concatenate([weights[p], weights[p + 1]], axis=1))
            for v in range(2):
                d = dev[p + v]
                slot = jnp.minimum(count[d], cap - 1)
                count[d] = slot + 1
                half = both[v * SUB : v * SUB + SUB, v * LANES : (v + 1) * LANES]
                a, b = place(d)
                out[b, pl.ds(a * per + slot * fields, fields), :] = half[0:fields] + half[fields : 2 * fields]
                line = ids[pl.ds(d, 1), :]
                ids[pl.ds(d, 1), :] = jnp.where(lane_slot == slot, lane_row + blk[p + v], line)
        return carry

    lax.fori_loop(0, parts, part, 0)

    def send(k, start, stop):
        return pltpu.make_async_copy(out.at[:, start:stop, :], out_h.at[:, start:stop, :], out_sem.at[k])

    send(0, 0, slot_rows).start()

    def halo(k):
        d = 2 * k
        turned = jnp.concatenate([slots(d + u) for u in range(2)], axis=0).T
        first, last = turned[0:1], turned[LANES - 1 : LANES]
        first_swapped = pltpu.roll(turned[0:SUB], HALF, 1)[0:1]
        last_swapped = pltpu.roll(turned[LANES - SUB : LANES], HALF, 1)[SUB - 1 : SUB]
        for u in range(2):
            _, b = place(d + u)
            east = jnp.where(b == lon - 1, d + u - (lon - 1), d + u + 1)
            west = jnp.where(b == 0, d + u + (lon - 1), d + u - 1)
            out[extra(d + u, 0)] = ids[pl.ds(d + u, 1), :].astype(f32)
            sides = jnp.where(lane < HALF, ids[pl.ds(east, 1), :], ids[pl.ds(west, 1), :])
            out[extra(d + u, 1)] = sides.astype(f32)
            column = first if u == 0 else first_swapped
            out[extra(west, 2)] = jnp.where(lane < HALF, column, out[extra(west, 2)])
            column = last_swapped if u == 0 else last
            out[extra(east, 2)] = jnp.where(lane < HALF, out[extra(east, 2)], column)

    def halos(k, carry):
        for u in range(4):
            halo(k * 4 + u)
        return carry

    lax.fori_loop(0, devices // 8, halos, 0)
    send(1, slot_rows, out.shape[1]).start()
    send(0, 0, slot_rows).wait()
    send(1, slot_rows, out.shape[1]).wait()


def regrid(cap, lat, lon, src, dev, blk, coupling, atm, mask, weights, depth, ocean, inverses):
    pairs, cells, width = weights.shape
    fields, levels, oy, ox = ocean.shape
    message = jax.ShapeDtypeStruct((fields, levels + SUB, ox), f32)
    batch = 64
    devices = lat * lon
    tall = lat * fields * cap + extra_rows(lat)
    return pl.pallas_call(
        functools.partial(regrid_kernel, cap, lat, lon, oy, batch),
        in_specs=[HBM] * 10,
        out_specs=[HBM, VMEM, VMEM],
        out_shape=[pltpu.HBM((lon, tall, LANES), f32), message, message],
        scratch_shapes=[
            pltpu.VMEM((lon, tall, LANES), f32),
            pltpu.VMEM((atm.shape[1] * SUB, LANES), f32),
            pltpu.VMEM((devices, LANES), jnp.int32),
            pltpu.SMEM((devices,), jnp.int32),
            pltpu.SMEM(src.shape, jnp.int32),
            pltpu.SMEM(dev.shape, jnp.int32),
            pltpu.SMEM(blk.shape, jnp.int32),
            pltpu.SMEM(coupling.shape, f32),
            pltpu.VMEM(atm.shape, bf16),
            pltpu.VMEM(mask.shape, jnp.int32),
            pltpu.VMEM(weights.shape, bf16),
            pltpu.VMEM(depth.shape, jnp.int32),
            pltpu.VMEM((2, fields, levels, ox), f32),
            pltpu.VMEM((2, fields, levels, levels), f32),
            pltpu.SemaphoreType.DMA((6,)),
            pltpu.SemaphoreType.DMA((2 * fields + 1, 2)),
            pltpu.SemaphoreType.DMA((pairs // batch,)),
            pltpu.SemaphoreType.DMA((2,)),
        ],
        compiler_params=pltpu.CompilerParams(vmem_limit_bytes=20 << 20),
        cost_estimate=pl.CostEstimate(flops=2 * 8 * pairs * cells * width, bytes_accessed=10 << 20, transcendentals=0),
        name="regrid",
    )(*in_hbm(src, dev, blk, coupling, atm, mask, weights, depth, ocean, inverses))


def mix_kernel(
    depth_h, state_h, inv_h, mixed_h, side_h, to_east, to_west, depth_ref, state, mixed, inv, side, in_sems, out_sems
):
    fields, oy, levels, _ = mixed.shape
    depth_copy = pltpu.make_async_copy(depth_h, depth_ref, in_sems.at[2 * fields, 0])
    depth_copy.start()

    def load(q, c):
        for i in range(SUB):
            row = c * SUB + i
            pltpu.make_async_copy(state_h.at[q, :, row, :], state.at[q, row], in_sems.at[2 * q, c]).start()
        here = (q, pl.ds(c * SUB, SUB))
        pltpu.make_async_copy(inv_h.at[here], inv.at[here], in_sems.at[2 * q + 1, c]).start()

    for c in range(oy // SUB):
        load(0, c)
    depth_copy.wait()
    level = iota((levels, LANES), 0)
    lane = iota((levels, LANES), 1)
    line = iota((1, LANES), 1)
    edge_depth = jnp.zeros((SUB, LANES), f32)
    for i in range(oy):
        turned = pltpu.roll(jnp.broadcast_to(depth_ref[i : i + 1, :].astype(f32), (SUB, LANES)), 2 * i + 1, 1)
        edge_depth = jnp.where(line // 2 == i, turned, edge_depth)

    def field(q, carry):
        @pl.when(q + 1 < fields)
        def _():
            for c in range(oy // SUB):
                load(q + 1, c)

        cells = jnp.zeros((levels, LANES), f32)
        for c in range(oy // SUB):
            here = (q, pl.ds(c * SUB, SUB))
            pltpu.make_async_copy(mixed_h.at[here], state.at[here], in_sems.at[2 * q, c]).wait()
            pltpu.make_async_copy(inv_h.at[here], inv.at[here], in_sems.at[2 * q + 1, c]).wait()
            for row in range(c * SUB, (c + 1) * SUB):
                a = inv[q, row, 0]
                m = solve_row(a, state[q, row], level < depth_ref[row : row + 1, :])
                mixed[q, row] = m
                cells = jnp.where(lane // 2 == row, pltpu.roll(m, 2 * row + 1, 1), cells)
                cells = jnp.where(lane // 2 == HALF // 2 + row, a[:, 0:1], cells)
            pltpu.make_async_copy(mixed.at[here], mixed_h.at[here], out_sems.at[q]).start()
        side[q, 0:levels] = cells
        side[q, levels : levels + SUB] = edge_depth
        return carry

    lax.fori_loop(0, fields, field, 0)
    side_copy = pltpu.make_async_copy(side, side_h, out_sems.at[fields])
    side_copy.start()
    even = line % 2 == 0
    for k in range(fields // 2):
        to_east[k] = jnp.where(even, side[2 * k], pltpu.roll(side[2 * k + 1], 1, 1))
        to_west[k] = jnp.where(even, pltpu.roll(side[2 * k], LANES - 1, 1), side[2 * k + 1])
    for q in range(fields):
        pltpu.make_async_copy(mixed.at[q], mixed_h.at[q], out_sems.at[q]).wait()
    side_copy.wait()


def mix(depth, state, inverses):
    fields, levels, oy, ox = state.shape
    edge_shape = jax.ShapeDtypeStruct((fields // 2, levels + SUB, ox), f32)
    full = (fields, oy, levels, ox)
    return pl.pallas_call(
        mix_kernel,
        in_specs=[HBM] * 3,
        out_specs=[HBM] * 2 + [VMEM] * 2,
        out_shape=[pltpu.HBM(full, f32), pltpu.HBM((fields, levels + SUB, ox), f32), edge_shape, edge_shape],
        scratch_shapes=[
            pltpu.VMEM(depth.shape, jnp.int32),
            pltpu.VMEM(full, f32),
            pltpu.VMEM(full, f32),
            pltpu.VMEM(inverses.shape, f32),
            pltpu.VMEM((fields, levels + SUB, ox), f32),
            pltpu.SemaphoreType.DMA((2 * fields + 1, oy // SUB)),
            pltpu.SemaphoreType.DMA((fields + 1,)),
        ],
        compiler_params=pltpu.CompilerParams(vmem_limit_bytes=32 << 20),
        cost_estimate=pl.CostEstimate(flops=2 * 4 * fields * oy * levels * levels * ox, bytes_accessed=16 << 20, transcendentals=0),
        name="mix",
    )(*in_hbm(depth, state, inverses))


def collect_kernel(cap, fields, oy, recv, after_mix, after_north, after_south, out):
    lat = out.shape[0]
    lon = recv.shape[0]
    per = fields * cap
    slot_rows = lat * per
    group = LANES // per
    forced = fields * oy
    square_row = iota((LANES, LANES), 0).astype(f32)
    line = iota((1, LANES), 1)
    row = iota((2 * oy, LANES), 0).astype(f32)
    lane_base = ((line % fields) * oy).astype(f32)
    lane_side = (line // HALF).astype(f32)
    small_row, small_lane = iota((SUB, LANES), 0), iota((SUB, LANES), 1)
    pick = jnp.where((small_lane % fields == small_row) & (small_lane % HALF < per), 1.0, 0.0).astype(bf16)
    nothing = jnp.zeros((fields, LANES), f32)
    for a in range(lat):
        total = jnp.zeros((LANES, 2 * LANES), f32)
        for tile in range(lon // group):
            places = [tile * group + s for s in range(group)]
            named = slice(slot_rows + 3 * a, slot_rows + 3 * a + 1)
            ids = recv[places[0], named, :]
            for s in range(1, group):
                ids = jnp.where(line // per == s, recv[places[s], named, :], ids)
            hot = jnp.where(square_row == ids, 1.0, 0.0).astype(bf16)
            high, low = split(jnp.concatenate([recv[p, a * per : (a + 1) * per, :] for p in places], axis=0))
            total = total + matmul(hot, jnp.concatenate([high, low], axis=1))
        total = total[:, :LANES] + total[:, LANES:]
        out[a, 0:forced] = total
        if a == 0:
            out[a, forced : forced + fields] = nothing
        if a == lat - 1:
            out[a, forced + fields : forced + 2 * fields] = nothing
        for q in range(fields):
            if a + 1 < lat:
                out[a + 1, forced + q : forced + q + 1] = total[q * oy + oy - 1 : q * oy + oy]
            if a > 0:
                out[a - 1, forced + fields + q : forced + fields + q + 1] = total[q * oy : q * oy + 1]
        spread = jnp.zeros((2 * oy, LANES), f32)
        for b in range(lon):
            extra = recv[b, slot_rows + 3 * a + 1 : slot_rows + 3 * a + 3, :]
            place = 2.0 * (extra[0:1] - lane_base) + lane_side
            spread = spread + jnp.where(place == row, extra[1:2], 0.0)
        high, low = split(padded_rows(spread, LANES).T)
        out[a, forced + SUB : forced + 2 * SUB] = matmul(pick, high) + matmul(pick, low)


def collect(cap, fields, oy, lat, received, after):
    return pl.pallas_call(
        functools.partial(collect_kernel, cap, fields, oy),
        in_specs=[VMEM] + [pl.BlockSpec(memory_space=pl.ANY)] * 3,
        out_specs=VMEM,
        out_shape=jax.ShapeDtypeStruct((lat, fields * oy + 2 * SUB, LANES), f32),
        compiler_params=pltpu.CompilerParams(vmem_limit_bytes=16 << 20),
        name="collect",
    )(received, *after)


def finish_kernel(
    recv, depth_ref, mixed_h, own_h, north_h, south_h, east, west,
    out_h, own, north, south, forcing, z, keep, halo, z_north, z_south, mixed, stage, edge_sems, in_sems, out_sems,
):
    fields, oy, levels, _ = mixed.shape
    level = iota((levels, LANES), 0)
    lanes = iota((levels, LANES), 1)
    square_row = iota((LANES, LANES), 0)
    square_lane = iota((LANES, LANES), 1)
    line = iota((1, LANES), 1)
    even = line % 2 == 0
    edges = [
        pltpu.make_async_copy(a, b, edge_sems.at[k])
        for k, (a, b) in enumerate(((own_h, own), (north_h, north), (south_h, south)))
    ]
    for copy in edges:
        copy.start()

    def load(q, c):
        here = (q, pl.ds(c * SUB, SUB))
        return pltpu.make_async_copy(mixed_h.at[here], mixed.at[here], in_sems.at[q, c])

    for c in range(oy // SUB):
        load(0, c).start()

    total = recv[0]
    for a in range(1, recv.shape[0]):
        total = total + recv[a]
    forced_rows = fields * oy
    forcing[...] = total[0:forced_rows]
    rows = total[forced_rows : forced_rows + SUB]
    columns = total[forced_rows + SUB :]

    for copy in edges:
        copy.wait()
    depth = depth_ref[...]
    wide = iota((oy, LANES), 1)

    def upright(ref):
        value = jnp.where(wide == 2 * iota((oy, LANES), 0), ref[0, levels : levels + 1, :], 0.0)
        return jnp.sum(value, axis=1, keepdims=True).astype(jnp.int32)

    to_east = jnp.where(wide == LANES - 1, upright(east), pltpu.roll(depth, LANES - 1, 1))
    to_west = jnp.where(wide == 0, upright(west), pltpu.roll(depth, 1, 1))
    to_north = jnp.concatenate([north[0, levels : levels + 1, :].astype(jnp.int32), depth[: oy - 1]], axis=0)
    to_south = jnp.concatenate([depth[1:], south[0, levels : levels + 1, :].astype(jnp.int32)], axis=0)
    for i in range(oy):
        sides = jnp.where(level < to_east[i : i + 1], diffusion_rate, 0.0)
        for other in (to_west, to_north, to_south):
            sides = sides + jnp.where(level < other[i : i + 1], diffusion_rate, 0.0)
        keep[i] = 1.0 - sides

    def outer(target, ref, start):
        names = padded_rows(
            jnp.concatenate([ref[q, levels + 1 : levels + 2, :] for q in range(fields)], axis=0), LANES
        ).T
        active = level < ref[0, levels : levels + 1, :].astype(jnp.int32)
        for q in range(fields):
            value = ref[q, 0:levels] + names[0:levels, q : q + 1] * rows[start + q : start + q + 1]
            target[q] = jnp.where(active, value, 0.0)

    outer(z_north, north, 0)
    outer(z_south, south, fields)
    for q in range(fields):
        if q % 2:
            cells = jnp.where(even, pltpu.roll(east[q // 2], LANES - 1, 1), west[q // 2])
        else:
            cells = jnp.where(even, east[q // 2], pltpu.roll(west[q // 2], 1, 1))
        names = pltpu.roll(cells, HALF, 1)
        active = level < cells[levels : levels + 1].astype(jnp.int32)
        value = cells[0:levels] + names[0:levels] * columns[q : q + 1]
        halo[q] = jnp.where(active & (line < 2 * oy), value, 0.0)

    both = jnp.where((square_row == square_lane + 1) | (square_row == square_lane - 1), 1.0, 0.0).astype(bf16)
    both = jnp.concatenate([both, both], axis=0)
    ones = jnp.ones((LANES, LANES), bf16)
    block = 2 * SUB
    ends = (lanes == 0) | (lanes == LANES - 1)

    def field(q, carry):
        @pl.when(q + 1 < fields)
        def _():
            for c in range(oy // SUB):
                load(q + 1, c).start()

        z[0] = z_north[q]
        z[oy + 1] = z_south[q]
        edge = halo[q]
        names = own[q, 0:levels]
        high = names.astype(bf16).astype(f32)
        names = jnp.where(even, high, names - high)

        def solve(c):
            rows_here = range(c * block, (c + 1) * block)
            for part in range(rows_here.start // SUB, rows_here.stop // SUB):
                load(q, part).wait()
            first = matmul(
                jnp.concatenate(
                    [jnp.where(lanes // 2 == HALF // 2 + r, names, 0.0).astype(bf16) for r in rows_here], axis=0
                ),
                ones,
            )
            for i, r in enumerate(rows_here):
                first_here = first[i * levels : (i + 1) * levels]
                forced = mixed[q, r] + first_here * forcing[pl.ds(q * oy + r, 1), :]
                z[r + 1] = jnp.where(level < depth_ref[r : r + 1, :], forced, 0.0)

        def diffuse(c):
            start = c * block
            high, low = split(z[start + 1 : start + 1 + block].reshape(block * levels, LANES))
            sides = matmul(jnp.concatenate([high, low], axis=1), both)
            for i in range(block):
                r = start + i
                outside = jnp.where(ends, pltpu.roll(edge, LANES - 1 - 2 * r, 1), 0.0)
                around = (z[r] + z[r + 2]) + (sides[i * levels : (i + 1) * levels] + outside)
                active = level < depth_ref[r : r + 1, :]
                stage[q, r] = jnp.where(active, z[r + 1] * keep[r] + diffusion_rate * around, mixed[q, r])
            for r in range(start, start + block):
                pltpu.make_async_copy(stage.at[q, r], out_h.at[q, :, r, :], out_sems.at[q]).start()

        solve(0)
        for c in range(1, oy // block):
            solve(c)
            diffuse(c - 1)
        diffuse(oy // block - 1)
        return carry

    lax.fori_loop(0, fields, field, 0)
    for q in range(fields):
        pltpu.make_async_copy(stage.at[q], mixed_h.at[q], out_sems.at[q]).wait()


def finish(received, depth, mixed, own, halos):
    fields, oy, levels, ox = mixed.shape
    edge = pltpu.VMEM((fields, levels, ox), f32)
    message = pltpu.VMEM((fields, levels + SUB, ox), f32)
    full = pltpu.VMEM((fields, oy, levels, ox), f32)
    return pl.pallas_call(
        finish_kernel,
        in_specs=[VMEM] * 2 + [HBM] * 4 + [VMEM] * 2,
        out_specs=HBM,
        out_shape=pltpu.HBM((fields, levels, oy, ox), f32),
        scratch_shapes=[
            message,
            message,
            message,
            pltpu.VMEM((fields * oy, ox), f32),
            pltpu.VMEM((oy + 2, levels, ox), f32),
            pltpu.VMEM((oy, levels, ox), f32),
            edge,
            edge,
            edge,
            full,
            full,
            pltpu.SemaphoreType.DMA((3,)),
            pltpu.SemaphoreType.DMA((fields, oy // SUB)),
            pltpu.SemaphoreType.DMA((fields,)),
        ],
        compiler_params=pltpu.CompilerParams(vmem_limit_bytes=32 << 20),
        cost_estimate=pl.CostEstimate(flops=20 * fields * oy * levels * ox, bytes_accessed=12 << 20, transcendentals=0),
        name="finish",
    )(received, depth, *in_hbm(mixed, own, *halos[0:2]), *halos[2:])


def shift(x, axis, step, wrap):
    count = lax.axis_size(axis)
    pairs = [(i, (i + step) % count) for i in range(count) if wrap or 0 <= i + step < count]
    return lax.ppermute(x, axis, pairs)


def on_device(
    atm_flux, sea_mask, src_block, dest_dev, dest_block, intersection_weights, coupling, inverses, ocean_state,
    depth_levels,
):
    lat, lon = lax.axis_size("lat"), lax.axis_size("lon")
    fields, _, oy, _ = ocean_state.shape
    cap = max(SUB, 2 * src_block.shape[0] // (lat * lon))
    slots, north, south = regrid(
        cap, lat, lon, src_block, dest_dev[:, 0], dest_block, coupling, atm_flux, sea_mask,
        intersection_weights, depth_levels, ocean_state, inverses,
    )
    in_plane = lax.all_to_all(slots, "lon", 0, 0, tiled=True)
    mixed, side, to_east, to_west = mix(depth_levels, ocean_state, inverses)
    halos = (
        shift(south, "lat", 1, False),
        shift(north, "lat", -1, False),
        shift(to_west, "lon", -1, True),
        shift(to_east, "lon", 1, True),
    )
    received = lax.all_to_all(collect(cap, fields, oy, lat, in_plane, (to_east, *halos[0:2])), "lat", 0, 0, tiled=True)
    return finish(received, depth_levels, mixed, side, halos)


def solution(mesh):
    placed = (
        P(None, "lat", "lon"),
        P("lat", "lon"),
        P(("lat", "lon")),
        P(("lat", "lon"), None),
        P(("lat", "lon")),
        P(("lat", "lon"), None, None),
        P(),
        P(None, "lat", "lon", None, None),
        P(None, None, "lat", "lon"),
        P("lat", "lon"),
    )
    return jax.shard_map(
        on_device,
        mesh=mesh,
        in_specs=placed,
        out_specs=P(None, None, "lat", "lon"),
        check_vma=False,
    )
```

```python
import functools

import jax
import jax.numpy as jnp
from jax import lax
from jax.experimental import pallas as pl
from jax.experimental.pallas import tpu as pltpu
from jax.sharding import PartitionSpec as P

diffusion_rate = 0.2
LANES = 128
HALF = 64
SUB = 8
f32 = jnp.float32
bf16 = jnp.bfloat16
HBM = pl.BlockSpec(memory_space=pltpu.HBM)
VMEM = pl.BlockSpec(memory_space=pltpu.VMEM)


def split(x):
    high = x.astype(bf16)
    return high, (x - high.astype(f32)).astype(bf16)


def in_hbm(*arrays):
    return [pltpu.with_memory_space_constraint(x, pltpu.HBM) for x in arrays]


def iota(shape, dim):
    return lax.broadcasted_iota(jnp.int32, shape, dim)


def matmul(a, b):
    return jnp.dot(a, b, preferred_element_type=f32)


def padded_rows(x, rows):
    return x if x.shape[0] == rows else jnp.concatenate([x, jnp.zeros((rows - x.shape[0], LANES), x.dtype)], axis=0)


def solve_row(a, x, active):
    levels = x.shape[0]
    a_high, a_low = split(a)
    r_high, r_low = split(jnp.where(active, x, 0.0))
    product = matmul(jnp.concatenate([a_high, a_low], axis=0), jnp.concatenate([r_high, r_low], axis=1))
    solved = product[:levels, :LANES] + (product[levels:, :LANES] + product[:levels, LANES:])
    return jnp.where(active, solved, x)


def outer_messages(refs, depth_ref, state, inv):
    _, fields, levels, _ = state.shape
    oy = depth_ref.shape[0]
    level = iota((levels, LANES), 0)
    for k, (row, ref) in enumerate(zip((0, oy - 1), refs)):
        depth = depth_ref[row : row + 1, :]
        names = jnp.zeros((levels, LANES), f32)
        for q in range(fields):
            a = inv[k, q]
            ref[q, 0:levels] = solve_row(a, state[k, q], level < depth)
            names = jnp.where(iota((levels, LANES), 1) == q, a[:, 0:1], names)
        names = padded_rows(names, LANES).T
        for q in range(fields):
            ref[q, levels : levels + SUB] = jnp.concatenate(
                [depth.astype(f32), names[q : q + 1], jnp.zeros((SUB - 2, LANES), f32)], axis=0
            )


def extra_rows(lat):
    return -(-3 * lat // SUB) * SUB


def regrid_kernel(
    cap, lat, lon, oy, batch,
    src_h, dev_h, blk_h, coupling_h, atm_h, mask_h, weights_h, depth_h, state_h, inv_h,
    out_h, north, south,
    out, rows, ids, count, src, dev, blk, coupling, atm, mask, weights, depth_ref, state, inv,
    small_sem, outer_sem, big_sem, out_sem,
):
    fluxes, atm_rows, _ = atm.shape
    fields = coupling.shape[0]
    devices = lat * lon
    per = fields * cap
    slot_rows = lat * per
    parts = weights.shape[0] // batch
    ahead = min(2, parts)

    def big(k):
        here = pl.ds(pl.multiple_of(k * batch, batch), batch)
        return pltpu.make_async_copy(weights_h.at[here], weights.at[here], big_sem.at[k])

    small = [
        pltpu.make_async_copy(a, b, small_sem.at[k])
        for k, (a, b) in enumerate(
            (
                (coupling_h, coupling), (atm_h, atm), (mask_h, mask),
                (src_h, src), (dev_h, dev), (blk_h, blk),
            )
        )
    ]
    outer = [pltpu.make_async_copy(depth_h, depth_ref, outer_sem.at[2 * fields, 0])]
    for q in range(fields):
        for k, row in enumerate((0, oy - 1)):
            outer.append(pltpu.make_async_copy(state_h.at[q, :, row, :], state.at[k, q], outer_sem.at[2 * q, k]))
            outer.append(pltpu.make_async_copy(inv_h.at[q, row, 0], inv.at[k, q], outer_sem.at[2 * q + 1, k]))
    for copy in small + outer:
        copy.start()
    for k in range(ahead):
        big(k).start()

    def clear_count(d, carry):
        count[d] = 0
        return carry

    def clear(b, carry):
        out[b] = jnp.zeros(out.shape[1:], f32)
        return carry

    lax.fori_loop(0, devices, clear_count, 0)
    lax.fori_loop(0, lon, clear, 0)
    ids[...] = jnp.full(ids.shape, -1, jnp.int32)
    for copy in small:
        copy.wait()
    for tile in range(atm_rows // 16):
        here = slice(tile * 16, tile * 16 + 16)
        sea = mask[here, :].astype(f32)
        flux = [atm[f, here, :].astype(f32) * sea for f in range(fluxes)]
        for q in range(fields):
            total = coupling[q, 0] * flux[0]
            for f in range(1, fluxes):
                total = total + coupling[q, f] * flux[f]
            high = total.astype(bf16).astype(f32)
            rows[pl.ds(tile * 16 * SUB + q, 16, stride=SUB), :] = high
            rows[pl.ds(tile * 16 * SUB + fields + q, 16, stride=SUB), :] = total - high

    for copy in outer:
        copy.wait()
    outer_messages((north, south), depth_ref, state, inv)

    lane = iota((1, LANES), 1)
    lane_slot = (lane % per) // fields
    lane_row = (lane % fields) * oy

    bits = lon.bit_length() - 1

    def place(d):
        if isinstance(d, int):
            return d // lon, d % lon
        if lon == 1 << bits:
            return lax.shift_right_logical(d, bits), d & (lon - 1)
        return lax.div(d, lon), lax.rem(d, lon)

    def extra(d, k):
        a, b = place(d)
        return b, pl.ds(slot_rows + 3 * a + k, 1)

    def slots(d):
        a, b = place(d)
        return padded_rows(out[b, a * per : (a + 1) * per, :], HALF)

    def part(k, carry):
        big(k).wait()

        @pl.when(k + ahead < parts)
        def _():
            big(k + ahead).start()

        for u in range(0, batch, 2):
            p = k * batch + u
            x = jnp.concatenate(
                [rows[pl.ds(pl.multiple_of(src[p + v] * SUB, SUB), SUB), :] for v in range(2)], axis=0
            ).astype(bf16)
            both = matmul(x, jnp.concatenate([weights[p], weights[p + 1]], axis=1))
            for v in range(2):
                d = dev[p + v]
                slot = jnp.minimum(count[d], cap - 1)
                count[d] = slot + 1
                half = both[v * SUB : v * SUB + SUB, v * LANES : (v + 1) * LANES]
                a, b = place(d)
                out[b, pl.ds(a * per + slot * fields, fields), :] = half[0:fields] + half[fields : 2 * fields]
                line = ids[pl.ds(d, 1), :]
                ids[pl.ds(d, 1), :] = jnp.where(lane_slot == slot, lane_row + blk[p + v], line)
        return carry

    lax.fori_loop(0, parts, part, 0)

    def send(k, start, stop):
        return pltpu.make_async_copy(out.at[:, start:stop, :], out_h.at[:, start:stop, :], out_sem.at[k])

    send(0, 0, slot_rows).start()

    def halo(k):
        d = 2 * k
        turned = jnp.concatenate([slots(d + u) for u in range(2)], axis=0).T
        first, last = turned[0:1], turned[LANES - 1 : LANES]
        first_swapped = pltpu.roll(turned[0:SUB], HALF, 1)[0:1]
        last_swapped = pltpu.roll(turned[LANES - SUB : LANES], HALF, 1)[SUB - 1 : SUB]
        for u in range(2):
            _, b = place(d + u)
            east = d + u - b + (b + 1) % lon
            west = d + u - b + (b - 1) % lon
            out[extra(d + u, 0)] = ids[pl.ds(d + u, 1), :].astype(f32)
            sides = jnp.where(lane < HALF, ids[pl.ds(east, 1), :], ids[pl.ds(west, 1), :])
            out[extra(d + u, 1)] = sides.astype(f32)
            column = first if u == 0 else first_swapped
            out[extra(west, 2)] = jnp.where(lane < HALF, column, out[extra(west, 2)])
            column = last_swapped if u == 0 else last
            out[extra(east, 2)] = jnp.where(lane < HALF, out[extra(east, 2)], column)

    for k in range(devices // 2):
        halo(k)
    send(1, slot_rows, out.shape[1]).start()
    send(0, 0, slot_rows).wait()
    send(1, slot_rows, out.shape[1]).wait()


def regrid(cap, lat, lon, src, dev, blk, coupling, atm, mask, weights, depth, ocean, inverses):
    pairs, cells, width = weights.shape
    fields, levels, oy, ox = ocean.shape
    message = jax.ShapeDtypeStruct((fields, levels + SUB, ox), f32)
    batch = 64
    devices = lat * lon
    tall = lat * fields * cap + extra_rows(lat)
    return pl.pallas_call(
        functools.partial(regrid_kernel, cap, lat, lon, oy, batch),
        in_specs=[HBM] * 10,
        out_specs=[HBM, VMEM, VMEM],
        out_shape=[pltpu.HBM((lon, tall, LANES), f32), message, message],
        scratch_shapes=[
            pltpu.VMEM((lon, tall, LANES), f32),
            pltpu.VMEM((atm.shape[1] * SUB, LANES), f32),
            pltpu.VMEM((devices, LANES), jnp.int32),
            pltpu.SMEM((devices,), jnp.int32),
            pltpu.SMEM(src.shape, jnp.int32),
            pltpu.SMEM(dev.shape, jnp.int32),
            pltpu.SMEM(blk.shape, jnp.int32),
            pltpu.SMEM(coupling.shape, f32),
            pltpu.VMEM(atm.shape, bf16),
            pltpu.VMEM(mask.shape, jnp.int32),
            pltpu.VMEM(weights.shape, bf16),
            pltpu.VMEM(depth.shape, jnp.int32),
            pltpu.VMEM((2, fields, levels, ox), f32),
            pltpu.VMEM((2, fields, levels, levels), f32),
            pltpu.SemaphoreType.DMA((6,)),
            pltpu.SemaphoreType.DMA((2 * fields + 1, 2)),
            pltpu.SemaphoreType.DMA((pairs // batch,)),
            pltpu.SemaphoreType.DMA((2,)),
        ],
        compiler_params=pltpu.CompilerParams(vmem_limit_bytes=20 << 20),
        cost_estimate=pl.CostEstimate(flops=2 * 8 * pairs * cells * width, bytes_accessed=10 << 20, transcendentals=0),
        name="regrid",
    )(*in_hbm(src, dev, blk, coupling, atm, mask, weights, depth, ocean, inverses))


def mix_kernel(
    depth_h, state_h, inv_h, mixed_h, side_h, to_east, to_west, depth_ref, state, mixed, inv, side, in_sems, out_sems
):
    fields, oy, levels, _ = mixed.shape
    depth_copy = pltpu.make_async_copy(depth_h, depth_ref, in_sems.at[2 * fields, 0])
    depth_copy.start()

    def load(q, c):
        for i in range(SUB):
            row = c * SUB + i
            pltpu.make_async_copy(state_h.at[q, :, row, :], state.at[q, row], in_sems.at[2 * q, c]).start()
        here = (q, pl.ds(c * SUB, SUB))
        pltpu.make_async_copy(inv_h.at[here], inv.at[here], in_sems.at[2 * q + 1, c]).start()

    for c in range(oy // SUB):
        load(0, c)
    depth_copy.wait()
    level = iota((levels, LANES), 0)
    lane = iota((levels, LANES), 1)
    line = iota((1, LANES), 1)
    edge_depth = jnp.zeros((SUB, LANES), f32)
    for i in range(oy):
        turned = pltpu.roll(jnp.broadcast_to(depth_ref[i : i + 1, :].astype(f32), (SUB, LANES)), 2 * i + 1, 1)
        edge_depth = jnp.where(line // 2 == i, turned, edge_depth)

    def field(q, carry):
        @pl.when(q + 1 < fields)
        def _():
            for c in range(oy // SUB):
                load(q + 1, c)

        cells = jnp.zeros((levels, LANES), f32)
        for c in range(oy // SUB):
            here = (q, pl.ds(c * SUB, SUB))
            pltpu.make_async_copy(mixed_h.at[here], state.at[here], in_sems.at[2 * q, c]).wait()
            pltpu.make_async_copy(inv_h.at[here], inv.at[here], in_sems.at[2 * q + 1, c]).wait()
            for row in range(c * SUB, (c + 1) * SUB):
                a = inv[q, row, 0]
                m = solve_row(a, state[q, row], level < depth_ref[row : row + 1, :])
                mixed[q, row] = m
                cells = jnp.where(lane // 2 == row, pltpu.roll(m, 2 * row + 1, 1), cells)
                cells = jnp.where(lane // 2 == HALF // 2 + row, a[:, 0:1], cells)
            pltpu.make_async_copy(mixed.at[here], mixed_h.at[here], out_sems.at[q]).start()
        side[q, 0:levels] = cells
        side[q, levels : levels + SUB] = edge_depth
        return carry

    lax.fori_loop(0, fields, field, 0)
    side_copy = pltpu.make_async_copy(side, side_h, out_sems.at[fields])
    side_copy.start()
    even = line % 2 == 0
    for k in range(fields // 2):
        to_east[k] = jnp.where(even, side[2 * k], pltpu.roll(side[2 * k + 1], 1, 1))
        to_west[k] = jnp.where(even, pltpu.roll(side[2 * k], LANES - 1, 1), side[2 * k + 1])
    for q in range(fields):
        pltpu.make_async_copy(mixed.at[q], mixed_h.at[q], out_sems.at[q]).wait()
    side_copy.wait()


def mix(depth, state, inverses):
    fields, levels, oy, ox = state.shape
    edge_shape = jax.ShapeDtypeStruct((fields // 2, levels + SUB, ox), f32)
    full = (fields, oy, levels, ox)
    return pl.pallas_call(
        mix_kernel,
        in_specs=[HBM] * 3,
        out_specs=[HBM] * 2 + [VMEM] * 2,
        out_shape=[pltpu.HBM(full, f32), pltpu.HBM((fields, levels + SUB, ox), f32), edge_shape, edge_shape],
        scratch_shapes=[
            pltpu.VMEM(depth.shape, jnp.int32),
            pltpu.VMEM(full, f32),
            pltpu.VMEM(full, f32),
            pltpu.VMEM(inverses.shape, f32),
            pltpu.VMEM((fields, levels + SUB, ox), f32),
            pltpu.SemaphoreType.DMA((2 * fields + 1, oy // SUB)),
            pltpu.SemaphoreType.DMA((fields + 1,)),
        ],
        compiler_params=pltpu.CompilerParams(vmem_limit_bytes=32 << 20),
        cost_estimate=pl.CostEstimate(flops=2 * 4 * fields * oy * levels * levels * ox, bytes_accessed=16 << 20, transcendentals=0),
        name="mix",
    )(*in_hbm(depth, state, inverses))


def collect_kernel(cap, fields, oy, recv, after_mix, after_north, after_south, out):
    lat = out.shape[0]
    lon = recv.shape[0]
    per = fields * cap
    slot_rows = lat * per
    group = LANES // per
    forced = fields * oy
    square_row = iota((LANES, LANES), 0).astype(f32)
    line = iota((1, LANES), 1)
    row = iota((2 * oy, LANES), 0).astype(f32)
    lane_base = ((line % fields) * oy).astype(f32)
    lane_side = (line // HALF).astype(f32)
    small_row, small_lane = iota((SUB, LANES), 0), iota((SUB, LANES), 1)
    pick = jnp.where((small_lane % fields == small_row) & (small_lane % HALF < per), 1.0, 0.0).astype(bf16)
    nothing = jnp.zeros((fields, LANES), f32)
    for a in range(lat):
        total = jnp.zeros((LANES, 2 * LANES), f32)
        for tile in range(lon // group):
            places = [tile * group + s for s in range(group)]
            named = slice(slot_rows + 3 * a, slot_rows + 3 * a + 1)
            ids = recv[places[0], named, :]
            for s in range(1, group):
                ids = jnp.where(line // per == s, recv[places[s], named, :], ids)
            hot = jnp.where(square_row == ids, 1.0, 0.0).astype(bf16)
            high, low = split(jnp.concatenate([recv[p, a * per : (a + 1) * per, :] for p in places], axis=0))
            total = total + matmul(hot, jnp.concatenate([high, low], axis=1))
        total = total[:, :LANES] + total[:, LANES:]
        out[a, 0:forced] = total
        if a == 0:
            out[a, forced : forced + fields] = nothing
        if a == lat - 1:
            out[a, forced + fields : forced + 2 * fields] = nothing
        for q in range(fields):
            if a + 1 < lat:
                out[a + 1, forced + q : forced + q + 1] = total[q * oy + oy - 1 : q * oy + oy]
            if a > 0:
                out[a - 1, forced + fields + q : forced + fields + q + 1] = total[q * oy : q * oy + 1]
        spread = jnp.zeros((2 * oy, LANES), f32)
        for b in range(lon):
            extra = recv[b, slot_rows + 3 * a + 1 : slot_rows + 3 * a + 3, :]
            place = 2.0 * (extra[0:1] - lane_base) + lane_side
            spread = spread + jnp.where(place == row, extra[1:2], 0.0)
        high, low = split(padded_rows(spread, LANES).T)
        out[a, forced + SUB : forced + 2 * SUB] = matmul(pick, high) + matmul(pick, low)


def collect(cap, fields, oy, lat, received, after):
    return pl.pallas_call(
        functools.partial(collect_kernel, cap, fields, oy),
        in_specs=[VMEM] + [pl.BlockSpec(memory_space=pl.ANY)] * 3,
        out_specs=VMEM,
        out_shape=jax.ShapeDtypeStruct((lat, fields * oy + 2 * SUB, LANES), f32),
        compiler_params=pltpu.CompilerParams(vmem_limit_bytes=16 << 20),
        name="collect",
    )(received, *after)


def finish_kernel(
    recv, depth_ref, mixed_h, own_h, north_h, south_h, east, west,
    out_h, own, north, south, forcing, z, keep, halo, z_north, z_south, mixed, stage, edge_sems, in_sems, out_sems,
):
    fields, oy, levels, _ = mixed.shape
    level = iota((levels, LANES), 0)
    lanes = iota((levels, LANES), 1)
    square_row = iota((LANES, LANES), 0)
    square_lane = iota((LANES, LANES), 1)
    line = iota((1, LANES), 1)
    even = line % 2 == 0
    edges = [
        pltpu.make_async_copy(a, b, edge_sems.at[k])
        for k, (a, b) in enumerate(((own_h, own), (north_h, north), (south_h, south)))
    ]
    for copy in edges:
        copy.start()

    def load(q, c):
        here = (q, pl.ds(c * SUB, SUB))
        return pltpu.make_async_copy(mixed_h.at[here], mixed.at[here], in_sems.at[q, c])

    for c in range(oy // SUB):
        load(0, c).start()

    total = recv[0]
    for a in range(1, recv.shape[0]):
        total = total + recv[a]
    forced_rows = fields * oy
    forcing[...] = total[0:forced_rows]
    rows = total[forced_rows : forced_rows + SUB]
    columns = total[forced_rows + SUB :]

    for copy in edges:
        copy.wait()
    depth = depth_ref[...]
    wide = iota((oy, LANES), 1)

    def upright(ref):
        value = jnp.where(wide == 2 * iota((oy, LANES), 0), ref[0, levels : levels + 1, :], 0.0)
        return jnp.sum(value, axis=1, keepdims=True).astype(jnp.int32)

    to_east = jnp.where(wide == LANES - 1, upright(east), pltpu.roll(depth, LANES - 1, 1))
    to_west = jnp.where(wide == 0, upright(west), pltpu.roll(depth, 1, 1))
    to_north = jnp.concatenate([north[0, levels : levels + 1, :].astype(jnp.int32), depth[: oy - 1]], axis=0)
    to_south = jnp.concatenate([depth[1:], south[0, levels : levels + 1, :].astype(jnp.int32)], axis=0)
    for i in range(oy):
        sides = jnp.where(level < to_east[i : i + 1], diffusion_rate, 0.0)
        for other in (to_west, to_north, to_south):
            sides = sides + jnp.where(level < other[i : i + 1], diffusion_rate, 0.0)
        keep[i] = 1.0 - sides

    def outer(target, ref, start):
        names = padded_rows(
            jnp.concatenate([ref[q, levels + 1 : levels + 2, :] for q in range(fields)], axis=0), LANES
        ).T
        active = level < ref[0, levels : levels + 1, :].astype(jnp.int32)
        for q in range(fields):
            value = ref[q, 0:levels] + names[0:levels, q : q + 1] * rows[start + q : start + q + 1]
            target[q] = jnp.where(active, value, 0.0)

    outer(z_north, north, 0)
    outer(z_south, south, fields)
    for q in range(fields):
        if q % 2:
            cells = jnp.where(even, pltpu.roll(east[q // 2], LANES - 1, 1), west[q // 2])
        else:
            cells = jnp.where(even, east[q // 2], pltpu.roll(west[q // 2], 1, 1))
        names = pltpu.roll(cells, HALF, 1)
        active = level < cells[levels : levels + 1].astype(jnp.int32)
        value = cells[0:levels] + names[0:levels] * columns[q : q + 1]
        halo[q] = jnp.where(active & (line < 2 * oy), value, 0.0)

    both = jnp.where((square_row == square_lane + 1) | (square_row == square_lane - 1), 1.0, 0.0).astype(bf16)
    both = jnp.concatenate([both, both], axis=0)
    ones = jnp.ones((LANES, LANES), bf16)
    block = 2 * SUB
    ends = (lanes == 0) | (lanes == LANES - 1)

    def field(q, carry):
        @pl.when(q + 1 < fields)
        def _():
            for c in range(oy // SUB):
                load(q + 1, c).start()

        z[0] = z_north[q]
        z[oy + 1] = z_south[q]
        edge = halo[q]
        names = own[q, 0:levels]
        high = names.astype(bf16).astype(f32)
        names = jnp.where(even, high, names - high)

        def solve(c):
            rows_here = range(c * block, (c + 1) * block)
            for part in range(rows_here.start // SUB, rows_here.stop // SUB):
                load(q, part).wait()
            first = matmul(
                jnp.concatenate(
                    [(names * jnp.where(line // 2 == HALF // 2 + r, 1.0, 0.0)).astype(bf16) for r in rows_here], axis=0
                ),
                ones,
            )
            for i, r in enumerate(rows_here):
                first_here = first[i * levels : (i + 1) * levels]
                forced = mixed[q, r] + first_here * forcing[pl.ds(q * oy + r, 1), :]
                z[r + 1] = jnp.where(level < depth_ref[r : r + 1, :], forced, 0.0)

        def diffuse(c):
            start = c * block
            high, low = split(z[start + 1 : start + 1 + block].reshape(block * levels, LANES))
            sides = matmul(jnp.concatenate([high, low], axis=1), both)
            for i in range(block):
                r = start + i
                outside = jnp.where(ends, pltpu.roll(edge, LANES - 1 - 2 * r, 1), 0.0)
                around = (z[r] + z[r + 2]) + (sides[i * levels : (i + 1) * levels] + outside)
                active = level < depth_ref[r : r + 1, :]
                stage[q, r] = jnp.where(active, z[r + 1] * keep[r] + diffusion_rate * around, mixed[q, r])
            for r in range(start, start + block):
                pltpu.make_async_copy(stage.at[q, r], out_h.at[q, :, r, :], out_sems.at[q]).start()

        solve(0)
        for c in range(1, oy // block):
            solve(c)
            diffuse(c - 1)
        diffuse(oy // block - 1)
        return carry

    lax.fori_loop(0, fields, field, 0)
    for q in range(fields):
        pltpu.make_async_copy(stage.at[q], mixed_h.at[q], out_sems.at[q]).wait()


def finish(received, depth, mixed, own, halos):
    fields, oy, levels, ox = mixed.shape
    edge = pltpu.VMEM((fields, levels, ox), f32)
    message = pltpu.VMEM((fields, levels + SUB, ox), f32)
    full = pltpu.VMEM((fields, oy, levels, ox), f32)
    return pl.pallas_call(
        finish_kernel,
        in_specs=[VMEM] * 2 + [HBM] * 4 + [VMEM] * 2,
        out_specs=HBM,
        out_shape=pltpu.HBM((fields, levels, oy, ox), f32),
        scratch_shapes=[
            message,
            message,
            message,
            pltpu.VMEM((fields * oy, ox), f32),
            pltpu.VMEM((oy + 2, levels, ox), f32),
            pltpu.VMEM((oy, levels, ox), f32),
            edge,
            edge,
            edge,
            full,
            full,
            pltpu.SemaphoreType.DMA((3,)),
            pltpu.SemaphoreType.DMA((fields, oy // SUB)),
            pltpu.SemaphoreType.DMA((fields,)),
        ],
        compiler_params=pltpu.CompilerParams(vmem_limit_bytes=32 << 20),
        cost_estimate=pl.CostEstimate(flops=20 * fields * oy * levels * ox, bytes_accessed=12 << 20, transcendentals=0),
        name="finish",
    )(received, depth, *in_hbm(mixed, own, *halos[0:2]), *halos[2:])


def shift(x, axis, step, wrap):
    count = lax.axis_size(axis)
    pairs = [(i, (i + step) % count) for i in range(count) if wrap or 0 <= i + step < count]
    return lax.ppermute(x, axis, pairs)


def on_device(
    atm_flux, sea_mask, src_block, dest_dev, dest_block, intersection_weights, coupling, inverses, ocean_state,
    depth_levels,
):
    lat, lon = lax.axis_size("lat"), lax.axis_size("lon")
    fields, _, oy, _ = ocean_state.shape
    cap = max(SUB, 2 * src_block.shape[0] // (lat * lon))
    slots, north, south = regrid(
        cap, lat, lon, src_block, dest_dev[:, 0], dest_block, coupling, atm_flux, sea_mask,
        intersection_weights, depth_levels, ocean_state, inverses,
    )
    in_plane = lax.all_to_all(slots, "lon", 0, 0, tiled=True)
    mixed, side, to_east, to_west = mix(depth_levels, ocean_state, inverses)
    halos = (
        shift(south, "lat", 1, False),
        shift(north, "lat", -1, False),
        shift(to_west, "lon", -1, True),
        shift(to_east, "lon", 1, True),
    )
    received = lax.all_to_all(collect(cap, fields, oy, lat, in_plane, (to_east, *halos[0:2])), "lat", 0, 0, tiled=True)
    return finish(received, depth_levels, mixed, side, halos)


def solution(mesh):
    placed = (
        P(None, "lat", "lon"),
        P("lat", "lon"),
        P(("lat", "lon")),
        P(("lat", "lon"), None),
        P(("lat", "lon")),
        P(("lat", "lon"), None, None),
        P(),
        P(None, "lat", "lon", None, None),
        P(None, None, "lat", "lon"),
        P("lat", "lon"),
    )
    return jax.shard_map(
        on_device,
        mesh=mesh,
        in_specs=placed,
        out_specs=P(None, None, "lat", "lon"),
        check_vma=False,
    )
```

```python
import functools

import jax
import jax.numpy as jnp
from jax import lax
from jax.experimental import pallas as pl
from jax.experimental.pallas import tpu as pltpu
from jax.sharding import PartitionSpec as P

diffusion_rate = 0.2
LANES = 128
HALF = 64
SUB = 8
f32 = jnp.float32
bf16 = jnp.bfloat16
HBM = pl.BlockSpec(memory_space=pltpu.HBM)
VMEM = pl.BlockSpec(memory_space=pltpu.VMEM)


def split(x):
    high = x.astype(bf16)
    return high, (x - high.astype(f32)).astype(bf16)


def in_hbm(*arrays):
    return [pltpu.with_memory_space_constraint(x, pltpu.HBM) for x in arrays]


def iota(shape, dim):
    return lax.broadcasted_iota(jnp.int32, shape, dim)


def matmul(a, b):
    return jnp.dot(a, b, preferred_element_type=f32)


def padded_rows(x, rows):
    return x if x.shape[0] == rows else jnp.concatenate([x, jnp.zeros((rows - x.shape[0], LANES), x.dtype)], axis=0)


def solve_row(a, x, active):
    levels = x.shape[0]
    a_high, a_low = split(a)
    r_high, r_low = split(jnp.where(active, x, 0.0))
    product = matmul(jnp.concatenate([a_high, a_low], axis=0), jnp.concatenate([r_high, r_low], axis=1))
    solved = product[:levels, :LANES] + (product[levels:, :LANES] + product[:levels, LANES:])
    return jnp.where(active, solved, x)


def outer_messages(refs, depth_ref, state, inv):
    _, fields, levels, _ = state.shape
    oy = depth_ref.shape[0]
    level = iota((levels, LANES), 0)
    for k, (row, ref) in enumerate(zip((0, oy - 1), refs)):
        depth = depth_ref[row : row + 1, :]
        names = jnp.zeros((levels, LANES), f32)
        for q in range(fields):
            a = inv[k, q]
            ref[q, 0:levels] = solve_row(a, state[k, q], level < depth)
            names = jnp.where(iota((levels, LANES), 1) == q, a[:, 0:1], names)
        names = padded_rows(names, LANES).T
        for q in range(fields):
            ref[q, levels : levels + SUB] = jnp.concatenate(
                [depth.astype(f32), names[q : q + 1], jnp.zeros((SUB - 2, LANES), f32)], axis=0
            )


def extra_rows(lat):
    return -(-3 * lat // SUB) * SUB


def regrid_kernel(
    cap, lat, lon, oy, batch,
    src_h, dev_h, blk_h, coupling_h, atm_h, mask_h, weights_h, depth_h, state_h, inv_h,
    out_h, north, south,
    out, rows, ids, count, src, dev, blk, coupling, atm, mask, weights, depth_ref, state, inv,
    small_sem, outer_sem, big_sem, out_sem,
):
    fluxes, atm_rows, _ = atm.shape
    fields = coupling.shape[0]
    devices = lat * lon
    per = fields * cap
    slot_rows = lat * per
    parts = weights.shape[0] // batch
    ahead = min(2, parts)

    def big(k):
        here = pl.ds(pl.multiple_of(k * batch, batch), batch)
        return pltpu.make_async_copy(weights_h.at[here], weights.at[here], big_sem.at[k])

    small = [
        pltpu.make_async_copy(a, b, small_sem.at[k])
        for k, (a, b) in enumerate(
            (
                (coupling_h, coupling), (atm_h, atm), (mask_h, mask),
                (src_h, src), (dev_h, dev), (blk_h, blk),
            )
        )
    ]
    outer = [pltpu.make_async_copy(depth_h, depth_ref, outer_sem.at[2 * fields, 0])]
    for q in range(fields):
        for k, row in enumerate((0, oy - 1)):
            outer.append(pltpu.make_async_copy(state_h.at[q, :, row, :], state.at[k, q], outer_sem.at[2 * q, k]))
            outer.append(pltpu.make_async_copy(inv_h.at[q, row, 0], inv.at[k, q], outer_sem.at[2 * q + 1, k]))
    for copy in small + outer:
        copy.start()
    for k in range(ahead):
        big(k).start()

    def clear_count(d, carry):
        count[d] = 0
        return carry

    def clear(b, carry):
        out[b] = jnp.zeros(out.shape[1:], f32)
        return carry

    lax.fori_loop(0, devices, clear_count, 0)
    lax.fori_loop(0, lon, clear, 0)
    ids[...] = jnp.full(ids.shape, -1, jnp.int32)
    for copy in small:
        copy.wait()
    for tile in range(atm_rows // 16):
        here = slice(tile * 16, tile * 16 + 16)
        sea = mask[here, :].astype(f32)
        flux = [atm[f, here, :].astype(f32) * sea for f in range(fluxes)]
        for q in range(fields):
            total = coupling[q, 0] * flux[0]
            for f in range(1, fluxes):
                total = total + coupling[q, f] * flux[f]
            high = total.astype(bf16).astype(f32)
            rows[pl.ds(tile * 16 * SUB + q, 16, stride=SUB), :] = high
            rows[pl.ds(tile * 16 * SUB + fields + q, 16, stride=SUB), :] = total - high

    for copy in outer:
        copy.wait()
    outer_messages((north, south), depth_ref, state, inv)

    lane = iota((1, LANES), 1)
    lane_slot = (lane % per) // fields
    lane_row = (lane % fields) * oy

    bits = lon.bit_length() - 1

    def place(d):
        if isinstance(d, int):
            return d // lon, d % lon
        if lon == 1 << bits:
            return lax.shift_right_logical(d, bits), d & (lon - 1)
        return lax.div(d, lon), lax.rem(d, lon)

    def extra(d, k):
        a, b = place(d)
        return b, pl.ds(slot_rows + 3 * a + k, 1)

    def slots(d):
        a, b = place(d)
        return padded_rows(out[b, a * per : (a + 1) * per, :], HALF)

    def part(k, carry):
        big(k).wait()

        @pl.when(k + ahead < parts)
        def _():
            big(k + ahead).start()

        for u in range(0, batch, 2):
            p = k * batch + u
            x = jnp.concatenate(
                [rows[pl.ds(pl.multiple_of(src[p + v] * SUB, SUB), SUB), :] for v in range(2)], axis=0
            ).astype(bf16)
            both = matmul(x, jnp.concatenate([weights[p], weights[p + 1]], axis=1))
            for v in range(2):
                d = dev[p + v]
                slot = jnp.minimum(count[d], cap - 1)
                count[d] = slot + 1
                half = both[v * SUB : v * SUB + SUB, v * LANES : (v + 1) * LANES]
                a, b = place(d)
                out[b, pl.ds(a * per + slot * fields, fields), :] = half[0:fields] + half[fields : 2 * fields]
                line = ids[pl.ds(d, 1), :]
                ids[pl.ds(d, 1), :] = jnp.where(lane_slot == slot, lane_row + blk[p + v], line)
        return carry

    lax.fori_loop(0, parts, part, 0)

    def send(k, start, stop):
        return pltpu.make_async_copy(out.at[:, start:stop, :], out_h.at[:, start:stop, :], out_sem.at[k])

    send(0, 0, slot_rows).start()

    def halo(k):
        d = 2 * k
        turned = jnp.concatenate([slots(d + u) for u in range(2)], axis=0).T
        first, last = turned[0:1], turned[LANES - 1 : LANES]
        first_swapped = pltpu.roll(turned[0:SUB], HALF, 1)[0:1]
        last_swapped = pltpu.roll(turned[LANES - SUB : LANES], HALF, 1)[SUB - 1 : SUB]
        for u in range(2):
            _, b = place(d + u)
            east = d + u - b + (b + 1) % lon
            west = d + u - b + (b - 1) % lon
            out[extra(d + u, 0)] = ids[pl.ds(d + u, 1), :].astype(f32)
            sides = jnp.where(lane < HALF, ids[pl.ds(east, 1), :], ids[pl.ds(west, 1), :])
            out[extra(d + u, 1)] = sides.astype(f32)
            column = first if u == 0 else first_swapped
            out[extra(west, 2)] = jnp.where(lane < HALF, column, out[extra(west, 2)])
            column = last_swapped if u == 0 else last
            out[extra(east, 2)] = jnp.where(lane < HALF, out[extra(east, 2)], column)

    for k in range(devices // 2):
        halo(k)
    send(1, slot_rows, out.shape[1]).start()
    send(0, 0, slot_rows).wait()
    send(1, slot_rows, out.shape[1]).wait()


def regrid(cap, lat, lon, src, dev, blk, coupling, atm, mask, weights, depth, ocean, inverses):
    pairs, cells, width = weights.shape
    fields, levels, oy, ox = ocean.shape
    message = jax.ShapeDtypeStruct((fields, levels + SUB, ox), f32)
    batch = 64
    devices = lat * lon
    tall = lat * fields * cap + extra_rows(lat)
    return pl.pallas_call(
        functools.partial(regrid_kernel, cap, lat, lon, oy, batch),
        in_specs=[HBM] * 10,
        out_specs=[HBM, VMEM, VMEM],
        out_shape=[pltpu.HBM((lon, tall, LANES), f32), message, message],
        scratch_shapes=[
            pltpu.VMEM((lon, tall, LANES), f32),
            pltpu.VMEM((atm.shape[1] * SUB, LANES), f32),
            pltpu.VMEM((devices, LANES), jnp.int32),
            pltpu.SMEM((devices,), jnp.int32),
            pltpu.SMEM(src.shape, jnp.int32),
            pltpu.SMEM(dev.shape, jnp.int32),
            pltpu.SMEM(blk.shape, jnp.int32),
            pltpu.SMEM(coupling.shape, f32),
            pltpu.VMEM(atm.shape, bf16),
            pltpu.VMEM(mask.shape, jnp.int32),
            pltpu.VMEM(weights.shape, bf16),
            pltpu.VMEM(depth.shape, jnp.int32),
            pltpu.VMEM((2, fields, levels, ox), f32),
            pltpu.VMEM((2, fields, levels, levels), f32),
            pltpu.SemaphoreType.DMA((6,)),
            pltpu.SemaphoreType.DMA((2 * fields + 1, 2)),
            pltpu.SemaphoreType.DMA((pairs // batch,)),
            pltpu.SemaphoreType.DMA((2,)),
        ],
        compiler_params=pltpu.CompilerParams(vmem_limit_bytes=20 << 20),
        cost_estimate=pl.CostEstimate(flops=2 * 8 * pairs * cells * width, bytes_accessed=10 << 20, transcendentals=0),
        name="regrid",
    )(*in_hbm(src, dev, blk, coupling, atm, mask, weights, depth, ocean, inverses))


def mix_kernel(
    depth_h, state_h, inv_h, mixed_h, side_h, to_east, to_west, depth_ref, state, mixed, inv, side, in_sems, out_sems
):
    fields, oy, levels, _ = mixed.shape
    depth_copy = pltpu.make_async_copy(depth_h, depth_ref, in_sems.at[2 * fields, 0])
    depth_copy.start()

    def load(q, c):
        for i in range(SUB):
            row = c * SUB + i
            pltpu.make_async_copy(state_h.at[q, :, row, :], state.at[q, row], in_sems.at[2 * q, c]).start()
        here = (q, pl.ds(c * SUB, SUB))
        pltpu.make_async_copy(inv_h.at[here], inv.at[here], in_sems.at[2 * q + 1, c]).start()

    for c in range(oy // SUB):
        load(0, c)
    depth_copy.wait()
    level = iota((levels, LANES), 0)
    lane = iota((levels, LANES), 1)
    line = iota((1, LANES), 1)
    edge_depth = jnp.zeros((SUB, LANES), f32)
    for i in range(oy):
        turned = pltpu.roll(jnp.broadcast_to(depth_ref[i : i + 1, :].astype(f32), (SUB, LANES)), 2 * i + 1, 1)
        edge_depth = jnp.where(line // 2 == i, turned, edge_depth)

    def field(q, carry):
        @pl.when(q + 1 < fields)
        def _():
            for c in range(oy // SUB):
                load(q + 1, c)

        cells = jnp.zeros((levels, LANES), f32)
        for c in range(oy // SUB):
            here = (q, pl.ds(c * SUB, SUB))
            pltpu.make_async_copy(mixed_h.at[here], state.at[here], in_sems.at[2 * q, c]).wait()
            pltpu.make_async_copy(inv_h.at[here], inv.at[here], in_sems.at[2 * q + 1, c]).wait()
            for row in range(c * SUB, (c + 1) * SUB):
                a = inv[q, row, 0]
                m = solve_row(a, state[q, row], level < depth_ref[row : row + 1, :])
                mixed[q, row] = m
                cells = jnp.where(lane // 2 == row, pltpu.roll(m, 2 * row + 1, 1), cells)
                cells = jnp.where(lane // 2 == HALF // 2 + row, a[:, 0:1], cells)
            pltpu.make_async_copy(mixed.at[here], mixed_h.at[here], out_sems.at[q]).start()
        side[q, 0:levels] = cells
        side[q, levels : levels + SUB] = edge_depth
        return carry

    lax.fori_loop(0, fields, field, 0)
    side_copy = pltpu.make_async_copy(side, side_h, out_sems.at[fields])
    side_copy.start()
    even = line % 2 == 0
    for k in range(fields // 2):
        to_east[k] = jnp.where(even, side[2 * k], pltpu.roll(side[2 * k + 1], 1, 1))
        to_west[k] = jnp.where(even, pltpu.roll(side[2 * k], LANES - 1, 1), side[2 * k + 1])
    for q in range(fields):
        pltpu.make_async_copy(mixed.at[q], mixed_h.at[q], out_sems.at[q]).wait()
    side_copy.wait()


def mix(depth, state, inverses):
    fields, levels, oy, ox = state.shape
    edge_shape = jax.ShapeDtypeStruct((fields // 2, levels + SUB, ox), f32)
    full = (fields, oy, levels, ox)
    return pl.pallas_call(
        mix_kernel,
        in_specs=[HBM] * 3,
        out_specs=[HBM] * 2 + [VMEM] * 2,
        out_shape=[pltpu.HBM(full, f32), pltpu.HBM((fields, levels + SUB, ox), f32), edge_shape, edge_shape],
        scratch_shapes=[
            pltpu.VMEM(depth.shape, jnp.int32),
            pltpu.VMEM(full, f32),
            pltpu.VMEM(full, f32),
            pltpu.VMEM(inverses.shape, f32),
            pltpu.VMEM((fields, levels + SUB, ox), f32),
            pltpu.SemaphoreType.DMA((2 * fields + 1, oy // SUB)),
            pltpu.SemaphoreType.DMA((fields + 1,)),
        ],
        compiler_params=pltpu.CompilerParams(vmem_limit_bytes=32 << 20),
        cost_estimate=pl.CostEstimate(flops=2 * 4 * fields * oy * levels * levels * ox, bytes_accessed=16 << 20, transcendentals=0),
        name="mix",
    )(*in_hbm(depth, state, inverses))


def collect_kernel(cap, fields, oy, recv, after_mix, after_north, after_south, out):
    lat = out.shape[0]
    lon = recv.shape[0]
    per = fields * cap
    slot_rows = lat * per
    group = LANES // per
    forced = fields * oy
    square_row = iota((LANES, LANES), 0).astype(f32)
    line = iota((1, LANES), 1)
    row = iota((2 * oy, LANES), 0).astype(f32)
    lane_base = ((line % fields) * oy).astype(f32)
    lane_side = (line // HALF).astype(f32)
    small_row, small_lane = iota((SUB, LANES), 0), iota((SUB, LANES), 1)
    pick = jnp.where((small_lane % fields == small_row) & (small_lane % HALF < per), 1.0, 0.0).astype(bf16)
    nothing = jnp.zeros((fields, LANES), f32)
    for a in range(lat):
        total = jnp.zeros((LANES, 2 * LANES), f32)
        for tile in range(lon // group):
            places = [tile * group + s for s in range(group)]
            named = slice(slot_rows + 3 * a, slot_rows + 3 * a + 1)
            ids = recv[places[0], named, :]
            for s in range(1, group):
                ids = jnp.where(line // per == s, recv[places[s], named, :], ids)
            hot = jnp.where(square_row == ids, 1.0, 0.0).astype(bf16)
            high, low = split(jnp.concatenate([recv[p, a * per : (a + 1) * per, :] for p in places], axis=0))
            total = total + matmul(hot, jnp.concatenate([high, low], axis=1))
        total = total[:, :LANES] + total[:, LANES:]
        out[a, 0:forced] = total
        if a == 0:
            out[a, forced : forced + fields] = nothing
        if a == lat - 1:
            out[a, forced + fields : forced + 2 * fields] = nothing
        for q in range(fields):
            if a + 1 < lat:
                out[a + 1, forced + q : forced + q + 1] = total[q * oy + oy - 1 : q * oy + oy]
            if a > 0:
                out[a - 1, forced + fields + q : forced + fields + q + 1] = total[q * oy : q * oy + 1]
        spread = jnp.zeros((2 * oy, LANES), f32)
        for b in range(lon):
            extra = recv[b, slot_rows + 3 * a + 1 : slot_rows + 3 * a + 3, :]
            place = 2.0 * (extra[0:1] - lane_base) + lane_side
            spread = spread + jnp.where(place == row, extra[1:2], 0.0)
        high, low = split(padded_rows(spread, LANES).T)
        out[a, forced + SUB : forced + 2 * SUB] = matmul(pick, high) + matmul(pick, low)


def collect(cap, fields, oy, lat, received, after):
    return pl.pallas_call(
        functools.partial(collect_kernel, cap, fields, oy),
        in_specs=[VMEM] + [pl.BlockSpec(memory_space=pl.ANY)] * 3,
        out_specs=VMEM,
        out_shape=jax.ShapeDtypeStruct((lat, fields * oy + 2 * SUB, LANES), f32),
        compiler_params=pltpu.CompilerParams(vmem_limit_bytes=16 << 20),
        name="collect",
    )(received, *after)


def finish_kernel(
    recv, depth_ref, mixed_h, own_h, north_h, south_h, east, west,
    out_h, own, north, south, forcing, z, keep, halo, z_north, z_south, mixed, stage, edge_sems, in_sems, out_sems,
):
    fields, oy, levels, _ = mixed.shape
    level = iota((levels, LANES), 0)
    lanes = iota((levels, LANES), 1)
    square_row = iota((LANES, LANES), 0)
    square_lane = iota((LANES, LANES), 1)
    line = iota((1, LANES), 1)
    even = line % 2 == 0
    edges = [
        pltpu.make_async_copy(a, b, edge_sems.at[k])
        for k, (a, b) in enumerate(((own_h, own), (north_h, north), (south_h, south)))
    ]
    for copy in edges:
        copy.start()

    def load(q, c):
        here = (q, pl.ds(c * SUB, SUB))
        return pltpu.make_async_copy(mixed_h.at[here], mixed.at[here], in_sems.at[q, c])

    for c in range(oy // SUB):
        load(0, c).start()

    total = recv[0]
    for a in range(1, recv.shape[0]):
        total = total + recv[a]
    forced_rows = fields * oy
    forcing[...] = total[0:forced_rows]
    rows = total[forced_rows : forced_rows + SUB]
    columns = total[forced_rows + SUB :]

    for copy in edges:
        copy.wait()
    depth = depth_ref[...]
    wide = iota((oy, LANES), 1)

    def upright(ref):
        value = jnp.where(wide == 2 * iota((oy, LANES), 0), ref[0, levels : levels + 1, :], 0.0)
        return jnp.sum(value, axis=1, keepdims=True).astype(jnp.int32)

    to_east = jnp.where(wide == LANES - 1, upright(east), pltpu.roll(depth, LANES - 1, 1))
    to_west = jnp.where(wide == 0, upright(west), pltpu.roll(depth, 1, 1))
    to_north = jnp.concatenate([north[0, levels : levels + 1, :].astype(jnp.int32), depth[: oy - 1]], axis=0)
    to_south = jnp.concatenate([depth[1:], south[0, levels : levels + 1, :].astype(jnp.int32)], axis=0)
    for i in range(oy):
        sides = jnp.where(level < to_east[i : i + 1], diffusion_rate, 0.0)
        for other in (to_west, to_north, to_south):
            sides = sides + jnp.where(level < other[i : i + 1], diffusion_rate, 0.0)
        keep[i] = 1.0 - sides

    def outer(target, ref, start):
        names = padded_rows(
            jnp.concatenate([ref[q, levels + 1 : levels + 2, :] for q in range(fields)], axis=0), LANES
        ).T
        active = level < ref[0, levels : levels + 1, :].astype(jnp.int32)
        for q in range(fields):
            value = ref[q, 0:levels] + names[0:levels, q : q + 1] * rows[start + q : start + q + 1]
            target[q] = jnp.where(active, value, 0.0)

    outer(z_north, north, 0)
    outer(z_south, south, fields)
    for q in range(fields):
        if q % 2:
            cells = jnp.where(even, pltpu.roll(east[q // 2], LANES - 1, 1), west[q // 2])
        else:
            cells = jnp.where(even, east[q // 2], pltpu.roll(west[q // 2], 1, 1))
        names = pltpu.roll(cells, HALF, 1)
        active = level < cells[levels : levels + 1].astype(jnp.int32)
        value = cells[0:levels] + names[0:levels] * columns[q : q + 1]
        halo[q] = jnp.where(active & (line < 2 * oy), value, 0.0)

    both = jnp.where((square_row == square_lane + 1) | (square_row == square_lane - 1), 1.0, 0.0).astype(bf16)
    both = jnp.concatenate([both, both], axis=0)
    ones = jnp.ones((LANES, LANES), bf16)
    block = 2 * SUB
    ends = (lanes == 0) | (lanes == LANES - 1)

    def field(q):
        if q + 1 < fields:
            for c in range(oy // SUB):
                load(q + 1, c).start()

        z[0] = z_north[q]
        z[oy + 1] = z_south[q]
        edge = halo[q]
        names = own[q, 0:levels]
        high = names.astype(bf16).astype(f32)
        names = jnp.where(even, high, names - high)

        def solve(c):
            rows_here = range(c * block, (c + 1) * block)
            for part in range(rows_here.start // SUB, rows_here.stop // SUB):
                load(q, part).wait()
            first = matmul(
                jnp.concatenate(
                    [(names * jnp.where(line // 2 == HALF // 2 + r, 1.0, 0.0)).astype(bf16) for r in rows_here], axis=0
                ),
                ones,
            )
            for i, r in enumerate(rows_here):
                first_here = first[i * levels : (i + 1) * levels]
                forced = mixed[q, r] + first_here * forcing[pl.ds(q * oy + r, 1), :]
                z[r + 1] = jnp.where(level < depth_ref[r : r + 1, :], forced, 0.0)

        def diffuse(c):
            start = c * block
            high, low = split(z[start + 1 : start + 1 + block].reshape(block * levels, LANES))
            sides = matmul(jnp.concatenate([high, low], axis=1), both)
            for i in range(block):
                r = start + i
                outside = jnp.where(ends, pltpu.roll(edge, LANES - 1 - 2 * r, 1), 0.0)
                around = (z[r] + z[r + 2]) + (sides[i * levels : (i + 1) * levels] + outside)
                active = level < depth_ref[r : r + 1, :]
                stage[q, r] = jnp.where(active, z[r + 1] * keep[r] + diffusion_rate * around, mixed[q, r])
            for r in range(start, start + block):
                pltpu.make_async_copy(stage.at[q, r], out_h.at[q, :, r, :], out_sems.at[q]).start()

        solve(0)
        for c in range(1, oy // block):
            solve(c)
            diffuse(c - 1)
        diffuse(oy // block - 1)

    for q in range(fields):
        field(q)
    for q in range(fields):
        pltpu.make_async_copy(stage.at[q], mixed_h.at[q], out_sems.at[q]).wait()


def finish(received, depth, mixed, own, halos):
    fields, oy, levels, ox = mixed.shape
    edge = pltpu.VMEM((fields, levels, ox), f32)
    message = pltpu.VMEM((fields, levels + SUB, ox), f32)
    full = pltpu.VMEM((fields, oy, levels, ox), f32)
    return pl.pallas_call(
        finish_kernel,
        in_specs=[VMEM] * 2 + [HBM] * 4 + [VMEM] * 2,
        out_specs=HBM,
        out_shape=pltpu.HBM((fields, levels, oy, ox), f32),
        scratch_shapes=[
            message,
            message,
            message,
            pltpu.VMEM((fields * oy, ox), f32),
            pltpu.VMEM((oy + 2, levels, ox), f32),
            pltpu.VMEM((oy, levels, ox), f32),
            edge,
            edge,
            edge,
            full,
            full,
            pltpu.SemaphoreType.DMA((3,)),
            pltpu.SemaphoreType.DMA((fields, oy // SUB)),
            pltpu.SemaphoreType.DMA((fields,)),
        ],
        compiler_params=pltpu.CompilerParams(vmem_limit_bytes=32 << 20),
        cost_estimate=pl.CostEstimate(flops=20 * fields * oy * levels * ox, bytes_accessed=12 << 20, transcendentals=0),
        name="finish",
    )(received, depth, *in_hbm(mixed, own, *halos[0:2]), *halos[2:])


def shift(x, axis, step, wrap):
    count = lax.axis_size(axis)
    pairs = [(i, (i + step) % count) for i in range(count) if wrap or 0 <= i + step < count]
    return lax.ppermute(x, axis, pairs)


def on_device(
    atm_flux, sea_mask, src_block, dest_dev, dest_block, intersection_weights, coupling, inverses, ocean_state,
    depth_levels,
):
    lat, lon = lax.axis_size("lat"), lax.axis_size("lon")
    fields, _, oy, _ = ocean_state.shape
    cap = max(SUB, 2 * src_block.shape[0] // (lat * lon))
    slots, north, south = regrid(
        cap, lat, lon, src_block, dest_dev[:, 0], dest_block, coupling, atm_flux, sea_mask,
        intersection_weights, depth_levels, ocean_state, inverses,
    )
    in_plane = lax.all_to_all(slots, "lon", 0, 0, tiled=True)
    mixed, side, to_east, to_west = mix(depth_levels, ocean_state, inverses)
    halos = (
        shift(south, "lat", 1, False),
        shift(north, "lat", -1, False),
        shift(to_west, "lon", -1, True),
        shift(to_east, "lon", 1, True),
    )
    received = lax.all_to_all(collect(cap, fields, oy, lat, in_plane, (to_east, *halos[0:2])), "lat", 0, 0, tiled=True)
    return finish(received, depth_levels, mixed, side, halos)


def solution(mesh):
    placed = (
        P(None, "lat", "lon"),
        P("lat", "lon"),
        P(("lat", "lon")),
        P(("lat", "lon"), None),
        P(("lat", "lon")),
        P(("lat", "lon"), None, None),
        P(),
        P(None, "lat", "lon", None, None),
        P(None, None, "lat", "lon"),
        P("lat", "lon"),
    )
    return jax.shard_map(
        on_device,
        mesh=mesh,
        in_specs=placed,
        out_specs=P(None, None, "lat", "lon"),
        check_vma=False,
    )
```

```python
import functools

import jax
import jax.numpy as jnp
from jax import lax
from jax.experimental import pallas as pl
from jax.experimental.pallas import tpu as pltpu
from jax.sharding import PartitionSpec as P

diffusion_rate = 0.2
LANES = 128
HALF = 64
SUB = 8
f32 = jnp.float32
bf16 = jnp.bfloat16
HBM = pl.BlockSpec(memory_space=pltpu.HBM)
VMEM = pl.BlockSpec(memory_space=pltpu.VMEM)


def split(x):
    high = x.astype(bf16)
    return high, (x - high.astype(f32)).astype(bf16)


def in_hbm(*arrays):
    return [pltpu.with_memory_space_constraint(x, pltpu.HBM) for x in arrays]


def iota(shape, dim):
    return lax.broadcasted_iota(jnp.int32, shape, dim)


def matmul(a, b):
    return jnp.dot(a, b, preferred_element_type=f32)


def padded_rows(x, rows):
    return x if x.shape[0] == rows else jnp.concatenate([x, jnp.zeros((rows - x.shape[0], LANES), x.dtype)], axis=0)


def solve_row(a, x, active):
    levels = x.shape[0]
    a_high, a_low = split(a)
    r_high, r_low = split(jnp.where(active, x, 0.0))
    product = matmul(jnp.concatenate([a_high, a_low], axis=0), jnp.concatenate([r_high, r_low], axis=1))
    solved = product[:levels, :LANES] + (product[levels:, :LANES] + product[:levels, LANES:])
    return jnp.where(active, solved, x)


def outer_messages(refs, depth_ref, state, inv):
    _, fields, levels, _ = state.shape
    oy = depth_ref.shape[0]
    level = iota((levels, LANES), 0)
    for k, (row, ref) in enumerate(zip((0, oy - 1), refs)):
        depth = depth_ref[row : row + 1, :]
        names = jnp.zeros((levels, LANES), f32)
        for q in range(fields):
            a = inv[k, q]
            ref[q, 0:levels] = solve_row(a, state[k, q], level < depth)
            names = jnp.where(iota((levels, LANES), 1) == q, a[:, 0:1], names)
        names = padded_rows(names, LANES).T
        for q in range(fields):
            ref[q, levels : levels + SUB] = jnp.concatenate(
                [depth.astype(f32), names[q : q + 1], jnp.zeros((SUB - 2, LANES), f32)], axis=0
            )


def extra_rows(lat):
    return -(-3 * lat // SUB) * SUB


def regrid_kernel(
    cap, lat, lon, oy, batch,
    src_h, dev_h, blk_h, coupling_h, atm_h, mask_h, weights_h, depth_h, state_h, inv_h,
    out_h, north, south,
    out, rows, ids, count, src, dev, blk, coupling, atm, mask, weights, depth_ref, state, inv,
    small_sem, outer_sem, big_sem, out_sem,
):
    fluxes, atm_rows, _ = atm.shape
    fields = coupling.shape[0]
    devices = lat * lon
    per = fields * cap
    slot_rows = lat * per
    parts = weights.shape[0] // batch
    ahead = min(3, parts)

    def big(k):
        here = pl.ds(k * batch, batch)
        return pltpu.make_async_copy(weights_h.at[here], weights.at[here], big_sem.at[k])

    small = [
        pltpu.make_async_copy(a, b, small_sem.at[k])
        for k, (a, b) in enumerate(
            (
                (coupling_h, coupling), (atm_h, atm), (mask_h, mask),
                (src_h, src), (dev_h, dev), (blk_h, blk),
            )
        )
    ]
    outer = [pltpu.make_async_copy(depth_h, depth_ref, outer_sem.at[2 * fields, 0])]
    for q in range(fields):
        for k, row in enumerate((0, oy - 1)):
            outer.append(pltpu.make_async_copy(state_h.at[q, :, row, :], state.at[k, q], outer_sem.at[2 * q, k]))
            outer.append(pltpu.make_async_copy(inv_h.at[q, row, 0], inv.at[k, q], outer_sem.at[2 * q + 1, k]))
    for copy in small + outer:
        copy.start()
    for k in range(ahead):
        big(k).start()

    def clear_count(d, carry):
        count[d] = 0
        return carry

    def clear(b, carry):
        out[b] = jnp.zeros(out.shape[1:], f32)
        return carry

    lax.fori_loop(0, devices, clear_count, 0)
    lax.fori_loop(0, lon, clear, 0)
    ids[...] = jnp.full(ids.shape, -1, jnp.int32)
    for copy in small:
        copy.wait()
    for tile in range(atm_rows // 16):
        here = slice(tile * 16, tile * 16 + 16)
        sea = mask[here, :].astype(f32)
        flux = [atm[f, here, :].astype(f32) * sea for f in range(fluxes)]
        for q in range(fields):
            total = coupling[q, 0] * flux[0]
            for f in range(1, fluxes):
                total = total + coupling[q, f] * flux[f]
            high = total.astype(bf16).astype(f32)
            rows[pl.ds(tile * 16 * SUB + q, 16, stride=SUB), :] = high
            rows[pl.ds(tile * 16 * SUB + fields + q, 16, stride=SUB), :] = total - high

    for copy in outer:
        copy.wait()
    outer_messages((north, south), depth_ref, state, inv)

    lane = iota((1, LANES), 1)
    lane_slot = (lane % per) // fields
    lane_row = (lane % fields) * oy

    bits = lon.bit_length() - 1

    def place(d):
        if isinstance(d, int):
            return d // lon, d % lon
        if lon == 1 << bits:
            return lax.shift_right_logical(d, bits), d & (lon - 1)
        return lax.div(d, lon), lax.rem(d, lon)

    def extra(d, k):
        a, b = place(d)
        return b, pl.ds(slot_rows + 3 * a + k, 1)

    def slots(d):
        a, b = place(d)
        return padded_rows(out[b, a * per : (a + 1) * per, :], HALF)

    def part(k):
        big(k).wait()
        if k + ahead < parts:
            big(k + ahead).start()

        for u in range(0, batch, 2):
            p = k * batch + u
            x = jnp.concatenate(
                [rows[pl.ds(pl.multiple_of(src[p + v] * SUB, SUB), SUB), :] for v in range(2)], axis=0
            ).astype(bf16)
            both = matmul(x, jnp.concatenate([weights[p], weights[p + 1]], axis=1))
            for v in range(2):
                d = dev[p + v]
                slot = jnp.minimum(count[d], cap - 1)
                count[d] = slot + 1
                half = both[v * SUB : v * SUB + SUB, v * LANES : (v + 1) * LANES]
                a, b = place(d)
                out[b, pl.ds(a * per + slot * fields, fields), :] = half[0:fields] + half[fields : 2 * fields]
                line = ids[pl.ds(d, 1), :]
                ids[pl.ds(d, 1), :] = jnp.where(lane_slot == slot, lane_row + blk[p + v], line)

    for k in range(parts):
        part(k)

    def send(k, start, stop):
        return pltpu.make_async_copy(out.at[:, start:stop, :], out_h.at[:, start:stop, :], out_sem.at[k])

    send(0, 0, slot_rows).start()

    def halo(k):
        d = 2 * k
        turned = jnp.concatenate([slots(d + u) for u in range(2)], axis=0).T
        first, last = turned[0:1], turned[LANES - 1 : LANES]
        first_swapped = pltpu.roll(turned[0:SUB], HALF, 1)[0:1]
        last_swapped = pltpu.roll(turned[LANES - SUB : LANES], HALF, 1)[SUB - 1 : SUB]
        for u in range(2):
            _, b = place(d + u)
            east = d + u - b + (b + 1) % lon
            west = d + u - b + (b - 1) % lon
            out[extra(d + u, 0)] = ids[pl.ds(d + u, 1), :].astype(f32)
            sides = jnp.where(lane < HALF, ids[pl.ds(east, 1), :], ids[pl.ds(west, 1), :])
            out[extra(d + u, 1)] = sides.astype(f32)
            column = first if u == 0 else first_swapped
            out[extra(west, 2)] = jnp.where(lane < HALF, column, out[extra(west, 2)])
            column = last_swapped if u == 0 else last
            out[extra(east, 2)] = jnp.where(lane < HALF, out[extra(east, 2)], column)

    for k in range(devices // 2):
        halo(k)
    send(1, slot_rows, out.shape[1]).start()
    send(0, 0, slot_rows).wait()
    send(1, slot_rows, out.shape[1]).wait()


def regrid(cap, lat, lon, src, dev, blk, coupling, atm, mask, weights, depth, ocean, inverses):
    pairs, cells, width = weights.shape
    fields, levels, oy, ox = ocean.shape
    message = jax.ShapeDtypeStruct((fields, levels + SUB, ox), f32)
    batch = 32
    devices = lat * lon
    tall = lat * fields * cap + extra_rows(lat)
    return pl.pallas_call(
        functools.partial(regrid_kernel, cap, lat, lon, oy, batch),
        in_specs=[HBM] * 10,
        out_specs=[HBM, VMEM, VMEM],
        out_shape=[pltpu.HBM((lon, tall, LANES), f32), message, message],
        scratch_shapes=[
            pltpu.VMEM((lon, tall, LANES), f32),
            pltpu.VMEM((atm.shape[1] * SUB, LANES), f32),
            pltpu.VMEM((devices, LANES), jnp.int32),
            pltpu.SMEM((devices,), jnp.int32),
            pltpu.SMEM(src.shape, jnp.int32),
            pltpu.SMEM(dev.shape, jnp.int32),
            pltpu.SMEM(blk.shape, jnp.int32),
            pltpu.SMEM(coupling.shape, f32),
            pltpu.VMEM(atm.shape, bf16),
            pltpu.VMEM(mask.shape, jnp.int32),
            pltpu.VMEM(weights.shape, bf16),
            pltpu.VMEM(depth.shape, jnp.int32),
            pltpu.VMEM((2, fields, levels, ox), f32),
            pltpu.VMEM((2, fields, levels, levels), f32),
            pltpu.SemaphoreType.DMA((6,)),
            pltpu.SemaphoreType.DMA((2 * fields + 1, 2)),
            pltpu.SemaphoreType.DMA((pairs // batch,)),
            pltpu.SemaphoreType.DMA((2,)),
        ],
        compiler_params=pltpu.CompilerParams(vmem_limit_bytes=20 << 20),
        cost_estimate=pl.CostEstimate(flops=2 * 8 * pairs * cells * width, bytes_accessed=10 << 20, transcendentals=0),
        name="regrid",
    )(*in_hbm(src, dev, blk, coupling, atm, mask, weights, depth, ocean, inverses))


def mix_kernel(
    depth_h, state_h, inv_h, mixed_h, side_h, to_east, to_west, depth_ref, state, mixed, inv, side, in_sems, out_sems
):
    fields, oy, levels, _ = mixed.shape
    depth_copy = pltpu.make_async_copy(depth_h, depth_ref, in_sems.at[2 * fields, 0])
    depth_copy.start()

    def load(q, c):
        for i in range(SUB):
            row = c * SUB + i
            pltpu.make_async_copy(state_h.at[q, :, row, :], state.at[q, row], in_sems.at[2 * q, c]).start()
        here = (q, pl.ds(c * SUB, SUB))
        pltpu.make_async_copy(inv_h.at[here], inv.at[here], in_sems.at[2 * q + 1, c]).start()

    for c in range(oy // SUB):
        load(0, c)
    depth_copy.wait()
    level = iota((levels, LANES), 0)
    lane = iota((levels, LANES), 1)
    line = iota((1, LANES), 1)
    edge_depth = jnp.zeros((SUB, LANES), f32)
    for i in range(oy):
        turned = pltpu.roll(jnp.broadcast_to(depth_ref[i : i + 1, :].astype(f32), (SUB, LANES)), 2 * i + 1, 1)
        edge_depth = jnp.where(line // 2 == i, turned, edge_depth)

    def field(q, carry):
        @pl.when(q + 1 < fields)
        def _():
            for c in range(oy // SUB):
                load(q + 1, c)

        cells = jnp.zeros((levels, LANES), f32)
        for c in range(oy // SUB):
            here = (q, pl.ds(c * SUB, SUB))
            pltpu.make_async_copy(mixed_h.at[here], state.at[here], in_sems.at[2 * q, c]).wait()
            pltpu.make_async_copy(inv_h.at[here], inv.at[here], in_sems.at[2 * q + 1, c]).wait()
            for row in range(c * SUB, (c + 1) * SUB):
                a = inv[q, row, 0]
                m = solve_row(a, state[q, row], level < depth_ref[row : row + 1, :])
                mixed[q, row] = m
                cells = jnp.where(lane // 2 == row, pltpu.roll(m, 2 * row + 1, 1), cells)
                cells = jnp.where(lane // 2 == HALF // 2 + row, a[:, 0:1], cells)
            pltpu.make_async_copy(mixed.at[here], mixed_h.at[here], out_sems.at[q]).start()
        side[q, 0:levels] = cells
        side[q, levels : levels + SUB] = edge_depth
        return carry

    lax.fori_loop(0, fields, field, 0)
    side_copy = pltpu.make_async_copy(side, side_h, out_sems.at[fields])
    side_copy.start()
    even = line % 2 == 0
    for k in range(fields // 2):
        to_east[k] = jnp.where(even, side[2 * k], pltpu.roll(side[2 * k + 1], 1, 1))
        to_west[k] = jnp.where(even, pltpu.roll(side[2 * k], LANES - 1, 1), side[2 * k + 1])
    for q in range(fields):
        pltpu.make_async_copy(mixed.at[q], mixed_h.at[q], out_sems.at[q]).wait()
    side_copy.wait()


def mix(depth, state, inverses):
    fields, levels, oy, ox = state.shape
    edge_shape = jax.ShapeDtypeStruct((fields // 2, levels + SUB, ox), f32)
    full = (fields, oy, levels, ox)
    return pl.pallas_call(
        mix_kernel,
        in_specs=[HBM] * 3,
        out_specs=[HBM] * 2 + [VMEM] * 2,
        out_shape=[pltpu.HBM(full, f32), pltpu.HBM((fields, levels + SUB, ox), f32), edge_shape, edge_shape],
        scratch_shapes=[
            pltpu.VMEM(depth.shape, jnp.int32),
            pltpu.VMEM(full, f32),
            pltpu.VMEM(full, f32),
            pltpu.VMEM(inverses.shape, f32),
            pltpu.VMEM((fields, levels + SUB, ox), f32),
            pltpu.SemaphoreType.DMA((2 * fields + 1, oy // SUB)),
            pltpu.SemaphoreType.DMA((fields + 1,)),
        ],
        compiler_params=pltpu.CompilerParams(vmem_limit_bytes=32 << 20),
        cost_estimate=pl.CostEstimate(flops=2 * 4 * fields * oy * levels * levels * ox, bytes_accessed=16 << 20, transcendentals=0),
        name="mix",
    )(*in_hbm(depth, state, inverses))


def collect_kernel(cap, fields, oy, recv, after_mix, after_north, after_south, out):
    lat = out.shape[0]
    lon = recv.shape[0]
    per = fields * cap
    slot_rows = lat * per
    group = LANES // per
    forced = fields * oy
    square_row = iota((LANES, LANES), 0).astype(f32)
    line = iota((1, LANES), 1)
    row = iota((2 * oy, LANES), 0).astype(f32)
    lane_base = ((line % fields) * oy).astype(f32)
    lane_side = (line // HALF).astype(f32)
    small_row, small_lane = iota((SUB, LANES), 0), iota((SUB, LANES), 1)
    pick = jnp.where((small_lane % fields == small_row) & (small_lane % HALF < per), 1.0, 0.0).astype(bf16)
    nothing = jnp.zeros((fields, LANES), f32)
    for a in range(lat):
        total = jnp.zeros((LANES, 2 * LANES), f32)
        for tile in range(lon // group):
            places = [tile * group + s for s in range(group)]
            named = slice(slot_rows + 3 * a, slot_rows + 3 * a + 1)
            ids = recv[places[0], named, :]
            for s in range(1, group):
                ids = jnp.where(line // per == s, recv[places[s], named, :], ids)
            hot = jnp.where(square_row == ids, 1.0, 0.0).astype(bf16)
            high, low = split(jnp.concatenate([recv[p, a * per : (a + 1) * per, :] for p in places], axis=0))
            total = total + matmul(hot, jnp.concatenate([high, low], axis=1))
        total = total[:, :LANES] + total[:, LANES:]
        out[a, 0:forced] = total
        if a == 0:
            out[a, forced : forced + fields] = nothing
        if a == lat - 1:
            out[a, forced + fields : forced + 2 * fields] = nothing
        for q in range(fields):
            if a + 1 < lat:
                out[a + 1, forced + q : forced + q + 1] = total[q * oy + oy - 1 : q * oy + oy]
            if a > 0:
                out[a - 1, forced + fields + q : forced + fields + q + 1] = total[q * oy : q * oy + 1]
        spread = jnp.zeros((2 * oy, LANES), f32)
        for b in range(lon):
            extra = recv[b, slot_rows + 3 * a + 1 : slot_rows + 3 * a + 3, :]
            place = 2.0 * (extra[0:1] - lane_base) + lane_side
            spread = spread + jnp.where(place == row, extra[1:2], 0.0)
        high, low = split(padded_rows(spread, LANES).T)
        out[a, forced + SUB : forced + 2 * SUB] = matmul(pick, high) + matmul(pick, low)


def collect(cap, fields, oy, lat, received, after):
    return pl.pallas_call(
        functools.partial(collect_kernel, cap, fields, oy),
        in_specs=[VMEM] + [pl.BlockSpec(memory_space=pl.ANY)] * 3,
        out_specs=VMEM,
        out_shape=jax.ShapeDtypeStruct((lat, fields * oy + 2 * SUB, LANES), f32),
        compiler_params=pltpu.CompilerParams(vmem_limit_bytes=16 << 20),
        name="collect",
    )(received, *after)


def finish_kernel(
    recv, depth_ref, mixed_h, own_h, north_h, south_h, east, west,
    out_h, own, north, south, forcing, z, keep, halo, z_north, z_south, mixed, stage, edge_sems, in_sems, out_sems,
):
    fields, oy, levels, _ = mixed.shape
    level = iota((levels, LANES), 0)
    lanes = iota((levels, LANES), 1)
    square_row = iota((LANES, LANES), 0)
    square_lane = iota((LANES, LANES), 1)
    line = iota((1, LANES), 1)
    even = line % 2 == 0
    edges = [
        pltpu.make_async_copy(a, b, edge_sems.at[k])
        for k, (a, b) in enumerate(((own_h, own), (north_h, north), (south_h, south)))
    ]
    for copy in edges:
        copy.start()

    def load(q, c):
        here = (q, pl.ds(c * SUB, SUB))
        return pltpu.make_async_copy(mixed_h.at[here], mixed.at[here], in_sems.at[q, c])

    for c in range(oy // SUB):
        load(0, c).start()

    total = recv[0]
    for a in range(1, recv.shape[0]):
        total = total + recv[a]
    forced_rows = fields * oy
    forcing[...] = total[0:forced_rows]
    rows = total[forced_rows : forced_rows + SUB]
    columns = total[forced_rows + SUB :]

    for copy in edges:
        copy.wait()
    depth = depth_ref[...]
    wide = iota((oy, LANES), 1)

    def upright(ref):
        value = jnp.where(wide == 2 * iota((oy, LANES), 0), ref[0, levels : levels + 1, :], 0.0)
        return jnp.sum(value, axis=1, keepdims=True).astype(jnp.int32)

    to_east = jnp.where(wide == LANES - 1, upright(east), pltpu.roll(depth, LANES - 1, 1))
    to_west = jnp.where(wide == 0, upright(west), pltpu.roll(depth, 1, 1))
    to_north = jnp.concatenate([north[0, levels : levels + 1, :].astype(jnp.int32), depth[: oy - 1]], axis=0)
    to_south = jnp.concatenate([depth[1:], south[0, levels : levels + 1, :].astype(jnp.int32)], axis=0)
    for i in range(oy):
        sides = jnp.where(level < to_east[i : i + 1], diffusion_rate, 0.0)
        for other in (to_west, to_north, to_south):
            sides = sides + jnp.where(level < other[i : i + 1], diffusion_rate, 0.0)
        keep[i] = 1.0 - sides

    def outer(target, ref, start):
        names = padded_rows(
            jnp.concatenate([ref[q, levels + 1 : levels + 2, :] for q in range(fields)], axis=0), LANES
        ).T
        active = level < ref[0, levels : levels + 1, :].astype(jnp.int32)
        for q in range(fields):
            value = ref[q, 0:levels] + names[0:levels, q : q + 1] * rows[start + q : start + q + 1]
            target[q] = jnp.where(active, value, 0.0)

    outer(z_north, north, 0)
    outer(z_south, south, fields)
    for q in range(fields):
        if q % 2:
            cells = jnp.where(even, pltpu.roll(east[q // 2], LANES - 1, 1), west[q // 2])
        else:
            cells = jnp.where(even, east[q // 2], pltpu.roll(west[q // 2], 1, 1))
        names = pltpu.roll(cells, HALF, 1)
        active = level < cells[levels : levels + 1].astype(jnp.int32)
        value = cells[0:levels] + names[0:levels] * columns[q : q + 1]
        halo[q] = jnp.where(active & (line < 2 * oy), value, 0.0)

    both = jnp.where((square_row == square_lane + 1) | (square_row == square_lane - 1), 1.0, 0.0).astype(bf16)
    both = jnp.concatenate([both, both], axis=0)
    ones = jnp.ones((LANES, LANES), bf16)
    block = 2 * SUB
    ends = (lanes == 0) | (lanes == LANES - 1)

    def field(q):
        if q + 1 < fields:
            for c in range(oy // SUB):
                load(q + 1, c).start()

        z[0] = z_north[q]
        z[oy + 1] = z_south[q]
        edge = halo[q]
        names = own[q, 0:levels]
        high = names.astype(bf16).astype(f32)
        names = jnp.where(even, high, names - high)

        def solve(c):
            rows_here = range(c * block, (c + 1) * block)
            for part in range(rows_here.start // SUB, rows_here.stop // SUB):
                load(q, part).wait()
            first = matmul(
                jnp.concatenate(
                    [(names * jnp.where(line // 2 == HALF // 2 + r, 1.0, 0.0)).astype(bf16) for r in rows_here], axis=0
                ),
                ones,
            )
            for i, r in enumerate(rows_here):
                first_here = first[i * levels : (i + 1) * levels]
                forced = mixed[q, r] + first_here * forcing[pl.ds(q * oy + r, 1), :]
                z[r + 1] = jnp.where(level < depth_ref[r : r + 1, :], forced, 0.0)

        def diffuse(c):
            start = c * block
            high, low = split(z[start + 1 : start + 1 + block].reshape(block * levels, LANES))
            sides = matmul(jnp.concatenate([high, low], axis=1), both)
            for i in range(block):
                r = start + i
                outside = jnp.where(ends, pltpu.roll(edge, LANES - 1 - 2 * r, 1), 0.0)
                around = (z[r] + z[r + 2]) + (sides[i * levels : (i + 1) * levels] + outside)
                active = level < depth_ref[r : r + 1, :]
                stage[q, r] = jnp.where(active, z[r + 1] * keep[r] + diffusion_rate * around, mixed[q, r])
            for r in range(start, start + block):
                pltpu.make_async_copy(stage.at[q, r], out_h.at[q, :, r, :], out_sems.at[q]).start()

        solve(0)
        for c in range(1, oy // block):
            solve(c)
            diffuse(c - 1)
        diffuse(oy // block - 1)

    for q in range(fields):
        field(q)
    for q in range(fields):
        pltpu.make_async_copy(stage.at[q], mixed_h.at[q], out_sems.at[q]).wait()


def finish(received, depth, mixed, own, halos):
    fields, oy, levels, ox = mixed.shape
    edge = pltpu.VMEM((fields, levels, ox), f32)
    message = pltpu.VMEM((fields, levels + SUB, ox), f32)
    full = pltpu.VMEM((fields, oy, levels, ox), f32)
    return pl.pallas_call(
        finish_kernel,
        in_specs=[VMEM] * 2 + [HBM] * 4 + [VMEM] * 2,
        out_specs=HBM,
        out_shape=pltpu.HBM((fields, levels, oy, ox), f32),
        scratch_shapes=[
            message,
            message,
            message,
            pltpu.VMEM((fields * oy, ox), f32),
            pltpu.VMEM((oy + 2, levels, ox), f32),
            pltpu.VMEM((oy, levels, ox), f32),
            edge,
            edge,
            edge,
            full,
            full,
            pltpu.SemaphoreType.DMA((3,)),
            pltpu.SemaphoreType.DMA((fields, oy // SUB)),
            pltpu.SemaphoreType.DMA((fields,)),
        ],
        compiler_params=pltpu.CompilerParams(vmem_limit_bytes=32 << 20),
        cost_estimate=pl.CostEstimate(flops=20 * fields * oy * levels * ox, bytes_accessed=12 << 20, transcendentals=0),
        name="finish",
    )(received, depth, *in_hbm(mixed, own, *halos[0:2]), *halos[2:])


def shift(x, axis, step, wrap):
    count = lax.axis_size(axis)
    pairs = [(i, (i + step) % count) for i in range(count) if wrap or 0 <= i + step < count]
    return lax.ppermute(x, axis, pairs)


def on_device(
    atm_flux, sea_mask, src_block, dest_dev, dest_block, intersection_weights, coupling, inverses, ocean_state,
    depth_levels,
):
    lat, lon = lax.axis_size("lat"), lax.axis_size("lon")
    fields, _, oy, _ = ocean_state.shape
    cap = max(SUB, 2 * src_block.shape[0] // (lat * lon))
    slots, north, south = regrid(
        cap, lat, lon, src_block, dest_dev[:, 0], dest_block, coupling, atm_flux, sea_mask,
        intersection_weights, depth_levels, ocean_state, inverses,
    )
    in_plane = lax.all_to_all(slots, "lon", 0, 0, tiled=True)
    mixed, side, to_east, to_west = mix(depth_levels, ocean_state, inverses)
    halos = (
        shift(south, "lat", 1, False),
        shift(north, "lat", -1, False),
        shift(to_west, "lon", -1, True),
        shift(to_east, "lon", 1, True),
    )
    received = lax.all_to_all(collect(cap, fields, oy, lat, in_plane, (to_east, *halos[0:2])), "lat", 0, 0, tiled=True)
    return finish(received, depth_levels, mixed, side, halos)


def solution(mesh):
    placed = (
        P(None, "lat", "lon"),
        P("lat", "lon"),
        P(("lat", "lon")),
        P(("lat", "lon"), None),
        P(("lat", "lon")),
        P(("lat", "lon"), None, None),
        P(),
        P(None, "lat", "lon", None, None),
        P(None, None, "lat", "lon"),
        P("lat", "lon"),
    )
    return jax.shard_map(
        on_device,
        mesh=mesh,
        in_specs=placed,
        out_specs=P(None, None, "lat", "lon"),
        check_vma=False,
    )
```
